32 devices in a mesh: section: 4 (over x, core), tp: 8 (over z, y).
Axes of the slice: x: 2, y: 2, z: 4, core: 2. Of those that a mesh axis runs over, the one named last changes fastest.
Arguments:
- grad_attn: bfloat16 [4, 8, 128, 128], P('section', 'tp'), may hold values from -6 to 6
- w_value: bfloat16 [4, 12288, 1024], P('section', 'tp'), may hold values from -0.0546875 to 0.0546875
- probs_own: bfloat16 [4, 8, 128, 128], P('section', 'tp'), may hold values from 0.0009994507 to 0.25
- probs_spare: bfloat16 [4, 8, 128, 128], P('section', 'tp'), may hold values from 0.0009994507 to 0.25
- evicted: int32 [4, 4], P('section'), may hold values from 0 to 1, as said below
- layer_input: bfloat16 [4, 128, 12288], P('section', None, 'tp'), may hold values from -6 to 6
- gain: float32 [4, 12288], P('section', 'tp'), may hold values from 0.1 to 1.9
Outputs:
- handed: bfloat16 [4, 128, 12288], P('section', None, 'tp')
The draws below stay inside these ranges and needn't reach their ends.
Inputs may be any that keep to these rules, and one draw needn't show every extreme that they name: Section 0 has every tile evicted.
All inputs are finite; a program needn't handle non-finite values.
Results may differ from the reference program's by a relative error of at most 0.0049.
Values may be sent and summed in bfloat16 or wider, within the bound.
No kernel may reach another device: no remote copies, remote signals or barrier semaphores. Data moves between devices by JAX's collectives and lax.ppermute only.
A program may use at most 64 MiB of HBM per device.

```python
import math
import jax
import jax.numpy as jnp
from jax import lax

D = 12288
HD = 128
TOK = 128
TILES = 4
SECTIONS = 4
HEADS = 8


def draw_evicted(key, part):
    values = jax.random.randint(key, (SECTIONS, TILES), 0, SECTIONS)
    section_rows = lax.broadcasted_iota(jnp.int32, (SECTIONS, TILES), 0)
    return (values >= section_rows).astype(jnp.int32)


def shard_levels(stream_key, extent, pieces, smallest, top_value):
    loudness, own = 1.0, jax.random.fold_in(stream_key, 6)
    for axis_at, shards_of in pieces:
        heights = jnp.exp(jax.random.uniform(jax.random.fold_in(own, axis_at), (shards_of,), jnp.float32, smallest / len(pieces), top_value / len(pieces)))
        loudness = loudness * jnp.repeat(heights, extent[axis_at] // shards_of).reshape([-1 if axis == axis_at else 1 for axis in range(len(extent))])
    return loudness


def noise(rng, shape, scale, limit, pieces=(), held_as=jnp.bfloat16):
    entries = scale * jax.random.normal(rng, shape, jnp.float32)
    if pieces:
        entries = entries * shard_levels(rng, shape, pieces, -0.22, 0.18)
    return jnp.clip(entries, -limit, limit).astype(held_as)


def setup_inputs(seed: int = 0) -> dict:
    splits = jax.random.split(jax.random.key(seed), 8)
    return {
        "grad_attn": noise(splits[0], (SECTIONS, HEADS, TOK, HD), 1.0, 6.0, ((0, 4), (1, 8))),
        "w_value": noise(splits[1], (SECTIONS, D, HEADS * HD), D ** -0.5, 0.0546875, ((0, 4), (1, 8))),
        "probs_own": jnp.clip(jnp.exp(math.log(0.25) - 5.5220104 * jax.random.uniform(splits[2], (SECTIONS, HEADS, TOK, TOK), jnp.float32) ** shard_levels(splits[2], (SECTIONS, HEADS, TOK, TOK), ((0, 4), (1, 8)), -0.2, 0.2)), 0.0009994507, 0.25).astype(jnp.bfloat16),
        "probs_spare": jnp.clip(jnp.exp(math.log(0.25) - 5.5220104 * jax.random.uniform(splits[3], (SECTIONS, HEADS, TOK, TOK), jnp.float32) ** shard_levels(splits[3], (SECTIONS, HEADS, TOK, TOK), ((0, 4), (1, 8)), -0.2, 0.2)), 0.0009994507, 0.25).astype(jnp.bfloat16),
        "evicted": draw_evicted(jax.random.fold_in(splits[7], 71), 0),
        "layer_input": noise(splits[5], (SECTIONS, TOK, D), 1.0, 6.0, ((0, 4), (2, 8))),
        "gain": jnp.clip(1.0 + 0.18 * jax.random.normal(splits[6], (SECTIONS, D), jnp.float32), 0.1, 1.9),
    }


def section_branch(args):
    grad_attn, weights, probs, flags, spare, inputs, gain = args
    mixed = jnp.where(flags[None, :, None] == 1, spare, probs)
    grad_value = jnp.einsum('hqk,hqd->hkd', mixed.astype(jnp.float32), grad_attn.astype(jnp.float32)).astype(jnp.bfloat16)
    flat = jnp.transpose(grad_value, (1, 0, 2)).reshape(TOK, HEADS * HD)
    grad_normed = jnp.dot(flat, weights.T, preferred_element_type=jnp.float32)
    values = inputs.astype(jnp.float32)
    squares = lax.optimization_barrier(jnp.sum(values * values, axis=1))
    inv = 1.0 / jnp.sqrt(squares / D + 1e-05)
    inner = lax.optimization_barrier(jnp.sum(gain[None, :] * grad_normed * values, axis=1))
    branch = gain[None, :] * grad_normed * inv[:, None] - values * (inner * inv ** 3 / D)[:, None]
    return branch.astype(jnp.bfloat16)

def reference(grad_attn, w_value, probs_own, probs_spare, evicted, layer_input, gain):
    flags = jnp.repeat(evicted, TOK // TILES, axis=1)
    spare = jnp.roll(probs_spare, -(SECTIONS // 2), axis=0)
    branch = lax.map(section_branch, (grad_attn, w_value, probs_own, flags, spare, layer_input, gain))
    return jnp.roll(branch, -1, axis=0)
```

```python
import jax
import jax.numpy as jnp
from jax import lax
from jax.sharding import PartitionSpec as P

D = 12288


def passed_along(block, axis, distance):
    devices = range(lax.axis_size(axis))
    route = [((i - distance) % len(devices), i) for i in devices]
    return lax.ppermute(block, axis, route)


def summed_over(block, axis):
    total = block
    for distance in range(1, lax.axis_size(axis)):
        total = total + passed_along(block, axis, distance)
    return total


def per_device(grad_attn, w_value, probs_own, probs_spare, evicted, layer_input, gain):
    sections = lax.axis_size("section")
    count = lax.axis_size("tp")
    fetched = passed_along(probs_spare, "section", sections // 2)
    tokens = probs_own.shape[2]
    head_size = grad_attn.shape[3]
    flags = jnp.repeat(evicted[0], tokens // evicted.shape[1])
    mixed = jnp.where(flags[None, :, None] == 1, fetched[0], probs_own[0])
    values = layer_input[0].astype(jnp.float32)
    scales = gain[0]
    grad_value = jnp.einsum(
        "qk,qd->kd", mixed[0], grad_attn[0, 0], preferred_element_type=jnp.float32
    ).astype(jnp.bfloat16)
    copies = jnp.broadcast_to(grad_value[None], (count, tokens, head_size))
    grads = lax.all_to_all(copies, "tp", 0, 0, tiled=True)
    flat = jnp.transpose(grads, (1, 0, 2)).reshape(tokens, count * head_size)
    grad_normed = lax.dot_general(
        flat, w_value[0], (((1,), (1,)), ((), ())), preferred_element_type=jnp.float32
    )
    scaled = scales[None, :] * grad_normed
    sums = jnp.stack([jnp.sum(values * values, axis=1), jnp.sum(scaled * values, axis=1)])
    squares, inner = summed_over(sums, "tp")
    inv = 1.0 / jnp.sqrt(squares / D + 1e-05)
    branch = scaled * inv[:, None] - values * (inner * inv**3 / D)[:, None]
    branch = branch.astype(jnp.bfloat16)[None]
    return passed_along(branch, "section", -1)


def solution(mesh):
    in_specs = (
        P("section", "tp", None, None),
        P("section", "tp", None),
        P("section", "tp", None, None),
        P("section", "tp", None, None),
        P("section", None),
        P("section", None, "tp"),
        P("section", "tp"),
    )
    out_specs = P("section", None, "tp")
    return jax.shard_map(
        per_device, mesh=mesh, in_specs=in_specs, out_specs=out_specs, check_vma=False
    )
```

```python
import functools

import jax
import jax.numpy as jnp
from jax import lax
from jax.experimental import pallas as pl
from jax.experimental.pallas import tpu as pltpu
from jax.sharding import PartitionSpec as P

D = 12288
LANES = 128


def passed_along(block, axis, distance):
    devices = range(lax.axis_size(axis))
    route = [((i - distance) % len(devices), i) for i in devices]
    return lax.ppermute(block, axis, route)


def swapped(block, axis, mask):
    return lax.ppermute(block, axis, [(i ^ mask, i) for i in range(lax.axis_size(axis))])


def in_vmem(array):
    return pltpu.with_memory_space_constraint(array, pltpu.VMEM)


def vmem_specs(count):
    return [pl.BlockSpec(memory_space=pltpu.VMEM)] * count


def mix_kernel(evicted_ref, own_ref, spare_ref, grad_ref, out_ref):
    tiles = evicted_ref.shape[1]
    rows = own_ref.shape[0] // tiles
    mixed = []
    for tile in range(tiles):
        part = pl.ds(tile * rows, rows)
        mixed.append(jnp.where(evicted_ref[0, tile] == 1, spare_ref[part, :], own_ref[part, :]))
    out_ref[...] = lax.dot_general(
        jnp.concatenate(mixed, axis=0),
        grad_ref[...],
        (((0,), (0,)), ((), ())),
        preferred_element_type=jnp.float32,
    ).astype(out_ref.dtype)


def value_gradient(evicted, own, spare, grad):
    return pl.pallas_call(
        mix_kernel,
        out_shape=pltpu.VMEM(grad.shape, jnp.bfloat16),
        in_specs=[pl.BlockSpec(memory_space=pltpu.SMEM)] + vmem_specs(3),
        out_specs=pl.BlockSpec(memory_space=pltpu.VMEM),
        compiler_params=pltpu.CompilerParams(vmem_limit_bytes=4 << 20),
    )(evicted, in_vmem(own), in_vmem(spare), in_vmem(grad))


def as_row(column):
    return jnp.broadcast_to(column, (column.shape[0], column.shape[0])).T[:1]


def project_kernel(head_of, counts, *refs):
    blocks = refs[: len(counts)]
    weight_ref, input_ref, gain_ref, scaled_ref, sums_ref, flat = refs[len(counts) :]
    place = 0
    for ref, count in zip(blocks, counts):
        for j in range(count):
            start = pl.multiple_of(head_of(place) * LANES, LANES)
            flat[:, pl.ds(start, LANES)] = ref[j]
            place += 1
    features = weight_ref.shape[0]
    tile = 256 if features % 256 == 0 else features
    tokens = input_ref.shape[0]
    squares = jnp.zeros((tokens, tile), jnp.float32)
    inner = jnp.zeros((tokens, tile), jnp.float32)
    for start in range(0, features, tile):
        part = pl.ds(start, tile)
        grad_normed = lax.dot_general(
            flat[...],
            weight_ref[part, :],
            (((1,), (1,)), ((), ())),
            preferred_element_type=jnp.float32,
        )
        scaled = grad_normed * gain_ref[:, part]
        values = input_ref[:, part].astype(jnp.float32)
        squares += values * values
        inner += scaled * values
        scaled_ref[:, part] = scaled.astype(scaled_ref.dtype)
    sums_ref[...] = jnp.concatenate(
        [as_row(jnp.sum(squares, axis=1, keepdims=True)), as_row(jnp.sum(inner, axis=1, keepdims=True))]
    )


def project(head_of, blocks, weights, inputs, gain):
    counts = tuple(block.shape[0] for block in blocks)
    tokens, features = inputs.shape
    return pl.pallas_call(
        functools.partial(project_kernel, head_of, counts),
        out_shape=(
            pltpu.VMEM((tokens, features), jnp.bfloat16),
            pltpu.VMEM((2, tokens), jnp.float32),
        ),
        in_specs=vmem_specs(len(blocks) + 3),
        out_specs=tuple(vmem_specs(2)),
        scratch_shapes=[pltpu.VMEM((tokens, weights.shape[1]), jnp.bfloat16)],
        compiler_params=pltpu.CompilerParams(vmem_limit_bytes=16 << 20),
    )(*[in_vmem(block) for block in blocks], in_vmem(weights), in_vmem(inputs), in_vmem(gain))


def finish_kernel(scaled_ref, input_ref, sums_ref, out_ref):
    tokens = scaled_ref.shape[0]
    sums = sums_ref[0]
    for j in range(1, sums_ref.shape[0]):
        sums = sums + sums_ref[j]
    inv = 1.0 / jnp.sqrt(sums[:1] / D + 1e-05)
    factor = sums[1:] * (inv * inv * inv) / D
    inv = jnp.broadcast_to(inv, (tokens, tokens)).T[:, :1]
    factor = jnp.broadcast_to(factor, (tokens, tokens)).T[:, :1]
    scaled = scaled_ref[...].astype(jnp.float32)
    values = input_ref[...].astype(jnp.float32)
    out_ref[...] = (scaled * inv - values * factor).astype(out_ref.dtype)


def finish(scaled, inputs, sums):
    return pl.pallas_call(
        finish_kernel,
        out_shape=jax.ShapeDtypeStruct(scaled.shape, jnp.bfloat16),
        in_specs=vmem_specs(3),
        out_specs=pl.BlockSpec(memory_space=pltpu.VMEM),
        compiler_params=pltpu.CompilerParams(vmem_limit_bytes=8 << 20),
    )(in_vmem(scaled), in_vmem(inputs), in_vmem(sums))


def gathered(block, axis):
    count = lax.axis_size(axis)
    if count != 8:
        return [lax.all_gather(block, axis)], lambda place: place
    far, near, side = 4, 2, 1
    own = block[None]
    a = swapped(own, axis, far)
    b = swapped(own, axis, near)
    c = swapped(jnp.concatenate([own, a]), axis, side)
    ab = swapped(a, axis, near)
    bc = swapped(c, axis, near)
    masks = (0, far, near, side, far | side, far | near, near | side, far | near | side)

    def head_of(place):
        return lax.axis_index(axis) ^ masks[place]

    return [own, a, b, c, ab, bc], head_of


def summed_copies(block, axis):
    copies = jnp.broadcast_to(block[None], (lax.axis_size(axis), *block.shape))
    return lax.all_to_all(copies, axis, 0, 0, tiled=True)


def per_device(grad_attn, w_value, probs_own, probs_spare, evicted, layer_input, gain):
    sections = lax.axis_size("section")
    spare = passed_along(probs_spare[0, 0], "section", sections // 2)
    next_input = passed_along(layer_input[0], "section", -1)
    grad_value = value_gradient(evicted, probs_own[0, 0], spare, grad_attn[0, 0])
    blocks, head_of = gathered(grad_value, "tp")
    scaled, sums = project(head_of, blocks, w_value[0], layer_input[0], gain)
    next_scaled = passed_along(scaled, "section", -1)
    next_sums = passed_along(sums, "section", -1)
    return finish(next_scaled, next_input, summed_copies(next_sums, "tp"))[None]


def solution(mesh):
    in_specs = (
        P("section", "tp", None, None),
        P("section", "tp", None),
        P("section", "tp", None, None),
        P("section", "tp", None, None),
        P("section", None),
        P("section", None, "tp"),
        P("section", "tp"),
    )
    out_specs = P("section", None, "tp")
    return jax.shard_map(
        per_device, mesh=mesh, in_specs=in_specs, out_specs=out_specs, check_vma=False
    )
```

```python
import functools

import jax
import jax.numpy as jnp
from jax import lax
from jax.experimental import pallas as pl
from jax.experimental.pallas import tpu as pltpu
from jax.sharding import PartitionSpec as P

D = 12288
LANES = 128
PIECES = 4


def passed_along(block, axis, distance):
    devices = range(lax.axis_size(axis))
    route = [((i - distance) % len(devices), i) for i in devices]
    return lax.ppermute(block, axis, route)


def swapped(block, axis, mask):
    return lax.ppermute(block, axis, [(i ^ mask, i) for i in range(lax.axis_size(axis))])


def in_vmem(array):
    return pltpu.with_memory_space_constraint(array, pltpu.VMEM)


def in_hbm(array):
    return pltpu.with_memory_space_constraint(array, pltpu.HBM)


def vmem_specs(count):
    return [pl.BlockSpec(memory_space=pltpu.VMEM)] * count


def load_kernel(grad_ref, weight_ref, own_ref, evicted_ref, input_ref, gain_ref, *rest):
    grad_out, weight_out, own_out, taken_out, input_out, gain_out, squares_ref = rest[:7]
    flags, sems = rest[7:]
    small = [
        pltpu.make_async_copy(evicted_ref, flags, sems.at[0]),
        pltpu.make_async_copy(own_ref, own_out, sems.at[1]),
        pltpu.make_async_copy(grad_ref, grad_out, sems.at[2]),
        pltpu.make_async_copy(gain_ref, gain_out, sems.at[3]),
        pltpu.make_async_copy(input_ref, input_out, sems.at[4]),
    ]
    for copy in small:
        copy.start()
    large = []
    features = weight_ref.shape[0]
    for j in range(PIECES):
        part = pl.ds(j * (features // PIECES), features // PIECES)
        large.append(
            pltpu.make_async_copy(weight_ref.at[part], weight_out.at[part], sems.at[5 + j])
        )
        large[-1].start()
    small[0].wait()
    small[1].wait()
    tiles = evicted_ref.shape[1]
    rows = own_ref.shape[0] // tiles
    for tile in range(tiles):
        part = pl.ds(tile * rows, rows)
        taken = jnp.full((rows, own_ref.shape[1]), flags[0, tile], jnp.int32).astype(jnp.float32)
        own = own_out[part, :].astype(jnp.float32)
        own_out[part, :] = ((1.0 - taken) * own).astype(own_out.dtype)
        taken_out[part, :] = taken.astype(taken_out.dtype)
    small[2].wait()
    small[3].wait()
    small[4].wait()
    values = input_out[...].astype(jnp.float32)
    squares_ref[...] = as_row(jnp.sum(values * values, axis=1, keepdims=True))
    for copy in large:
        copy.wait()


def load(grad, weights, own, evicted, inputs, gain):
    return pl.pallas_call(
        load_kernel,
        out_shape=(
            pltpu.VMEM(grad.shape, grad.dtype),
            pltpu.VMEM(weights.shape, weights.dtype),
            pltpu.VMEM(own.shape, own.dtype),
            pltpu.VMEM(own.shape, own.dtype),
            pltpu.VMEM(inputs.shape, inputs.dtype),
            pltpu.VMEM(gain.shape, gain.dtype),
            pltpu.VMEM((1, inputs.shape[0]), jnp.float32),
        ),
        in_specs=[pl.BlockSpec(memory_space=pltpu.HBM)] * 6,
        out_specs=tuple(vmem_specs(7)),
        scratch_shapes=[
            pltpu.SMEM(evicted.shape, evicted.dtype),
            pltpu.SemaphoreType.DMA((5 + PIECES,)),
        ],
        cost_estimate=pl.CostEstimate(flops=1 << 20, bytes_accessed=4 << 20, transcendentals=0),
        compiler_params=pltpu.CompilerParams(vmem_limit_bytes=4 << 20),
    )(*map(in_hbm, (grad, weights, own, evicted, inputs, gain)))


def mix_kernel(own_ref, taken_ref, spare_ref, grad_ref, out_ref):
    out_ref[...] = lax.dot_general(
        own_ref[...] + taken_ref[...] * spare_ref[...],
        grad_ref[...],
        (((0,), (0,)), ((), ())),
        preferred_element_type=jnp.float32,
    ).astype(out_ref.dtype)


def value_gradient(own, taken, spare, grad):
    return pl.pallas_call(
        mix_kernel,
        out_shape=pltpu.VMEM(grad.shape, jnp.bfloat16),
        in_specs=vmem_specs(4),
        out_specs=pl.BlockSpec(memory_space=pltpu.VMEM),
        compiler_params=pltpu.CompilerParams(vmem_limit_bytes=4 << 20),
    )(*map(in_vmem, (own, taken, spare, grad)))


def as_row(column):
    return jnp.broadcast_to(column, (column.shape[0], column.shape[0])).T[:1]


def project_kernel(head_of, counts, *refs):
    blocks = refs[: len(counts)]
    weight_ref, input_ref, gain_ref, squares_ref, scaled_ref, sums_ref, flat = refs[len(counts) :]
    place = 0
    for ref, count in zip(blocks, counts):
        for j in range(count):
            start = pl.multiple_of(head_of(place) * LANES, LANES)
            flat[:, pl.ds(start, LANES)] = ref[j]
            place += 1
    features = weight_ref.shape[0]
    tile = 256 if features % 256 == 0 else features
    tokens = input_ref.shape[0]
    inner = jnp.zeros((tokens, tile), jnp.float32)
    for start in range(0, features, tile):
        part = pl.ds(start, tile)
        grad_normed = lax.dot_general(
            flat[...],
            weight_ref[part, :],
            (((1,), (1,)), ((), ())),
            preferred_element_type=jnp.float32,
        )
        scaled = grad_normed * gain_ref[:, part]
        values = input_ref[:, part].astype(jnp.float32)
        inner += scaled * values
        scaled_ref[:, part] = scaled.astype(scaled_ref.dtype)
    sums_ref[:1, :] = squares_ref[...]
    sums_ref[1:, :] = as_row(jnp.sum(inner, axis=1, keepdims=True))


def project(head_of, blocks, weights, inputs, gain, squares):
    counts = tuple(block.shape[0] for block in blocks)
    tokens, features = inputs.shape
    return pl.pallas_call(
        functools.partial(project_kernel, head_of, counts),
        out_shape=(
            pltpu.VMEM((tokens, features), jnp.bfloat16),
            pltpu.VMEM((2, tokens), jnp.float32),
        ),
        in_specs=vmem_specs(len(blocks) + 4),
        out_specs=tuple(vmem_specs(2)),
        scratch_shapes=[pltpu.VMEM((tokens, weights.shape[1]), jnp.bfloat16)],
        compiler_params=pltpu.CompilerParams(vmem_limit_bytes=16 << 20),
    )(*map(in_vmem, (*blocks, weights, inputs, gain, squares)))


def finish_kernel(scaled_ref, input_ref, *refs):
    sums_refs, out_ref = refs[:-1], refs[-1]
    tokens = scaled_ref.shape[0]
    sums = sums_refs[0][...]
    for ref in sums_refs[1:]:
        sums = sums + ref[...]
    inv = 1.0 / jnp.sqrt(sums[:1] / D + 1e-05)
    factor = sums[1:] * (inv * inv * inv) / D
    inv = jnp.broadcast_to(inv, (tokens, tokens)).T[:, :1]
    factor = jnp.broadcast_to(factor, (tokens, tokens)).T[:, :1]
    scaled = scaled_ref[...].astype(jnp.float32)
    values = input_ref[...].astype(jnp.float32)
    out_ref[...] = (scaled * inv - values * factor).astype(out_ref.dtype)


def finish(scaled, inputs, sums):
    return pl.pallas_call(
        finish_kernel,
        out_shape=jax.ShapeDtypeStruct(scaled.shape, jnp.bfloat16),
        in_specs=vmem_specs(2 + len(sums)),
        out_specs=pl.BlockSpec(memory_space=pltpu.VMEM),
        compiler_params=pltpu.CompilerParams(vmem_limit_bytes=8 << 20),
    )(*map(in_vmem, (scaled, inputs, *sums)))


FAR, NEAR, SIDE = 4, 2, 1


def gathered(block, axis):
    if lax.axis_size(axis) != 8:
        return [lax.all_gather(block, axis)], lambda place: place
    own = block[None]
    pair = jnp.concatenate([own, swapped(own, axis, FAR)])
    blocks = [pair] + [swapped(pair, axis, mask) for mask in (NEAR | SIDE, NEAR, SIDE)]
    masks = [low | far for low in (0, NEAR | SIDE, NEAR, SIDE) for far in (0, FAR)]

    def head_of(place):
        return lax.axis_index(axis) ^ masks[place]

    return blocks, head_of


def handed_sums(sums, sections, count):
    if count != 8:
        return [passed_along(lax.psum(sums, "tp"), "section", -1)]
    pair = sums + swapped(sums, "tp", FAR)
    parts = []
    for mask in (NEAR | SIDE, NEAR, SIDE, 0):
        route = [
            ((s + 1) % sections * count + (i ^ mask), s * count + i)
            for s in range(sections)
            for i in range(count)
        ]
        parts.append(lax.ppermute(pair, ("section", "tp"), route))
    return parts


def per_device(grad_attn, w_value, probs_own, probs_spare, evicted, layer_input, gain):
    sections, count = lax.axis_size("section"), lax.axis_size("tp")
    spare = passed_along(probs_spare[0, 0], "section", sections // 2)
    next_input = passed_along(layer_input[0], "section", -1)
    grad, weights, own, taken, inputs, gains, squares = load(
        grad_attn[0, 0], w_value[0], probs_own[0, 0], evicted, layer_input[0], gain
    )
    grad_value = value_gradient(own, taken, spare, grad)
    blocks, head_of = gathered(grad_value, "tp")
    scaled, sums = project(head_of, blocks, weights, inputs, gains, squares)
    next_scaled = passed_along(scaled, "section", -1)
    return finish(next_scaled, next_input, handed_sums(sums, sections, count))[None]


def solution(mesh):
    in_specs = (
        P("section", "tp", None, None),
        P("section", "tp", None),
        P("section", "tp", None, None),
        P("section", "tp", None, None),
        P("section", None),
        P("section", None, "tp"),
        P("section", "tp"),
    )
    out_specs = P("section", None, "tp")
    return jax.shard_map(
        per_device, mesh=mesh, in_specs=in_specs, out_specs=out_specs, check_vma=False
    )
```

```python
import functools

import jax
import jax.numpy as jnp
from jax import lax
from jax.experimental import pallas as pl
from jax.experimental.pallas import tpu as pltpu
from jax.sharding import PartitionSpec as P

D = 12288
LANES = 128
PIECES = 4
EXTRA = 16


def passed_along(block, axis, distance):
    devices = range(lax.axis_size(axis))
    route = [((i - distance) % len(devices), i) for i in devices]
    return lax.ppermute(block, axis, route)


def swapped(block, axis, mask):
    return lax.ppermute(block, axis, [(i ^ mask, i) for i in range(lax.axis_size(axis))])


def in_vmem(array):
    return pltpu.with_memory_space_constraint(array, pltpu.VMEM)


def in_hbm(array):
    return pltpu.with_memory_space_constraint(array, pltpu.HBM)


def vmem_specs(count):
    return [pl.BlockSpec(memory_space=pltpu.VMEM)] * count


def as_row(column):
    return jnp.broadcast_to(column, (column.shape[0], column.shape[0])).T[:1]


def as_column(row):
    return jnp.broadcast_to(row, (row.shape[1], row.shape[1])).T[:, :1]


def as_parts(row):
    parts = []
    for _ in range(3):
        parts.append(row.astype(jnp.bfloat16).astype(jnp.float32))
        row = row - parts[-1]
    rest = jnp.zeros((EXTRA - 3, row.shape[1]), jnp.float32)
    return jnp.concatenate(parts + [rest]).astype(jnp.bfloat16)


def load_kernel(grad_ref, weight_ref, own_ref, evicted_ref, input_ref, gain_ref, *rest):
    grad_out, weight_out, own_out, taken_out, input_out, gain_out, squares_ref, reach_ref = rest[:8]
    flags, sems = rest[8:]
    small = [
        pltpu.make_async_copy(evicted_ref, flags, sems.at[0]),
        pltpu.make_async_copy(own_ref, own_out, sems.at[1]),
        pltpu.make_async_copy(grad_ref, grad_out, sems.at[2]),
        pltpu.make_async_copy(gain_ref, gain_out, sems.at[3]),
        pltpu.make_async_copy(input_ref, input_out, sems.at[4]),
    ]
    for copy in small:
        copy.start()
    large = []
    features = weight_ref.shape[0]
    for j in range(PIECES):
        part = pl.ds(j * (features // PIECES), features // PIECES)
        large.append(
            pltpu.make_async_copy(weight_ref.at[part], weight_out.at[part], sems.at[5 + j])
        )
        large[-1].start()
    small[0].wait()
    small[1].wait()
    tiles = evicted_ref.shape[1]
    rows = own_ref.shape[0] // tiles
    for tile in range(tiles):
        part = pl.ds(tile * rows, rows)
        taken = jnp.full((rows, own_ref.shape[1]), flags[0, tile], jnp.int32).astype(jnp.float32)
        own = own_out[part, :].astype(jnp.float32)
        own_out[part, :] = ((1.0 - taken) * own).astype(own_out.dtype)
        taken_out[part, :] = taken.astype(taken_out.dtype)
    small[2].wait()
    small[3].wait()
    small[4].wait()
    values = input_out[...].astype(jnp.float32)
    squares_ref[...] = as_parts(as_row(jnp.sum(values * values, axis=1, keepdims=True)))
    gained = (values * gain_out[...]).astype(jnp.bfloat16)
    reach = jnp.zeros(reach_ref.shape, jnp.float32)
    for j, copy in enumerate(large):
        copy.wait()
        part = slice(j * (features // PIECES), (j + 1) * (features // PIECES))
        reach += jnp.dot(gained[:, part], weight_out[part, :], preferred_element_type=jnp.float32)
    reach_ref[...] = reach.astype(reach_ref.dtype)


def load(grad, weights, own, evicted, inputs, gain):
    return pl.pallas_call(
        load_kernel,
        out_shape=(
            pltpu.VMEM(grad.shape, grad.dtype),
            pltpu.VMEM(weights.shape, weights.dtype),
            pltpu.VMEM(own.shape, own.dtype),
            pltpu.VMEM(own.shape, own.dtype),
            pltpu.VMEM(inputs.shape, inputs.dtype),
            pltpu.VMEM(gain.shape, gain.dtype),
            pltpu.VMEM((EXTRA, inputs.shape[0]), jnp.bfloat16),
            jax.ShapeDtypeStruct((inputs.shape[0], weights.shape[1]), jnp.bfloat16),
        ),
        in_specs=[pl.BlockSpec(memory_space=pltpu.HBM)] * 6,
        out_specs=tuple(vmem_specs(8)),
        scratch_shapes=[
            pltpu.SMEM(evicted.shape, evicted.dtype),
            pltpu.SemaphoreType.DMA((5 + PIECES,)),
        ],
        cost_estimate=pl.CostEstimate(flops=1 << 20, bytes_accessed=4 << 20, transcendentals=0),
        compiler_params=pltpu.CompilerParams(vmem_limit_bytes=8 << 20),
    )(*map(in_hbm, (grad, weights, own, evicted, inputs, gain)))


def mix_kernel(own_ref, taken_ref, spare_ref, grad_ref, squares_ref, out_ref):
    tokens = own_ref.shape[1]
    out_ref[tokens:, :] = squares_ref[...]
    out_ref[:tokens, :] = lax.dot_general(
        own_ref[...] + taken_ref[...] * spare_ref[...],
        grad_ref[...],
        (((0,), (0,)), ((), ())),
        preferred_element_type=jnp.float32,
    ).astype(out_ref.dtype)


def value_gradient(own, taken, spare, grad, squares):
    return pl.pallas_call(
        mix_kernel,
        out_shape=pltpu.VMEM((own.shape[1] + EXTRA, grad.shape[1]), jnp.bfloat16),
        in_specs=vmem_specs(5),
        out_specs=pl.BlockSpec(memory_space=pltpu.VMEM),
        compiler_params=pltpu.CompilerParams(vmem_limit_bytes=8 << 20),
    )(*map(in_vmem, (own, taken, spare, grad, squares)))


def project_kernel(head_of, counts, *refs):
    blocks = refs[: len(counts)]
    weight_ref, input_ref, gain_ref, reach_ref, out_ref, flat = refs[len(counts) :]
    tokens, features = input_ref.shape
    squares = jnp.zeros((EXTRA, tokens), jnp.float32)
    place = 0
    for ref, count in zip(blocks, counts):
        for j in range(count):
            start = pl.multiple_of(head_of(place) * LANES, LANES)
            flat[:, pl.ds(start, LANES)] = ref[j, :tokens, :]
            squares += ref[j, tokens:, :].astype(jnp.float32)
            place += 1
    squares = jnp.sum(squares, axis=0, keepdims=True)
    inv = 1.0 / jnp.sqrt(squares / D + 1e-05)
    products = flat[...].astype(jnp.float32) * reach_ref[...].astype(jnp.float32)
    inner = jnp.sum(products, axis=1, keepdims=True)
    inv = as_column(inv)
    factor = inner * (inv * inv * inv) / D
    tile = 256 if features % 256 == 0 else features
    for start in range(0, features, tile):
        part = pl.ds(start, tile)
        grad_normed = lax.dot_general(
            flat[...],
            weight_ref[part, :],
            (((1,), (1,)), ((), ())),
            preferred_element_type=jnp.float32,
        )
        values = input_ref[:, part].astype(jnp.float32)
        branch = grad_normed * gain_ref[:, part] * inv - values * factor
        out_ref[:, part] = branch.astype(out_ref.dtype)


def project(head_of, blocks, weights, inputs, gain, reach):
    counts = tuple(block.shape[0] for block in blocks)
    tokens, features = inputs.shape
    return pl.pallas_call(
        functools.partial(project_kernel, head_of, counts),
        out_shape=pltpu.VMEM((tokens, features), jnp.bfloat16),
        in_specs=vmem_specs(len(blocks) + 4),
        out_specs=pl.BlockSpec(memory_space=pltpu.VMEM),
        scratch_shapes=[pltpu.VMEM((tokens, weights.shape[1]), jnp.bfloat16)],
        compiler_params=pltpu.CompilerParams(vmem_limit_bytes=16 << 20),
    )(*map(in_vmem, (*blocks, weights, inputs, gain, reach)))


FAR, NEAR, SIDE = 4, 2, 1


def gathered(block, axis):
    if lax.axis_size(axis) != 8:
        return [lax.all_gather(block, axis)], lambda place: place
    own = block[None]
    pair = jnp.concatenate([own, swapped(own, axis, FAR)])
    blocks = [pair] + [swapped(pair, axis, mask) for mask in (NEAR | SIDE, NEAR, SIDE)]
    masks = [low | far for low in (0, NEAR | SIDE, NEAR, SIDE) for far in (0, FAR)]

    def head_of(place):
        return lax.axis_index(axis) ^ masks[place]

    return blocks, head_of


def per_device(grad_attn, w_value, probs_own, probs_spare, evicted, layer_input, gain):
    sections = lax.axis_size("section")
    spare = passed_along(probs_spare[0, 0], "section", sections // 2)
    grad, weights, own, taken, inputs, gains, squares, reach = load(
        grad_attn[0, 0], w_value[0], probs_own[0, 0], evicted, layer_input[0], gain
    )
    reach = lax.psum(reach, "tp")
    grad_value = value_gradient(own, taken, spare, grad, squares)
    blocks, head_of = gathered(grad_value, "tp")
    branch = project(head_of, blocks, weights, inputs, gains, reach)
    return passed_along(branch, "section", -1)[None]


def solution(mesh):
    in_specs = (
        P("section", "tp", None, None),
        P("section", "tp", None),
        P("section", "tp", None, None),
        P("section", "tp", None, None),
        P("section", None),
        P("section", None, "tp"),
        P("section", "tp"),
    )
    out_specs = P("section", None, "tp")
    return jax.shard_map(
        per_device, mesh=mesh, in_specs=in_specs, out_specs=out_specs, check_vma=False
    )
```

```python
import functools

import jax
import jax.numpy as jnp
from jax import lax
from jax.experimental import pallas as pl
from jax.experimental.pallas import tpu as pltpu
from jax.sharding import PartitionSpec as P

D = 12288
LANES = 128
PIECES = 4


def passed_along(block, axis, distance):
    devices = range(lax.axis_size(axis))
    route = [((i - distance) % len(devices), i) for i in devices]
    return lax.ppermute(block, axis, route)


def swapped(block, axis, mask):
    return lax.ppermute(block, axis, [(i ^ mask, i) for i in range(lax.axis_size(axis))])


def in_vmem(array):
    return pltpu.with_memory_space_constraint(array, pltpu.VMEM)


def in_hbm(array):
    return pltpu.with_memory_space_constraint(array, pltpu.HBM)


def vmem_specs(count):
    return [pl.BlockSpec(memory_space=pltpu.VMEM)] * count


def pack_kernel(own_ref, grad_ref, out_ref, sems):
    copies = [
        pltpu.make_async_copy(own_ref, out_ref.at[0], sems.at[0]),
        pltpu.make_async_copy(grad_ref, out_ref.at[1], sems.at[1]),
    ]
    for copy in copies:
        copy.start()
    for copy in copies:
        copy.wait()


def pack(own, grad):
    return pl.pallas_call(
        pack_kernel,
        out_shape=pltpu.VMEM((2, *own.shape), own.dtype),
        in_specs=[pl.BlockSpec(memory_space=pltpu.HBM)] * 2,
        out_specs=pl.BlockSpec(memory_space=pltpu.VMEM),
        scratch_shapes=[pltpu.SemaphoreType.DMA((2,))],
        cost_estimate=pl.CostEstimate(flops=1, bytes_accessed=1 << 17, transcendentals=0),
        compiler_params=pltpu.CompilerParams(vmem_limit_bytes=4 << 20),
    )(in_hbm(own), in_hbm(grad))


def load_kernel(weight_ref, evicted_ref, input_ref, gain_ref, *rest):
    weight_out, taken_out, input_out, gain_out, squares_ref, flags, sems = rest
    small = [
        pltpu.make_async_copy(evicted_ref, flags, sems.at[0]),
        pltpu.make_async_copy(input_ref, input_out, sems.at[1]),
        pltpu.make_async_copy(gain_ref, gain_out, sems.at[2]),
    ]
    for copy in small:
        copy.start()
    large = []
    features = weight_ref.shape[0]
    for j in range(PIECES):
        part = pl.ds(j * (features // PIECES), features // PIECES)
        large.append(
            pltpu.make_async_copy(weight_ref.at[part], weight_out.at[part], sems.at[3 + j])
        )
        large[-1].start()
    small[0].wait()
    tiles = evicted_ref.shape[1]
    rows = taken_out.shape[0] // tiles
    for tile in range(tiles):
        part = pl.ds(tile * rows, rows)
        taken = jnp.full((rows, taken_out.shape[1]), flags[0, tile], jnp.int32)
        taken_out[part, :] = taken.astype(jnp.float32).astype(taken_out.dtype)
    small[1].wait()
    values = input_out[...].astype(jnp.float32)
    squares_ref[...] = as_row(jnp.sum(values * values, axis=1, keepdims=True))
    small[2].wait()
    for copy in large:
        copy.wait()


def load(weights, evicted, inputs, gain):
    tokens = inputs.shape[0]
    return pl.pallas_call(
        load_kernel,
        out_shape=(
            pltpu.VMEM(weights.shape, weights.dtype),
            pltpu.VMEM((tokens, tokens), jnp.bfloat16),
            pltpu.VMEM(inputs.shape, inputs.dtype),
            pltpu.VMEM(gain.shape, gain.dtype),
            pltpu.VMEM((1, tokens), jnp.float32),
        ),
        in_specs=[pl.BlockSpec(memory_space=pltpu.HBM)] * 4,
        out_specs=tuple(vmem_specs(5)),
        scratch_shapes=[
            pltpu.SMEM(evicted.shape, evicted.dtype),
            pltpu.SemaphoreType.DMA((3 + PIECES,)),
        ],
        cost_estimate=pl.CostEstimate(flops=1 << 20, bytes_accessed=4 << 20, transcendentals=0),
        compiler_params=pltpu.CompilerParams(vmem_limit_bytes=4 << 20),
    )(*map(in_hbm, (weights, evicted, inputs, gain)))


def mix_kernel(taken_ref, *refs):
    out_ref = refs[-1]
    taken = taken_ref[...]
    for j in range(out_ref.shape[0]):
        packed_ref, spare_ref = refs[2 * j], refs[2 * j + 1]
        out_ref[j] = lax.dot_general(
            packed_ref[0] * (1 - taken) + spare_ref[...] * taken,
            packed_ref[1],
            (((0,), (0,)), ((), ())),
            preferred_element_type=jnp.float32,
        ).astype(out_ref.dtype)


def value_gradients(taken, heads):
    return pl.pallas_call(
        mix_kernel,
        out_shape=pltpu.VMEM((len(heads), *heads[0][1].shape), jnp.bfloat16),
        in_specs=vmem_specs(1 + 2 * len(heads)),
        out_specs=pl.BlockSpec(memory_space=pltpu.VMEM),
        compiler_params=pltpu.CompilerParams(vmem_limit_bytes=4 << 20),
    )(*map(in_vmem, (taken, *[array for head in heads for array in head])))


def as_row(column):
    return jnp.broadcast_to(column, (column.shape[0], column.shape[0])).T[:1]


def project_kernel(head_of, counts, *refs):
    blocks = refs[: len(counts)]
    weight_ref, input_ref, gain_ref, squares_ref, scaled_ref, sums_ref, flat = refs[len(counts) :]
    place = 0
    for ref, count in zip(blocks, counts):
        for j in range(count):
            start = pl.multiple_of(head_of(place) * LANES, LANES)
            flat[:, pl.ds(start, LANES)] = ref[j]
            place += 1
    features = weight_ref.shape[0]
    tile = 256 if features % 256 == 0 else features
    tokens = input_ref.shape[0]
    inner = jnp.zeros((tokens, tile), jnp.float32)
    for start in range(0, features, tile):
        part = pl.ds(start, tile)
        grad_normed = lax.dot_general(
            flat[...],
            weight_ref[part, :],
            (((1,), (1,)), ((), ())),
            preferred_element_type=jnp.float32,
        )
        scaled = grad_normed * gain_ref[:, part]
        values = input_ref[:, part].astype(jnp.float32)
        inner += scaled * values
        scaled_ref[:, part] = scaled.astype(scaled_ref.dtype)
    sums_ref[:1, :] = squares_ref[...]
    sums_ref[1:, :] = as_row(jnp.sum(inner, axis=1, keepdims=True))


def project(head_of, blocks, weights, inputs, gain, squares):
    counts = tuple(block.shape[0] for block in blocks)
    tokens, features = inputs.shape
    return pl.pallas_call(
        functools.partial(project_kernel, head_of, counts),
        out_shape=(
            pltpu.VMEM((tokens, features), jnp.bfloat16),
            pltpu.VMEM((2, tokens), jnp.float32),
        ),
        in_specs=vmem_specs(len(blocks) + 4),
        out_specs=tuple(vmem_specs(2)),
        scratch_shapes=[pltpu.VMEM((tokens, weights.shape[1]), jnp.bfloat16)],
        compiler_params=pltpu.CompilerParams(vmem_limit_bytes=16 << 20),
    )(*map(in_vmem, (*blocks, weights, inputs, gain, squares)))


def finish_kernel(scaled_ref, input_ref, *refs):
    sums_refs, out_ref = refs[:-1], refs[-1]
    tokens = scaled_ref.shape[0]
    sums = sums_refs[0][...]
    for ref in sums_refs[1:]:
        sums = sums + ref[...]
    inv = 1.0 / jnp.sqrt(sums[:1] / D + 1e-05)
    factor = sums[1:] * (inv * inv * inv) / D
    inv = jnp.broadcast_to(inv, (tokens, tokens)).T[:, :1]
    factor = jnp.broadcast_to(factor, (tokens, tokens)).T[:, :1]
    scaled = scaled_ref[...].astype(jnp.float32)
    values = input_ref[...].astype(jnp.float32)
    out_ref[...] = (scaled * inv - values * factor).astype(out_ref.dtype)


def finish(scaled, inputs, sums):
    return pl.pallas_call(
        finish_kernel,
        out_shape=jax.ShapeDtypeStruct(scaled.shape, jnp.bfloat16),
        in_specs=vmem_specs(2 + len(sums)),
        out_specs=pl.BlockSpec(memory_space=pltpu.VMEM),
        compiler_params=pltpu.CompilerParams(vmem_limit_bytes=8 << 20),
    )(*map(in_vmem, (scaled, inputs, *sums)))


FAR, NEAR, SIDE = 4, 2, 1


def handed_over(block, sections, count, distance, mask):
    route = [
        ((s - distance) % sections * count + (i ^ mask), s * count + i)
        for s in range(sections)
        for i in range(count)
    ]
    return lax.ppermute(block, ("section", "tp"), route)


def gathered(pair, axis):
    if lax.axis_size(axis) != 8:
        return [lax.all_gather(pair[0], axis)], lambda place: place
    blocks = [pair] + [swapped(pair, axis, mask) for mask in (NEAR | SIDE, NEAR, SIDE)]
    masks = [low | far for low in (0, NEAR | SIDE, NEAR, SIDE) for far in (0, FAR)]

    def head_of(place):
        return lax.axis_index(axis) ^ masks[place]

    return blocks, head_of


def handed_sums(sums, sections, count):
    if count != 8:
        return [passed_along(lax.psum(sums, "tp"), "section", -1)]
    pair = sums + swapped(sums, "tp", FAR)
    return [
        handed_over(pair, sections, count, -1, mask) for mask in (NEAR | SIDE, NEAR, SIDE, 0)
    ]


def per_device(grad_attn, w_value, probs_own, probs_spare, evicted, layer_input, gain):
    sections, count = lax.axis_size("section"), lax.axis_size("tp")
    packed = pack(probs_own[0, 0], grad_attn[0, 0])
    masks = (0, FAR) if count == 8 else (0,)
    heads = []
    for mask in masks:
        spare = handed_over(probs_spare[0, 0], sections, count, sections // 2, mask)
        heads.append((swapped(packed, "tp", mask) if mask else packed, spare))
    next_input = passed_along(layer_input[0], "section", -1)
    weights, taken, inputs, gains, squares = load(w_value[0], evicted, layer_input[0], gain)
    pair = value_gradients(taken, heads)
    blocks, head_of = gathered(pair, "tp")
    scaled, sums = project(head_of, blocks, weights, inputs, gains, squares)
    next_scaled = passed_along(scaled, "section", -1)
    return finish(next_scaled, next_input, handed_sums(sums, sections, count))[None]


def solution(mesh):
    in_specs = (
        P("section", "tp", None, None),
        P("section", "tp", None),
        P("section", "tp", None, None),
        P("section", "tp", None, None),
        P("section", None),
        P("section", None, "tp"),
        P("section", "tp"),
    )
    out_specs = P("section", None, "tp")
    return jax.shard_map(
        per_device, mesh=mesh, in_specs=in_specs, out_specs=out_specs, check_vma=False
    )
```

```python
import functools

import jax
import jax.numpy as jnp
from jax import lax
from jax.experimental import pallas as pl
from jax.experimental.pallas import tpu as pltpu
from jax.sharding import PartitionSpec as P

D = 12288
LANES = 128
PIECES = 4
EXTRA = 16
HIDES = pl.CostEstimate(flops=1 << 35, bytes_accessed=1 << 25, transcendentals=0)


def passed_along(block, axis, distance):
    devices = range(lax.axis_size(axis))
    route = [((i - distance) % len(devices), i) for i in devices]
    return lax.ppermute(block, axis, route)


def swapped(block, axis, mask):
    return lax.ppermute(block, axis, [(i ^ mask, i) for i in range(lax.axis_size(axis))])


def in_vmem(array):
    return pltpu.with_memory_space_constraint(array, pltpu.VMEM)


def in_hbm(array):
    return pltpu.with_memory_space_constraint(array, pltpu.HBM)


def vmem_specs(count):
    return [pl.BlockSpec(memory_space=pltpu.VMEM)] * count


def as_row(column):
    return jnp.broadcast_to(column, (column.shape[0], column.shape[0])).T[:1]


def as_column(row):
    return jnp.broadcast_to(row, (row.shape[1], row.shape[1])).T[:, :1]


def split(values):
    parts = []
    for _ in range(3):
        parts.append(values.astype(jnp.bfloat16).astype(jnp.float32))
        values = values - parts[-1]
    return parts


def as_parts(row):
    rest = jnp.zeros((EXTRA - 3, row.shape[1]), jnp.float32)
    return jnp.concatenate(split(row) + [rest]).astype(jnp.bfloat16)


def pack_kernel(own_ref, grad_ref, out_ref, sems):
    copies = [
        pltpu.make_async_copy(own_ref, out_ref.at[0], sems.at[0]),
        pltpu.make_async_copy(grad_ref, out_ref.at[1], sems.at[1]),
    ]
    for copy in copies:
        copy.start()
    for copy in copies:
        copy.wait()


def pack(own, grad):
    return pl.pallas_call(
        pack_kernel,
        out_shape=pltpu.VMEM((2, *own.shape), own.dtype),
        in_specs=[pl.BlockSpec(memory_space=pltpu.HBM)] * 2,
        out_specs=pl.BlockSpec(memory_space=pltpu.VMEM),
        scratch_shapes=[pltpu.SemaphoreType.DMA((2,))],
        cost_estimate=pl.CostEstimate(flops=1, bytes_accessed=1 << 17, transcendentals=0),
        compiler_params=pltpu.CompilerParams(vmem_limit_bytes=4 << 20),
    )(in_hbm(own), in_hbm(grad))


def load_kernel(weight_ref, evicted_ref, input_ref, gain_ref, *rest):
    weight_out, taken_out, input_out, gain_out, reach_ref, flags, sems = rest
    small = [
        pltpu.make_async_copy(evicted_ref, flags, sems.at[0]),
        pltpu.make_async_copy(gain_ref, gain_out, sems.at[1]),
        pltpu.make_async_copy(input_ref, input_out, sems.at[2]),
    ]
    for copy in small:
        copy.start()
    large = []
    features = weight_ref.shape[0]
    for j in range(PIECES):
        part = pl.ds(j * (features // PIECES), features // PIECES)
        large.append(
            pltpu.make_async_copy(weight_ref.at[part], weight_out.at[part], sems.at[3 + j])
        )
        large[-1].start()
    small[0].wait()
    tiles = evicted_ref.shape[1]
    rows = taken_out.shape[0] // tiles
    for tile in range(tiles):
        part = pl.ds(tile * rows, rows)
        taken = jnp.full((rows, taken_out.shape[1]), flags[0, tile], jnp.int32)
        taken_out[part, :] = taken.astype(jnp.float32).astype(taken_out.dtype)
    small[1].wait()
    small[2].wait()
    values = input_out[...].astype(jnp.float32)
    tokens = values.shape[0]
    reach_ref[tokens:, :] = jnp.zeros_like(reach_ref[tokens:, :])
    squares = as_row(jnp.sum(values * values, axis=1, keepdims=True))
    reach_ref[tokens:, :tokens] = as_parts(squares)
    gained = (values * gain_out[...]).astype(jnp.bfloat16)
    reach = jnp.zeros((tokens, weight_out.shape[1]), jnp.float32)
    for j, copy in enumerate(large):
        copy.wait()
        part = slice(j * (features // PIECES), (j + 1) * (features // PIECES))
        reach += jnp.dot(gained[:, part], weight_out[part, :], preferred_element_type=jnp.float32)
    reach_ref[:tokens, :] = reach.astype(reach_ref.dtype)


def load(weights, evicted, inputs, gain):
    tokens = inputs.shape[0]
    return pl.pallas_call(
        load_kernel,
        out_shape=(
            pltpu.VMEM(weights.shape, weights.dtype),
            pltpu.VMEM((tokens, tokens), jnp.bfloat16),
            pltpu.VMEM(inputs.shape, inputs.dtype),
            pltpu.VMEM(gain.shape, gain.dtype),
            pltpu.VMEM((tokens + EXTRA, weights.shape[1]), jnp.bfloat16),
        ),
        in_specs=[pl.BlockSpec(memory_space=pltpu.HBM)] * 4,
        out_specs=tuple(vmem_specs(5)),
        scratch_shapes=[
            pltpu.SMEM(evicted.shape, evicted.dtype),
            pltpu.SemaphoreType.DMA((3 + PIECES,)),
        ],
        cost_estimate=HIDES,
        compiler_params=pltpu.CompilerParams(vmem_limit_bytes=8 << 20),
    )(*map(in_hbm, (weights, evicted, inputs, gain)))


def mix_kernel(taken_ref, *refs):
    out_ref = refs[-1]
    taken = taken_ref[...]
    for j in range(out_ref.shape[0]):
        packed_ref, spare_ref = refs[2 * j], refs[2 * j + 1]
        out_ref[j] = lax.dot_general(
            packed_ref[0] * (1 - taken) + spare_ref[...] * taken,
            packed_ref[1],
            (((0,), (0,)), ((), ())),
            preferred_element_type=jnp.float32,
        ).astype(out_ref.dtype)


def value_gradients(taken, heads):
    return pl.pallas_call(
        mix_kernel,
        out_shape=pltpu.VMEM((len(heads), *heads[0][1].shape), jnp.bfloat16),
        in_specs=vmem_specs(1 + 2 * len(heads)),
        out_specs=pl.BlockSpec(memory_space=pltpu.VMEM),
        cost_estimate=HIDES,
        compiler_params=pltpu.CompilerParams(vmem_limit_bytes=4 << 20),
    )(*map(in_vmem, (taken, *[array for head in heads for array in head])))


def project_kernel(head_of, counts, *refs):
    blocks = refs[: len(counts)]
    rest = refs[len(counts) :]
    weight_ref, input_ref, gain_ref, *reach_refs, scaled_ref, sums_ref, flat = rest
    tokens, features = input_ref.shape
    place = 0
    for ref, count in zip(blocks, counts):
        for j in range(count):
            start = pl.multiple_of(head_of(place) * LANES, LANES)
            flat[:, pl.ds(start, LANES)] = ref[j]
            place += 1
    tile = 256 if features % 256 == 0 else features
    for start in range(0, features, tile):
        part = pl.ds(start, tile)
        grad_normed = lax.dot_general(
            flat[...],
            weight_ref[part, :],
            (((1,), (1,)), ((), ())),
            preferred_element_type=jnp.float32,
        )
        scaled_ref[:, part] = (grad_normed * gain_ref[:, part]).astype(scaled_ref.dtype)
    reach = sum(ref[:tokens, :].astype(jnp.float32) for ref in reach_refs)
    squares = sum(ref[tokens:, :tokens].astype(jnp.float32) for ref in reach_refs)
    squares = jnp.sum(squares, axis=0, keepdims=True)
    inner = jnp.sum(flat[...].astype(jnp.float32) * reach, axis=1, keepdims=True)
    sums_ref[:1, :] = squares
    sums_ref[1:, :] = as_row(inner)
    lane = lax.broadcasted_iota(jnp.int32, (tokens, LANES), 1)
    extra = jnp.zeros((tokens, LANES), jnp.float32)
    for j, part in enumerate(split(as_column(squares)) + split(inner)):
        extra = jnp.where(lane == j, part, extra)
    scaled_ref[:, features:] = extra.astype(scaled_ref.dtype)


def project(head_of, blocks, weights, inputs, gain, reaches):
    counts = tuple(block.shape[0] for block in blocks)
    tokens, features = inputs.shape
    return pl.pallas_call(
        functools.partial(project_kernel, head_of, counts),
        out_shape=(
            pltpu.VMEM((tokens, features + LANES), jnp.bfloat16),
            pltpu.VMEM((2, tokens), jnp.float32),
        ),
        in_specs=vmem_specs(len(blocks) + 3 + len(reaches)),
        out_specs=tuple(vmem_specs(2)),
        scratch_shapes=[pltpu.VMEM((tokens, weights.shape[1]), jnp.bfloat16)],
        cost_estimate=HIDES,
        compiler_params=pltpu.CompilerParams(vmem_limit_bytes=16 << 20),
    )(*map(in_vmem, (*blocks, weights, inputs, gain, *reaches)))


def finish_kernel(scaled_ref, input_ref, *refs):
    sums_refs, out_ref = refs[:-1], refs[-1]
    features = input_ref.shape[1]
    extra = scaled_ref[:, features:].astype(jnp.float32)
    lane = lax.broadcasted_iota(jnp.int32, extra.shape, 1)
    squares = jnp.sum(jnp.where(lane < 3, extra, 0.0), axis=1, keepdims=True)
    inner = jnp.sum(jnp.where(lane < 3, 0.0, extra), axis=1, keepdims=True)
    if sums_refs:
        sums = sum(ref[...] for ref in sums_refs)
        squares = squares + as_column(sums[:1])
        inner = inner + as_column(sums[1:])
    inv = 1.0 / jnp.sqrt(squares / D + 1e-05)
    factor = inner * (inv * inv * inv) / D
    scaled = scaled_ref[:, :features].astype(jnp.float32)
    values = input_ref[...].astype(jnp.float32)
    out_ref[...] = (scaled * inv - values * factor).astype(out_ref.dtype)


def finish(scaled, inputs, sums):
    return pl.pallas_call(
        finish_kernel,
        out_shape=jax.ShapeDtypeStruct(inputs.shape, jnp.bfloat16),
        in_specs=vmem_specs(2 + len(sums)),
        out_specs=pl.BlockSpec(memory_space=pltpu.VMEM),
        compiler_params=pltpu.CompilerParams(vmem_limit_bytes=8 << 20),
    )(*map(in_vmem, (scaled, inputs, *sums)))


FAR, NEAR, SIDE = 4, 2, 1


def handed_over(block, sections, count, distance, mask):
    route = [
        ((s - distance) % sections * count + (i ^ mask), s * count + i)
        for s in range(sections)
        for i in range(count)
    ]
    return lax.ppermute(block, ("section", "tp"), route)


def gathered(pair, axis):
    if lax.axis_size(axis) != 8:
        return [lax.all_gather(pair[0], axis)], lambda place: place
    blocks = [pair] + [swapped(pair, axis, mask) for mask in (NEAR | SIDE, NEAR, SIDE)]
    masks = [low | far for low in (0, NEAR | SIDE, NEAR, SIDE) for far in (0, FAR)]

    def head_of(place):
        return lax.axis_index(axis) ^ masks[place]

    return blocks, head_of


def per_device(grad_attn, w_value, probs_own, probs_spare, evicted, layer_input, gain):
    sections, count = lax.axis_size("section"), lax.axis_size("tp")
    packed = pack(probs_own[0, 0], grad_attn[0, 0])
    heads = []
    for mask in (0, FAR) if count == 8 else (0,):
        spare = handed_over(probs_spare[0, 0], sections, count, sections // 2, mask)
        heads.append((swapped(packed, "tp", mask) if mask else packed, spare))
    weights, taken, inputs, gains, reach = load(w_value[0], evicted, layer_input[0], gain)
    next_input = passed_along(inputs, "section", -1)
    if count == 8:
        reaches = [reach, swapped(reach, "tp", SIDE)]
    else:
        reaches = [lax.psum(reach, "tp")]
    pair = value_gradients(taken, heads)
    blocks, head_of = gathered(pair, "tp")
    scaled, sums = project(head_of, blocks, weights, inputs, gains, reaches)
    next_scaled = passed_along(scaled, "section", -1)
    next_sums = []
    for mask in (FAR | NEAR, FAR, NEAR) if count == 8 else ():
        if mask == NEAR:
            sums, next_input = lax.optimization_barrier((sums, next_input))
        next_sums.append(handed_over(sums, sections, count, -1, mask))
    return finish(next_scaled, next_input, next_sums)[None]


def solution(mesh):
    in_specs = (
        P("section", "tp", None, None),
        P("section", "tp", None),
        P("section", "tp", None, None),
        P("section", "tp", None, None),
        P("section", None),
        P("section", None, "tp"),
        P("section", "tp"),
    )
    out_specs = P("section", None, "tp")
    return jax.shard_map(
        per_device, mesh=mesh, in_specs=in_specs, out_specs=out_specs, check_vma=False
    )
```

```python
import functools

import jax
import jax.numpy as jnp
from jax import lax
from jax.experimental import pallas as pl
from jax.experimental.pallas import tpu as pltpu
from jax.sharding import PartitionSpec as P

D = 12288
LANES = 128
PIECES = 4
EXTRA = 16
HIDES = pl.CostEstimate(flops=1 << 35, bytes_accessed=1 << 25, transcendentals=0)


def passed_along(block, axis, distance):
    devices = range(lax.axis_size(axis))
    route = [((i - distance) % len(devices), i) for i in devices]
    return lax.ppermute(block, axis, route)


def swapped(block, axis, mask):
    return lax.ppermute(block, axis, [(i ^ mask, i) for i in range(lax.axis_size(axis))])


def in_vmem(array):
    return pltpu.with_memory_space_constraint(array, pltpu.VMEM)


def in_hbm(array):
    return pltpu.with_memory_space_constraint(array, pltpu.HBM)


def vmem_specs(count):
    return [pl.BlockSpec(memory_space=pltpu.VMEM)] * count


def as_row(column):
    return jnp.broadcast_to(column, (column.shape[0], column.shape[0])).T[:1]


def as_column(row):
    return jnp.broadcast_to(row, (row.shape[1], row.shape[1])).T[:, :1]


def split(values):
    parts = []
    for _ in range(3):
        parts.append(values.astype(jnp.bfloat16).astype(jnp.float32))
        values = values - parts[-1]
    return parts


def as_parts(row):
    rest = jnp.zeros((EXTRA - 3, row.shape[1]), jnp.float32)
    return jnp.concatenate(split(row) + [rest]).astype(jnp.bfloat16)


def pack_kernel(own_ref, grad_ref, out_ref, sems):
    copies = [
        pltpu.make_async_copy(own_ref, out_ref.at[0], sems.at[0]),
        pltpu.make_async_copy(grad_ref, out_ref.at[1], sems.at[1]),
    ]
    for copy in copies:
        copy.start()
    for copy in copies:
        copy.wait()


def pack(own, grad):
    return pl.pallas_call(
        pack_kernel,
        out_shape=pltpu.VMEM((2, *own.shape), own.dtype),
        in_specs=[pl.BlockSpec(memory_space=pltpu.HBM)] * 2,
        out_specs=pl.BlockSpec(memory_space=pltpu.VMEM),
        scratch_shapes=[pltpu.SemaphoreType.DMA((2,))],
        cost_estimate=pl.CostEstimate(flops=1, bytes_accessed=1 << 17, transcendentals=0),
        compiler_params=pltpu.CompilerParams(vmem_limit_bytes=4 << 20),
    )(in_hbm(own), in_hbm(grad))


def load_kernel(weight_ref, evicted_ref, input_ref, gain_ref, *rest):
    weight_out, taken_out, input_out, gain_out, reach_ref, flags, sems = rest
    small = [
        pltpu.make_async_copy(evicted_ref, flags, sems.at[0]),
        pltpu.make_async_copy(gain_ref, gain_out, sems.at[1]),
        pltpu.make_async_copy(input_ref, input_out, sems.at[2]),
    ]
    for copy in small:
        copy.start()
    large = []
    features = weight_ref.shape[0]
    for j in range(PIECES):
        part = pl.ds(j * (features // PIECES), features // PIECES)
        large.append(
            pltpu.make_async_copy(weight_ref.at[part], weight_out.at[part], sems.at[3 + j])
        )
        large[-1].start()
    small[0].wait()
    tiles = evicted_ref.shape[1]
    rows = taken_out.shape[0] // tiles
    for tile in range(tiles):
        part = pl.ds(tile * rows, rows)
        taken = jnp.full((rows, taken_out.shape[1]), flags[0, tile], jnp.int32)
        taken_out[part, :] = taken.astype(jnp.float32).astype(taken_out.dtype)
    small[1].wait()
    small[2].wait()
    values = input_out[...].astype(jnp.float32)
    tokens = values.shape[0]
    reach_ref[tokens:, :] = jnp.zeros_like(reach_ref[tokens:, :])
    squares = as_row(jnp.sum(values * values, axis=1, keepdims=True))
    reach_ref[tokens:, :tokens] = as_parts(squares)
    gained = (values * gain_out[...]).astype(jnp.bfloat16)
    reach = jnp.zeros((tokens, weight_out.shape[1]), jnp.float32)
    for j, copy in enumerate(large):
        copy.wait()
        part = slice(j * (features // PIECES), (j + 1) * (features // PIECES))
        reach += jnp.dot(gained[:, part], weight_out[part, :], preferred_element_type=jnp.float32)
    reach_ref[:tokens, :] = reach.astype(reach_ref.dtype)


def load(weights, evicted, inputs, gain):
    tokens = inputs.shape[0]
    return pl.pallas_call(
        load_kernel,
        out_shape=(
            pltpu.VMEM(weights.shape, weights.dtype),
            pltpu.VMEM((tokens, tokens), jnp.bfloat16),
            pltpu.VMEM(inputs.shape, inputs.dtype),
            pltpu.VMEM(gain.shape, gain.dtype),
            pltpu.VMEM((tokens + EXTRA, weights.shape[1]), jnp.bfloat16),
        ),
        in_specs=[pl.BlockSpec(memory_space=pltpu.HBM)] * 4,
        out_specs=tuple(vmem_specs(5)),
        scratch_shapes=[
            pltpu.SMEM(evicted.shape, evicted.dtype),
            pltpu.SemaphoreType.DMA((3 + PIECES,)),
        ],
        cost_estimate=HIDES,
        compiler_params=pltpu.CompilerParams(vmem_limit_bytes=8 << 20),
    )(*map(in_hbm, (weights, evicted, inputs, gain)))


def mix_kernel(taken_ref, *refs):
    out_ref = refs[-1]
    taken = taken_ref[...]
    for j in range(out_ref.shape[0]):
        packed_ref, spare_ref = refs[2 * j], refs[2 * j + 1]
        out_ref[j] = lax.dot_general(
            packed_ref[0] * (1 - taken) + spare_ref[...] * taken,
            packed_ref[1],
            (((0,), (0,)), ((), ())),
            preferred_element_type=jnp.float32,
        ).astype(out_ref.dtype)


def value_gradients(taken, heads):
    return pl.pallas_call(
        mix_kernel,
        out_shape=pltpu.VMEM((len(heads), *heads[0][1].shape), jnp.bfloat16),
        in_specs=vmem_specs(1 + 2 * len(heads)),
        out_specs=pl.BlockSpec(memory_space=pltpu.VMEM),
        cost_estimate=HIDES,
        compiler_params=pltpu.CompilerParams(vmem_limit_bytes=4 << 20),
    )(*map(in_vmem, (taken, *[array for head in heads for array in head])))


def project_kernel(head_of, counts, *refs):
    blocks = refs[: len(counts)]
    rest = refs[len(counts) :]
    weight_ref, input_ref, gain_ref, *reach_refs, scaled_ref, sums_ref, flat = rest
    tokens, features = input_ref.shape
    place = 0
    for ref, count in zip(blocks, counts):
        for j in range(count):
            start = pl.multiple_of(head_of(place) * LANES, LANES)
            flat[:, pl.ds(start, LANES)] = ref[j]
            place += 1
    tile = 256 if features % 256 == 0 else features
    for start in range(0, features, tile):
        part = pl.ds(start, tile)
        grad_normed = lax.dot_general(
            flat[...],
            weight_ref[part, :],
            (((1,), (1,)), ((), ())),
            preferred_element_type=jnp.float32,
        )
        scaled_ref[:, part] = (grad_normed * gain_ref[:, part]).astype(scaled_ref.dtype)
    reach = sum(ref[:tokens, :].astype(jnp.float32) for ref in reach_refs)
    squares = sum(ref[tokens:, :tokens].astype(jnp.float32) for ref in reach_refs)
    squares = jnp.sum(squares, axis=0, keepdims=True)
    inner = jnp.sum(flat[...].astype(jnp.float32) * reach, axis=1, keepdims=True)
    sums_ref[:1, :] = squares
    sums_ref[1:, :] = as_row(inner)
    lane = lax.broadcasted_iota(jnp.int32, (tokens, LANES), 1)
    extra = jnp.zeros((tokens, LANES), jnp.float32)
    for j, part in enumerate(split(as_column(squares)) + split(inner)):
        extra = jnp.where(lane == j, part, extra)
    scaled_ref[:, features:] = extra.astype(scaled_ref.dtype)


def project(head_of, blocks, weights, inputs, gain, reaches):
    counts = tuple(block.shape[0] for block in blocks)
    tokens, features = inputs.shape
    return pl.pallas_call(
        functools.partial(project_kernel, head_of, counts),
        out_shape=(
            pltpu.VMEM((tokens, features + LANES), jnp.bfloat16),
            pltpu.VMEM((2, tokens), jnp.float32),
        ),
        in_specs=vmem_specs(len(blocks) + 3 + len(reaches)),
        out_specs=tuple(vmem_specs(2)),
        scratch_shapes=[pltpu.VMEM((tokens, weights.shape[1]), jnp.bfloat16)],
        cost_estimate=HIDES,
        compiler_params=pltpu.CompilerParams(vmem_limit_bytes=16 << 20),
    )(*map(in_vmem, (*blocks, weights, inputs, gain, *reaches)))


def finish_kernel(scaled_ref, input_ref, *refs):
    sums_refs, out_ref = refs[:-1], refs[-1]
    features = input_ref.shape[1]
    extra = scaled_ref[:, features:].astype(jnp.float32)
    lane = lax.broadcasted_iota(jnp.int32, extra.shape, 1)
    squares = jnp.sum(jnp.where(lane < 3, extra, 0.0), axis=1, keepdims=True)
    inner = jnp.sum(jnp.where(lane < 3, 0.0, extra), axis=1, keepdims=True)
    if sums_refs:
        sums = sum(ref[...] for ref in sums_refs)
        squares = squares + as_column(sums[:1])
        inner = inner + as_column(sums[1:])
    inv = 1.0 / jnp.sqrt(squares / D + 1e-05)
    factor = inner * (inv * inv * inv) / D
    scaled = scaled_ref[:, :features].astype(jnp.float32)
    values = input_ref[...].astype(jnp.float32)
    out_ref[...] = (scaled * inv - values * factor).astype(out_ref.dtype)


def finish(scaled, inputs, sums):
    return pl.pallas_call(
        finish_kernel,
        out_shape=jax.ShapeDtypeStruct(inputs.shape, jnp.bfloat16),
        in_specs=vmem_specs(2 + len(sums)),
        out_specs=pl.BlockSpec(memory_space=pltpu.VMEM),
        compiler_params=pltpu.CompilerParams(vmem_limit_bytes=8 << 20),
    )(*map(in_vmem, (scaled, inputs, *sums)))


FAR, NEAR, SIDE = 4, 2, 1
LINE = (NEAR, FAR, FAR | NEAR)


def handed_over(block, sections, count, distance, mask):
    route = [
        ((s - distance) % sections * count + (i ^ mask), s * count + i)
        for s in range(sections)
        for i in range(count)
    ]
    return lax.ppermute(block, ("section", "tp"), route)


def gathered(pair, axis):
    if lax.axis_size(axis) != 8:
        return [lax.all_gather(pair[0], axis)], lambda place: place
    blocks = [pair] + [swapped(pair, axis, mask) for mask in LINE]
    masks = [far | side for far in (0, *LINE) for side in (0, SIDE)]

    def head_of(place):
        return lax.axis_index(axis) ^ masks[place]

    return blocks, head_of


def per_device(grad_attn, w_value, probs_own, probs_spare, evicted, layer_input, gain):
    sections, count = lax.axis_size("section"), lax.axis_size("tp")
    packed = pack(probs_own[0, 0], grad_attn[0, 0])
    heads = []
    for mask in (0, SIDE) if count == 8 else (0,):
        spare = handed_over(probs_spare[0, 0], sections, count, sections // 2, mask)
        heads.append((swapped(packed, "tp", mask) if mask else packed, spare))
    weights, taken, inputs, gains, reach = load(w_value[0], evicted, layer_input[0], gain)
    next_input = passed_along(inputs, "section", -1)
    if count == 8:
        reaches = [reach, swapped(reach, "tp", SIDE)]
    else:
        reaches = [lax.psum(reach, "tp")]
    pair = value_gradients(taken, heads)
    blocks, head_of = gathered(pair, "tp")
    scaled, sums = project(head_of, blocks, weights, inputs, gains, reaches)
    scaled, next_input = lax.optimization_barrier((scaled, next_input))
    next_scaled = passed_along(scaled, "section", -1)
    next_sums = []
    for mask in LINE if count == 8 else ():
        next_sums.append(handed_over(sums, sections, count, -1, mask))
    return finish(next_scaled, next_input, next_sums)[None]


def solution(mesh):
    in_specs = (
        P("section", "tp", None, None),
        P("section", "tp", None),
        P("section", "tp", None, None),
        P("section", "tp", None, None),
        P("section", None),
        P("section", None, "tp"),
        P("section", "tp"),
    )
    out_specs = P("section", None, "tp")
    return jax.shard_map(
        per_device, mesh=mesh, in_specs=in_specs, out_specs=out_specs, check_vma=False
    )
```

```python
import functools

import jax
import jax.numpy as jnp
from jax import lax
from jax.experimental import pallas as pl
from jax.experimental.pallas import tpu as pltpu
from jax.sharding import PartitionSpec as P

D = 12288
LANES = 128
EXTRA = 16
HIDES = pl.CostEstimate(flops=1 << 35, bytes_accessed=1 << 25, transcendentals=0)


def passed_along(block, axis, distance):
    devices = range(lax.axis_size(axis))
    route = [((i - distance) % len(devices), i) for i in devices]
    return lax.ppermute(block, axis, route)


def swapped(block, axis, mask):
    return lax.ppermute(block, axis, [(i ^ mask, i) for i in range(lax.axis_size(axis))])


def in_vmem(array):
    return pltpu.with_memory_space_constraint(array, pltpu.VMEM)


def in_hbm(array):
    return pltpu.with_memory_space_constraint(array, pltpu.HBM)


def vmem_specs(count):
    return [pl.BlockSpec(memory_space=pltpu.VMEM)] * count


def as_row(column):
    return jnp.broadcast_to(column, (column.shape[0], column.shape[0])).T[:1]


def as_column(row):
    return jnp.broadcast_to(row, (row.shape[1], row.shape[1])).T[:, :1]


def split(values):
    parts = []
    for _ in range(3):
        parts.append(values.astype(jnp.bfloat16).astype(jnp.float32))
        values = values - parts[-1]
    return parts


def as_parts(row):
    rest = jnp.zeros((EXTRA - 3, row.shape[1]), jnp.float32)
    return jnp.concatenate(split(row) + [rest]).astype(jnp.bfloat16)


def pack_kernel(own_ref, grad_ref, evicted_ref, out_ref, taken_ref, flags, sems):
    copies = [
        pltpu.make_async_copy(evicted_ref, flags, sems.at[0]),
        pltpu.make_async_copy(own_ref, out_ref.at[0], sems.at[1]),
        pltpu.make_async_copy(grad_ref, out_ref.at[1], sems.at[2]),
    ]
    for copy in copies:
        copy.start()
    copies[0].wait()
    tiles = evicted_ref.shape[1]
    rows = taken_ref.shape[0] // tiles
    for tile in range(tiles):
        part = pl.ds(tile * rows, rows)
        taken = jnp.full((rows, taken_ref.shape[1]), flags[0, tile], jnp.int32)
        taken_ref[part, :] = taken.astype(jnp.float32).astype(taken_ref.dtype)
    copies[1].wait()
    copies[2].wait()


def pack(own, grad, evicted):
    return pl.pallas_call(
        pack_kernel,
        out_shape=(pltpu.VMEM((2, *own.shape), own.dtype), pltpu.VMEM(own.shape, own.dtype)),
        in_specs=[pl.BlockSpec(memory_space=pltpu.HBM)] * 3,
        out_specs=tuple(vmem_specs(2)),
        scratch_shapes=[
            pltpu.SMEM(evicted.shape, evicted.dtype),
            pltpu.SemaphoreType.DMA((3,)),
        ],
        cost_estimate=HIDES,
        compiler_params=pltpu.CompilerParams(vmem_limit_bytes=4 << 20),
    )(*map(in_hbm, (own, grad, evicted)))


def reach_kernel(weight_ref, input_ref, gain_ref, reach_ref):
    tokens, features = input_ref.shape
    values = input_ref[...].astype(jnp.float32)
    reach_ref[tokens:, :] = jnp.zeros_like(reach_ref[tokens:, :])
    squares = as_row(jnp.sum(values * values, axis=1, keepdims=True))
    reach_ref[tokens:, :tokens] = as_parts(squares)
    gained = (values * gain_ref[...]).astype(jnp.bfloat16)
    reach = jnp.dot(gained, weight_ref[...], preferred_element_type=jnp.float32)
    reach_ref[:tokens, :] = reach.astype(reach_ref.dtype)


def reach_of(weights, inputs, gain):
    return pl.pallas_call(
        reach_kernel,
        out_shape=pltpu.VMEM((inputs.shape[0] + EXTRA, weights.shape[1]), jnp.bfloat16),
        in_specs=vmem_specs(3),
        out_specs=pl.BlockSpec(memory_space=pltpu.VMEM),
        cost_estimate=HIDES,
        compiler_params=pltpu.CompilerParams(vmem_limit_bytes=8 << 20),
    )(*map(in_vmem, (weights, inputs, gain)))


def mix_kernel(taken_ref, *refs):
    out_ref = refs[-1]
    taken = taken_ref[...]
    for j in range(out_ref.shape[0]):
        packed_ref, spare_ref = refs[2 * j], refs[2 * j + 1]
        out_ref[j] = lax.dot_general(
            packed_ref[0] * (1 - taken) + spare_ref[...] * taken,
            packed_ref[1],
            (((0,), (0,)), ((), ())),
            preferred_element_type=jnp.float32,
        ).astype(out_ref.dtype)


def value_gradients(taken, heads):
    return pl.pallas_call(
        mix_kernel,
        out_shape=pltpu.VMEM((len(heads), *heads[0][1].shape), jnp.bfloat16),
        in_specs=vmem_specs(1 + 2 * len(heads)),
        out_specs=pl.BlockSpec(memory_space=pltpu.VMEM),
        cost_estimate=HIDES,
        compiler_params=pltpu.CompilerParams(vmem_limit_bytes=4 << 20),
    )(*map(in_vmem, (taken, *[array for head in heads for array in head])))


def project_kernel(head_of, counts, *refs):
    blocks = refs[: len(counts)]
    rest = refs[len(counts) :]
    weight_ref, input_ref, gain_ref, *reach_refs, scaled_ref, sums_ref, flat = rest
    tokens, features = input_ref.shape
    place = 0
    for ref, count in zip(blocks, counts):
        for j in range(count):
            start = pl.multiple_of(head_of(place) * LANES, LANES)
            flat[:, pl.ds(start, LANES)] = ref[j]
            place += 1
    tile = 256 if features % 256 == 0 else features
    for start in range(0, features, tile):
        part = pl.ds(start, tile)
        grad_normed = lax.dot_general(
            flat[...],
            weight_ref[part, :],
            (((1,), (1,)), ((), ())),
            preferred_element_type=jnp.float32,
        )
        scaled_ref[:, part] = (grad_normed * gain_ref[:, part]).astype(scaled_ref.dtype)
    reach = sum(ref[:tokens, :].astype(jnp.float32) for ref in reach_refs)
    squares = sum(ref[tokens:, :tokens].astype(jnp.float32) for ref in reach_refs)
    squares = jnp.sum(squares, axis=0, keepdims=True)
    inner = jnp.sum(flat[...].astype(jnp.float32) * reach, axis=1, keepdims=True)
    sums_ref[:1, :] = squares
    sums_ref[1:, :] = as_row(inner)
    lane = lax.broadcasted_iota(jnp.int32, (tokens, LANES), 1)
    extra = jnp.zeros((tokens, LANES), jnp.float32)
    for j, part in enumerate(split(as_column(squares)) + split(inner)):
        extra = jnp.where(lane == j, part, extra)
    scaled_ref[:, features:] = extra.astype(scaled_ref.dtype)


def project(head_of, blocks, weights, inputs, gain, reaches):
    counts = tuple(block.shape[0] for block in blocks)
    tokens, features = inputs.shape
    return pl.pallas_call(
        functools.partial(project_kernel, head_of, counts),
        out_shape=(
            pltpu.VMEM((tokens, features + LANES), jnp.bfloat16),
            pltpu.VMEM((2, tokens), jnp.float32),
        ),
        in_specs=vmem_specs(len(blocks) + 3 + len(reaches)),
        out_specs=tuple(vmem_specs(2)),
        scratch_shapes=[pltpu.VMEM((tokens, weights.shape[1]), jnp.bfloat16)],
        cost_estimate=HIDES,
        compiler_params=pltpu.CompilerParams(vmem_limit_bytes=16 << 20),
    )(*map(in_vmem, (*blocks, weights, inputs, gain, *reaches)))


def finish_kernel(scaled_ref, input_ref, *refs):
    sums_refs, out_ref = refs[:-1], refs[-1]
    features = input_ref.shape[1]
    extra = scaled_ref[:, features:].astype(jnp.float32)
    lane = lax.broadcasted_iota(jnp.int32, extra.shape, 1)
    squares = jnp.sum(jnp.where(lane < 3, extra, 0.0), axis=1, keepdims=True)
    inner = jnp.sum(jnp.where(lane < 3, 0.0, extra), axis=1, keepdims=True)
    if sums_refs:
        sums = sum(ref[...] for ref in sums_refs)
        squares = squares + as_column(sums[:1])
        inner = inner + as_column(sums[1:])
    inv = 1.0 / jnp.sqrt(squares / D + 1e-05)
    factor = inner * (inv * inv * inv) / D
    scaled = scaled_ref[:, :features].astype(jnp.float32)
    values = input_ref[...].astype(jnp.float32)
    out_ref[...] = (scaled * inv - values * factor).astype(out_ref.dtype)


def finish(scaled, inputs, sums):
    return pl.pallas_call(
        finish_kernel,
        out_shape=jax.ShapeDtypeStruct(inputs.shape, jnp.bfloat16),
        in_specs=vmem_specs(2 + len(sums)),
        out_specs=pl.BlockSpec(memory_space=pltpu.VMEM),
        compiler_params=pltpu.CompilerParams(vmem_limit_bytes=8 << 20),
    )(*map(in_vmem, (scaled, inputs, *sums)))


FAR, NEAR, SIDE = 4, 2, 1
LINE = (NEAR, FAR, FAR | NEAR)


def handed_over(block, sections, count, distance, mask):
    route = [
        ((s - distance) % sections * count + (i ^ mask), s * count + i)
        for s in range(sections)
        for i in range(count)
    ]
    return lax.ppermute(block, ("section", "tp"), route)


def gathered(pair, axis):
    if lax.axis_size(axis) != 8:
        return [lax.all_gather(pair[0], axis)], lambda place: place
    blocks = [pair] + [swapped(pair, axis, mask) for mask in LINE]
    masks = [far | side for far in (0, *LINE) for side in (0, SIDE)]

    def head_of(place):
        return lax.axis_index(axis) ^ masks[place]

    return blocks, head_of


def per_device(grad_attn, w_value, probs_own, probs_spare, evicted, layer_input, gain):
    sections, count = lax.axis_size("section"), lax.axis_size("tp")
    packed, taken = pack(probs_own[0, 0], grad_attn[0, 0], evicted)
    heads = []
    for mask in (0, SIDE) if count == 8 else (0,):
        spare = handed_over(probs_spare[0, 0], sections, count, sections // 2, mask)
        heads.append((swapped(packed, "tp", mask) if mask else packed, spare))
    weights, inputs = w_value[0], layer_input[0]
    next_input = passed_along(inputs, "section", -1)
    reach = reach_of(weights, inputs, gain)
    if count == 8:
        reaches = [reach, swapped(reach, "tp", SIDE)]
        reaches[1], next_input = lax.optimization_barrier((reaches[1], next_input))
    else:
        reaches = [lax.psum(reach, "tp")]
    pair = value_gradients(taken, heads)
    blocks, head_of = gathered(pair, "tp")
    scaled, sums = project(head_of, blocks, weights, inputs, gain, reaches)
    next_scaled = passed_along(scaled, "section", -1)
    next_sums = []
    for mask in LINE if count == 8 else ():
        next_sums.append(handed_over(sums, sections, count, -1, mask))
    return finish(next_scaled, next_input, next_sums)[None]


def solution(mesh):
    in_specs = (
        P("section", "tp", None, None),
        P("section", "tp", None),
        P("section", "tp", None, None),
        P("section", "tp", None, None),
        P("section", None),
        P("section", None, "tp"),
        P("section", "tp"),
    )
    out_specs = P("section", None, "tp")
    return jax.shard_map(
        per_device, mesh=mesh, in_specs=in_specs, out_specs=out_specs, check_vma=False
    )
```

```python
import functools

import jax
import jax.numpy as jnp
from jax import lax
from jax.experimental import pallas as pl
from jax.experimental.pallas import tpu as pltpu
from jax.sharding import PartitionSpec as P

D = 12288
LANES = 128
PIECES = 4
EXTRA = 16
HIDES = pl.CostEstimate(flops=1 << 35, bytes_accessed=1 << 25, transcendentals=0)


def passed_along(block, axis, distance):
    devices = range(lax.axis_size(axis))
    route = [((i - distance) % len(devices), i) for i in devices]
    return lax.ppermute(block, axis, route)


def swapped(block, axis, mask):
    return lax.ppermute(block, axis, [(i ^ mask, i) for i in range(lax.axis_size(axis))])


def in_vmem(array):
    return pltpu.with_memory_space_constraint(array, pltpu.VMEM)


def in_hbm(array):
    return pltpu.with_memory_space_constraint(array, pltpu.HBM)


def vmem_specs(count):
    return [pl.BlockSpec(memory_space=pltpu.VMEM)] * count


def as_row(column):
    return jnp.broadcast_to(column, (column.shape[0], column.shape[0])).T[:1]


def as_column(row):
    return jnp.broadcast_to(row, (row.shape[1], row.shape[1])).T[:, :1]


def split(values):
    parts = []
    for _ in range(3):
        parts.append(values.astype(jnp.bfloat16).astype(jnp.float32))
        values = values - parts[-1]
    return parts


def as_parts(row):
    rest = jnp.zeros((EXTRA - 3, row.shape[1]), jnp.float32)
    return jnp.concatenate(split(row) + [rest]).astype(jnp.bfloat16)


def pack_kernel(own_ref, grad_ref, spare_ref, evicted_ref, *refs):
    out_ref, spare_out, taken_ref, flags, sems = refs
    copies = [
        pltpu.make_async_copy(evicted_ref, flags, sems.at[0]),
        pltpu.make_async_copy(own_ref, out_ref.at[0], sems.at[1]),
        pltpu.make_async_copy(grad_ref, out_ref.at[1], sems.at[2]),
        pltpu.make_async_copy(spare_ref, spare_out, sems.at[3]),
    ]
    for copy in copies:
        copy.start()
    copies[0].wait()
    tiles = evicted_ref.shape[1]
    rows = taken_ref.shape[0] // tiles
    for tile in range(tiles):
        part = pl.ds(tile * rows, rows)
        taken = jnp.full((rows, taken_ref.shape[1]), flags[0, tile], jnp.int32)
        taken_ref[part, :] = taken.astype(jnp.float32).astype(taken_ref.dtype)
    for copy in copies[1:]:
        copy.wait()


def pack(own, grad, spare, evicted):
    return pl.pallas_call(
        pack_kernel,
        out_shape=(
            pltpu.VMEM((2, *own.shape), own.dtype),
            pltpu.VMEM(spare.shape, spare.dtype),
            pltpu.VMEM(own.shape, own.dtype),
        ),
        in_specs=[pl.BlockSpec(memory_space=pltpu.HBM)] * 4,
        out_specs=tuple(vmem_specs(3)),
        scratch_shapes=[
            pltpu.SMEM(evicted.shape, evicted.dtype),
            pltpu.SemaphoreType.DMA((4,)),
        ],
        cost_estimate=HIDES,
        compiler_params=pltpu.CompilerParams(vmem_limit_bytes=4 << 20),
    )(*map(in_hbm, (own, grad, spare, evicted)))


def reach_kernel(weight_ref, input_ref, gain_ref, reach_ref):
    tokens, features = input_ref.shape
    values = input_ref[...].astype(jnp.float32)
    reach_ref[tokens:, :] = jnp.zeros_like(reach_ref[tokens:, :])
    squares = as_row(jnp.sum(values * values, axis=1, keepdims=True))
    reach_ref[tokens:, :tokens] = as_parts(squares)
    gained = (values * gain_ref[...]).astype(jnp.bfloat16)
    reach = jnp.dot(gained, weight_ref[...], preferred_element_type=jnp.float32)
    reach_ref[:tokens, :] = reach.astype(reach_ref.dtype)


def reach_of(weights, inputs, gain):
    return pl.pallas_call(
        reach_kernel,
        out_shape=pltpu.VMEM((inputs.shape[0] + EXTRA, weights.shape[1]), jnp.bfloat16),
        in_specs=vmem_specs(3),
        out_specs=pl.BlockSpec(memory_space=pltpu.VMEM),
        cost_estimate=HIDES,
        compiler_params=pltpu.CompilerParams(vmem_limit_bytes=8 << 20),
    )(*map(in_vmem, (weights, inputs, gain)))


def mix_kernel(taken_ref, *refs):
    out_ref = refs[-1]
    taken = taken_ref[...]
    for j in range(out_ref.shape[0]):
        packed_ref, spare_ref = refs[len(refs) - 2 - j], refs[j]
        out_ref[j] = lax.dot_general(
            packed_ref[0] * (1 - taken) + spare_ref[...] * taken,
            packed_ref[1],
            (((0,), (0,)), ((), ())),
            preferred_element_type=jnp.float32,
        ).astype(out_ref.dtype)


def value_gradients(taken, heads):
    return pl.pallas_call(
        mix_kernel,
        out_shape=pltpu.VMEM((len(heads), *heads[0][1].shape), jnp.bfloat16),
        in_specs=vmem_specs(1 + 2 * len(heads)),
        out_specs=pl.BlockSpec(memory_space=pltpu.VMEM),
        cost_estimate=HIDES,
        compiler_params=pltpu.CompilerParams(vmem_limit_bytes=4 << 20),
    )(*map(in_vmem, (taken, *[spare for _, spare in heads], *[packed for packed, _ in heads[::-1]])))


def project_kernel(head_of, counts, *refs):
    blocks = refs[: len(counts)]
    rest = refs[len(counts) :]
    weight_ref, input_ref, gain_ref, *reach_refs, scaled_ref, sums_ref, flat = rest
    tokens, features = input_ref.shape
    place = 0
    for ref, count in zip(blocks, counts):
        for j in range(count):
            start = pl.multiple_of(head_of(place) * LANES, LANES)
            flat[:, pl.ds(start, LANES)] = ref[j]
            place += 1
    tile = 256 if features % 256 == 0 else features
    for start in range(0, features, tile):
        part = pl.ds(start, tile)
        grad_normed = lax.dot_general(
            flat[...],
            weight_ref[part, :],
            (((1,), (1,)), ((), ())),
            preferred_element_type=jnp.float32,
        )
        scaled_ref[:, part] = (grad_normed * gain_ref[:, part]).astype(scaled_ref.dtype)
    reach = sum(ref[:tokens, :].astype(jnp.float32) for ref in reach_refs)
    squares = sum(ref[tokens:, :tokens].astype(jnp.float32) for ref in reach_refs)
    squares = jnp.sum(squares, axis=0, keepdims=True)
    inner = jnp.sum(flat[...].astype(jnp.float32) * reach, axis=1, keepdims=True)
    sums_ref[:1, :] = squares
    sums_ref[1:, :] = as_row(inner)
    lane = lax.broadcasted_iota(jnp.int32, (tokens, LANES), 1)
    extra = jnp.zeros((tokens, LANES), jnp.float32)
    for j, part in enumerate(split(as_column(squares)) + split(inner)):
        extra = jnp.where(lane == j, part, extra)
    scaled_ref[:, features:] = extra.astype(scaled_ref.dtype)


def project(head_of, blocks, weights, inputs, gain, reaches):
    counts = tuple(block.shape[0] for block in blocks)
    tokens, features = inputs.shape
    return pl.pallas_call(
        functools.partial(project_kernel, head_of, counts),
        out_shape=(
            pltpu.VMEM((tokens, features + LANES), jnp.bfloat16),
            pltpu.VMEM((2, tokens), jnp.float32),
        ),
        in_specs=vmem_specs(len(blocks) + 3 + len(reaches)),
        out_specs=tuple(vmem_specs(2)),
        scratch_shapes=[pltpu.VMEM((tokens, weights.shape[1]), jnp.bfloat16)],
        cost_estimate=HIDES,
        compiler_params=pltpu.CompilerParams(vmem_limit_bytes=16 << 20),
    )(*map(in_vmem, (*blocks, weights, inputs, gain, *reaches)))


def finish_kernel(scaled_ref, input_ref, *refs):
    *sums_refs, out_ref, held, sems = refs
    tokens, features = input_ref.shape
    extra = scaled_ref[:, features:].astype(jnp.float32)
    lane = lax.broadcasted_iota(jnp.int32, extra.shape, 1)
    squares = jnp.sum(jnp.where(lane < 3, extra, 0.0), axis=1, keepdims=True)
    inner = jnp.sum(jnp.where(lane < 3, 0.0, extra), axis=1, keepdims=True)
    if sums_refs:
        sums = sum(ref[...] for ref in sums_refs)
        squares = squares + as_column(sums[:1])
        inner = inner + as_column(sums[1:])
    inv = 1.0 / jnp.sqrt(squares / D + 1e-05)
    factor = inner * (inv * inv * inv) / D
    rows = tokens // PIECES
    copies = []
    for j in range(PIECES):
        part = slice(j * rows, (j + 1) * rows)
        scaled = scaled_ref[part, :features].astype(jnp.float32)
        values = input_ref[part, :].astype(jnp.float32)
        held[part, :] = (scaled * inv[part] - values * factor[part]).astype(held.dtype)
        copies.append(pltpu.make_async_copy(held.at[part], out_ref.at[part], sems.at[j]))
        copies[-1].start()
    for copy in copies:
        copy.wait()


def finish(scaled, inputs, sums):
    return pl.pallas_call(
        finish_kernel,
        out_shape=pltpu.HBM(inputs.shape, jnp.bfloat16),
        in_specs=vmem_specs(2 + len(sums)),
        out_specs=pl.BlockSpec(memory_space=pltpu.HBM),
        scratch_shapes=[
            pltpu.VMEM(inputs.shape, jnp.bfloat16),
            pltpu.SemaphoreType.DMA((PIECES,)),
        ],
        compiler_params=pltpu.CompilerParams(vmem_limit_bytes=8 << 20),
    )(*map(in_vmem, (scaled, inputs, *sums)))


FAR, NEAR, SIDE = 4, 2, 1
LINE = (NEAR, FAR, FAR | NEAR)


def handed_over(block, sections, count, distance, mask):
    route = [
        ((s - distance) % sections * count + (i ^ mask), s * count + i)
        for s in range(sections)
        for i in range(count)
    ]
    return lax.ppermute(block, ("section", "tp"), route)


def gathered(pair, axis):
    if lax.axis_size(axis) != 8:
        return [lax.all_gather(pair[0], axis)], lambda place: place
    blocks = [pair] + [swapped(pair, axis, mask) for mask in LINE]
    masks = [far | side for far in (0, *LINE) for side in (0, SIDE)]

    def head_of(place):
        return lax.axis_index(axis) ^ masks[place]

    return blocks, head_of


def per_device(grad_attn, w_value, probs_own, probs_spare, evicted, layer_input, gain):
    sections, count = lax.axis_size("section"), lax.axis_size("tp")
    packed, spares, taken = pack(probs_own[0, 0], grad_attn[0, 0], probs_spare[0, 0], evicted)
    heads = []
    for mask in (0, SIDE) if count == 8 else (0,):
        spare = handed_over(spares, sections, count, sections // 2, mask)
        heads.append((swapped(packed, "tp", mask) if mask else packed, spare))
    weights, inputs = w_value[0], layer_input[0]
    next_input = passed_along(inputs, "section", -1)
    reach = reach_of(weights, inputs, gain)
    if count == 8:
        reaches = [reach, swapped(reach, "tp", SIDE)]
        reaches[1], next_input = lax.optimization_barrier((reaches[1], next_input))
    else:
        reaches = [lax.psum(reach, "tp")]
    pair = value_gradients(taken, heads)
    blocks, head_of = gathered(pair, "tp")
    scaled, sums = project(head_of, blocks, weights, inputs, gain, reaches)
    next_scaled = passed_along(scaled, "section", -1)
    next_sums = []
    for mask in LINE if count == 8 else ():
        next_sums.append(handed_over(sums, sections, count, -1, mask))
    return finish(next_scaled, next_input, next_sums)[None]


def solution(mesh):
    in_specs = (
        P("section", "tp", None, None),
        P("section", "tp", None),
        P("section", "tp", None, None),
        P("section", "tp", None, None),
        P("section", None),
        P("section", None, "tp"),
        P("section", "tp"),
    )
    out_specs = P("section", None, "tp")
    return jax.shard_map(
        per_device, mesh=mesh, in_specs=in_specs, out_specs=out_specs, check_vma=False
    )
```

```python
import functools

import jax
import jax.numpy as jnp
from jax import lax
from jax.experimental import pallas as pl
from jax.experimental.pallas import tpu as pltpu
from jax.sharding import PartitionSpec as P

D = 12288
LANES = 128
PIECES = 4
EXTRA = 16
HIDES = pl.CostEstimate(flops=1 << 35, bytes_accessed=1 << 25, transcendentals=0)


def passed_along(block, axis, distance):
    devices = range(lax.axis_size(axis))
    route = [((i - distance) % len(devices), i) for i in devices]
    return lax.ppermute(block, axis, route)


def swapped(block, axis, mask):
    return lax.ppermute(block, axis, [(i ^ mask, i) for i in range(lax.axis_size(axis))])


def in_vmem(array):
    return pltpu.with_memory_space_constraint(array, pltpu.VMEM)


def in_hbm(array):
    return pltpu.with_memory_space_constraint(array, pltpu.HBM)


def vmem_specs(count):
    return [pl.BlockSpec(memory_space=pltpu.VMEM)] * count


def as_row(column):
    return jnp.broadcast_to(column, (column.shape[0], column.shape[0])).T[:1]


def as_column(row):
    return jnp.broadcast_to(row, (row.shape[1], row.shape[1])).T[:, :1]


def split(values):
    parts = []
    for _ in range(3):
        parts.append(values.astype(jnp.bfloat16).astype(jnp.float32))
        values = values - parts[-1]
    return parts


def as_parts(row):
    rest = jnp.zeros((EXTRA - 3, row.shape[1]), jnp.float32)
    return jnp.concatenate(split(row) + [rest]).astype(jnp.bfloat16)


def pack_kernel(own_ref, grad_ref, spare_ref, evicted_ref, *refs):
    out_ref, spare_out, taken_ref, flags, sems = refs
    copies = [
        pltpu.make_async_copy(evicted_ref, flags, sems.at[0]),
        pltpu.make_async_copy(own_ref, out_ref.at[0], sems.at[1]),
        pltpu.make_async_copy(grad_ref, out_ref.at[1], sems.at[2]),
        pltpu.make_async_copy(spare_ref, spare_out, sems.at[3]),
    ]
    for copy in copies:
        copy.start()
    copies[0].wait()
    tiles = evicted_ref.shape[1]
    rows = taken_ref.shape[0] // tiles
    for tile in range(tiles):
        part = pl.ds(tile * rows, rows)
        taken = jnp.full((rows, taken_ref.shape[1]), flags[0, tile], jnp.int32)
        taken_ref[part, :] = taken.astype(jnp.float32).astype(taken_ref.dtype)
    for copy in copies[1:]:
        copy.wait()


def pack(own, grad, spare, evicted):
    return pl.pallas_call(
        pack_kernel,
        out_shape=(
            pltpu.VMEM((2, *own.shape), own.dtype),
            pltpu.VMEM(spare.shape, spare.dtype),
            pltpu.VMEM(own.shape, own.dtype),
        ),
        in_specs=[pl.BlockSpec(memory_space=pltpu.HBM)] * 4,
        out_specs=tuple(vmem_specs(3)),
        scratch_shapes=[
            pltpu.SMEM(evicted.shape, evicted.dtype),
            pltpu.SemaphoreType.DMA((4,)),
        ],
        cost_estimate=HIDES,
        compiler_params=pltpu.CompilerParams(vmem_limit_bytes=4 << 20),
    )(*map(in_hbm, (own, grad, spare, evicted)))


def reach_kernel(weight_ref, input_ref, gain_ref, first_ref, reach_ref):
    del first_ref
    tokens, features = input_ref.shape
    values = input_ref[...].astype(jnp.float32)
    reach_ref[tokens:, :] = jnp.zeros_like(reach_ref[tokens:, :])
    squares = as_row(jnp.sum(values * values, axis=1, keepdims=True))
    reach_ref[tokens:, :tokens] = as_parts(squares)
    gained = (values * gain_ref[...]).astype(jnp.bfloat16)
    reach = jnp.dot(gained, weight_ref[...], preferred_element_type=jnp.float32)
    reach_ref[:tokens, :] = reach.astype(reach_ref.dtype)


def reach_of(weights, inputs, gain, first):
    return pl.pallas_call(
        reach_kernel,
        out_shape=pltpu.VMEM((inputs.shape[0] + EXTRA, weights.shape[1]), jnp.bfloat16),
        in_specs=vmem_specs(4),
        out_specs=pl.BlockSpec(memory_space=pltpu.VMEM),
        cost_estimate=HIDES,
        compiler_params=pltpu.CompilerParams(vmem_limit_bytes=8 << 20),
    )(*map(in_vmem, (weights, inputs, gain, first)))


def mix_kernel(taken_ref, *refs):
    out_ref = refs[-1]
    taken = taken_ref[...]
    for j in range(out_ref.shape[0]):
        packed_ref, spare_ref = refs[len(refs) - 2 - j], refs[j]
        out_ref[j] = lax.dot_general(
            packed_ref[0] * (1 - taken) + spare_ref[...] * taken,
            packed_ref[1],
            (((0,), (0,)), ((), ())),
            preferred_element_type=jnp.float32,
        ).astype(out_ref.dtype)


def value_gradients(taken, heads):
    return pl.pallas_call(
        mix_kernel,
        out_shape=pltpu.VMEM((len(heads), *heads[0][1].shape), jnp.bfloat16),
        in_specs=vmem_specs(1 + 2 * len(heads)),
        out_specs=pl.BlockSpec(memory_space=pltpu.VMEM),
        cost_estimate=HIDES,
        compiler_params=pltpu.CompilerParams(vmem_limit_bytes=4 << 20),
    )(*map(in_vmem, (taken, *[spare for _, spare in heads], *[packed for packed, _ in heads[::-1]])))


def project_kernel(head_of, counts, *refs):
    blocks = refs[: len(counts)]
    rest = refs[len(counts) :]
    weight_ref, input_ref, gain_ref, *reach_refs, scaled_ref, sums_ref, flat = rest
    tokens, features = input_ref.shape
    place = 0
    for ref, count in zip(blocks, counts):
        for j in range(count):
            start = pl.multiple_of(head_of(place) * LANES, LANES)
            flat[:, pl.ds(start, LANES)] = ref[j]
            place += 1
    tile = 256 if features % 256 == 0 else features
    for start in range(0, features, tile):
        part = pl.ds(start, tile)
        grad_normed = lax.dot_general(
            flat[...],
            weight_ref[part, :],
            (((1,), (1,)), ((), ())),
            preferred_element_type=jnp.float32,
        )
        scaled_ref[:, part] = (grad_normed * gain_ref[:, part]).astype(scaled_ref.dtype)
    reach = sum(ref[:tokens, :].astype(jnp.float32) for ref in reach_refs)
    squares = sum(ref[tokens:, :tokens].astype(jnp.float32) for ref in reach_refs)
    squares = jnp.sum(squares, axis=0, keepdims=True)
    inner = jnp.sum(flat[...].astype(jnp.float32) * reach, axis=1, keepdims=True)
    sums_ref[:1, :] = squares
    sums_ref[1:, :] = as_row(inner)
    lane = lax.broadcasted_iota(jnp.int32, (tokens, LANES), 1)
    extra = jnp.zeros((tokens, LANES), jnp.float32)
    for j, part in enumerate(split(as_column(squares)) + split(inner)):
        extra = jnp.where(lane == j, part, extra)
    scaled_ref[:, features:] = extra.astype(scaled_ref.dtype)


def project(head_of, blocks, weights, inputs, gain, reaches):
    counts = tuple(block.shape[0] for block in blocks)
    tokens, features = inputs.shape
    return pl.pallas_call(
        functools.partial(project_kernel, head_of, counts),
        out_shape=(
            pltpu.VMEM((tokens, features + LANES), jnp.bfloat16),
            pltpu.VMEM((2, tokens), jnp.float32),
        ),
        in_specs=vmem_specs(len(blocks) + 3 + len(reaches)),
        out_specs=tuple(vmem_specs(2)),
        scratch_shapes=[pltpu.VMEM((tokens, weights.shape[1]), jnp.bfloat16)],
        cost_estimate=HIDES,
        compiler_params=pltpu.CompilerParams(vmem_limit_bytes=16 << 20),
    )(*map(in_vmem, (*blocks, weights, inputs, gain, *reaches)))


def finish_kernel(scaled_ref, input_ref, *refs):
    *sums_refs, out_ref, held, sems = refs
    tokens, features = input_ref.shape
    extra = scaled_ref[:, features:].astype(jnp.float32)
    lane = lax.broadcasted_iota(jnp.int32, extra.shape, 1)
    squares = jnp.sum(jnp.where(lane < 3, extra, 0.0), axis=1, keepdims=True)
    inner = jnp.sum(jnp.where(lane < 3, 0.0, extra), axis=1, keepdims=True)
    if sums_refs:
        sums = sum(ref[...] for ref in sums_refs)
        squares = squares + as_column(sums[:1])
        inner = inner + as_column(sums[1:])
    inv = 1.0 / jnp.sqrt(squares / D + 1e-05)
    factor = inner * (inv * inv * inv) / D
    rows = tokens // PIECES
    copies = []
    for j in range(PIECES):
        part = slice(j * rows, (j + 1) * rows)
        scaled = scaled_ref[part, :features].astype(jnp.float32)
        values = input_ref[part, :].astype(jnp.float32)
        held[part, :] = (scaled * inv[part] - values * factor[part]).astype(held.dtype)
        copies.append(pltpu.make_async_copy(held.at[part], out_ref.at[part], sems.at[j]))
        copies[-1].start()
    for copy in copies:
        copy.wait()


def finish(scaled, inputs, sums):
    return pl.pallas_call(
        finish_kernel,
        out_shape=pltpu.HBM(inputs.shape, jnp.bfloat16),
        in_specs=vmem_specs(2 + len(sums)),
        out_specs=pl.BlockSpec(memory_space=pltpu.HBM),
        scratch_shapes=[
            pltpu.VMEM(inputs.shape, jnp.bfloat16),
            pltpu.SemaphoreType.DMA((PIECES,)),
        ],
        compiler_params=pltpu.CompilerParams(vmem_limit_bytes=8 << 20),
    )(*map(in_vmem, (scaled, inputs, *sums)))


FAR, NEAR, SIDE = 4, 2, 1
LINE = (NEAR, FAR, FAR | NEAR)


def handed_over(block, sections, count, distance, mask):
    route = [
        ((s - distance) % sections * count + (i ^ mask), s * count + i)
        for s in range(sections)
        for i in range(count)
    ]
    return lax.ppermute(block, ("section", "tp"), route)


def gathered(pair, axis):
    if lax.axis_size(axis) != 8:
        return [lax.all_gather(pair[0], axis)], lambda place: place
    blocks = [pair] + [swapped(pair, axis, mask) for mask in LINE]
    masks = [far | side for far in (0, *LINE) for side in (0, SIDE)]

    def head_of(place):
        return lax.axis_index(axis) ^ masks[place]

    return blocks, head_of


def per_device(grad_attn, w_value, probs_own, probs_spare, evicted, layer_input, gain):
    sections, count = lax.axis_size("section"), lax.axis_size("tp")
    packed, spares, taken = pack(probs_own[0, 0], grad_attn[0, 0], probs_spare[0, 0], evicted)
    heads = []
    for mask in (0, SIDE) if count == 8 else (0,):
        spare = handed_over(spares, sections, count, sections // 2, mask)
        heads.append((swapped(packed, "tp", mask) if mask else packed, spare))
    weights, inputs = w_value[0], layer_input[0]
    next_input = passed_along(inputs, "section", -1)
    reach = reach_of(weights, inputs, gain, heads[-1][0])
    if count == 8:
        reaches = [reach, swapped(reach, "tp", SIDE)]
        reaches[1], next_input = lax.optimization_barrier((reaches[1], next_input))
    else:
        reaches = [lax.psum(reach, "tp")]
    pair = value_gradients(taken, heads)
    blocks, head_of = gathered(pair, "tp")
    scaled, sums = project(head_of, blocks, weights, inputs, gain, reaches)
    next_scaled = passed_along(scaled, "section", -1)
    next_sums = []
    for mask in LINE if count == 8 else ():
        next_sums.append(handed_over(sums, sections, count, -1, mask))
    return finish(next_scaled, next_input, next_sums)[None]


def solution(mesh):
    in_specs = (
        P("section", "tp", None, None),
        P("section", "tp", None),
        P("section", "tp", None, None),
        P("section", "tp", None, None),
        P("section", None),
        P("section", None, "tp"),
        P("section", "tp"),
    )
    out_specs = P("section", None, "tp")
    return jax.shard_map(
        per_device, mesh=mesh, in_specs=in_specs, out_specs=out_specs, check_vma=False
    )
```

```python
import functools

import jax
import jax.numpy as jnp
from jax import lax
from jax.experimental import pallas as pl
from jax.experimental.pallas import tpu as pltpu
from jax.sharding import PartitionSpec as P

D = 12288
LANES = 128
PIECES = 4
EXTRA = 16
HIDES = pl.CostEstimate(flops=1 << 35, bytes_accessed=1 << 25, transcendentals=0)


def passed_along(block, axis, distance):
    devices = range(lax.axis_size(axis))
    route = [((i - distance) % len(devices), i) for i in devices]
    return lax.ppermute(block, axis, route)


def swapped(block, axis, mask):
    return lax.ppermute(block, axis, [(i ^ mask, i) for i in range(lax.axis_size(axis))])


def in_vmem(array):
    return pltpu.with_memory_space_constraint(array, pltpu.VMEM)


def in_hbm(array):
    return pltpu.with_memory_space_constraint(array, pltpu.HBM)


def vmem_specs(count):
    return [pl.BlockSpec(memory_space=pltpu.VMEM)] * count


def as_row(column):
    return jnp.broadcast_to(column, (column.shape[0], column.shape[0])).T[:1]


def as_column(row):
    return jnp.broadcast_to(row, (row.shape[1], row.shape[1])).T[:, :1]


def split(values):
    parts = []
    for _ in range(3):
        parts.append(values.astype(jnp.bfloat16).astype(jnp.float32))
        values = values - parts[-1]
    return parts


def as_parts(row):
    rest = jnp.zeros((EXTRA - 3, row.shape[1]), jnp.float32)
    return jnp.concatenate(split(row) + [rest]).astype(jnp.bfloat16)


def pack_kernel(own_ref, grad_ref, spare_ref, evicted_ref, *refs):
    out_ref, spare_out, taken_ref, flags, sems = refs
    copies = [
        pltpu.make_async_copy(evicted_ref, flags, sems.at[0]),
        pltpu.make_async_copy(own_ref, out_ref.at[0], sems.at[1]),
        pltpu.make_async_copy(grad_ref, out_ref.at[1], sems.at[2]),
        pltpu.make_async_copy(spare_ref, spare_out, sems.at[3]),
    ]
    for copy in copies:
        copy.start()
    copies[0].wait()
    tiles = evicted_ref.shape[1]
    rows = taken_ref.shape[0] // tiles
    for tile in range(tiles):
        part = pl.ds(tile * rows, rows)
        taken = jnp.full((rows, taken_ref.shape[1]), flags[0, tile], jnp.int32)
        taken_ref[part, :] = taken.astype(jnp.float32).astype(taken_ref.dtype)
    for copy in copies[1:]:
        copy.wait()


def pack(own, grad, spare, evicted):
    return pl.pallas_call(
        pack_kernel,
        out_shape=(
            pltpu.VMEM((2, *own.shape), own.dtype),
            pltpu.VMEM(spare.shape, spare.dtype),
            pltpu.VMEM(own.shape, own.dtype),
        ),
        in_specs=[pl.BlockSpec(memory_space=pltpu.HBM)] * 4,
        out_specs=tuple(vmem_specs(3)),
        scratch_shapes=[
            pltpu.SMEM(evicted.shape, evicted.dtype),
            pltpu.SemaphoreType.DMA((4,)),
        ],
        cost_estimate=HIDES,
        compiler_params=pltpu.CompilerParams(vmem_limit_bytes=4 << 20),
    )(*map(in_hbm, (own, grad, spare, evicted)))


def reach_kernel(weight_ref, input_ref, gain_ref, first_ref, reach_ref):
    del first_ref
    tokens, features = input_ref.shape
    values = input_ref[...].astype(jnp.float32)
    reach_ref[tokens:, :] = jnp.zeros_like(reach_ref[tokens:, :])
    squares = as_row(jnp.sum(values * values, axis=1, keepdims=True))
    reach_ref[tokens:, :tokens] = as_parts(squares)
    gained = (values * gain_ref[...]).astype(jnp.bfloat16)
    reach = jnp.dot(gained, weight_ref[...], preferred_element_type=jnp.float32)
    reach_ref[:tokens, :] = reach.astype(reach_ref.dtype)


def reach_of(weights, inputs, gain, first):
    return pl.pallas_call(
        reach_kernel,
        out_shape=pltpu.VMEM((inputs.shape[0] + EXTRA, weights.shape[1]), jnp.bfloat16),
        in_specs=vmem_specs(4),
        out_specs=pl.BlockSpec(memory_space=pltpu.VMEM),
        cost_estimate=HIDES,
        compiler_params=pltpu.CompilerParams(vmem_limit_bytes=8 << 20),
    )(*map(in_vmem, (weights, inputs, gain, first)))


def mix_kernel(taken_ref, *refs):
    out_ref = refs[-1]
    taken = taken_ref[...]
    for j in range(out_ref.shape[0]):
        packed_ref, spare_ref = refs[len(refs) - 2 - j], refs[j]
        out_ref[j] = lax.dot_general(
            packed_ref[0] * (1 - taken) + spare_ref[...] * taken,
            packed_ref[1],
            (((0,), (0,)), ((), ())),
            preferred_element_type=jnp.float32,
        ).astype(out_ref.dtype)


def value_gradients(taken, heads):
    return pl.pallas_call(
        mix_kernel,
        out_shape=pltpu.VMEM((len(heads), *heads[0][1].shape), jnp.bfloat16),
        in_specs=vmem_specs(1 + 2 * len(heads)),
        out_specs=pl.BlockSpec(memory_space=pltpu.VMEM),
        cost_estimate=HIDES,
        compiler_params=pltpu.CompilerParams(vmem_limit_bytes=4 << 20),
    )(*map(in_vmem, (taken, *[spare for _, spare in heads], *[packed for packed, _ in heads[::-1]])))


def column_tile(features):
    return 256 if features % 256 == 0 else features


def fill(flat, blocks, head_of, first):
    groups = []
    for ref in blocks:
        count = ref.shape[0]
        for j in range(count):
            start = pl.multiple_of(head_of(first + j) * LANES, LANES)
            flat[:, pl.ds(start, LANES)] = ref[j]
        width = count * LANES
        groups.append((pl.multiple_of(head_of(first) // count * width, width), width))
        first += count
    return groups


def times_weights(flat, groups, weight_ref, part):
    products = [
        lax.dot_general(
            flat[:, pl.ds(start, width)],
            weight_ref[part, pl.ds(start, width)],
            (((1,), (1,)), ((), ())),
            preferred_element_type=jnp.float32,
        )
        for start, width in groups
    ]
    return sum(products[1:], products[0])


def early_kernel(head_of, *refs):
    *blocks, weight_ref, out_ref, flat = refs
    groups = fill(flat, blocks, head_of, 0)
    features = weight_ref.shape[0]
    tile = column_tile(features)
    for start in range(0, features, tile):
        part = pl.ds(start, tile)
        out_ref[:, part] = times_weights(flat, groups, weight_ref, part)


def project_early(head_of, blocks, weights):
    tokens = blocks[0].shape[1]
    return pl.pallas_call(
        functools.partial(early_kernel, head_of),
        out_shape=pltpu.VMEM((tokens, weights.shape[0]), jnp.float32),
        in_specs=vmem_specs(len(blocks) + 1),
        out_specs=pl.BlockSpec(memory_space=pltpu.VMEM),
        scratch_shapes=[pltpu.VMEM((tokens, weights.shape[1]), jnp.bfloat16)],
        cost_estimate=pl.CostEstimate(flops=1 << 16, bytes_accessed=1 << 12, transcendentals=0),
        compiler_params=pltpu.CompilerParams(vmem_limit_bytes=16 << 20),
    )(*map(in_vmem, (*blocks, weights)))


def project_kernel(head_of, sizes, *refs):
    blocks = refs[: sizes[0]]
    early_refs = refs[sizes[0] : sizes[0] + sizes[1]]
    rest = refs[sizes[0] + sizes[1] :]
    weight_ref, input_ref, gain_ref, *reach_refs, scaled_ref, sums_ref, flat = rest
    tokens, features = input_ref.shape
    groups = fill(flat, blocks, head_of, 0)
    if early_refs:
        groups = groups[EARLY:]
    tile = column_tile(features)
    for start in range(0, features, tile):
        part = pl.ds(start, tile)
        grad_normed = times_weights(flat, groups, weight_ref, part)
        for ref in early_refs:
            grad_normed = grad_normed + ref[:, part]
        scaled_ref[:, part] = (grad_normed * gain_ref[:, part]).astype(scaled_ref.dtype)
    reach = sum(ref[:tokens, :].astype(jnp.float32) for ref in reach_refs)
    squares = sum(ref[tokens:, :tokens].astype(jnp.float32) for ref in reach_refs)
    squares = jnp.sum(squares, axis=0, keepdims=True)
    inner = jnp.sum(flat[...].astype(jnp.float32) * reach, axis=1, keepdims=True)
    sums_ref[:1, :] = squares
    sums_ref[1:, :] = as_row(inner)
    lane = lax.broadcasted_iota(jnp.int32, (tokens, LANES), 1)
    extra = jnp.zeros((tokens, LANES), jnp.float32)
    for j, part in enumerate(split(as_column(squares)) + split(inner)):
        extra = jnp.where(lane == j, part, extra)
    scaled_ref[:, features:] = extra.astype(scaled_ref.dtype)


def project(head_of, blocks, early, weights, inputs, gain, reaches):
    tokens, features = inputs.shape
    operands = (*blocks, *early, weights, inputs, gain, *reaches)
    return pl.pallas_call(
        functools.partial(project_kernel, head_of, (len(blocks), len(early))),
        out_shape=(
            pltpu.VMEM((tokens, features + LANES), jnp.bfloat16),
            pltpu.VMEM((2, tokens), jnp.float32),
        ),
        in_specs=vmem_specs(len(operands)),
        out_specs=tuple(vmem_specs(2)),
        scratch_shapes=[pltpu.VMEM((tokens, weights.shape[1]), jnp.bfloat16)],
        cost_estimate=HIDES,
        compiler_params=pltpu.CompilerParams(vmem_limit_bytes=16 << 20),
    )(*map(in_vmem, operands))


def finish_kernel(scaled_ref, input_ref, *refs):
    *sums_refs, out_ref, held, sems = refs
    tokens, features = input_ref.shape
    extra = scaled_ref[:, features:].astype(jnp.float32)
    lane = lax.broadcasted_iota(jnp.int32, extra.shape, 1)
    squares = jnp.sum(jnp.where(lane < 3, extra, 0.0), axis=1, keepdims=True)
    inner = jnp.sum(jnp.where(lane < 3, 0.0, extra), axis=1, keepdims=True)
    if sums_refs:
        sums = sum(ref[...] for ref in sums_refs)
        squares = squares + as_column(sums[:1])
        inner = inner + as_column(sums[1:])
    inv = 1.0 / jnp.sqrt(squares / D + 1e-05)
    factor = inner * (inv * inv * inv) / D
    rows = tokens // PIECES
    copies = []
    for j in range(PIECES):
        part = slice(j * rows, (j + 1) * rows)
        scaled = scaled_ref[part, :features].astype(jnp.float32)
        values = input_ref[part, :].astype(jnp.float32)
        held[part, :] = (scaled * inv[part] - values * factor[part]).astype(held.dtype)
        copies.append(pltpu.make_async_copy(held.at[part], out_ref.at[part], sems.at[j]))
        copies[-1].start()
    for copy in copies:
        copy.wait()


def finish(scaled, inputs, sums):
    return pl.pallas_call(
        finish_kernel,
        out_shape=pltpu.HBM(inputs.shape, jnp.bfloat16),
        in_specs=vmem_specs(2 + len(sums)),
        out_specs=pl.BlockSpec(memory_space=pltpu.HBM),
        scratch_shapes=[
            pltpu.VMEM(inputs.shape, jnp.bfloat16),
            pltpu.SemaphoreType.DMA((PIECES,)),
        ],
        compiler_params=pltpu.CompilerParams(vmem_limit_bytes=8 << 20),
    )(*map(in_vmem, (scaled, inputs, *sums)))


FAR, NEAR, SIDE = 4, 2, 1
LINE = (FAR | NEAR, NEAR, FAR)
EARLY = 2


def handed_over(block, sections, count, distance, mask):
    route = [
        ((s - distance) % sections * count + (i ^ mask), s * count + i)
        for s in range(sections)
        for i in range(count)
    ]
    return lax.ppermute(block, ("section", "tp"), route)


def gathered(pair, axis):
    if lax.axis_size(axis) != 8:
        return [lax.all_gather(pair[0], axis)], lambda place: place
    blocks = [pair] + [swapped(pair, axis, mask) for mask in LINE]
    masks = [far | side for far in (0, *LINE) for side in (0, SIDE)]

    def head_of(place):
        return lax.axis_index(axis) ^ masks[place]

    return blocks, head_of


def per_device(grad_attn, w_value, probs_own, probs_spare, evicted, layer_input, gain):
    sections, count = lax.axis_size("section"), lax.axis_size("tp")
    packed, spares, taken = pack(probs_own[0, 0], grad_attn[0, 0], probs_spare[0, 0], evicted)
    heads = []
    for mask in (0, SIDE) if count == 8 else (0,):
        spare = handed_over(spares, sections, count, sections // 2, mask)
        heads.append((swapped(packed, "tp", mask) if mask else packed, spare))
    weights, inputs = w_value[0], layer_input[0]
    next_input = passed_along(inputs, "section", -1)
    reach = reach_of(weights, inputs, gain, heads[-1][0])
    if count == 8:
        reaches = [reach, swapped(reach, "tp", SIDE)]
        reaches[1], next_input = lax.optimization_barrier((reaches[1], next_input))
    else:
        reaches = [lax.psum(reach, "tp")]
    pair = value_gradients(taken, heads)
    blocks, head_of = gathered(pair, "tp")
    early = [project_early(head_of, blocks[:EARLY], weights)] if count == 8 else []
    scaled, sums = project(head_of, blocks, early, weights, inputs, gain, reaches)
    next_scaled = passed_along(scaled, "section", -1)
    next_sums = []
    for mask in (NEAR, FAR, FAR | NEAR) if count == 8 else ():
        next_sums.append(handed_over(sums, sections, count, -1, mask))
    return finish(next_scaled, next_input, next_sums)[None]


def solution(mesh):
    in_specs = (
        P("section", "tp", None, None),
        P("section", "tp", None),
        P("section", "tp", None, None),
        P("section", "tp", None, None),
        P("section", None),
        P("section", None, "tp"),
        P("section", "tp"),
    )
    out_specs = P("section", None, "tp")
    return jax.shard_map(
        per_device, mesh=mesh, in_specs=in_specs, out_specs=out_specs, check_vma=False
    )
```

```python
import functools

import jax
import jax.numpy as jnp
from jax import lax
from jax.experimental import pallas as pl
from jax.experimental.pallas import tpu as pltpu
from jax.sharding import PartitionSpec as P

D = 12288
LANES = 128
PIECES = 4
EXTRA = 16
SHORT = pl.CostEstimate(flops=1 << 16, bytes_accessed=1 << 12, transcendentals=0)
HIDES = pl.CostEstimate(flops=1 << 35, bytes_accessed=1 << 25, transcendentals=0)


def passed_along(block, axis, distance):
    devices = range(lax.axis_size(axis))
    route = [((i - distance) % len(devices), i) for i in devices]
    return lax.ppermute(block, axis, route)


def swapped(block, axis, mask):
    return lax.ppermute(block, axis, [(i ^ mask, i) for i in range(lax.axis_size(axis))])


def in_vmem(array):
    return pltpu.with_memory_space_constraint(array, pltpu.VMEM)


def in_hbm(array):
    return pltpu.with_memory_space_constraint(array, pltpu.HBM)


def vmem_specs(count):
    return [pl.BlockSpec(memory_space=pltpu.VMEM)] * count


def as_row(column):
    return jnp.broadcast_to(column, (column.shape[0], column.shape[0])).T[:1]


def as_column(row):
    return jnp.broadcast_to(row, (row.shape[1], row.shape[1])).T[:, :1]


def split(values):
    parts = []
    for _ in range(3):
        parts.append(values.astype(jnp.bfloat16).astype(jnp.float32))
        values = values - parts[-1]
    return parts


def as_parts(row):
    rest = jnp.zeros((EXTRA - 3, row.shape[1]), jnp.float32)
    return jnp.concatenate(split(row) + [rest]).astype(jnp.bfloat16)


def pack_kernel(own_ref, grad_ref, spare_ref, evicted_ref, *refs):
    out_ref, spare_out, taken_ref, flags, sems = refs
    copies = [
        pltpu.make_async_copy(evicted_ref, flags, sems.at[0]),
        pltpu.make_async_copy(own_ref, out_ref.at[0], sems.at[1]),
        pltpu.make_async_copy(grad_ref, out_ref.at[1], sems.at[2]),
        pltpu.make_async_copy(spare_ref, spare_out, sems.at[3]),
    ]
    for copy in copies:
        copy.start()
    copies[0].wait()
    tiles = evicted_ref.shape[1]
    rows = taken_ref.shape[0] // tiles
    for tile in range(tiles):
        part = pl.ds(tile * rows, rows)
        taken = jnp.full((rows, taken_ref.shape[1]), flags[0, tile], jnp.int32)
        taken_ref[part, :] = taken.astype(jnp.float32).astype(taken_ref.dtype)
    for copy in copies[1:]:
        copy.wait()


def pack(own, grad, spare, evicted):
    return pl.pallas_call(
        pack_kernel,
        out_shape=(
            pltpu.VMEM((2, *own.shape), own.dtype),
            pltpu.VMEM(spare.shape, spare.dtype),
            pltpu.VMEM(own.shape, own.dtype),
        ),
        in_specs=[pl.BlockSpec(memory_space=pltpu.HBM)] * 4,
        out_specs=tuple(vmem_specs(3)),
        scratch_shapes=[
            pltpu.SMEM(evicted.shape, evicted.dtype),
            pltpu.SemaphoreType.DMA((4,)),
        ],
        cost_estimate=HIDES,
        compiler_params=pltpu.CompilerParams(vmem_limit_bytes=4 << 20),
    )(*map(in_hbm, (own, grad, spare, evicted)))


def reach_kernel(weight_ref, input_ref, gain_ref, reach_ref):
    tokens, features = input_ref.shape
    values = input_ref[...].astype(jnp.float32)
    reach_ref[tokens:, :] = jnp.zeros_like(reach_ref[tokens:, :])
    squares = as_row(jnp.sum(values * values, axis=1, keepdims=True))
    reach_ref[tokens:, :tokens] = as_parts(squares)
    gained = (values * gain_ref[...]).astype(jnp.bfloat16)
    reach = jnp.dot(gained, weight_ref[...], preferred_element_type=jnp.float32)
    reach_ref[:tokens, :] = reach.astype(reach_ref.dtype)


def reach_of(weights, inputs, gain):
    return pl.pallas_call(
        reach_kernel,
        out_shape=pltpu.VMEM((inputs.shape[0] + EXTRA, weights.shape[1]), jnp.bfloat16),
        in_specs=vmem_specs(3),
        out_specs=pl.BlockSpec(memory_space=pltpu.VMEM),
        cost_estimate=SHORT,
        compiler_params=pltpu.CompilerParams(vmem_limit_bytes=8 << 20),
    )(*map(in_vmem, (weights, inputs, gain)))


def mix_kernel(taken_ref, *refs):
    out_ref = refs[-1]
    taken = taken_ref[...]
    for j in range(out_ref.shape[0]):
        packed_ref, spare_ref = refs[len(refs) - 2 - j], refs[j]
        out_ref[j] = lax.dot_general(
            packed_ref[0] * (1 - taken) + spare_ref[...] * taken,
            packed_ref[1],
            (((0,), (0,)), ((), ())),
            preferred_element_type=jnp.float32,
        ).astype(out_ref.dtype)


def value_gradients(taken, heads):
    return pl.pallas_call(
        mix_kernel,
        out_shape=pltpu.VMEM((len(heads), *heads[0][1].shape), jnp.bfloat16),
        in_specs=vmem_specs(1 + 2 * len(heads)),
        out_specs=pl.BlockSpec(memory_space=pltpu.VMEM),
        cost_estimate=HIDES,
        compiler_params=pltpu.CompilerParams(vmem_limit_bytes=4 << 20),
    )(*map(in_vmem, (taken, *[spare for _, spare in heads], *[packed for packed, _ in heads[::-1]])))


def column_tile(features):
    return 256 if features % 256 == 0 else features


def fill(flat, blocks, head_of, first):
    groups = []
    for ref in blocks:
        count = ref.shape[0]
        for j in range(count):
            start = pl.multiple_of(head_of(first + j) * LANES, LANES)
            flat[:, pl.ds(start, LANES)] = ref[j]
        width = count * LANES
        groups.append((pl.multiple_of(head_of(first) // count * width, width), width))
        first += count
    return groups


def times_weights(flat, groups, weight_ref, part):
    products = [
        lax.dot_general(
            flat[:, pl.ds(start, width)],
            weight_ref[part, pl.ds(start, width)],
            (((1,), (1,)), ((), ())),
            preferred_element_type=jnp.float32,
        )
        for start, width in groups
    ]
    return sum(products[1:], products[0])


def early_kernel(head_of, *refs):
    *blocks, weight_ref, out_ref, flat = refs
    groups = fill(flat, blocks, head_of, 0)
    features = weight_ref.shape[0]
    tile = column_tile(features)
    for start in range(0, features, tile):
        part = pl.ds(start, tile)
        out_ref[:, part] = times_weights(flat, groups, weight_ref, part)


def project_early(head_of, blocks, weights):
    tokens = blocks[0].shape[1]
    return pl.pallas_call(
        functools.partial(early_kernel, head_of),
        out_shape=pltpu.VMEM((tokens, weights.shape[0]), jnp.float32),
        in_specs=vmem_specs(len(blocks) + 1),
        out_specs=pl.BlockSpec(memory_space=pltpu.VMEM),
        scratch_shapes=[pltpu.VMEM((tokens, weights.shape[1]), jnp.bfloat16)],
        cost_estimate=SHORT,
        compiler_params=pltpu.CompilerParams(vmem_limit_bytes=16 << 20),
    )(*map(in_vmem, (*blocks, weights)))


def project_kernel(head_of, sizes, *refs):
    blocks = refs[: sizes[0]]
    early_refs = refs[sizes[0] : sizes[0] + sizes[1]]
    rest = refs[sizes[0] + sizes[1] :]
    weight_ref, input_ref, gain_ref, *reach_refs, scaled_ref, sums_ref, flat = rest
    tokens, features = input_ref.shape
    groups = fill(flat, blocks, head_of, 0)
    if early_refs:
        groups = groups[EARLY:]
    tile = column_tile(features)
    for start in range(0, features, tile):
        part = pl.ds(start, tile)
        grad_normed = times_weights(flat, groups, weight_ref, part)
        for ref in early_refs:
            grad_normed = grad_normed + ref[:, part]
        scaled_ref[:, part] = (grad_normed * gain_ref[:, part]).astype(scaled_ref.dtype)
    reach = sum(ref[:tokens, :].astype(jnp.float32) for ref in reach_refs)
    squares = sum(ref[tokens:, :tokens].astype(jnp.float32) for ref in reach_refs)
    squares = jnp.sum(squares, axis=0, keepdims=True)
    inner = jnp.sum(flat[...].astype(jnp.float32) * reach, axis=1, keepdims=True)
    sums_ref[:1, :] = squares
    sums_ref[1:, :] = as_row(inner)
    lane = lax.broadcasted_iota(jnp.int32, (tokens, LANES), 1)
    extra = jnp.zeros((tokens, LANES), jnp.float32)
    for j, part in enumerate(split(as_column(squares)) + split(inner)):
        extra = jnp.where(lane == j, part, extra)
    scaled_ref[:, features:] = extra.astype(scaled_ref.dtype)


def project(head_of, blocks, early, weights, inputs, gain, reaches):
    tokens, features = inputs.shape
    operands = (*blocks, *early, weights, inputs, gain, *reaches)
    return pl.pallas_call(
        functools.partial(project_kernel, head_of, (len(blocks), len(early))),
        out_shape=(
            pltpu.VMEM((tokens, features + LANES), jnp.bfloat16),
            pltpu.VMEM((2, tokens), jnp.float32),
        ),
        in_specs=vmem_specs(len(operands)),
        out_specs=tuple(vmem_specs(2)),
        scratch_shapes=[pltpu.VMEM((tokens, weights.shape[1]), jnp.bfloat16)],
        cost_estimate=HIDES,
        compiler_params=pltpu.CompilerParams(vmem_limit_bytes=16 << 20),
    )(*map(in_vmem, operands))


def finish_kernel(scaled_ref, input_ref, *refs):
    *sums_refs, out_ref, held, sems = refs
    tokens, features = input_ref.shape
    extra = scaled_ref[:, features:].astype(jnp.float32)
    lane = lax.broadcasted_iota(jnp.int32, extra.shape, 1)
    squares = jnp.sum(jnp.where(lane < 3, extra, 0.0), axis=1, keepdims=True)
    inner = jnp.sum(jnp.where(lane < 3, 0.0, extra), axis=1, keepdims=True)
    if sums_refs:
        sums = sum(ref[...] for ref in sums_refs)
        squares = squares + as_column(sums[:1])
        inner = inner + as_column(sums[1:])
    inv = 1.0 / jnp.sqrt(squares / D + 1e-05)
    factor = inner * (inv * inv * inv) / D
    rows = tokens // PIECES
    copies = []
    for j in range(PIECES):
        part = slice(j * rows, (j + 1) * rows)
        scaled = scaled_ref[part, :features].astype(jnp.float32)
        values = input_ref[part, :].astype(jnp.float32)
        held[part, :] = (scaled * inv[part] - values * factor[part]).astype(held.dtype)
        copies.append(pltpu.make_async_copy(held.at[part], out_ref.at[part], sems.at[j]))
        copies[-1].start()
    for copy in copies:
        copy.wait()


def finish(scaled, inputs, sums):
    return pl.pallas_call(
        finish_kernel,
        out_shape=pltpu.HBM(inputs.shape, jnp.bfloat16),
        in_specs=vmem_specs(2 + len(sums)),
        out_specs=pl.BlockSpec(memory_space=pltpu.HBM),
        scratch_shapes=[
            pltpu.VMEM(inputs.shape, jnp.bfloat16),
            pltpu.SemaphoreType.DMA((PIECES,)),
        ],
        compiler_params=pltpu.CompilerParams(vmem_limit_bytes=8 << 20),
    )(*map(in_vmem, (scaled, inputs, *sums)))


FAR, NEAR, SIDE = 4, 2, 1
LINE = ((FAR | NEAR, NEAR), (NEAR, FAR | NEAR), (FAR, FAR))
EARLY = 2


def handed_over(block, sections, count, distance, mask):
    route = [
        ((s - distance) % sections * count + (i ^ mask), s * count + i)
        for s in range(sections)
        for i in range(count)
    ]
    return lax.ppermute(block, ("section", "tp"), route)


def gathered(pair, axis):
    count = lax.axis_size(axis)
    if count != 8:
        return [lax.all_gather(pair[0], axis)], lambda place: place
    blocks = [pair]
    for masks in LINE:
        route = [
            (s * count + (i ^ masks[s % 2]), s * count + i)
            for s in range(lax.axis_size("section"))
            for i in range(count)
        ]
        blocks.append(lax.ppermute(pair, ("section", axis), route))

    def head_of(place):
        even, odd = ((0, 0), *LINE)[place // 2]
        mask = even + lax.rem(lax.axis_index("section"), 2) * (odd - even)
        return lax.axis_index(axis) ^ mask ^ (place % 2 * SIDE)

    return blocks, head_of


def per_device(grad_attn, w_value, probs_own, probs_spare, evicted, layer_input, gain):
    sections, count = lax.axis_size("section"), lax.axis_size("tp")
    packed, spares, taken = pack(probs_own[0, 0], grad_attn[0, 0], probs_spare[0, 0], evicted)
    heads = []
    for mask in (0, SIDE) if count == 8 else (0,):
        spare = handed_over(spares, sections, count, sections // 2, mask)
        heads.append((swapped(packed, "tp", mask) if mask else packed, spare))
    weights, inputs = w_value[0], layer_input[0]
    next_input = passed_along(inputs, "section", -1)
    reach = reach_of(weights, inputs, gain)
    if count == 8:
        reach, swap = lax.optimization_barrier((reach, heads[1][0]))
        heads[1] = (swap, heads[1][1])
        reaches = [reach, swapped(reach, "tp", SIDE)]
        reaches[1], next_input = lax.optimization_barrier((reaches[1], next_input))
    else:
        reaches = [lax.psum(reach, "tp")]
    pair = value_gradients(taken, heads)
    blocks, head_of = gathered(pair, "tp")
    early = [project_early(head_of, blocks[:EARLY], weights)] if count == 8 else []
    scaled, sums = project(head_of, blocks, early, weights, inputs, gain, reaches)
    next_scaled = passed_along(scaled, "section", -1)
    next_sums = []
    for mask in (NEAR, FAR, FAR | NEAR) if count == 8 else ():
        next_sums.append(handed_over(sums, sections, count, -1, mask))
    return finish(next_scaled, next_input, next_sums)[None]


def solution(mesh):
    in_specs = (
        P("section", "tp", None, None),
        P("section", "tp", None),
        P("section", "tp", None, None),
        P("section", "tp", None, None),
        P("section", None),
        P("section", None, "tp"),
        P("section", "tp"),
    )
    out_specs = P("section", None, "tp")
    return jax.shard_map(
        per_device, mesh=mesh, in_specs=in_specs, out_specs=out_specs, check_vma=False
    )
```

```python
import functools

import jax
import jax.numpy as jnp
from jax import lax
from jax.experimental import pallas as pl
from jax.experimental.pallas import tpu as pltpu
from jax.sharding import PartitionSpec as P

D = 12288
LANES = 128
PIECES = 4
EXTRA = 16
SHORT = pl.CostEstimate(flops=1 << 16, bytes_accessed=1 << 12, transcendentals=0)
HIDES = pl.CostEstimate(flops=1 << 35, bytes_accessed=1 << 25, transcendentals=0)


def passed_along(block, axis, distance):
    devices = range(lax.axis_size(axis))
    route = [((i - distance) % len(devices), i) for i in devices]
    return lax.ppermute(block, axis, route)


def swapped(block, axis, mask):
    return lax.ppermute(block, axis, [(i ^ mask, i) for i in range(lax.axis_size(axis))])


def in_vmem(array):
    return pltpu.with_memory_space_constraint(array, pltpu.VMEM)


def in_hbm(array):
    return pltpu.with_memory_space_constraint(array, pltpu.HBM)


def vmem_specs(count):
    return [pl.BlockSpec(memory_space=pltpu.VMEM)] * count


def as_row(column):
    return jnp.broadcast_to(column, (column.shape[0], column.shape[0])).T[:1]


def as_column(row):
    return jnp.broadcast_to(row, (row.shape[1], row.shape[1])).T[:, :1]


def split(values):
    parts = []
    for _ in range(3):
        parts.append(values.astype(jnp.bfloat16).astype(jnp.float32))
        values = values - parts[-1]
    return parts


def as_parts(row):
    rest = jnp.zeros((EXTRA - 3, row.shape[1]), jnp.float32)
    return jnp.concatenate(split(row) + [rest]).astype(jnp.bfloat16)


def load_kernel(grad_ref, weight_ref, own_ref, evicted_ref, input_ref, gain_ref, *rest):
    grad_out, weight_out, own_out, taken_out, input_out, gain_out, reach_ref = rest[:7]
    flags, sems = rest[7:]
    small = [
        pltpu.make_async_copy(evicted_ref, flags, sems.at[0]),
        pltpu.make_async_copy(own_ref, own_out, sems.at[1]),
        pltpu.make_async_copy(grad_ref, grad_out, sems.at[2]),
        pltpu.make_async_copy(gain_ref, gain_out, sems.at[3]),
        pltpu.make_async_copy(input_ref, input_out, sems.at[4]),
    ]
    for copy in small:
        copy.start()
    large = []
    features = weight_ref.shape[0]
    for j in range(PIECES):
        part = pl.ds(j * (features // PIECES), features // PIECES)
        large.append(
            pltpu.make_async_copy(weight_ref.at[part], weight_out.at[part], sems.at[5 + j])
        )
        large[-1].start()
    small[0].wait()
    small[1].wait()
    tiles = evicted_ref.shape[1]
    rows = own_ref.shape[0] // tiles
    for tile in range(tiles):
        part = pl.ds(tile * rows, rows)
        taken = jnp.full((rows, own_ref.shape[1]), flags[0, tile], jnp.int32).astype(jnp.float32)
        own = own_out[part, :].astype(jnp.float32)
        own_out[part, :] = ((1.0 - taken) * own).astype(own_out.dtype)
        taken_out[part, :] = taken.astype(taken_out.dtype)
    small[2].wait()
    small[3].wait()
    small[4].wait()
    values = input_out[...].astype(jnp.float32)
    tokens = values.shape[0]
    reach_ref[tokens:, :] = jnp.zeros_like(reach_ref[tokens:, :])
    squares = as_row(jnp.sum(values * values, axis=1, keepdims=True))
    reach_ref[tokens:, :tokens] = as_parts(squares)
    gained = (values * gain_out[...]).astype(jnp.bfloat16)
    reach = jnp.zeros((tokens, weight_out.shape[1]), jnp.float32)
    for j, copy in enumerate(large):
        copy.wait()
        part = slice(j * (features // PIECES), (j + 1) * (features // PIECES))
        reach += jnp.dot(gained[:, part], weight_out[part, :], preferred_element_type=jnp.float32)
    reach_ref[:tokens, :] = reach.astype(reach_ref.dtype)


def load(grad, weights, own, evicted, inputs, gain):
    return pl.pallas_call(
        load_kernel,
        out_shape=(
            pltpu.VMEM(grad.shape, grad.dtype),
            pltpu.VMEM(weights.shape, weights.dtype),
            pltpu.VMEM(own.shape, own.dtype),
            pltpu.VMEM(own.shape, own.dtype),
            pltpu.VMEM(inputs.shape, inputs.dtype),
            pltpu.VMEM(gain.shape, gain.dtype),
            pltpu.VMEM((inputs.shape[0] + EXTRA, weights.shape[1]), jnp.bfloat16),
        ),
        in_specs=[pl.BlockSpec(memory_space=pltpu.HBM)] * 6,
        out_specs=tuple(vmem_specs(7)),
        scratch_shapes=[
            pltpu.SMEM(evicted.shape, evicted.dtype),
            pltpu.SemaphoreType.DMA((5 + PIECES,)),
        ],
        cost_estimate=HIDES,
        compiler_params=pltpu.CompilerParams(vmem_limit_bytes=8 << 20),
    )(*map(in_hbm, (grad, weights, own, evicted, inputs, gain)))


def mix_kernel(own_ref, taken_ref, spare_ref, grad_ref, out_ref):
    out_ref[0] = lax.dot_general(
        own_ref[...] + spare_ref[...] * taken_ref[...],
        grad_ref[...],
        (((0,), (0,)), ((), ())),
        preferred_element_type=jnp.float32,
    ).astype(out_ref.dtype)


def value_gradient(own, taken, spare, grad):
    return pl.pallas_call(
        mix_kernel,
        out_shape=pltpu.VMEM((1, *grad.shape), jnp.bfloat16),
        in_specs=vmem_specs(4),
        out_specs=pl.BlockSpec(memory_space=pltpu.VMEM),
        cost_estimate=SHORT,
        compiler_params=pltpu.CompilerParams(vmem_limit_bytes=4 << 20),
    )(*map(in_vmem, (own, taken, spare, grad)))


def join_kernel(own_ref, other_ref, out_ref):
    out_ref[0] = own_ref[0]
    out_ref[1] = other_ref[0]


def join(own, other):
    return pl.pallas_call(
        join_kernel,
        out_shape=pltpu.VMEM((2, *own.shape[1:]), own.dtype),
        in_specs=vmem_specs(2),
        out_specs=pl.BlockSpec(memory_space=pltpu.VMEM),
        cost_estimate=HIDES,
        compiler_params=pltpu.CompilerParams(vmem_limit_bytes=4 << 20),
    )(in_vmem(own), in_vmem(other))


def column_tile(features):
    return 256 if features % 256 == 0 else features


def fill(flat, blocks, head_of, first):
    groups = []
    for ref in blocks:
        count = ref.shape[0]
        for j in range(count):
            start = pl.multiple_of(head_of(first + j) * LANES, LANES)
            flat[:, pl.ds(start, LANES)] = ref[j]
        width = count * LANES
        groups.append((pl.multiple_of(head_of(first) // count * width, width), width))
        first += count
    return groups


def times_weights(flat, groups, weight_ref, part):
    products = [
        lax.dot_general(
            flat[:, pl.ds(start, width)],
            weight_ref[part, pl.ds(start, width)],
            (((1,), (1,)), ((), ())),
            preferred_element_type=jnp.float32,
        )
        for start, width in groups
    ]
    return sum(products[1:], products[0])


def early_kernel(head_of, *refs):
    *blocks, weight_ref, out_ref, flat = refs
    groups = fill(flat, blocks, head_of, 0)
    features = weight_ref.shape[0]
    tile = column_tile(features)
    for start in range(0, features, tile):
        part = pl.ds(start, tile)
        out_ref[:, part] = times_weights(flat, groups, weight_ref, part)


def project_early(head_of, blocks, weights):
    tokens = blocks[0].shape[1]
    return pl.pallas_call(
        functools.partial(early_kernel, head_of),
        out_shape=pltpu.VMEM((tokens, weights.shape[0]), jnp.float32),
        in_specs=vmem_specs(len(blocks) + 1),
        out_specs=pl.BlockSpec(memory_space=pltpu.VMEM),
        scratch_shapes=[pltpu.VMEM((tokens, weights.shape[1]), jnp.bfloat16)],
        cost_estimate=SHORT,
        compiler_params=pltpu.CompilerParams(vmem_limit_bytes=16 << 20),
    )(*map(in_vmem, (*blocks, weights)))


def project_kernel(head_of, sizes, *refs):
    blocks = refs[: sizes[0]]
    early_refs = refs[sizes[0] : sizes[0] + sizes[1]]
    rest = refs[sizes[0] + sizes[1] :]
    weight_ref, input_ref, gain_ref, *reach_refs, scaled_ref, sums_ref, flat = rest
    tokens, features = input_ref.shape
    groups = fill(flat, blocks, head_of, 0)
    if early_refs:
        groups = groups[EARLY:]
    tile = column_tile(features)
    for start in range(0, features, tile):
        part = pl.ds(start, tile)
        grad_normed = times_weights(flat, groups, weight_ref, part)
        for ref in early_refs:
            grad_normed = grad_normed + ref[:, part]
        scaled_ref[:, part] = (grad_normed * gain_ref[:, part]).astype(scaled_ref.dtype)
    reach = sum(ref[:tokens, :].astype(jnp.float32) for ref in reach_refs)
    squares = sum(ref[tokens:, :tokens].astype(jnp.float32) for ref in reach_refs)
    squares = jnp.sum(squares, axis=0, keepdims=True)
    inner = jnp.sum(flat[...].astype(jnp.float32) * reach, axis=1, keepdims=True)
    sums_ref[:1, :] = squares
    sums_ref[1:, :] = as_row(inner)
    lane = lax.broadcasted_iota(jnp.int32, (tokens, LANES), 1)
    extra = jnp.zeros((tokens, LANES), jnp.float32)
    for j, part in enumerate(split(as_column(squares)) + split(inner)):
        extra = jnp.where(lane == j, part, extra)
    scaled_ref[:, features:] = extra.astype(scaled_ref.dtype)


def project(head_of, blocks, early, weights, inputs, gain, reaches):
    tokens, features = inputs.shape
    operands = (*blocks, *early, weights, inputs, gain, *reaches)
    return pl.pallas_call(
        functools.partial(project_kernel, head_of, (len(blocks), len(early))),
        out_shape=(
            pltpu.VMEM((tokens, features + LANES), jnp.bfloat16),
            pltpu.VMEM((2, tokens), jnp.float32),
        ),
        in_specs=vmem_specs(len(operands)),
        out_specs=tuple(vmem_specs(2)),
        scratch_shapes=[pltpu.VMEM((tokens, weights.shape[1]), jnp.bfloat16)],
        cost_estimate=HIDES,
        compiler_params=pltpu.CompilerParams(vmem_limit_bytes=16 << 20),
    )(*map(in_vmem, operands))


def finish_kernel(scaled_ref, input_ref, *refs):
    *sums_refs, out_ref, held, sems = refs
    tokens, features = input_ref.shape
    extra = scaled_ref[:, features:].astype(jnp.float32)
    lane = lax.broadcasted_iota(jnp.int32, extra.shape, 1)
    squares = jnp.sum(jnp.where(lane < 3, extra, 0.0), axis=1, keepdims=True)
    inner = jnp.sum(jnp.where(lane < 3, 0.0, extra), axis=1, keepdims=True)
    if sums_refs:
        sums = sum(ref[...] for ref in sums_refs)
        squares = squares + as_column(sums[:1])
        inner = inner + as_column(sums[1:])
    inv = 1.0 / jnp.sqrt(squares / D + 1e-05)
    factor = inner * (inv * inv * inv) / D
    rows = tokens // PIECES
    copies = []
    for j in range(PIECES):
        part = slice(j * rows, (j + 1) * rows)
        scaled = scaled_ref[part, :features].astype(jnp.float32)
        values = input_ref[part, :].astype(jnp.float32)
        held[part, :] = (scaled * inv[part] - values * factor[part]).astype(held.dtype)
        copies.append(pltpu.make_async_copy(held.at[part], out_ref.at[part], sems.at[j]))
        copies[-1].start()
    for copy in copies:
        copy.wait()


def finish(scaled, inputs, sums):
    return pl.pallas_call(
        finish_kernel,
        out_shape=pltpu.HBM(inputs.shape, jnp.bfloat16),
        in_specs=vmem_specs(2 + len(sums)),
        out_specs=pl.BlockSpec(memory_space=pltpu.HBM),
        scratch_shapes=[
            pltpu.VMEM(inputs.shape, jnp.bfloat16),
            pltpu.SemaphoreType.DMA((PIECES,)),
        ],
        compiler_params=pltpu.CompilerParams(vmem_limit_bytes=8 << 20),
    )(*map(in_vmem, (scaled, inputs, *sums)))


FAR, NEAR, SIDE = 4, 2, 1
LINE = (FAR | NEAR, NEAR, FAR)
EARLY = 2


def handed_over(block, sections, count, distance, mask):
    route = [
        ((s - distance) % sections * count + (i ^ mask), s * count + i)
        for s in range(sections)
        for i in range(count)
    ]
    return lax.ppermute(block, ("section", "tp"), route)


def gathered(pair, axis):
    if lax.axis_size(axis) != 8:
        return [lax.all_gather(pair[0], axis)], lambda place: place
    blocks = [pair] + [swapped(pair, axis, mask) for mask in LINE]
    masks = [far | side for far in (0, *LINE) for side in (0, SIDE)]

    def head_of(place):
        return lax.axis_index(axis) ^ masks[place]

    return blocks, head_of


def per_device(grad_attn, w_value, probs_own, probs_spare, evicted, layer_input, gain):
    sections, count = lax.axis_size("section"), lax.axis_size("tp")
    spare = passed_along(probs_spare[0, 0], "section", sections // 2)
    grad, weights, own, taken, inputs, gains, reach = load(
        grad_attn[0, 0], w_value[0], probs_own[0, 0], evicted, layer_input[0], gain
    )
    next_input = passed_along(inputs, "section", -1)
    if count == 8:
        reaches = [reach, swapped(reach, "tp", SIDE)]
        reaches[1], next_input = lax.optimization_barrier((reaches[1], next_input))
    else:
        reaches = [lax.psum(reach, "tp")]
    held = value_gradient(own, taken, spare, grad)
    pair = join(held, swapped(held, "tp", SIDE)) if count == 8 else held
    blocks, head_of = gathered(pair, "tp")
    early = [project_early(head_of, blocks[:EARLY], weights)] if count == 8 else []
    scaled, sums = project(head_of, blocks, early, weights, inputs, gains, reaches)
    next_scaled = passed_along(scaled, "section", -1)
    next_sums = []
    for mask in (NEAR, FAR, FAR | NEAR) if count == 8 else ():
        next_sums.append(handed_over(sums, sections, count, -1, mask))
    return finish(next_scaled, next_input, next_sums)[None]


def solution(mesh):
    in_specs = (
        P("section", "tp", None, None),
        P("section", "tp", None),
        P("section", "tp", None, None),
        P("section", "tp", None, None),
        P("section", None),
        P("section", None, "tp"),
        P("section", "tp"),
    )
    out_specs = P("section", None, "tp")
    return jax.shard_map(
        per_device, mesh=mesh, in_specs=in_specs, out_specs=out_specs, check_vma=False
    )
```

```python
import functools

import jax
import jax.numpy as jnp
from jax import lax
from jax.experimental import pallas as pl
from jax.experimental.pallas import tpu as pltpu
from jax.sharding import PartitionSpec as P

D = 12288
LANES = 128
PIECES = 4
EXTRA = 16
HIDES = pl.CostEstimate(flops=1 << 35, bytes_accessed=1 << 25, transcendentals=0)


def passed_along(block, axis, distance):
    devices = range(lax.axis_size(axis))
    route = [((i - distance) % len(devices), i) for i in devices]
    return lax.ppermute(block, axis, route)


def swapped(block, axis, mask):
    return lax.ppermute(block, axis, [(i ^ mask, i) for i in range(lax.axis_size(axis))])


def in_vmem(array):
    return pltpu.with_memory_space_constraint(array, pltpu.VMEM)


def in_hbm(array):
    return pltpu.with_memory_space_constraint(array, pltpu.HBM)


def vmem_specs(count):
    return [pl.BlockSpec(memory_space=pltpu.VMEM)] * count


def as_row(column):
    return jnp.broadcast_to(column, (column.shape[0], column.shape[0])).T[:1]


def as_column(row):
    return jnp.broadcast_to(row, (row.shape[1], row.shape[1])).T[:, :1]


def split(values):
    parts = []
    for _ in range(3):
        parts.append(values.astype(jnp.bfloat16).astype(jnp.float32))
        values = values - parts[-1]
    return parts


def as_parts(row):
    rest = jnp.zeros((EXTRA - 3, row.shape[1]), jnp.float32)
    return jnp.concatenate(split(row) + [rest]).astype(jnp.bfloat16)


def pack_kernel(own_ref, grad_ref, spare_ref, evicted_ref, *refs):
    out_ref, spare_out, taken_ref, flags, sems = refs
    copies = [
        pltpu.make_async_copy(evicted_ref, flags, sems.at[0]),
        pltpu.make_async_copy(own_ref, out_ref.at[0], sems.at[1]),
        pltpu.make_async_copy(grad_ref, out_ref.at[1], sems.at[2]),
        pltpu.make_async_copy(spare_ref, spare_out, sems.at[3]),
    ]
    for copy in copies:
        copy.start()
    copies[0].wait()
    tiles = evicted_ref.shape[1]
    rows = taken_ref.shape[0] // tiles
    for tile in range(tiles):
        part = pl.ds(tile * rows, rows)
        taken = jnp.full((rows, taken_ref.shape[1]), flags[0, tile], jnp.int32)
        taken_ref[part, :] = taken.astype(jnp.float32).astype(taken_ref.dtype)
    for copy in copies[1:]:
        copy.wait()


def pack(own, grad, spare, evicted):
    return pl.pallas_call(
        pack_kernel,
        out_shape=(
            pltpu.VMEM((2, *own.shape), own.dtype),
            pltpu.VMEM(spare.shape, spare.dtype),
            pltpu.VMEM(own.shape, own.dtype),
        ),
        in_specs=[pl.BlockSpec(memory_space=pltpu.HBM)] * 4,
        out_specs=tuple(vmem_specs(3)),
        scratch_shapes=[
            pltpu.SMEM(evicted.shape, evicted.dtype),
            pltpu.SemaphoreType.DMA((4,)),
        ],
        cost_estimate=HIDES,
        compiler_params=pltpu.CompilerParams(vmem_limit_bytes=4 << 20),
    )(*map(in_hbm, (own, grad, spare, evicted)))


def reach_kernel(weight_ref, input_ref, gain_ref, first_ref, reach_ref):
    del first_ref
    tokens, features = input_ref.shape
    values = input_ref[...].astype(jnp.float32)
    reach_ref[tokens:, :] = jnp.zeros_like(reach_ref[tokens:, :])
    squares = as_row(jnp.sum(values * values, axis=1, keepdims=True))
    reach_ref[tokens:, :tokens] = as_parts(squares)
    gained = (values * gain_ref[...]).astype(jnp.bfloat16)
    reach = jnp.dot(gained, weight_ref[...], preferred_element_type=jnp.float32)
    reach_ref[:tokens, :] = reach.astype(reach_ref.dtype)


def reach_of(weights, inputs, gain, first):
    return pl.pallas_call(
        reach_kernel,
        out_shape=pltpu.VMEM((inputs.shape[0] + EXTRA, weights.shape[1]), jnp.bfloat16),
        in_specs=vmem_specs(4),
        out_specs=pl.BlockSpec(memory_space=pltpu.VMEM),
        cost_estimate=HIDES,
        compiler_params=pltpu.CompilerParams(vmem_limit_bytes=8 << 20),
    )(*map(in_vmem, (weights, inputs, gain, first)))


def mix_kernel(taken_ref, *refs):
    out_ref = refs[-1]
    taken = taken_ref[...]
    for j in range(out_ref.shape[0]):
        packed_ref, spare_ref = refs[len(refs) - 2 - j], refs[j]
        out_ref[j] = lax.dot_general(
            packed_ref[0] * (1 - taken) + spare_ref[...] * taken,
            packed_ref[1],
            (((0,), (0,)), ((), ())),
            preferred_element_type=jnp.float32,
        ).astype(out_ref.dtype)


def value_gradients(taken, heads):
    return pl.pallas_call(
        mix_kernel,
        out_shape=pltpu.VMEM((len(heads), *heads[0][1].shape), jnp.bfloat16),
        in_specs=vmem_specs(1 + 2 * len(heads)),
        out_specs=pl.BlockSpec(memory_space=pltpu.VMEM),
        cost_estimate=HIDES,
        compiler_params=pltpu.CompilerParams(vmem_limit_bytes=4 << 20),
    )(*map(in_vmem, (taken, *[spare for _, spare in heads], *[packed for packed, _ in heads[::-1]])))


def column_tile(features):
    return 256 if features % 256 == 0 else features


def block_of(refs, j):
    return sum((ref[j] for ref in refs[1:]), refs[0][j])


def fill(flat, head_of, parts):
    groups = []
    for kind, refs in parts:
        count = refs[0].shape[0]
        for j in range(count):
            start = pl.multiple_of(head_of(kind, j) * LANES, LANES)
            flat[:, pl.ds(start, LANES)] = block_of(refs, j)
        width = count * LANES
        groups.append((pl.multiple_of(head_of(kind, 0) // count * width, width), width))
    return groups


def times_weights(flat, groups, weight_ref, part):
    products = [
        lax.dot_general(
            flat[:, pl.ds(start, width)],
            weight_ref[part, pl.ds(start, width)],
            (((1,), (1,)), ((), ())),
            preferred_element_type=jnp.float32,
        )
        for start, width in groups
    ]
    return sum(products[1:], products[0])


def early_kernel(head_of, pair_ref, far_ref, weight_ref, out_ref, flat):
    groups = fill(flat, head_of, [(0, [pair_ref]), (FAR | NEAR, [far_ref])])
    features = weight_ref.shape[0]
    tile = column_tile(features)
    for start in range(0, features, tile):
        part = pl.ds(start, tile)
        out_ref[:, part] = times_weights(flat, groups, weight_ref, part)


def project_early(head_of, blocks, weights):
    tokens = blocks[0].shape[1]
    return pl.pallas_call(
        functools.partial(early_kernel, head_of),
        out_shape=pltpu.VMEM((tokens, weights.shape[0]), jnp.float32),
        in_specs=vmem_specs(len(blocks) + 1),
        out_specs=pl.BlockSpec(memory_space=pltpu.VMEM),
        scratch_shapes=[pltpu.VMEM((tokens, weights.shape[1]), jnp.bfloat16)],
        cost_estimate=pl.CostEstimate(flops=1 << 16, bytes_accessed=1 << 12, transcendentals=0),
        compiler_params=pltpu.CompilerParams(vmem_limit_bytes=16 << 20),
    )(*map(in_vmem, (*blocks, weights)))


def project_kernel(head_of, kinds, late, *refs):
    blocks, refs = refs[: len(kinds)], refs[len(kinds) :]
    weight_ref, input_ref, gain_ref, *rest, scaled_ref, sums_ref, flat = refs
    early_refs, reach_refs = (rest[:1], rest[1:]) if late else ([], rest)
    tokens, features = input_ref.shape
    parts = {}
    for kind, ref in zip(kinds, blocks):
        parts.setdefault(kind, []).append(ref)
    kept = list(parts)
    groups = dict(zip(kept, fill(flat, head_of, [(kind, parts[kind]) for kind in kept])))

    def scale(chosen):
        tile = column_tile(features)
        for start in range(0, features, tile):
            part = pl.ds(start, tile)
            grad_normed = times_weights(flat, chosen, weight_ref, part)
            for ref in early_refs:
                grad_normed = grad_normed + ref[:, part]
            scaled_ref[:, part] = (grad_normed * gain_ref[:, part]).astype(scaled_ref.dtype)

    if late:
        upper = head_of(0, 0) // FAR
        pl.when(upper == 1)(lambda: scale([groups[NEAR], groups[FAR]]))
        pl.when(upper == 0)(lambda: scale([groups[NEAR], groups[FAR], groups[FAR | NEAR]]))
    else:
        scale(list(groups.values()))
    reach = sum(ref[:tokens, :].astype(jnp.float32) for ref in reach_refs)
    squares = sum(ref[tokens:, :tokens].astype(jnp.float32) for ref in reach_refs)
    squares = jnp.sum(squares, axis=0, keepdims=True)
    inner = jnp.sum(flat[...].astype(jnp.float32) * reach, axis=1, keepdims=True)
    sums_ref[:1, :] = squares
    sums_ref[1:, :] = as_row(inner)
    lane = lax.broadcasted_iota(jnp.int32, (tokens, LANES), 1)
    extra = jnp.zeros((tokens, LANES), jnp.float32)
    for j, part in enumerate(split(as_column(squares)) + split(inner)):
        extra = jnp.where(lane == j, part, extra)
    scaled_ref[:, features:] = extra.astype(scaled_ref.dtype)


def project(head_of, kinds, blocks, early, weights, inputs, gain, reaches):
    tokens, features = inputs.shape
    operands = (*blocks, weights, inputs, gain, *early, *reaches)
    return pl.pallas_call(
        functools.partial(project_kernel, head_of, kinds, bool(early)),
        out_shape=(
            pltpu.VMEM((tokens, features + LANES), jnp.bfloat16),
            pltpu.VMEM((2, tokens), jnp.float32),
        ),
        in_specs=vmem_specs(len(operands)),
        out_specs=tuple(vmem_specs(2)),
        scratch_shapes=[pltpu.VMEM((tokens, weights.shape[1]), jnp.bfloat16)],
        cost_estimate=HIDES,
        compiler_params=pltpu.CompilerParams(vmem_limit_bytes=16 << 20),
    )(*map(in_vmem, operands))


def finish_kernel(scaled_ref, input_ref, *refs):
    *sums_refs, out_ref, held, sems = refs
    tokens, features = input_ref.shape
    extra = scaled_ref[:, features:].astype(jnp.float32)
    lane = lax.broadcasted_iota(jnp.int32, extra.shape, 1)
    squares = jnp.sum(jnp.where(lane < 3, extra, 0.0), axis=1, keepdims=True)
    inner = jnp.sum(jnp.where(lane < 3, 0.0, extra), axis=1, keepdims=True)
    if sums_refs:
        sums = sum(ref[...] for ref in sums_refs)
        squares = squares + as_column(sums[:1])
        inner = inner + as_column(sums[1:])
    inv = 1.0 / jnp.sqrt(squares / D + 1e-05)
    factor = inner * (inv * inv * inv) / D
    rows = tokens // PIECES
    copies = []
    for j in range(PIECES):
        part = slice(j * rows, (j + 1) * rows)
        scaled = scaled_ref[part, :features].astype(jnp.float32)
        values = input_ref[part, :].astype(jnp.float32)
        held[part, :] = (scaled * inv[part] - values * factor[part]).astype(held.dtype)
        copies.append(pltpu.make_async_copy(held.at[part], out_ref.at[part], sems.at[j]))
        copies[-1].start()
    for copy in copies:
        copy.wait()


def finish(scaled, inputs, sums):
    return pl.pallas_call(
        finish_kernel,
        out_shape=pltpu.HBM(inputs.shape, jnp.bfloat16),
        in_specs=vmem_specs(2 + len(sums)),
        out_specs=pl.BlockSpec(memory_space=pltpu.HBM),
        scratch_shapes=[
            pltpu.VMEM(inputs.shape, jnp.bfloat16),
            pltpu.SemaphoreType.DMA((PIECES,)),
        ],
        compiler_params=pltpu.CompilerParams(vmem_limit_bytes=8 << 20),
    )(*map(in_vmem, (scaled, inputs, *sums)))


FAR, NEAR, SIDE = 4, 2, 1
LOWER, UPPER = (0,), (1,)


def handed_over(block, sections, count, distance, mask, halves=LOWER + UPPER):
    route = [
        ((s - distance) % sections * count + (i ^ mask), s * count + i)
        for s in range(sections)
        for i in range(count)
        if count != 8 or i // FAR in halves
    ]
    return lax.ppermute(block, ("section", "tp"), route)


def gathered(pair, next_input, sections, count):
    if count != 8:
        return (0,), [lax.all_gather(pair[0], "tp")], lambda kind, j: j, next_input
    wanted = ((FAR | NEAR, LOWER), (FAR, LOWER + UPPER), (FAR | NEAR, UPPER))
    blocks = [handed_over(pair, sections, count, 0, mask, halves) for mask, halves in wanted]
    late, next_input = lax.optimization_barrier((pair, next_input))
    near = handed_over(late, sections, count, 0, NEAR)
    kinds = (0, FAR | NEAR, NEAR, FAR, FAR | NEAR)

    def head_of(kind, j):
        return lax.axis_index("tp") ^ kind ^ (j * SIDE)

    return kinds, [pair, blocks[2], near, blocks[1], blocks[0]], head_of, next_input


def per_device(grad_attn, w_value, probs_own, probs_spare, evicted, layer_input, gain):
    sections, count = lax.axis_size("section"), lax.axis_size("tp")
    packed, spares, taken = pack(probs_own[0, 0], grad_attn[0, 0], probs_spare[0, 0], evicted)
    heads = []
    for mask in (0, SIDE) if count == 8 else (0,):
        spare = handed_over(spares, sections, count, sections // 2, mask)
        heads.append((swapped(packed, "tp", mask) if mask else packed, spare))
    weights, inputs = w_value[0], layer_input[0]
    next_input = passed_along(inputs, "section", -1)
    reach = reach_of(weights, inputs, gain, heads[-1][0])
    if count == 8:
        reaches = [reach, swapped(reach, "tp", SIDE)]
    else:
        reaches = [lax.psum(reach, "tp")]
    pair = value_gradients(taken, heads)
    kinds, blocks, head_of, next_input = gathered(pair, next_input, sections, count)
    early = [project_early(head_of, blocks[:2], weights)] if count == 8 else []
    scaled, sums = project(head_of, kinds, blocks, early, weights, inputs, gain, reaches)
    next_scaled = passed_along(scaled, "section", -1)
    hops = (
        (FAR | NEAR, UPPER),
        (FAR, LOWER + UPPER),
        (NEAR, LOWER + UPPER),
        (FAR | NEAR, LOWER),
    )
    next_sums = [
        handed_over(sums, sections, count, -1, mask, halves)
        for mask, halves in hops
        if count == 8
    ]
    return finish(next_scaled, next_input, next_sums)[None]


def solution(mesh):
    in_specs = (
        P("section", "tp", None, None),
        P("section", "tp", None),
        P("section", "tp", None, None),
        P("section", "tp", None, None),
        P("section", None),
        P("section", None, "tp"),
        P("section", "tp"),
    )
    out_specs = P("section", None, "tp")
    return jax.shard_map(
        per_device, mesh=mesh, in_specs=in_specs, out_specs=out_specs, check_vma=False
    )
```

```python
import functools

import jax
import jax.numpy as jnp
from jax import lax
from jax.experimental import pallas as pl
from jax.experimental.pallas import tpu as pltpu
from jax.sharding import PartitionSpec as P

D = 12288
LANES = 128
PIECES = (0, 3, 5, 7, 8)
EXTRA = 16
HIDES = pl.CostEstimate(flops=1 << 35, bytes_accessed=1 << 25, transcendentals=0)


def passed_along(block, axis, distance):
    devices = range(lax.axis_size(axis))
    route = [((i - distance) % len(devices), i) for i in devices]
    return lax.ppermute(block, axis, route)


def swapped(block, axis, mask):
    return lax.ppermute(block, axis, [(i ^ mask, i) for i in range(lax.axis_size(axis))])


def in_vmem(array):
    return pltpu.with_memory_space_constraint(array, pltpu.VMEM)


def in_hbm(array):
    return pltpu.with_memory_space_constraint(array, pltpu.HBM)


def vmem_specs(count):
    return [pl.BlockSpec(memory_space=pltpu.VMEM)] * count


def as_row(column):
    return jnp.broadcast_to(column, (column.shape[0], column.shape[0])).T[:1]


def standing(rows):
    tokens = rows.shape[1]
    return jnp.concatenate([rows, jnp.zeros((tokens - rows.shape[0], tokens), rows.dtype)]).T


def split(values):
    parts = []
    for _ in range(3):
        parts.append(values.astype(jnp.bfloat16).astype(jnp.float32))
        values = values - parts[-1]
    return parts


def as_parts(row):
    rest = jnp.zeros((EXTRA - 3, row.shape[1]), jnp.float32)
    return jnp.concatenate(split(row) + [rest]).astype(jnp.bfloat16)


def pack_kernel(own_ref, grad_ref, spare_ref, evicted_ref, *refs):
    out_ref, spare_out, taken_ref, flags, sems = refs
    copies = [
        pltpu.make_async_copy(evicted_ref, flags, sems.at[0]),
        pltpu.make_async_copy(own_ref, out_ref.at[0], sems.at[1]),
        pltpu.make_async_copy(grad_ref, out_ref.at[1], sems.at[2]),
        pltpu.make_async_copy(spare_ref, spare_out, sems.at[3]),
    ]
    for copy in copies:
        copy.start()
    copies[0].wait()
    tiles = evicted_ref.shape[1]
    rows = taken_ref.shape[0] // tiles
    for tile in range(tiles):
        part = pl.ds(tile * rows, rows)
        taken = jnp.full((rows, taken_ref.shape[1]), flags[0, tile], jnp.int32)
        taken_ref[part, :] = taken.astype(jnp.float32).astype(taken_ref.dtype)
    for copy in copies[1:]:
        copy.wait()


def pack(own, grad, spare, evicted):
    return pl.pallas_call(
        pack_kernel,
        out_shape=(
            pltpu.VMEM((2, *own.shape), own.dtype),
            pltpu.VMEM(spare.shape, spare.dtype),
            pltpu.VMEM(own.shape, own.dtype),
        ),
        in_specs=[pl.BlockSpec(memory_space=pltpu.HBM)] * 4,
        out_specs=tuple(vmem_specs(3)),
        scratch_shapes=[
            pltpu.SMEM(evicted.shape, evicted.dtype),
            pltpu.SemaphoreType.DMA((4,)),
        ],
        cost_estimate=HIDES,
        compiler_params=pltpu.CompilerParams(vmem_limit_bytes=4 << 20),
    )(*map(in_hbm, (own, grad, spare, evicted)))


def reach_kernel(weight_ref, input_ref, gain_ref, first_ref, reach_ref):
    del first_ref
    tokens, features = input_ref.shape
    values = input_ref[...].astype(jnp.float32)
    reach_ref[tokens:, :] = jnp.zeros_like(reach_ref[tokens:, :])
    squares = as_row(jnp.sum(values * values, axis=1, keepdims=True))
    reach_ref[tokens:, :tokens] = as_parts(squares)
    gained = (values * gain_ref[...]).astype(jnp.bfloat16)
    reach = jnp.dot(gained, weight_ref[...], preferred_element_type=jnp.float32)
    reach_ref[:tokens, :] = reach.astype(reach_ref.dtype)


def reach_of(weights, inputs, gain, first):
    return pl.pallas_call(
        reach_kernel,
        out_shape=pltpu.VMEM((inputs.shape[0] + EXTRA, weights.shape[1]), jnp.bfloat16),
        in_specs=vmem_specs(4),
        out_specs=pl.BlockSpec(memory_space=pltpu.VMEM),
        cost_estimate=HIDES,
        compiler_params=pltpu.CompilerParams(vmem_limit_bytes=8 << 20),
    )(*map(in_vmem, (weights, inputs, gain, first)))


def mix_kernel(taken_ref, *refs):
    out_ref = refs[-1]
    taken = taken_ref[...]
    for j in range(out_ref.shape[0]):
        packed_ref, spare_ref = refs[len(refs) - 2 - j], refs[j]
        out_ref[j] = lax.dot_general(
            packed_ref[0] * (1 - taken) + spare_ref[...] * taken,
            packed_ref[1],
            (((0,), (0,)), ((), ())),
            preferred_element_type=jnp.float32,
        ).astype(out_ref.dtype)


def value_gradients(taken, heads):
    return pl.pallas_call(
        mix_kernel,
        out_shape=pltpu.VMEM((len(heads), *heads[0][1].shape), jnp.bfloat16),
        in_specs=vmem_specs(1 + 2 * len(heads)),
        out_specs=pl.BlockSpec(memory_space=pltpu.VMEM),
        cost_estimate=HIDES,
        compiler_params=pltpu.CompilerParams(vmem_limit_bytes=4 << 20),
    )(*map(in_vmem, (taken, *[spare for _, spare in heads], *[packed for packed, _ in heads[::-1]])))


def column_tile(features):
    return 256 if features % 256 == 0 else features


def fill(flat, blocks, head_of, first):
    groups = []
    for ref in blocks:
        count = ref.shape[0]
        for j in range(count):
            start = pl.multiple_of(head_of(first + j) * LANES, LANES)
            flat[:, pl.ds(start, LANES)] = ref[j]
        width = count * LANES
        groups.append((pl.multiple_of(head_of(first) // count * width, width), width))
        first += count
    return groups


def times_weights(flat, groups, weight_ref, part):
    products = [
        lax.dot_general(
            flat[:, pl.ds(start, width)],
            weight_ref[part, pl.ds(start, width)],
            (((1,), (1,)), ((), ())),
            preferred_element_type=jnp.float32,
        )
        for start, width in groups
    ]
    return sum(products[1:], products[0])


def early_kernel(head_of, *refs):
    *blocks, weight_ref, out_ref, flat = refs
    groups = fill(flat, blocks, head_of, 0)
    features = weight_ref.shape[0]
    tile = column_tile(features)
    for start in range(0, features, tile):
        part = pl.ds(start, tile)
        out_ref[:, part] = times_weights(flat, groups, weight_ref, part)


def project_early(head_of, blocks, weights):
    tokens = blocks[0].shape[1]
    return pl.pallas_call(
        functools.partial(early_kernel, head_of),
        out_shape=pltpu.VMEM((tokens, weights.shape[0]), jnp.float32),
        in_specs=vmem_specs(len(blocks) + 1),
        out_specs=pl.BlockSpec(memory_space=pltpu.VMEM),
        scratch_shapes=[pltpu.VMEM((tokens, weights.shape[1]), jnp.bfloat16)],
        cost_estimate=pl.CostEstimate(flops=1 << 16, bytes_accessed=1 << 12, transcendentals=0),
        compiler_params=pltpu.CompilerParams(vmem_limit_bytes=16 << 20),
    )(*map(in_vmem, (*blocks, weights)))


def project_kernel(head_of, sizes, *refs):
    blocks = refs[: sizes[0]]
    early_refs = refs[sizes[0] : sizes[0] + sizes[1]]
    rest = refs[sizes[0] + sizes[1] :]
    weight_ref, input_ref, gain_ref, *reach_refs, scaled_ref, sums_ref, flat = rest
    tokens, features = input_ref.shape
    groups = fill(flat, blocks, head_of, 0)
    if early_refs:
        groups = groups[EARLY:]
    tile = column_tile(features)
    for start in range(0, features, tile):
        part = pl.ds(start, tile)
        grad_normed = times_weights(flat, groups, weight_ref, part)
        for ref in early_refs:
            grad_normed = grad_normed + ref[:, part]
        scaled_ref[:, part] = (grad_normed * gain_ref[:, part]).astype(scaled_ref.dtype)
    reach = sum(ref[:tokens, :].astype(jnp.float32) for ref in reach_refs)
    squares = sum(ref[tokens:, :tokens].astype(jnp.float32) for ref in reach_refs)
    squares = jnp.sum(squares, axis=0, keepdims=True)
    inner = jnp.sum(flat[...].astype(jnp.float32) * reach, axis=1, keepdims=True)
    inner = as_row(inner)
    sums_ref[:1, :] = squares
    sums_ref[1:, :] = inner
    rows = jnp.concatenate([*split(squares), *split(inner), jnp.zeros((2, tokens), jnp.float32)])
    scaled_ref[:, features:] = standing(rows).astype(scaled_ref.dtype)


def project(head_of, blocks, early, weights, inputs, gain, reaches):
    tokens, features = inputs.shape
    operands = (*blocks, *early, weights, inputs, gain, *reaches)
    return pl.pallas_call(
        functools.partial(project_kernel, head_of, (len(blocks), len(early))),
        out_shape=(
            pltpu.VMEM((tokens, features + LANES), jnp.bfloat16),
            pltpu.VMEM((2, tokens), jnp.float32),
        ),
        in_specs=vmem_specs(len(operands)),
        out_specs=tuple(vmem_specs(2)),
        scratch_shapes=[pltpu.VMEM((tokens, weights.shape[1]), jnp.bfloat16)],
        cost_estimate=HIDES,
        compiler_params=pltpu.CompilerParams(vmem_limit_bytes=16 << 20),
    )(*map(in_vmem, operands))


def finish_kernel(scaled_ref, input_ref, *refs):
    *sums_refs, out_ref, held, sems = refs
    tokens, features = input_ref.shape
    extra = scaled_ref[:, features:].astype(jnp.float32).T
    squares = extra[0:1] + extra[1:2] + extra[2:3]
    inner = extra[3:4] + extra[4:5] + extra[5:6]
    for ref in sums_refs:
        squares = squares + ref[:1, :]
        inner = inner + ref[1:, :]
    inv = 1.0 / jnp.sqrt(squares / D + 1e-05)
    factor = inner * (inv * inv * inv) / D
    rows = jnp.concatenate([inv, factor, jnp.zeros((6, tokens), jnp.float32)])
    columns = standing(rows)
    inv, factor = columns[:, 0:1], columns[:, 1:2]
    copies = []
    for j in range(len(PIECES) - 1):
        part = slice(PIECES[j] * tokens // 8, PIECES[j + 1] * tokens // 8)
        scaled = scaled_ref[part, :features].astype(jnp.float32)
        values = input_ref[part, :].astype(jnp.float32)
        held[part, :] = (scaled * inv[part] - values * factor[part]).astype(held.dtype)
        copies.append(pltpu.make_async_copy(held.at[part], out_ref.at[part], sems.at[j]))
        copies[-1].start()
    for copy in copies:
        copy.wait()


def finish(scaled, inputs, sums):
    return pl.pallas_call(
        finish_kernel,
        out_shape=pltpu.HBM(inputs.shape, jnp.bfloat16),
        in_specs=vmem_specs(2 + len(sums)),
        out_specs=pl.BlockSpec(memory_space=pltpu.HBM),
        scratch_shapes=[
            pltpu.VMEM(inputs.shape, jnp.bfloat16),
            pltpu.SemaphoreType.DMA((len(PIECES) - 1,)),
        ],
        compiler_params=pltpu.CompilerParams(vmem_limit_bytes=8 << 20),
    )(*map(in_vmem, (scaled, inputs, *sums)))


FAR, NEAR, SIDE = 4, 2, 1
LINE = (FAR | NEAR, NEAR, FAR)
EARLY = 2


def handed_over(block, sections, count, distance, mask):
    route = [
        ((s - distance) % sections * count + (i ^ mask), s * count + i)
        for s in range(sections)
        for i in range(count)
    ]
    return lax.ppermute(block, ("section", "tp"), route)


def gathered(pair, axis):
    if lax.axis_size(axis) != 8:
        return [lax.all_gather(pair[0], axis)], lambda place: place
    blocks = [pair] + [swapped(pair, axis, mask) for mask in LINE]
    masks = [far | side for far in (0, *LINE) for side in (0, SIDE)]

    def head_of(place):
        return lax.axis_index(axis) ^ masks[place]

    return blocks, head_of


def per_device(grad_attn, w_value, probs_own, probs_spare, evicted, layer_input, gain):
    sections, count = lax.axis_size("section"), lax.axis_size("tp")
    packed, spares, taken = pack(probs_own[0, 0], grad_attn[0, 0], probs_spare[0, 0], evicted)
    heads = []
    for mask in (0, SIDE) if count == 8 else (0,):
        spare = handed_over(spares, sections, count, sections // 2, mask)
        heads.append((swapped(packed, "tp", mask) if mask else packed, spare))
    weights, inputs = w_value[0], layer_input[0]
    next_input = passed_along(inputs, "section", -1)
    reach = reach_of(weights, inputs, gain, heads[-1][0])
    if count == 8:
        reaches = [reach, swapped(reach, "tp", SIDE)]
        reaches[1], next_input = lax.optimization_barrier((reaches[1], next_input))
    else:
        reaches = [lax.psum(reach, "tp")]
    pair = value_gradients(taken, heads)
    blocks, head_of = gathered(pair, "tp")
    early = [project_early(head_of, blocks[:EARLY], weights)] if count == 8 else []
    scaled, sums = project(head_of, blocks, early, weights, inputs, gain, reaches)
    next_scaled = passed_along(scaled, "section", -1)
    next_sums = []
    for mask in (NEAR, FAR, FAR | NEAR) if count == 8 else ():
        next_sums.append(handed_over(sums, sections, count, -1, mask))
    return finish(next_scaled, next_input, next_sums)[None]


def solution(mesh):
    in_specs = (
        P("section", "tp", None, None),
        P("section", "tp", None),
        P("section", "tp", None, None),
        P("section", "tp", None, None),
        P("section", None),
        P("section", None, "tp"),
        P("section", "tp"),
    )
    out_specs = P("section", None, "tp")
    return jax.shard_map(
        per_device, mesh=mesh, in_specs=in_specs, out_specs=out_specs, check_vma=False
    )
```

```python
import functools

import jax
import jax.numpy as jnp
from jax import lax
from jax.experimental import pallas as pl
from jax.experimental.pallas import tpu as pltpu
from jax.sharding import PartitionSpec as P

D = 12288
LANES = 128
PIECES = (0, 3, 5, 7, 8)
EXTRA = 16
SHORT = pl.CostEstimate(flops=1 << 16, bytes_accessed=1 << 12, transcendentals=0)
HIDES = pl.CostEstimate(flops=1 << 35, bytes_accessed=1 << 25, transcendentals=0)


def passed_along(block, axis, distance):
    devices = range(lax.axis_size(axis))
    route = [((i - distance) % len(devices), i) for i in devices]
    return lax.ppermute(block, axis, route)


def swapped(block, axis, mask):
    return lax.ppermute(block, axis, [(i ^ mask, i) for i in range(lax.axis_size(axis))])


def in_vmem(array):
    return pltpu.with_memory_space_constraint(array, pltpu.VMEM)


def in_hbm(array):
    return pltpu.with_memory_space_constraint(array, pltpu.HBM)


def vmem_specs(count):
    return [pl.BlockSpec(memory_space=pltpu.VMEM)] * count


def as_row(column):
    return jnp.broadcast_to(column, (column.shape[0], column.shape[0])).T[:1]


def standing(rows):
    tokens = rows.shape[1]
    return jnp.concatenate([rows, jnp.zeros((tokens - rows.shape[0], tokens), rows.dtype)]).T


def split(values):
    parts = []
    for _ in range(3):
        parts.append(values.astype(jnp.bfloat16).astype(jnp.float32))
        values = values - parts[-1]
    return parts


def as_parts(row):
    rest = jnp.zeros((EXTRA - 3, row.shape[1]), jnp.float32)
    return jnp.concatenate(split(row) + [rest]).astype(jnp.bfloat16)


def pack_kernel(own_ref, grad_ref, spare_ref, evicted_ref, *refs):
    out_ref, spare_out, taken_ref, flags, sems = refs
    copies = [
        pltpu.make_async_copy(evicted_ref, flags, sems.at[0]),
        pltpu.make_async_copy(own_ref, out_ref.at[0], sems.at[1]),
        pltpu.make_async_copy(grad_ref, out_ref.at[1], sems.at[2]),
        pltpu.make_async_copy(spare_ref, spare_out, sems.at[3]),
    ]
    for copy in copies:
        copy.start()
    copies[0].wait()
    tiles = evicted_ref.shape[1]
    rows = taken_ref.shape[0] // tiles
    for tile in range(tiles):
        part = pl.ds(tile * rows, rows)
        taken = jnp.full((rows, taken_ref.shape[1]), flags[0, tile], jnp.int32)
        taken_ref[part, :] = taken.astype(jnp.float32).astype(taken_ref.dtype)
    for copy in copies[1:]:
        copy.wait()


def pack(own, grad, spare, evicted):
    return pl.pallas_call(
        pack_kernel,
        out_shape=(
            pltpu.VMEM((2, *own.shape), own.dtype),
            pltpu.VMEM(spare.shape, spare.dtype),
            pltpu.VMEM(own.shape, own.dtype),
        ),
        in_specs=[pl.BlockSpec(memory_space=pltpu.HBM)] * 4,
        out_specs=tuple(vmem_specs(3)),
        scratch_shapes=[
            pltpu.SMEM(evicted.shape, evicted.dtype),
            pltpu.SemaphoreType.DMA((4,)),
        ],
        cost_estimate=HIDES,
        compiler_params=pltpu.CompilerParams(vmem_limit_bytes=4 << 20),
    )(*map(in_hbm, (own, grad, spare, evicted)))


def reach_kernel(weight_ref, input_ref, gain_ref, reach_ref):
    tokens, features = input_ref.shape
    values = input_ref[...].astype(jnp.float32)
    reach_ref[tokens:, :] = jnp.zeros_like(reach_ref[tokens:, :])
    squares = as_row(jnp.sum(values * values, axis=1, keepdims=True))
    reach_ref[tokens:, :tokens] = as_parts(squares)
    gained = (values * gain_ref[...]).astype(jnp.bfloat16)
    reach = jnp.dot(gained, weight_ref[...], preferred_element_type=jnp.float32)
    reach_ref[:tokens, :] = reach.astype(reach_ref.dtype)


def reach_of(weights, inputs, gain):
    return pl.pallas_call(
        reach_kernel,
        out_shape=pltpu.VMEM((inputs.shape[0] + EXTRA, weights.shape[1]), jnp.bfloat16),
        in_specs=vmem_specs(3),
        out_specs=pl.BlockSpec(memory_space=pltpu.VMEM),
        cost_estimate=SHORT,
        compiler_params=pltpu.CompilerParams(vmem_limit_bytes=8 << 20),
    )(*map(in_vmem, (weights, inputs, gain)))


def mix_kernel(taken_ref, *refs):
    out_ref = refs[-1]
    taken = taken_ref[...]
    for j in range(out_ref.shape[0]):
        packed_ref, spare_ref = refs[len(refs) - 2 - j], refs[j]
        out_ref[j] = lax.dot_general(
            packed_ref[0] * (1 - taken) + spare_ref[...] * taken,
            packed_ref[1],
            (((0,), (0,)), ((), ())),
            preferred_element_type=jnp.float32,
        ).astype(out_ref.dtype)


def value_gradients(taken, heads):
    return pl.pallas_call(
        mix_kernel,
        out_shape=pltpu.VMEM((len(heads), *heads[0][1].shape), jnp.bfloat16),
        in_specs=vmem_specs(1 + 2 * len(heads)),
        out_specs=pl.BlockSpec(memory_space=pltpu.VMEM),
        cost_estimate=HIDES,
        compiler_params=pltpu.CompilerParams(vmem_limit_bytes=4 << 20),
    )(*map(in_vmem, (taken, *[spare for _, spare in heads], *[packed for packed, _ in heads[::-1]])))


def column_tile(features):
    return 256 if features % 256 == 0 else features


def fill(flat, blocks, head_of, first):
    groups = []
    for ref in blocks:
        count = ref.shape[0]
        for j in range(count):
            start = pl.multiple_of(head_of(first + j) * LANES, LANES)
            flat[:, pl.ds(start, LANES)] = ref[j]
        width = count * LANES
        groups.append((pl.multiple_of(head_of(first) // count * width, width), width))
        first += count
    return groups


def times_weights(flat, groups, weight_ref, part):
    products = [
        lax.dot_general(
            flat[:, pl.ds(start, width)],
            weight_ref[part, pl.ds(start, width)],
            (((1,), (1,)), ((), ())),
            preferred_element_type=jnp.float32,
        )
        for start, width in groups
    ]
    return sum(products[1:], products[0])


def early_kernel(head_of, *refs):
    *blocks, weight_ref, out_ref, flat = refs
    groups = fill(flat, blocks, head_of, 0)
    features = weight_ref.shape[0]
    tile = column_tile(features)
    for start in range(0, features, tile):
        part = pl.ds(start, tile)
        out_ref[:, part] = times_weights(flat, groups, weight_ref, part)


def project_early(head_of, blocks, weights):
    tokens = blocks[0].shape[1]
    return pl.pallas_call(
        functools.partial(early_kernel, head_of),
        out_shape=pltpu.VMEM((tokens, weights.shape[0]), jnp.float32),
        in_specs=vmem_specs(len(blocks) + 1),
        out_specs=pl.BlockSpec(memory_space=pltpu.VMEM),
        scratch_shapes=[pltpu.VMEM((tokens, weights.shape[1]), jnp.bfloat16)],
        cost_estimate=SHORT,
        compiler_params=pltpu.CompilerParams(vmem_limit_bytes=16 << 20),
    )(*map(in_vmem, (*blocks, weights)))


def project_kernel(head_of, sizes, *refs):
    blocks = refs[: sizes[0]]
    early_refs = refs[sizes[0] : sizes[0] + sizes[1]]
    rest = refs[sizes[0] + sizes[1] :]
    weight_ref, input_ref, gain_ref, *reach_refs, scaled_ref, sums_ref, flat = rest
    tokens, features = input_ref.shape
    groups = fill(flat, blocks, head_of, 0)
    if early_refs:
        groups = groups[EARLY:]
    tile = column_tile(features)
    for start in range(0, features, tile):
        part = pl.ds(start, tile)
        grad_normed = times_weights(flat, groups, weight_ref, part)
        for ref in early_refs:
            grad_normed = grad_normed + ref[:, part]
        scaled_ref[:, part] = (grad_normed * gain_ref[:, part]).astype(scaled_ref.dtype)
    reach = sum(ref[:tokens, :].astype(jnp.float32) for ref in reach_refs)
    squares = sum(ref[tokens:, :tokens].astype(jnp.float32) for ref in reach_refs)
    squares = jnp.sum(squares, axis=0, keepdims=True)
    inner = jnp.sum(flat[...].astype(jnp.float32) * reach, axis=1, keepdims=True)
    inner = as_row(inner)
    sums_ref[:1, :] = squares
    sums_ref[1:, :] = inner
    rows = jnp.concatenate([*split(squares), *split(inner), jnp.zeros((2, tokens), jnp.float32)])
    scaled_ref[:, features:] = standing(rows).astype(scaled_ref.dtype)


def project(head_of, blocks, early, weights, inputs, gain, reaches):
    tokens, features = inputs.shape
    operands = (*blocks, *early, weights, inputs, gain, *reaches)
    return pl.pallas_call(
        functools.partial(project_kernel, head_of, (len(blocks), len(early))),
        out_shape=(
            pltpu.VMEM((tokens, features + LANES), jnp.bfloat16),
            pltpu.VMEM((2, tokens), jnp.float32),
        ),
        in_specs=vmem_specs(len(operands)),
        out_specs=tuple(vmem_specs(2)),
        scratch_shapes=[pltpu.VMEM((tokens, weights.shape[1]), jnp.bfloat16)],
        cost_estimate=HIDES,
        compiler_params=pltpu.CompilerParams(vmem_limit_bytes=16 << 20),
    )(*map(in_vmem, operands))


def finish_kernel(scaled_ref, input_ref, *refs):
    *sums_refs, out_ref, held, sems = refs
    tokens, features = input_ref.shape
    extra = scaled_ref[:, features:].astype(jnp.float32).T
    squares = extra[0:1] + extra[1:2] + extra[2:3]
    inner = extra[3:4] + extra[4:5] + extra[5:6]
    for ref in sums_refs:
        squares = squares + ref[:1, :]
        inner = inner + ref[1:, :]
    inv = 1.0 / jnp.sqrt(squares / D + 1e-05)
    factor = inner * (inv * inv * inv) / D
    rows = jnp.concatenate([inv, factor, jnp.zeros((6, tokens), jnp.float32)])
    columns = standing(rows)
    inv, factor = columns[:, 0:1], columns[:, 1:2]
    copies = []
    for j in range(len(PIECES) - 1):
        part = slice(PIECES[j] * tokens // 8, PIECES[j + 1] * tokens // 8)
        scaled = scaled_ref[part, :features].astype(jnp.float32)
        values = input_ref[part, :].astype(jnp.float32)
        held[part, :] = (scaled * inv[part] - values * factor[part]).astype(held.dtype)
        copies.append(pltpu.make_async_copy(held.at[part], out_ref.at[part], sems.at[j]))
        copies[-1].start()
    for copy in copies:
        copy.wait()


def finish(scaled, inputs, sums):
    return pl.pallas_call(
        finish_kernel,
        out_shape=pltpu.HBM(inputs.shape, jnp.bfloat16),
        in_specs=vmem_specs(2 + len(sums)),
        out_specs=pl.BlockSpec(memory_space=pltpu.HBM),
        scratch_shapes=[
            pltpu.VMEM(inputs.shape, jnp.bfloat16),
            pltpu.SemaphoreType.DMA((len(PIECES) - 1,)),
        ],
        compiler_params=pltpu.CompilerParams(vmem_limit_bytes=8 << 20),
    )(*map(in_vmem, (scaled, inputs, *sums)))


FAR, NEAR, SIDE = 4, 2, 1
LINE = (FAR | NEAR, NEAR, FAR)
EARLY = 2


def handed_over(block, sections, count, distance, mask):
    route = [
        ((s - distance) % sections * count + (i ^ mask), s * count + i)
        for s in range(sections)
        for i in range(count)
    ]
    return lax.ppermute(block, ("section", "tp"), route)


def gathered(pair, axis):
    if lax.axis_size(axis) != 8:
        return [lax.all_gather(pair[0], axis)], lambda place: place
    blocks = [pair] + [swapped(pair, axis, mask) for mask in LINE]
    masks = [far | side for far in (0, *LINE) for side in (0, SIDE)]

    def head_of(place):
        return lax.axis_index(axis) ^ masks[place]

    return blocks, head_of


def per_device(grad_attn, w_value, probs_own, probs_spare, evicted, layer_input, gain):
    sections, count = lax.axis_size("section"), lax.axis_size("tp")
    packed, spares, taken = pack(probs_own[0, 0], grad_attn[0, 0], probs_spare[0, 0], evicted)
    heads = []
    for mask in (0, SIDE) if count == 8 else (0,):
        spare = handed_over(spares, sections, count, sections // 2, mask)
        heads.append((swapped(packed, "tp", mask) if mask else packed, spare))
    weights, inputs = w_value[0], layer_input[0]
    reach = reach_of(weights, inputs, gain)
    if count == 8:
        swap, spare = heads[1]
        reach, sent, swap = lax.optimization_barrier((reach, inputs, swap))
        heads[1] = swap, spare
        reaches = [reach, swapped(reach, "tp", SIDE)]
        next_input = passed_along(sent, "section", -1)
        reaches[1], next_input = lax.optimization_barrier((reaches[1], next_input))
    else:
        reaches = [lax.psum(reach, "tp")]
        next_input = passed_along(inputs, "section", -1)
    pair = value_gradients(taken, heads)
    blocks, head_of = gathered(pair, "tp")
    early = [project_early(head_of, blocks[:EARLY], weights)] if count == 8 else []
    scaled, sums = project(head_of, blocks, early, weights, inputs, gain, reaches)
    next_scaled = passed_along(scaled, "section", -1)
    next_sums = []
    for mask in (NEAR, FAR, FAR | NEAR) if count == 8 else ():
        next_sums.append(handed_over(sums, sections, count, -1, mask))
    return finish(next_scaled, next_input, next_sums)[None]


def solution(mesh):
    in_specs = (
        P("section", "tp", None, None),
        P("section", "tp", None),
        P("section", "tp", None, None),
        P("section", "tp", None, None),
        P("section", None),
        P("section", None, "tp"),
        P("section", "tp"),
    )
    out_specs = P("section", None, "tp")
    return jax.shard_map(
        per_device, mesh=mesh, in_specs=in_specs, out_specs=out_specs, check_vma=False
    )
```

```python
import functools

import jax
import jax.numpy as jnp
from jax import lax
from jax.experimental import pallas as pl
from jax.experimental.pallas import tpu as pltpu
from jax.sharding import PartitionSpec as P

D = 12288
LANES = 128
PIECES = (0, 3, 5, 7, 8)
EXTRA = 16
HIDES = pl.CostEstimate(flops=1 << 35, bytes_accessed=1 << 25, transcendentals=0)


def passed_along(block, axis, distance):
    devices = range(lax.axis_size(axis))
    route = [((i - distance) % len(devices), i) for i in devices]
    return lax.ppermute(block, axis, route)


def swapped(block, axis, mask):
    return lax.ppermute(block, axis, [(i ^ mask, i) for i in range(lax.axis_size(axis))])


def in_vmem(array):
    return pltpu.with_memory_space_constraint(array, pltpu.VMEM)


def in_hbm(array):
    return pltpu.with_memory_space_constraint(array, pltpu.HBM)


def vmem_specs(count):
    return [pl.BlockSpec(memory_space=pltpu.VMEM)] * count


def as_row(column):
    return jnp.broadcast_to(column, (column.shape[0], column.shape[0])).T[:1]


def chosen(rows, lanes, pick):
    row = lax.broadcasted_iota(jnp.int32, (rows, lanes), 0)
    lane = lax.broadcasted_iota(jnp.int32, (rows, lanes), 1)
    return pick(row, lane).astype(jnp.float32).astype(jnp.bfloat16)


def product(left, right, left_dim, right_dim):
    return lax.dot_general(
        left, right, (((left_dim,), (right_dim,)), ((), ())), preferred_element_type=jnp.float32
    )


def split(values):
    parts = []
    for _ in range(3):
        parts.append(values.astype(jnp.bfloat16).astype(jnp.float32))
        values = values - parts[-1]
    return parts


def as_parts(row, rows):
    rest = [jnp.zeros((rows - 3, row.shape[1]), jnp.float32)] if rows > 3 else []
    return jnp.concatenate(split(row) + rest)


def pack_kernel(own_ref, grad_ref, spare_ref, out_ref, spare_out, sems):
    copies = [
        pltpu.make_async_copy(own_ref, out_ref.at[0], sems.at[0]),
        pltpu.make_async_copy(grad_ref, out_ref.at[1], sems.at[1]),
        pltpu.make_async_copy(spare_ref, spare_out, sems.at[2]),
    ]
    for copy in copies:
        copy.start()
    for copy in copies:
        copy.wait()


def pack(own, grad, spare):
    return pl.pallas_call(
        pack_kernel,
        out_shape=(
            pltpu.VMEM((2, *own.shape), own.dtype),
            pltpu.VMEM(spare.shape, spare.dtype),
        ),
        in_specs=[pl.BlockSpec(memory_space=pltpu.HBM)] * 3,
        out_specs=tuple(vmem_specs(2)),
        scratch_shapes=[pltpu.SemaphoreType.DMA((3,))],
        cost_estimate=HIDES,
        compiler_params=pltpu.CompilerParams(vmem_limit_bytes=4 << 20),
    )(*map(in_hbm, (own, grad, spare)))


def reach_kernel(weight_ref, input_ref, gain_ref, first_ref, evicted_ref, *refs):
    del first_ref
    reach_ref, taken_ref, flags, sem = refs
    copy = pltpu.make_async_copy(evicted_ref, flags, sem)
    copy.start()
    tokens, features = input_ref.shape
    values = input_ref[...].astype(jnp.float32)
    reach_ref[tokens:, :] = jnp.zeros_like(reach_ref[tokens:, :])
    squares = as_row(jnp.sum(values * values, axis=1, keepdims=True))
    reach_ref[tokens:, :tokens] = as_parts(squares, EXTRA).astype(reach_ref.dtype)
    gained = (values * gain_ref[...]).astype(jnp.bfloat16)
    reach = jnp.dot(gained, weight_ref[...], preferred_element_type=jnp.float32)
    reach_ref[:tokens, :] = reach.astype(reach_ref.dtype)
    copy.wait()
    tiles = evicted_ref.shape[1]
    rows = tokens // tiles
    for tile in range(tiles):
        part = pl.ds(tile * rows, rows)
        taken = jnp.full((rows, tokens), flags[0, tile], jnp.int32)
        taken_ref[part, :] = taken.astype(jnp.float32).astype(taken_ref.dtype)


def reach_of(weights, inputs, gain, first, evicted):
    tokens = inputs.shape[0]
    return pl.pallas_call(
        reach_kernel,
        out_shape=(
            pltpu.VMEM((tokens + EXTRA, weights.shape[1]), jnp.bfloat16),
            pltpu.VMEM((tokens, tokens), jnp.bfloat16),
        ),
        in_specs=vmem_specs(4) + [pl.BlockSpec(memory_space=pltpu.HBM)],
        out_specs=tuple(vmem_specs(2)),
        scratch_shapes=[pltpu.SMEM(evicted.shape, evicted.dtype), pltpu.SemaphoreType.DMA(())],
        cost_estimate=HIDES,
        compiler_params=pltpu.CompilerParams(vmem_limit_bytes=8 << 20),
    )(*map(in_vmem, (weights, inputs, gain, first)), in_hbm(evicted))


def mix_kernel(taken_ref, *refs):
    out_ref = refs[-1]
    taken = taken_ref[...]
    for j in range(out_ref.shape[0]):
        packed_ref, spare_ref = refs[len(refs) - 2 - j], refs[j]
        out_ref[j] = lax.dot_general(
            packed_ref[0] * (1 - taken) + spare_ref[...] * taken,
            packed_ref[1],
            (((0,), (0,)), ((), ())),
            preferred_element_type=jnp.float32,
        ).astype(out_ref.dtype)


def value_gradients(taken, heads):
    return pl.pallas_call(
        mix_kernel,
        out_shape=pltpu.VMEM((len(heads), *heads[0][1].shape), jnp.bfloat16),
        in_specs=vmem_specs(1 + 2 * len(heads)),
        out_specs=pl.BlockSpec(memory_space=pltpu.VMEM),
        cost_estimate=HIDES,
        compiler_params=pltpu.CompilerParams(vmem_limit_bytes=4 << 20),
    )(*map(in_vmem, (taken, *[spare for _, spare in heads], *[packed for packed, _ in heads[::-1]])))


def column_tile(features):
    return 256 if features % 256 == 0 else features


def fill(flat, blocks, head_of, first):
    groups = []
    for ref in blocks:
        count = ref.shape[0]
        for j in range(count):
            start = pl.multiple_of(head_of(first + j) * LANES, LANES)
            flat[:, pl.ds(start, LANES)] = ref[j]
        width = count * LANES
        groups.append((pl.multiple_of(head_of(first) // count * width, width), width))
        first += count
    return groups


def times_weights(flat, groups, weight_ref, part):
    products = [
        lax.dot_general(
            flat[:, pl.ds(start, width)],
            weight_ref[part, pl.ds(start, width)],
            (((1,), (1,)), ((), ())),
            preferred_element_type=jnp.float32,
        )
        for start, width in groups
    ]
    return sum(products[1:], products[0])


def early_kernel(head_of, *refs):
    *blocks, weight_ref, out_ref, flat = refs
    groups = fill(flat, blocks, head_of, 0)
    features = weight_ref.shape[0]
    tile = column_tile(features)
    for start in range(0, features, tile):
        part = pl.ds(start, tile)
        out_ref[:, part] = times_weights(flat, groups, weight_ref, part)


def project_early(head_of, blocks, weights):
    tokens = blocks[0].shape[1]
    return pl.pallas_call(
        functools.partial(early_kernel, head_of),
        out_shape=pltpu.VMEM((tokens, weights.shape[0]), jnp.float32),
        in_specs=vmem_specs(len(blocks) + 1),
        out_specs=pl.BlockSpec(memory_space=pltpu.VMEM),
        scratch_shapes=[pltpu.VMEM((tokens, weights.shape[1]), jnp.bfloat16)],
        cost_estimate=pl.CostEstimate(flops=1 << 16, bytes_accessed=1 << 12, transcendentals=0),
        compiler_params=pltpu.CompilerParams(vmem_limit_bytes=16 << 20),
    )(*map(in_vmem, (*blocks, weights)))


def project_kernel(head_of, sizes, *refs):
    blocks = refs[: sizes[0]]
    early_refs = refs[sizes[0] : sizes[0] + sizes[1]]
    rest = refs[sizes[0] + sizes[1] :]
    weight_ref, input_ref, gain_ref, *reach_refs, scaled_ref, sums_ref, flat = rest
    tokens, features = input_ref.shape
    groups = fill(flat, blocks, head_of, 0)
    if early_refs:
        groups = groups[EARLY:]
    tile = column_tile(features)
    for start in range(0, features, tile):
        part = pl.ds(start, tile)
        grad_normed = times_weights(flat, groups, weight_ref, part)
        for ref in early_refs:
            grad_normed = grad_normed + ref[:, part]
        scaled_ref[:, part] = (grad_normed * gain_ref[:, part]).astype(scaled_ref.dtype)
    reach = sum(ref[:tokens, :].astype(jnp.float32) for ref in reach_refs)
    squares = sum(ref[tokens:, :tokens].astype(jnp.float32) for ref in reach_refs)
    squares = jnp.sum(squares, axis=0, keepdims=True)
    products = flat[...].astype(jnp.float32) * reach
    folded = products[:, :LANES]
    for start in range(LANES, products.shape[1], LANES):
        folded = folded + products[:, start : start + LANES]
    ones = jnp.ones((EXTRA, LANES), jnp.bfloat16)
    inner = sum(product(ones, part.astype(jnp.bfloat16), 1, 1) for part in split(folded))[:1]
    sums_ref[:1, :] = squares
    sums_ref[1:, :] = inner
    parts = jnp.concatenate([as_parts(squares, 3), as_parts(inner, EXTRA - 3)])
    places = chosen(EXTRA, LANES, lambda row, lane: row == lane)
    scaled_ref[:, features:] = product(parts.astype(jnp.bfloat16), places, 0, 0).astype(
        scaled_ref.dtype
    )


def project(head_of, blocks, early, weights, inputs, gain, reaches):
    tokens, features = inputs.shape
    operands = (*blocks, *early, weights, inputs, gain, *reaches)
    return pl.pallas_call(
        functools.partial(project_kernel, head_of, (len(blocks), len(early))),
        out_shape=(
            pltpu.VMEM((tokens, features + LANES), jnp.bfloat16),
            pltpu.VMEM((2, tokens), jnp.float32),
        ),
        in_specs=vmem_specs(len(operands)),
        out_specs=tuple(vmem_specs(2)),
        scratch_shapes=[pltpu.VMEM((tokens, weights.shape[1]), jnp.bfloat16)],
        cost_estimate=HIDES,
        compiler_params=pltpu.CompilerParams(vmem_limit_bytes=16 << 20),
    )(*map(in_vmem, operands))


def finish_kernel(scaled_ref, input_ref, *refs):
    *sums_refs, out_ref, held, sems = refs
    tokens, features = input_ref.shape
    places = chosen(EXTRA, LANES, lambda row, lane: (lane < 6) & (lane // 3 == row))
    sums = product(places, scaled_ref[:, features:], 1, 1)[:2]
    for ref in sums_refs:
        sums = sums + ref[...]
    inv = 1.0 / jnp.sqrt(sums[:1] / D + 1e-05)
    factor = sums[1:] * (inv * inv * inv) / D
    parts = jnp.concatenate([as_parts(inv, 3), as_parts(factor, EXTRA - 3)])
    spread = chosen(EXTRA, 2 * LANES, lambda row, lane: (row < 6) & (row // 3 == lane // LANES))
    columns = product(parts.astype(jnp.bfloat16), spread, 0, 0)
    inv, factor = columns[:, :LANES], columns[:, LANES:]
    copies = []
    for j in range(len(PIECES) - 1):
        part = slice(PIECES[j] * tokens // 8, PIECES[j + 1] * tokens // 8)
        for start in range(0, features, LANES):
            lanes = slice(start, start + LANES)
            scaled = scaled_ref[part, lanes].astype(jnp.float32)
            values = input_ref[part, lanes].astype(jnp.float32)
            held[part, lanes] = (scaled * inv[part] - values * factor[part]).astype(held.dtype)
        copies.append(pltpu.make_async_copy(held.at[part], out_ref.at[part], sems.at[j]))
        copies[-1].start()
    for copy in copies:
        copy.wait()


def finish(scaled, inputs, sums):
    return pl.pallas_call(
        finish_kernel,
        out_shape=pltpu.HBM(inputs.shape, jnp.bfloat16),
        in_specs=vmem_specs(2 + len(sums)),
        out_specs=pl.BlockSpec(memory_space=pltpu.HBM),
        scratch_shapes=[
            pltpu.VMEM(inputs.shape, jnp.bfloat16),
            pltpu.SemaphoreType.DMA((len(PIECES) - 1,)),
        ],
        compiler_params=pltpu.CompilerParams(vmem_limit_bytes=8 << 20),
    )(*map(in_vmem, (scaled, inputs, *sums)))


FAR, NEAR, SIDE = 4, 2, 1
LINE = (FAR | NEAR, NEAR, FAR)
EARLY = 2


def handed_over(block, sections, count, distance, mask):
    route = [
        ((s - distance) % sections * count + (i ^ mask), s * count + i)
        for s in range(sections)
        for i in range(count)
    ]
    return lax.ppermute(block, ("section", "tp"), route)


def gathered(pair, axis):
    if lax.axis_size(axis) != 8:
        return [lax.all_gather(pair[0], axis)], lambda place: place
    blocks = [pair] + [swapped(pair, axis, mask) for mask in LINE]
    masks = [far | side for far in (0, *LINE) for side in (0, SIDE)]

    def head_of(place):
        return lax.axis_index(axis) ^ masks[place]

    return blocks, head_of


def per_device(grad_attn, w_value, probs_own, probs_spare, evicted, layer_input, gain):
    sections, count = lax.axis_size("section"), lax.axis_size("tp")
    packed, spares = pack(probs_own[0, 0], grad_attn[0, 0], probs_spare[0, 0])
    heads = []
    for mask in (0, SIDE) if count == 8 else (0,):
        spare = handed_over(spares, sections, count, sections // 2, mask)
        heads.append((swapped(packed, "tp", mask) if mask else packed, spare))
    weights, inputs = w_value[0], layer_input[0]
    next_input = passed_along(inputs, "section", -1)
    reach, taken = reach_of(weights, inputs, gain, heads[-1][0], evicted)
    if count == 8:
        reaches = [reach, swapped(reach, "tp", SIDE)]
        reaches[1], next_input = lax.optimization_barrier((reaches[1], next_input))
    else:
        reaches = [lax.psum(reach, "tp")]
    pair = value_gradients(taken, heads)
    blocks, head_of = gathered(pair, "tp")
    early = [project_early(head_of, blocks[:EARLY], weights)] if count == 8 else []
    scaled, sums = project(head_of, blocks, early, weights, inputs, gain, reaches)
    next_scaled = passed_along(scaled, "section", -1)
    next_sums = []
    for mask in (NEAR, FAR, FAR | NEAR) if count == 8 else ():
        next_sums.append(handed_over(sums, sections, count, -1, mask))
    return finish(next_scaled, next_input, next_sums)[None]


def solution(mesh):
    in_specs = (
        P("section", "tp", None, None),
        P("section", "tp", None),
        P("section", "tp", None, None),
        P("section", "tp", None, None),
        P("section", None),
        P("section", None, "tp"),
        P("section", "tp"),
    )
    out_specs = P("section", None, "tp")
    return jax.shard_map(
        per_device, mesh=mesh, in_specs=in_specs, out_specs=out_specs, check_vma=False
    )
```

```python
import functools

import jax
import jax.numpy as jnp
from jax import lax
from jax.experimental import pallas as pl
from jax.experimental.pallas import tpu as pltpu
from jax.sharding import PartitionSpec as P

D = 12288
LANES = 128
PIECES = (0, 3, 5, 7, 8)
EXTRA = 16
HIDES = pl.CostEstimate(flops=1 << 35, bytes_accessed=1 << 25, transcendentals=0)


def passed_along(block, axis, distance):
    devices = range(lax.axis_size(axis))
    route = [((i - distance) % len(devices), i) for i in devices]
    return lax.ppermute(block, axis, route)


def swapped(block, axis, mask):
    return lax.ppermute(block, axis, [(i ^ mask, i) for i in range(lax.axis_size(axis))])


def in_vmem(array):
    return pltpu.with_memory_space_constraint(array, pltpu.VMEM)


def in_hbm(array):
    return pltpu.with_memory_space_constraint(array, pltpu.HBM)


def vmem_specs(count):
    return [pl.BlockSpec(memory_space=pltpu.VMEM)] * count


def as_row(column):
    return jnp.broadcast_to(column, (column.shape[0], column.shape[0])).T[:1]


def standing(rows):
    tokens = rows.shape[1]
    return jnp.concatenate([rows, jnp.zeros((tokens - rows.shape[0], tokens), rows.dtype)]).T


def split(values):
    parts = []
    for _ in range(3):
        parts.append(values.astype(jnp.bfloat16).astype(jnp.float32))
        values = values - parts[-1]
    return parts


def as_parts(row):
    rest = jnp.zeros((EXTRA - 3, row.shape[1]), jnp.float32)
    return jnp.concatenate(split(row) + [rest]).astype(jnp.bfloat16)


def pack_kernel(own_ref, grad_ref, spare_ref, evicted_ref, *refs):
    out_ref, spare_out, taken_ref, flags, sems = refs
    copies = [
        pltpu.make_async_copy(evicted_ref, flags, sems.at[0]),
        pltpu.make_async_copy(own_ref, out_ref.at[0], sems.at[1]),
        pltpu.make_async_copy(grad_ref, out_ref.at[1], sems.at[2]),
        pltpu.make_async_copy(spare_ref, spare_out, sems.at[3]),
    ]
    for copy in copies:
        copy.start()
    copies[0].wait()
    tiles = evicted_ref.shape[1]
    rows = taken_ref.shape[0] // tiles
    for tile in range(tiles):
        part = pl.ds(tile * rows, rows)
        taken = jnp.full((rows, taken_ref.shape[1]), flags[0, tile], jnp.int32)
        taken_ref[part, :] = taken.astype(jnp.float32).astype(taken_ref.dtype)
    for copy in copies[1:]:
        copy.wait()


def pack(own, grad, spare, evicted):
    return pl.pallas_call(
        pack_kernel,
        out_shape=(
            pltpu.VMEM((2, *own.shape), own.dtype),
            pltpu.VMEM(spare.shape, spare.dtype),
            pltpu.VMEM(own.shape, own.dtype),
        ),
        in_specs=[pl.BlockSpec(memory_space=pltpu.HBM)] * 4,
        out_specs=tuple(vmem_specs(3)),
        scratch_shapes=[
            pltpu.SMEM(evicted.shape, evicted.dtype),
            pltpu.SemaphoreType.DMA((4,)),
        ],
        cost_estimate=HIDES,
        compiler_params=pltpu.CompilerParams(vmem_limit_bytes=4 << 20),
    )(*map(in_hbm, (own, grad, spare, evicted)))


def reach_kernel(weight_ref, input_ref, gain_ref, first_ref, reach_ref):
    del first_ref
    tokens, features = input_ref.shape
    values = input_ref[...].astype(jnp.float32)
    reach_ref[tokens:, :] = jnp.zeros_like(reach_ref[tokens:, :])
    squares = as_row(jnp.sum(values * values, axis=1, keepdims=True))
    reach_ref[tokens:, :tokens] = as_parts(squares)
    gained = (values * gain_ref[...]).astype(jnp.bfloat16)
    reach = jnp.dot(gained, weight_ref[...], preferred_element_type=jnp.float32)
    reach_ref[:tokens, :] = reach.astype(reach_ref.dtype)


def reach_of(weights, inputs, gain, first):
    return pl.pallas_call(
        reach_kernel,
        out_shape=pltpu.VMEM((inputs.shape[0] + EXTRA, weights.shape[1]), jnp.bfloat16),
        in_specs=vmem_specs(4),
        out_specs=pl.BlockSpec(memory_space=pltpu.VMEM),
        cost_estimate=HIDES,
        compiler_params=pltpu.CompilerParams(vmem_limit_bytes=8 << 20),
    )(*map(in_vmem, (weights, inputs, gain, first)))


def mix_kernel(taken_ref, *refs):
    out_ref = refs[-1]
    taken = taken_ref[...]
    for j in range(out_ref.shape[1]):
        packed_ref, spare_ref = refs[len(refs) - 2 - j], refs[j]
        value = lax.dot_general(
            packed_ref[0] * (1 - taken) + spare_ref[...] * taken,
            packed_ref[1],
            (((0,), (0,)), ((), ())),
            preferred_element_type=jnp.float32,
        ).astype(out_ref.dtype)
        for copy in range(out_ref.shape[0]):
            out_ref[copy, j] = value


def value_gradients(taken, heads, copies):
    return pl.pallas_call(
        mix_kernel,
        out_shape=pltpu.VMEM((copies, len(heads), *heads[0][1].shape), jnp.bfloat16),
        in_specs=vmem_specs(1 + 2 * len(heads)),
        out_specs=pl.BlockSpec(memory_space=pltpu.VMEM),
        cost_estimate=HIDES,
        compiler_params=pltpu.CompilerParams(vmem_limit_bytes=4 << 20),
    )(*map(in_vmem, (taken, *[spare for _, spare in heads], *[packed for packed, _ in heads[::-1]])))


def column_tile(features):
    return 256 if features % 256 == 0 else features


def fill(flat, blocks, head_of, first):
    groups = []
    for ref in blocks:
        count = ref.shape[0]
        for j in range(count):
            start = pl.multiple_of(head_of(first + j) * LANES, LANES)
            flat[:, pl.ds(start, LANES)] = ref[j]
        width = count * LANES
        groups.append((pl.multiple_of(head_of(first) // count * width, width), width))
        first += count
    return groups


def times_weights(flat, groups, weight_ref, part):
    products = [
        lax.dot_general(
            flat[:, pl.ds(start, width)],
            weight_ref[part, pl.ds(start, width)],
            (((1,), (1,)), ((), ())),
            preferred_element_type=jnp.float32,
        )
        for start, width in groups
    ]
    return sum(products[1:], products[0])


def early_kernel(head_of, *refs):
    *blocks, weight_ref, out_ref, flat = refs
    groups = fill(flat, blocks, head_of, 0)
    features = weight_ref.shape[0]
    tile = column_tile(features)
    for start in range(0, features, tile):
        part = pl.ds(start, tile)
        out_ref[:, part] = times_weights(flat, groups, weight_ref, part)


def project_early(head_of, blocks, weights):
    tokens = blocks[0].shape[1]
    return pl.pallas_call(
        functools.partial(early_kernel, head_of),
        out_shape=pltpu.VMEM((tokens, weights.shape[0]), jnp.float32),
        in_specs=vmem_specs(len(blocks) + 1),
        out_specs=pl.BlockSpec(memory_space=pltpu.VMEM),
        scratch_shapes=[pltpu.VMEM((tokens, weights.shape[1]), jnp.bfloat16)],
        cost_estimate=pl.CostEstimate(flops=1 << 16, bytes_accessed=1 << 12, transcendentals=0),
        compiler_params=pltpu.CompilerParams(vmem_limit_bytes=16 << 20),
    )(*map(in_vmem, (*blocks, weights)))


def project_kernel(head_of, sizes, *refs):
    blocks = refs[: sizes[0]]
    early_refs = refs[sizes[0] : sizes[0] + sizes[1]]
    rest = refs[sizes[0] + sizes[1] :]
    weight_ref, input_ref, gain_ref, *reach_refs, scaled_ref, sums_ref, flat = rest
    tokens, features = input_ref.shape
    groups = fill(flat, blocks, head_of, 0)
    if early_refs:
        groups = groups[EARLY:]
    tile = column_tile(features)
    for start in range(0, features, tile):
        part = pl.ds(start, tile)
        grad_normed = times_weights(flat, groups, weight_ref, part)
        for ref in early_refs:
            grad_normed = grad_normed + ref[:, part]
        scaled_ref[:, part] = (grad_normed * gain_ref[:, part]).astype(scaled_ref.dtype)
    reach = sum(ref[:tokens, :].astype(jnp.float32) for ref in reach_refs)
    squares = sum(ref[tokens:, :tokens].astype(jnp.float32) for ref in reach_refs)
    squares = jnp.sum(squares, axis=0, keepdims=True)
    inner = jnp.sum(flat[...].astype(jnp.float32) * reach, axis=1, keepdims=True)
    inner = as_row(inner)
    sums_ref[:1, :] = squares
    sums_ref[1:, :] = inner
    rows = jnp.concatenate([*split(squares), *split(inner), jnp.zeros((2, tokens), jnp.float32)])
    scaled_ref[:, features:] = standing(rows).astype(scaled_ref.dtype)


def project(head_of, blocks, early, weights, inputs, gain, reaches):
    tokens, features = inputs.shape
    operands = (*blocks, *early, weights, inputs, gain, *reaches)
    return pl.pallas_call(
        functools.partial(project_kernel, head_of, (len(blocks), len(early))),
        out_shape=(
            pltpu.VMEM((tokens, features + LANES), jnp.bfloat16),
            pltpu.VMEM((2, tokens), jnp.float32),
        ),
        in_specs=vmem_specs(len(operands)),
        out_specs=tuple(vmem_specs(2)),
        scratch_shapes=[pltpu.VMEM((tokens, weights.shape[1]), jnp.bfloat16)],
        cost_estimate=HIDES,
        compiler_params=pltpu.CompilerParams(vmem_limit_bytes=16 << 20),
    )(*map(in_vmem, operands))


def finish_kernel(scaled_ref, input_ref, *refs):
    *sums_refs, out_ref, held, sems = refs
    tokens, features = input_ref.shape
    extra = scaled_ref[:, features:].astype(jnp.float32).T
    squares = extra[0:1] + extra[1:2] + extra[2:3]
    inner = extra[3:4] + extra[4:5] + extra[5:6]
    for ref in sums_refs:
        squares = squares + ref[:1, :]
        inner = inner + ref[1:, :]
    inv = 1.0 / jnp.sqrt(squares / D + 1e-05)
    factor = inner * (inv * inv * inv) / D
    rows = jnp.concatenate([inv, factor, jnp.zeros((6, tokens), jnp.float32)])
    columns = standing(rows)
    inv, factor = columns[:, 0:1], columns[:, 1:2]
    copies = []
    for j in range(len(PIECES) - 1):
        part = slice(PIECES[j] * tokens // 8, PIECES[j + 1] * tokens // 8)
        scaled = scaled_ref[part, :features].astype(jnp.float32)
        values = input_ref[part, :].astype(jnp.float32)
        held[part, :] = (scaled * inv[part] - values * factor[part]).astype(held.dtype)
        copies.append(pltpu.make_async_copy(held.at[part], out_ref.at[part], sems.at[j]))
        copies[-1].start()
    for copy in copies:
        copy.wait()


def finish(scaled, inputs, sums):
    return pl.pallas_call(
        finish_kernel,
        out_shape=pltpu.HBM(inputs.shape, jnp.bfloat16),
        in_specs=vmem_specs(2 + len(sums)),
        out_specs=pl.BlockSpec(memory_space=pltpu.HBM),
        scratch_shapes=[
            pltpu.VMEM(inputs.shape, jnp.bfloat16),
            pltpu.SemaphoreType.DMA((len(PIECES) - 1,)),
        ],
        compiler_params=pltpu.CompilerParams(vmem_limit_bytes=8 << 20),
    )(*map(in_vmem, (scaled, inputs, *sums)))


FAR, NEAR, SIDE = 4, 2, 1
LINE = (FAR | NEAR, NEAR, FAR)
EARLY = 2


def handed_over(block, sections, count, distance, mask):
    route = [
        ((s - distance) % sections * count + (i ^ mask), s * count + i)
        for s in range(sections)
        for i in range(count)
    ]
    return lax.ppermute(block, ("section", "tp"), route)


def gathered(pairs, axis):
    if pairs.shape[0] == 1:
        return [lax.all_gather(pairs[0, 0], axis)], lambda place: place
    count = lax.axis_size(axis)
    groups = [[i for i in range(count) if i % 2 == side] for side in range(2)]
    blocks = lax.all_to_all(pairs, axis, 0, 0, axis_index_groups=groups, tiled=True)

    def head_of(place):
        return (place - place % 2) + (lax.rem(lax.axis_index(axis), 2) ^ (place % 2))

    return [blocks.reshape(count, *blocks.shape[2:])], head_of


def per_device(grad_attn, w_value, probs_own, probs_spare, evicted, layer_input, gain):
    sections, count = lax.axis_size("section"), lax.axis_size("tp")
    packed, spares, taken = pack(probs_own[0, 0], grad_attn[0, 0], probs_spare[0, 0], evicted)
    heads = []
    for mask in (0, SIDE) if count == 8 else (0,):
        spare = handed_over(spares, sections, count, sections // 2, mask)
        heads.append((swapped(packed, "tp", mask) if mask else packed, spare))
    weights, inputs = w_value[0], layer_input[0]
    next_input = passed_along(inputs, "section", -1)
    reach = reach_of(weights, inputs, gain, heads[-1][0])
    if count == 8:
        reaches = [reach, swapped(reach, "tp", SIDE)]
        reaches[1], next_input = lax.optimization_barrier((reaches[1], next_input))
    else:
        reaches = [lax.psum(reach, "tp")]
    pairs = value_gradients(taken, heads, count // 2 if count == 8 else 1)
    blocks, head_of = gathered(pairs, "tp")
    early = []
    scaled, sums = project(head_of, blocks, early, weights, inputs, gain, reaches)
    next_scaled = passed_along(scaled, "section", -1)
    next_sums = []
    for mask in (NEAR, FAR, FAR | NEAR) if count == 8 else ():
        next_sums.append(handed_over(sums, sections, count, -1, mask))
    return finish(next_scaled, next_input, next_sums)[None]


def solution(mesh):
    in_specs = (
        P("section", "tp", None, None),
        P("section", "tp", None),
        P("section", "tp", None, None),
        P("section", "tp", None, None),
        P("section", None),
        P("section", None, "tp"),
        P("section", "tp"),
    )
    out_specs = P("section", None, "tp")
    return jax.shard_map(
        per_device, mesh=mesh, in_specs=in_specs, out_specs=out_specs, check_vma=False
    )
```

```python
import functools

import jax
import jax.numpy as jnp
from jax import lax
from jax.experimental import pallas as pl
from jax.experimental.pallas import tpu as pltpu
from jax.sharding import PartitionSpec as P

D = 12288
LANES = 128
PIECES = (0, 3, 5, 7, 8)
EXTRA = 16
HIDES = pl.CostEstimate(flops=1 << 35, bytes_accessed=1 << 25, transcendentals=0)


def passed_along(block, axis, distance):
    devices = range(lax.axis_size(axis))
    route = [((i - distance) % len(devices), i) for i in devices]
    return lax.ppermute(block, axis, route)


def swapped(block, axis, mask):
    return lax.ppermute(block, axis, [(i ^ mask, i) for i in range(lax.axis_size(axis))])


def in_vmem(array):
    return pltpu.with_memory_space_constraint(array, pltpu.VMEM)


def in_hbm(array):
    return pltpu.with_memory_space_constraint(array, pltpu.HBM)


def vmem_specs(count):
    return [pl.BlockSpec(memory_space=pltpu.VMEM)] * count


def as_row(column):
    return jnp.broadcast_to(column, (column.shape[0], column.shape[0])).T[:1]


def standing(rows):
    tokens = rows.shape[1]
    return jnp.concatenate([rows, jnp.zeros((tokens - rows.shape[0], tokens), rows.dtype)]).T


def split(values):
    parts = []
    for _ in range(3):
        parts.append(values.astype(jnp.bfloat16).astype(jnp.float32))
        values = values - parts[-1]
    return parts


def own_ratio(squares, inner):
    return inner / jnp.maximum(squares, 1e-30)


def as_parts(row):
    rest = jnp.zeros((EXTRA - 3, row.shape[1]), jnp.float32)
    return jnp.concatenate(split(row) + [rest]).astype(jnp.bfloat16)


def pack_kernel(own_ref, grad_ref, spare_ref, evicted_ref, *refs):
    out_ref, spare_out, taken_ref, flags, sems = refs
    copies = [
        pltpu.make_async_copy(evicted_ref, flags, sems.at[0]),
        pltpu.make_async_copy(own_ref, out_ref.at[0], sems.at[1]),
        pltpu.make_async_copy(grad_ref, out_ref.at[1], sems.at[2]),
        pltpu.make_async_copy(spare_ref, spare_out, sems.at[3]),
    ]
    for copy in copies:
        copy.start()
    copies[0].wait()
    tiles = evicted_ref.shape[1]
    rows = taken_ref.shape[0] // tiles
    for tile in range(tiles):
        part = pl.ds(tile * rows, rows)
        taken = jnp.full((rows, taken_ref.shape[1]), flags[0, tile], jnp.int32)
        taken_ref[part, :] = taken.astype(jnp.float32).astype(taken_ref.dtype)
    for copy in copies[1:]:
        copy.wait()


def pack(own, grad, spare, evicted):
    return pl.pallas_call(
        pack_kernel,
        out_shape=(
            pltpu.VMEM((2, *own.shape), own.dtype),
            pltpu.VMEM(spare.shape, spare.dtype),
            pltpu.VMEM(own.shape, own.dtype),
        ),
        in_specs=[pl.BlockSpec(memory_space=pltpu.HBM)] * 4,
        out_specs=tuple(vmem_specs(3)),
        scratch_shapes=[
            pltpu.SMEM(evicted.shape, evicted.dtype),
            pltpu.SemaphoreType.DMA((4,)),
        ],
        cost_estimate=HIDES,
        compiler_params=pltpu.CompilerParams(vmem_limit_bytes=4 << 20),
    )(*map(in_hbm, (own, grad, spare, evicted)))


def reach_kernel(weight_ref, input_ref, gain_ref, first_ref, reach_ref, own_ref):
    del first_ref
    tokens, features = input_ref.shape
    values = input_ref[...].astype(jnp.float32)
    reach_ref[tokens:, :] = jnp.zeros_like(reach_ref[tokens:, :])
    squares = as_row(jnp.sum(values * values, axis=1, keepdims=True))
    reach_ref[tokens:, :tokens] = as_parts(squares)
    gained = (values * gain_ref[...]).astype(jnp.bfloat16)
    reach = jnp.dot(gained, weight_ref[...], preferred_element_type=jnp.float32)
    reach_ref[:tokens, :] = reach.astype(reach_ref.dtype)
    own_ref[:tokens, :] = reach
    own_ref[tokens:, :] = reach_ref[tokens:, :].astype(own_ref.dtype)


def reach_of(weights, inputs, gain, first):
    return pl.pallas_call(
        reach_kernel,
        out_shape=tuple(
            pltpu.VMEM((inputs.shape[0] + EXTRA, weights.shape[1]), dtype)
            for dtype in (jnp.bfloat16, jnp.float32)
        ),
        in_specs=vmem_specs(4),
        out_specs=tuple(vmem_specs(2)),
        cost_estimate=HIDES,
        compiler_params=pltpu.CompilerParams(vmem_limit_bytes=8 << 20),
    )(*map(in_vmem, (weights, inputs, gain, first)))


def mix_kernel(taken_ref, *refs):
    out_ref = refs[-1]
    taken = taken_ref[...]
    for j in range(out_ref.shape[0]):
        packed_ref, spare_ref = refs[len(refs) - 2 - j], refs[j]
        out_ref[j] = lax.dot_general(
            packed_ref[0] * (1 - taken) + spare_ref[...] * taken,
            packed_ref[1],
            (((0,), (0,)), ((), ())),
            preferred_element_type=jnp.float32,
        ).astype(out_ref.dtype)


def value_gradients(taken, heads):
    return pl.pallas_call(
        mix_kernel,
        out_shape=pltpu.VMEM((len(heads), *heads[0][1].shape), jnp.bfloat16),
        in_specs=vmem_specs(1 + 2 * len(heads)),
        out_specs=pl.BlockSpec(memory_space=pltpu.VMEM),
        cost_estimate=HIDES,
        compiler_params=pltpu.CompilerParams(vmem_limit_bytes=4 << 20),
    )(*map(in_vmem, (taken, *[spare for _, spare in heads], *[packed for packed, _ in heads[::-1]])))


def column_tile(features):
    return 256 if features % 256 == 0 else features


def fill(flat, blocks, head_of, first):
    groups = []
    for ref in blocks:
        count = ref.shape[0]
        for j in range(count):
            start = pl.multiple_of(head_of(first + j) * LANES, LANES)
            flat[:, pl.ds(start, LANES)] = ref[j]
        width = count * LANES
        groups.append((pl.multiple_of(head_of(first) // count * width, width), width))
        first += count
    return groups


def times_weights(flat, groups, weight_ref, part):
    products = [
        lax.dot_general(
            flat[:, pl.ds(start, width)],
            weight_ref[part, pl.ds(start, width)],
            (((1,), (1,)), ((), ())),
            preferred_element_type=jnp.float32,
        )
        for start, width in groups
    ]
    return sum(products[1:], products[0])


def early_kernel(head_of, *refs):
    *blocks, weight_ref, out_ref, flat = refs
    groups = fill(flat, blocks, head_of, 0)
    features = weight_ref.shape[0]
    tile = column_tile(features)
    for start in range(0, features, tile):
        part = pl.ds(start, tile)
        out_ref[:, part] = times_weights(flat, groups, weight_ref, part)


def project_early(head_of, blocks, weights):
    tokens = blocks[0].shape[1]
    return pl.pallas_call(
        functools.partial(early_kernel, head_of),
        out_shape=pltpu.VMEM((tokens, weights.shape[0]), jnp.float32),
        in_specs=vmem_specs(len(blocks) + 1),
        out_specs=pl.BlockSpec(memory_space=pltpu.VMEM),
        scratch_shapes=[pltpu.VMEM((tokens, weights.shape[1]), jnp.bfloat16)],
        cost_estimate=pl.CostEstimate(flops=1 << 16, bytes_accessed=1 << 12, transcendentals=0),
        compiler_params=pltpu.CompilerParams(vmem_limit_bytes=16 << 20),
    )(*map(in_vmem, (*blocks, weights)))


def project_kernel(head_of, sizes, *refs):
    blocks = refs[: sizes[0]]
    early_refs = refs[sizes[0] : sizes[0] + sizes[1]]
    rest = refs[sizes[0] + sizes[1] :]
    weight_ref, input_ref, gain_ref, *reach_refs, scaled_ref, sums_ref, flat = rest
    tokens, features = input_ref.shape
    groups = fill(flat, blocks, head_of, 0)
    if early_refs:
        groups = groups[EARLY:]
    reach = sum(ref[:tokens, :].astype(jnp.float32) for ref in reach_refs)
    squares = sum(ref[tokens:, :tokens].astype(jnp.float32) for ref in reach_refs)
    squares = jnp.sum(squares, axis=0, keepdims=True)
    inner = as_row(jnp.sum(flat[...].astype(jnp.float32) * reach, axis=1, keepdims=True))
    sums_ref[:1, :] = squares
    sums_ref[1:, :] = inner
    rho = own_ratio(squares, inner)
    rows = [*split(squares), *split(inner), rho, jnp.zeros((1, tokens), jnp.float32)]
    columns = standing(jnp.concatenate(rows))
    scaled_ref[:, features:] = columns.astype(scaled_ref.dtype)
    rho = columns[:, 6:7]
    tile = column_tile(features)
    for start in range(0, features, tile):
        part = pl.ds(start, tile)
        grad_normed = times_weights(flat, groups, weight_ref, part)
        for ref in early_refs:
            grad_normed = grad_normed + ref[:, part]
        values = input_ref[:, part].astype(jnp.float32)
        scaled_ref[:, part] = (grad_normed * gain_ref[:, part] - values * rho).astype(
            scaled_ref.dtype
        )


def project(head_of, blocks, early, weights, inputs, gain, reaches):
    tokens, features = inputs.shape
    operands = (*blocks, *early, weights, inputs, gain, *reaches)
    return pl.pallas_call(
        functools.partial(project_kernel, head_of, (len(blocks), len(early))),
        out_shape=(
            pltpu.VMEM((tokens, features + LANES), jnp.bfloat16),
            pltpu.VMEM((2, tokens), jnp.float32),
        ),
        in_specs=vmem_specs(len(operands)),
        out_specs=tuple(vmem_specs(2)),
        scratch_shapes=[pltpu.VMEM((tokens, weights.shape[1]), jnp.bfloat16)],
        cost_estimate=HIDES,
        compiler_params=pltpu.CompilerParams(vmem_limit_bytes=16 << 20),
    )(*map(in_vmem, operands))


def finish_kernel(scaled_ref, input_ref, *refs):
    *sums_refs, out_ref, held, sems = refs
    tokens, features = input_ref.shape
    extra = scaled_ref[:, features:].astype(jnp.float32).T
    squares = extra[0:1] + extra[1:2] + extra[2:3]
    inner = extra[3:4] + extra[4:5] + extra[5:6]
    rho = own_ratio(squares, inner)
    for ref in sums_refs:
        squares = squares + ref[:1, :]
        inner = inner + ref[1:, :]
    inv = 1.0 / jnp.sqrt(squares / D + 1e-05)
    factor = inner * (inv * inv * inv) / D - inv * rho
    rows = jnp.concatenate([inv, factor, jnp.zeros((6, tokens), jnp.float32)])
    columns = standing(rows)
    inv, factor = columns[:, 0:1], columns[:, 1:2]
    copies = []
    for j in range(len(PIECES) - 1):
        part = slice(PIECES[j] * tokens // 8, PIECES[j + 1] * tokens // 8)
        scaled = scaled_ref[part, :features].astype(jnp.float32)
        values = input_ref[part, :].astype(jnp.float32)
        held[part, :] = (scaled * inv[part] - values * factor[part]).astype(held.dtype)
        copies.append(pltpu.make_async_copy(held.at[part], out_ref.at[part], sems.at[j]))
        copies[-1].start()
    for copy in copies:
        copy.wait()


def finish(scaled, inputs, sums):
    return pl.pallas_call(
        finish_kernel,
        out_shape=pltpu.HBM(inputs.shape, jnp.bfloat16),
        in_specs=vmem_specs(2 + len(sums)),
        out_specs=pl.BlockSpec(memory_space=pltpu.HBM),
        scratch_shapes=[
            pltpu.VMEM(inputs.shape, jnp.bfloat16),
            pltpu.SemaphoreType.DMA((len(PIECES) - 1,)),
        ],
        compiler_params=pltpu.CompilerParams(vmem_limit_bytes=8 << 20),
    )(*map(in_vmem, (scaled, inputs, *sums)))


FAR, NEAR, SIDE = 4, 2, 1
LINE = (FAR | NEAR, NEAR, FAR)
EARLY = 2


def handed_over(block, sections, count, distance, mask):
    route = [
        ((s - distance) % sections * count + (i ^ mask), s * count + i)
        for s in range(sections)
        for i in range(count)
    ]
    return lax.ppermute(block, ("section", "tp"), route)


def gathered(pair, axis):
    if lax.axis_size(axis) != 8:
        return [lax.all_gather(pair[0], axis)], lambda place: place
    blocks = [pair] + [swapped(pair, axis, mask) for mask in LINE]
    masks = [far | side for far in (0, *LINE) for side in (0, SIDE)]

    def head_of(place):
        return lax.axis_index(axis) ^ masks[place]

    return blocks, head_of


def per_device(grad_attn, w_value, probs_own, probs_spare, evicted, layer_input, gain):
    sections, count = lax.axis_size("section"), lax.axis_size("tp")
    packed, spares, taken = pack(probs_own[0, 0], grad_attn[0, 0], probs_spare[0, 0], evicted)
    heads = []
    for mask in (0, SIDE) if count == 8 else (0,):
        spare = handed_over(spares, sections, count, sections // 2, mask)
        heads.append((swapped(packed, "tp", mask) if mask else packed, spare))
    weights, inputs = w_value[0], layer_input[0]
    next_input = passed_along(inputs, "section", -1)
    reach, own_reach = reach_of(weights, inputs, gain, heads[-1][0])
    if count == 8:
        reaches = [own_reach, swapped(reach, "tp", SIDE)]
        reaches[1], next_input = lax.optimization_barrier((reaches[1], next_input))
    else:
        reaches = [lax.psum(own_reach, "tp")]
    pair = value_gradients(taken, heads)
    blocks, head_of = gathered(pair, "tp")
    early = [project_early(head_of, blocks[:EARLY], weights)] if count == 8 else []
    scaled, sums = project(head_of, blocks, early, weights, inputs, gain, reaches)
    next_scaled = passed_along(scaled, "section", -1)
    next_sums = []
    for mask in (NEAR, FAR, FAR | NEAR) if count == 8 else ():
        next_sums.append(handed_over(sums, sections, count, -1, mask))
    return finish(next_scaled, next_input, next_sums)[None]


def solution(mesh):
    in_specs = (
        P("section", "tp", None, None),
        P("section", "tp", None),
        P("section", "tp", None, None),
        P("section", "tp", None, None),
        P("section", None),
        P("section", None, "tp"),
        P("section", "tp"),
    )
    out_specs = P("section", None, "tp")
    return jax.shard_map(
        per_device, mesh=mesh, in_specs=in_specs, out_specs=out_specs, check_vma=False
    )
```

```python
import functools

import jax
import jax.numpy as jnp
from jax import lax
from jax.experimental import pallas as pl
from jax.experimental.pallas import tpu as pltpu
from jax.sharding import PartitionSpec as P

D = 12288
LANES = 128
PIECES = (0, 3, 5, 7, 8)
EXTRA = 16
HIDES = pl.CostEstimate(flops=1 << 35, bytes_accessed=1 << 25, transcendentals=0)


def passed_along(block, axis, distance):
    devices = range(lax.axis_size(axis))
    route = [((i - distance) % len(devices), i) for i in devices]
    return lax.ppermute(block, axis, route)


def swapped(block, axis, mask):
    return lax.ppermute(block, axis, [(i ^ mask, i) for i in range(lax.axis_size(axis))])


def in_vmem(array):
    return pltpu.with_memory_space_constraint(array, pltpu.VMEM)


def in_hbm(array):
    return pltpu.with_memory_space_constraint(array, pltpu.HBM)


def vmem_specs(count):
    return [pl.BlockSpec(memory_space=pltpu.VMEM)] * count


def as_row(column):
    return jnp.broadcast_to(column, (column.shape[0], column.shape[0])).T[:1]


def standing(rows):
    tokens = rows.shape[1]
    return jnp.concatenate([rows, jnp.zeros((tokens - rows.shape[0], tokens), rows.dtype)]).T


def split(values):
    parts = []
    for _ in range(3):
        parts.append(values.astype(jnp.bfloat16).astype(jnp.float32))
        values = values - parts[-1]
    return parts


def own_ratio(squares, inner):
    return inner / jnp.maximum(squares, 1e-30)


def as_parts(row):
    rest = jnp.zeros((EXTRA - 3, row.shape[1]), jnp.float32)
    return jnp.concatenate(split(row) + [rest]).astype(jnp.bfloat16)


def pack_kernel(own_ref, grad_ref, spare_ref, evicted_ref, *refs):
    out_ref, spare_out, taken_ref, flags, sems = refs
    copies = [
        pltpu.make_async_copy(evicted_ref, flags, sems.at[0]),
        pltpu.make_async_copy(own_ref, out_ref.at[0], sems.at[1]),
        pltpu.make_async_copy(grad_ref, out_ref.at[1], sems.at[2]),
        pltpu.make_async_copy(spare_ref, spare_out, sems.at[3]),
    ]
    for copy in copies:
        copy.start()
    copies[0].wait()
    tiles = evicted_ref.shape[1]
    rows = taken_ref.shape[0] // tiles
    for tile in range(tiles):
        part = pl.ds(tile * rows, rows)
        taken = jnp.full((rows, taken_ref.shape[1]), flags[0, tile], jnp.int32)
        taken_ref[part, :] = taken.astype(jnp.float32).astype(taken_ref.dtype)
    for copy in copies[1:]:
        copy.wait()


def pack(own, grad, spare, evicted):
    return pl.pallas_call(
        pack_kernel,
        out_shape=(
            pltpu.VMEM((2, *own.shape), own.dtype),
            pltpu.VMEM(spare.shape, spare.dtype),
            pltpu.VMEM(own.shape, own.dtype),
        ),
        in_specs=[pl.BlockSpec(memory_space=pltpu.HBM)] * 4,
        out_specs=tuple(vmem_specs(3)),
        scratch_shapes=[
            pltpu.SMEM(evicted.shape, evicted.dtype),
            pltpu.SemaphoreType.DMA((4,)),
        ],
        cost_estimate=HIDES,
        compiler_params=pltpu.CompilerParams(vmem_limit_bytes=4 << 20),
    )(*map(in_hbm, (own, grad, spare, evicted)))


def reach_kernel(weight_ref, input_ref, gain_ref, first_ref, reach_ref, own_ref):
    del first_ref
    tokens, features = input_ref.shape
    values = input_ref[...].astype(jnp.float32)
    reach_ref[tokens:, :] = jnp.zeros_like(reach_ref[tokens:, :])
    squares = as_row(jnp.sum(values * values, axis=1, keepdims=True))
    reach_ref[tokens:, :tokens] = as_parts(squares)
    gained = (values * gain_ref[...]).astype(jnp.bfloat16)
    reach = jnp.dot(gained, weight_ref[...], preferred_element_type=jnp.float32)
    reach_ref[:tokens, :] = reach.astype(reach_ref.dtype)
    own_ref[:tokens, :] = reach
    own_ref[tokens:, :] = reach_ref[tokens:, :].astype(own_ref.dtype)


def reach_of(weights, inputs, gain, first):
    return pl.pallas_call(
        reach_kernel,
        out_shape=tuple(
            pltpu.VMEM((inputs.shape[0] + EXTRA, weights.shape[1]), dtype)
            for dtype in (jnp.bfloat16, jnp.float32)
        ),
        in_specs=vmem_specs(4),
        out_specs=tuple(vmem_specs(2)),
        cost_estimate=HIDES,
        compiler_params=pltpu.CompilerParams(vmem_limit_bytes=8 << 20),
    )(*map(in_vmem, (weights, inputs, gain, first)))


def mix_kernel(taken_ref, *refs):
    out_ref = refs[-1]
    taken = taken_ref[...]
    for j in range(out_ref.shape[0]):
        packed_ref, spare_ref = refs[len(refs) - 2 - j], refs[j]
        out_ref[j] = lax.dot_general(
            packed_ref[0] * (1 - taken) + spare_ref[...] * taken,
            packed_ref[1],
            (((0,), (0,)), ((), ())),
            preferred_element_type=jnp.float32,
        ).astype(out_ref.dtype)


def value_gradients(taken, heads):
    return pl.pallas_call(
        mix_kernel,
        out_shape=pltpu.VMEM((len(heads), *heads[0][1].shape), jnp.bfloat16),
        in_specs=vmem_specs(1 + 2 * len(heads)),
        out_specs=pl.BlockSpec(memory_space=pltpu.VMEM),
        cost_estimate=HIDES,
        compiler_params=pltpu.CompilerParams(vmem_limit_bytes=4 << 20),
    )(*map(in_vmem, (taken, *[spare for _, spare in heads], *[packed for packed, _ in heads[::-1]])))


def column_tile(features):
    return 256 if features % 256 == 0 else features


def fill(flat, blocks, head_of, first):
    groups = []
    for ref in blocks:
        count = ref.shape[0]
        for j in range(count):
            start = pl.multiple_of(head_of(first + j) * LANES, LANES)
            flat[:, pl.ds(start, LANES)] = ref[j]
        width = count * LANES
        groups.append((pl.multiple_of(head_of(first) // count * width, width), width))
        first += count
    return groups


def times_weights(flat, groups, weight_ref, part):
    products = [
        lax.dot_general(
            flat[:, pl.ds(start, width)],
            weight_ref[part, pl.ds(start, width)],
            (((1,), (1,)), ((), ())),
            preferred_element_type=jnp.float32,
        )
        for start, width in groups
    ]
    return sum(products[1:], products[0])


def early_kernel(head_of, *refs):
    *blocks, weight_ref, out_ref, flat = refs
    groups = fill(flat, blocks, head_of, 0)
    features = weight_ref.shape[0]
    tile = column_tile(features)
    for start in range(0, features, tile):
        part = pl.ds(start, tile)
        out_ref[:, part] = times_weights(flat, groups, weight_ref, part)


def project_early(head_of, blocks, weights):
    tokens = blocks[0].shape[1]
    return pl.pallas_call(
        functools.partial(early_kernel, head_of),
        out_shape=pltpu.VMEM((tokens, weights.shape[0]), jnp.float32),
        in_specs=vmem_specs(len(blocks) + 1),
        out_specs=pl.BlockSpec(memory_space=pltpu.VMEM),
        scratch_shapes=[pltpu.VMEM((tokens, weights.shape[1]), jnp.bfloat16)],
        cost_estimate=pl.CostEstimate(flops=1 << 16, bytes_accessed=1 << 12, transcendentals=0),
        compiler_params=pltpu.CompilerParams(vmem_limit_bytes=16 << 20),
    )(*map(in_vmem, (*blocks, weights)))


def project_kernel(head_of, sizes, *refs):
    blocks = refs[: sizes[0]]
    early_refs = refs[sizes[0] : sizes[0] + sizes[1]]
    rest = refs[sizes[0] + sizes[1] :]
    weight_ref, input_ref, gain_ref, *reach_refs, scaled_ref, sums_ref, flat = rest
    tokens, features = input_ref.shape
    groups = fill(flat, blocks, head_of, 0)
    if early_refs:
        groups = groups[EARLY:]
    reach = sum(ref[:tokens, :].astype(jnp.float32) for ref in reach_refs)
    squares = sum(ref[tokens:, :tokens].astype(jnp.float32) for ref in reach_refs)
    squares = jnp.sum(squares, axis=0, keepdims=True)
    inner = as_row(jnp.sum(flat[...].astype(jnp.float32) * reach, axis=1, keepdims=True))
    sums_ref[:1, :] = squares
    sums_ref[1:, :] = inner
    rho = own_ratio(squares, inner)
    rows = [*split(squares), *split(inner), rho, jnp.zeros((1, tokens), jnp.float32)]
    columns = standing(jnp.concatenate(rows))
    scaled_ref[:, features:] = columns.astype(scaled_ref.dtype)
    rho = columns[:, 6:7]
    tile = column_tile(features)
    for start in range(0, features, tile):
        part = pl.ds(start, tile)
        grad_normed = times_weights(flat, groups, weight_ref, part)
        for ref in early_refs:
            grad_normed = grad_normed + ref[:, part]
        values = input_ref[:, part].astype(jnp.float32)
        scaled_ref[:, part] = (grad_normed * gain_ref[:, part] - values * rho).astype(
            scaled_ref.dtype
        )


def project(head_of, blocks, early, weights, inputs, gain, reaches):
    tokens, features = inputs.shape
    operands = (*blocks, *early, weights, inputs, gain, *reaches)
    return pl.pallas_call(
        functools.partial(project_kernel, head_of, (len(blocks), len(early))),
        out_shape=(
            pltpu.VMEM((tokens, features + LANES), jnp.bfloat16),
            pltpu.VMEM((2, tokens), jnp.float32),
        ),
        in_specs=vmem_specs(len(operands)),
        out_specs=tuple(vmem_specs(2)),
        scratch_shapes=[pltpu.VMEM((tokens, weights.shape[1]), jnp.bfloat16)],
        cost_estimate=HIDES,
        compiler_params=pltpu.CompilerParams(vmem_limit_bytes=16 << 20),
    )(*map(in_vmem, operands))


def finish_kernel(scaled_ref, input_ref, *refs):
    *sums_refs, out_ref, held, sems = refs
    tokens, features = input_ref.shape
    extra = scaled_ref[:, features:].astype(jnp.float32).T
    squares = extra[0:1] + extra[1:2] + extra[2:3]
    inner = extra[3:4] + extra[4:5] + extra[5:6]
    rho = own_ratio(squares, inner)
    for ref in sums_refs:
        squares = squares + ref[:1, :]
        inner = inner + ref[1:, :]
    inv = 1.0 / jnp.sqrt(squares / D + 1e-05)
    factor = inner * (inv * inv * inv) / D - inv * rho
    rows = jnp.concatenate([inv, factor, jnp.zeros((6, tokens), jnp.float32)])
    columns = standing(rows)
    inv, factor = columns[:, 0:1], columns[:, 1:2]
    copies = []
    for j in range(len(PIECES) - 1):
        part = slice(PIECES[j] * tokens // 8, PIECES[j + 1] * tokens // 8)
        scaled = scaled_ref[part, :features].astype(jnp.float32)
        values = input_ref[part, :].astype(jnp.float32)
        held[part, :] = (scaled * inv[part] - values * factor[part]).astype(held.dtype)
        copies.append(pltpu.make_async_copy(held.at[part], out_ref.at[part], sems.at[j]))
        copies[-1].start()
    for copy in copies:
        copy.wait()


def finish(scaled, inputs, sums):
    return pl.pallas_call(
        finish_kernel,
        out_shape=pltpu.HBM(inputs.shape, jnp.bfloat16),
        in_specs=vmem_specs(2 + len(sums)),
        out_specs=pl.BlockSpec(memory_space=pltpu.HBM),
        scratch_shapes=[
            pltpu.VMEM(inputs.shape, jnp.bfloat16),
            pltpu.SemaphoreType.DMA((len(PIECES) - 1,)),
        ],
        compiler_params=pltpu.CompilerParams(vmem_limit_bytes=8 << 20),
    )(*map(in_vmem, (scaled, inputs, *sums)))


FAR, NEAR, SIDE = 4, 2, 1
LINE = (FAR, NEAR, FAR | NEAR)
EARLY = 2


def handed_over(block, sections, count, distance, mask):
    route = [
        ((s - distance) % sections * count + (i ^ mask), s * count + i)
        for s in range(sections)
        for i in range(count)
    ]
    return lax.ppermute(block, ("section", "tp"), route)


def gathered(pair, axis):
    if lax.axis_size(axis) != 8:
        return [lax.all_gather(pair[0], axis)], lambda place: place
    blocks = [pair] + [swapped(pair, axis, mask) for mask in LINE]
    masks = [far | side for far in (0, *LINE) for side in (0, SIDE)]

    def head_of(place):
        return lax.axis_index(axis) ^ masks[place]

    return blocks, head_of


def per_device(grad_attn, w_value, probs_own, probs_spare, evicted, layer_input, gain):
    sections, count = lax.axis_size("section"), lax.axis_size("tp")
    packed, spares, taken = pack(probs_own[0, 0], grad_attn[0, 0], probs_spare[0, 0], evicted)
    heads = []
    for mask in (0, SIDE) if count == 8 else (0,):
        spare = handed_over(spares, sections, count, sections // 2, mask)
        heads.append((swapped(packed, "tp", mask) if mask else packed, spare))
    weights, inputs = w_value[0], layer_input[0]
    next_input = passed_along(inputs, "section", -1)
    reach, own_reach = reach_of(weights, inputs, gain, heads[-1][0])
    if count == 8:
        reaches = [own_reach, swapped(reach, "tp", SIDE)]
        reaches[1], next_input = lax.optimization_barrier((reaches[1], next_input))
    else:
        reaches = [lax.psum(own_reach, "tp")]
    pair = value_gradients(taken, heads)
    blocks, head_of = gathered(pair, "tp")
    early = [project_early(head_of, blocks[:EARLY], weights)] if count == 8 else []
    scaled, sums = project(head_of, blocks, early, weights, inputs, gain, reaches)
    next_scaled = passed_along(scaled, "section", -1)
    next_sums = []
    for mask in (NEAR, FAR, FAR | NEAR) if count == 8 else ():
        next_sums.append(handed_over(sums, sections, count, -1, mask))
    return finish(next_scaled, next_input, next_sums)[None]


def solution(mesh):
    in_specs = (
        P("section", "tp", None, None),
        P("section", "tp", None),
        P("section", "tp", None, None),
        P("section", "tp", None, None),
        P("section", None),
        P("section", None, "tp"),
        P("section", "tp"),
    )
    out_specs = P("section", None, "tp")
    return jax.shard_map(
        per_device, mesh=mesh, in_specs=in_specs, out_specs=out_specs, check_vma=False
    )
```

```python
import functools

import jax
import jax.numpy as jnp
from jax import lax
from jax.experimental import pallas as pl
from jax.experimental.pallas import tpu as pltpu
from jax.sharding import PartitionSpec as P

D = 12288
LANES = 128
PIECES = (0, 3, 5, 7, 8)
EXTRA = 16
SHORT = pl.CostEstimate(flops=1 << 16, bytes_accessed=1 << 12, transcendentals=0)
HALF = pl.CostEstimate(flops=1 << 31, bytes_accessed=1 << 16, transcendentals=0)
HIDES = pl.CostEstimate(flops=1 << 35, bytes_accessed=1 << 25, transcendentals=0)


def passed_along(block, axis, distance):
    devices = range(lax.axis_size(axis))
    route = [((i - distance) % len(devices), i) for i in devices]
    return lax.ppermute(block, axis, route)


def swapped(block, axis, mask):
    return lax.ppermute(block, axis, [(i ^ mask, i) for i in range(lax.axis_size(axis))])


def in_vmem(array):
    return pltpu.with_memory_space_constraint(array, pltpu.VMEM)


def in_hbm(array):
    return pltpu.with_memory_space_constraint(array, pltpu.HBM)


def vmem_specs(count):
    return [pl.BlockSpec(memory_space=pltpu.VMEM)] * count


def as_row(column):
    return jnp.broadcast_to(column, (column.shape[0], column.shape[0])).T[:1]


def standing(rows):
    tokens = rows.shape[1]
    return jnp.concatenate([rows, jnp.zeros((tokens - rows.shape[0], tokens), rows.dtype)]).T


def split(values):
    parts = []
    for _ in range(3):
        parts.append(values.astype(jnp.bfloat16).astype(jnp.float32))
        values = values - parts[-1]
    return parts


def own_ratio(squares, inner):
    return inner / jnp.maximum(squares, 1e-30)


def as_parts(row):
    rest = jnp.zeros((EXTRA - 3, row.shape[1]), jnp.float32)
    return jnp.concatenate(split(row) + [rest]).astype(jnp.bfloat16)


def pack_kernel(own_ref, grad_ref, spare_ref, evicted_ref, *refs):
    out_ref, spare_out, taken_ref, flags, sems = refs
    copies = [
        pltpu.make_async_copy(evicted_ref, flags, sems.at[0]),
        pltpu.make_async_copy(own_ref, out_ref.at[0], sems.at[1]),
        pltpu.make_async_copy(grad_ref, out_ref.at[1], sems.at[2]),
        pltpu.make_async_copy(spare_ref, spare_out, sems.at[3]),
    ]
    for copy in copies:
        copy.start()
    copies[0].wait()
    tiles = evicted_ref.shape[1]
    rows = taken_ref.shape[0] // tiles
    for tile in range(tiles):
        part = pl.ds(tile * rows, rows)
        taken = jnp.full((rows, taken_ref.shape[1]), flags[0, tile], jnp.int32)
        taken_ref[part, :] = taken.astype(jnp.float32).astype(taken_ref.dtype)
    for copy in copies[1:]:
        copy.wait()


def pack(own, grad, spare, evicted):
    return pl.pallas_call(
        pack_kernel,
        out_shape=(
            pltpu.VMEM((2, *own.shape), own.dtype),
            pltpu.VMEM(spare.shape, spare.dtype),
            pltpu.VMEM(own.shape, own.dtype),
        ),
        in_specs=[pl.BlockSpec(memory_space=pltpu.HBM)] * 4,
        out_specs=tuple(vmem_specs(3)),
        scratch_shapes=[
            pltpu.SMEM(evicted.shape, evicted.dtype),
            pltpu.SemaphoreType.DMA((4,)),
        ],
        cost_estimate=HIDES,
        compiler_params=pltpu.CompilerParams(vmem_limit_bytes=4 << 20),
    )(*map(in_hbm, (own, grad, spare, evicted)))


def reach_kernel(weight_ref, input_ref, gain_ref, reach_ref, own_ref):
    tokens, features = input_ref.shape
    values = input_ref[...].astype(jnp.float32)
    reach_ref[tokens:, :] = jnp.zeros_like(reach_ref[tokens:, :])
    squares = as_row(jnp.sum(values * values, axis=1, keepdims=True))
    reach_ref[tokens:, :tokens] = as_parts(squares)
    gained = (values * gain_ref[...]).astype(jnp.bfloat16)
    reach = jnp.dot(gained, weight_ref[...], preferred_element_type=jnp.float32)
    reach_ref[:tokens, :] = reach.astype(reach_ref.dtype)
    own_ref[:tokens, :] = reach
    own_ref[tokens:, :] = reach_ref[tokens:, :].astype(own_ref.dtype)


def reach_of(weights, inputs, gain, first):
    return pl.pallas_call(
        reach_kernel,
        out_shape=tuple(
            pltpu.VMEM((inputs.shape[0] + EXTRA, weights.shape[1]), dtype)
            for dtype in (jnp.bfloat16, jnp.float32)
        ),
        in_specs=vmem_specs(3),
        out_specs=tuple(vmem_specs(2)),
        cost_estimate=SHORT,
        compiler_params=pltpu.CompilerParams(vmem_limit_bytes=8 << 20),
    )(*map(in_vmem, (weights, inputs, gain)))


def mix_kernel(taken_ref, *refs):
    out_ref = refs[-1]
    taken = taken_ref[...]
    for j in range(out_ref.shape[0]):
        packed_ref, spare_ref = refs[len(refs) - 2 - j], refs[j]
        out_ref[j] = lax.dot_general(
            packed_ref[0] * (1 - taken) + spare_ref[...] * taken,
            packed_ref[1],
            (((0,), (0,)), ((), ())),
            preferred_element_type=jnp.float32,
        ).astype(out_ref.dtype)


def value_gradients(taken, heads):
    return pl.pallas_call(
        mix_kernel,
        out_shape=pltpu.VMEM((len(heads), *heads[0][1].shape), jnp.bfloat16),
        in_specs=vmem_specs(1 + 2 * len(heads)),
        out_specs=pl.BlockSpec(memory_space=pltpu.VMEM),
        cost_estimate=HALF,
        compiler_params=pltpu.CompilerParams(vmem_limit_bytes=4 << 20),
    )(*map(in_vmem, (taken, *[spare for _, spare in heads], *[packed for packed, _ in heads[::-1]])))


def column_tile(features):
    return 256 if features % 256 == 0 else features


def fill(flat, blocks, head_of, first):
    groups = []
    for ref in blocks:
        count = ref.shape[0]
        for j in range(count):
            start = pl.multiple_of(head_of(first + j) * LANES, LANES)
            flat[:, pl.ds(start, LANES)] = ref[j]
        width = count * LANES
        groups.append((pl.multiple_of(head_of(first) // count * width, width), width))
        first += count
    return groups


def times_weights(flat, groups, weight_ref, part):
    products = [
        lax.dot_general(
            flat[:, pl.ds(start, width)],
            weight_ref[part, pl.ds(start, width)],
            (((1,), (1,)), ((), ())),
            preferred_element_type=jnp.float32,
        )
        for start, width in groups
    ]
    return sum(products[1:], products[0])


def early_kernel(head_of, *refs):
    *blocks, weight_ref, out_ref, flat = refs
    groups = fill(flat, blocks, head_of, 0)
    features = weight_ref.shape[0]
    tile = column_tile(features)
    for start in range(0, features, tile):
        part = pl.ds(start, tile)
        out_ref[:, part] = times_weights(flat, groups, weight_ref, part)


def project_early(head_of, blocks, weights):
    tokens = blocks[0].shape[1]
    return pl.pallas_call(
        functools.partial(early_kernel, head_of),
        out_shape=pltpu.VMEM((tokens, weights.shape[0]), jnp.float32),
        in_specs=vmem_specs(len(blocks) + 1),
        out_specs=pl.BlockSpec(memory_space=pltpu.VMEM),
        scratch_shapes=[pltpu.VMEM((tokens, weights.shape[1]), jnp.bfloat16)],
        cost_estimate=SHORT,
        compiler_params=pltpu.CompilerParams(vmem_limit_bytes=16 << 20),
    )(*map(in_vmem, (*blocks, weights)))


def project_kernel(head_of, sizes, *refs):
    blocks = refs[: sizes[0]]
    early_refs = refs[sizes[0] : sizes[0] + sizes[1]]
    rest = refs[sizes[0] + sizes[1] :]
    weight_ref, input_ref, gain_ref, *reach_refs, scaled_ref, sums_ref, flat = rest
    tokens, features = input_ref.shape
    groups = fill(flat, blocks, head_of, 0)
    if early_refs:
        groups = groups[EARLY:]
    reach = sum(ref[:tokens, :].astype(jnp.float32) for ref in reach_refs)
    squares = sum(ref[tokens:, :tokens].astype(jnp.float32) for ref in reach_refs)
    squares = jnp.sum(squares, axis=0, keepdims=True)
    inner = as_row(jnp.sum(flat[...].astype(jnp.float32) * reach, axis=1, keepdims=True))
    sums_ref[:1, :] = squares
    sums_ref[1:, :] = inner
    rho = own_ratio(squares, inner)
    rows = [*split(squares), *split(inner), rho, jnp.zeros((1, tokens), jnp.float32)]
    columns = standing(jnp.concatenate(rows))
    scaled_ref[:, features:] = columns.astype(scaled_ref.dtype)
    rho = columns[:, 6:7]
    tile = column_tile(features)
    for start in range(0, features, tile):
        part = pl.ds(start, tile)
        grad_normed = times_weights(flat, groups, weight_ref, part)
        for ref in early_refs:
            grad_normed = grad_normed + ref[:, part]
        values = input_ref[:, part].astype(jnp.float32)
        scaled_ref[:, part] = (grad_normed * gain_ref[:, part] - values * rho).astype(
            scaled_ref.dtype
        )


def project(head_of, blocks, early, weights, inputs, gain, reaches):
    tokens, features = inputs.shape
    operands = (*blocks, *early, weights, inputs, gain, *reaches)
    return pl.pallas_call(
        functools.partial(project_kernel, head_of, (len(blocks), len(early))),
        out_shape=(
            pltpu.VMEM((tokens, features + LANES), jnp.bfloat16),
            pltpu.VMEM((2, tokens), jnp.float32),
        ),
        in_specs=vmem_specs(len(operands)),
        out_specs=tuple(vmem_specs(2)),
        scratch_shapes=[pltpu.VMEM((tokens, weights.shape[1]), jnp.bfloat16)],
        cost_estimate=HIDES,
        compiler_params=pltpu.CompilerParams(vmem_limit_bytes=16 << 20),
    )(*map(in_vmem, operands))


def finish_kernel(scaled_ref, input_ref, *refs):
    *sums_refs, out_ref, held, sems = refs
    tokens, features = input_ref.shape
    extra = scaled_ref[:, features:].astype(jnp.float32).T
    squares = extra[0:1] + extra[1:2] + extra[2:3]
    inner = extra[3:4] + extra[4:5] + extra[5:6]
    rho = own_ratio(squares, inner)
    for ref in sums_refs:
        squares = squares + ref[:1, :]
        inner = inner + ref[1:, :]
    inv = 1.0 / jnp.sqrt(squares / D + 1e-05)
    factor = inner * (inv * inv * inv) / D - inv * rho
    rows = jnp.concatenate([inv, factor, jnp.zeros((6, tokens), jnp.float32)])
    columns = standing(rows)
    inv, factor = columns[:, 0:1], columns[:, 1:2]
    copies = []
    for j in range(len(PIECES) - 1):
        part = slice(PIECES[j] * tokens // 8, PIECES[j + 1] * tokens // 8)
        scaled = scaled_ref[part, :features].astype(jnp.float32)
        values = input_ref[part, :].astype(jnp.float32)
        held[part, :] = (scaled * inv[part] - values * factor[part]).astype(held.dtype)
        copies.append(pltpu.make_async_copy(held.at[part], out_ref.at[part], sems.at[j]))
        copies[-1].start()
    for copy in copies:
        copy.wait()


def finish(scaled, inputs, sums):
    return pl.pallas_call(
        finish_kernel,
        out_shape=pltpu.HBM(inputs.shape, jnp.bfloat16),
        in_specs=vmem_specs(2 + len(sums)),
        out_specs=pl.BlockSpec(memory_space=pltpu.HBM),
        scratch_shapes=[
            pltpu.VMEM(inputs.shape, jnp.bfloat16),
            pltpu.SemaphoreType.DMA((len(PIECES) - 1,)),
        ],
        compiler_params=pltpu.CompilerParams(vmem_limit_bytes=8 << 20),
    )(*map(in_vmem, (scaled, inputs, *sums)))


FAR, NEAR, SIDE = 4, 2, 1
LINE = (FAR | NEAR, NEAR, FAR)
EARLY = 2


def handed_over(block, sections, count, distance, mask):
    route = [
        ((s - distance) % sections * count + (i ^ mask), s * count + i)
        for s in range(sections)
        for i in range(count)
    ]
    return lax.ppermute(block, ("section", "tp"), route)


def gathered(pair, axis):
    if lax.axis_size(axis) != 8:
        return [lax.all_gather(pair[0], axis)], lambda place: place
    blocks = [pair] + [swapped(pair, axis, mask) for mask in LINE]
    masks = [far | side for far in (0, *LINE) for side in (0, SIDE)]

    def head_of(place):
        return lax.axis_index(axis) ^ masks[place]

    return blocks, head_of


def per_device(grad_attn, w_value, probs_own, probs_spare, evicted, layer_input, gain):
    sections, count = lax.axis_size("section"), lax.axis_size("tp")
    packed, spares, taken = pack(probs_own[0, 0], grad_attn[0, 0], probs_spare[0, 0], evicted)
    heads = []
    for mask in (0, SIDE) if count == 8 else (0,):
        spare = handed_over(spares, sections, count, sections // 2, mask)
        heads.append((swapped(packed, "tp", mask) if mask else packed, spare))
    weights, inputs = w_value[0], layer_input[0]
    next_input = passed_along(inputs, "section", -1)
    reach, own_reach = reach_of(weights, inputs, gain, heads[-1][0])
    if count == 8:
        reach, swap = lax.optimization_barrier((reach, heads[1][0]))
        heads[1] = (swap, heads[1][1])
        reaches = [own_reach, swapped(reach, "tp", SIDE)]
        reaches[1], next_input = lax.optimization_barrier((reaches[1], next_input))
    else:
        reaches = [lax.psum(own_reach, "tp")]
    pair = value_gradients(taken, heads)
    blocks, head_of = gathered(pair, "tp")
    early = [project_early(head_of, blocks[:EARLY], weights)] if count == 8 else []
    scaled, sums = project(head_of, blocks, early, weights, inputs, gain, reaches)
    next_scaled = passed_along(scaled, "section", -1)
    next_sums = []
    for mask in (NEAR, FAR, FAR | NEAR) if count == 8 else ():
        next_sums.append(handed_over(sums, sections, count, -1, mask))
    return finish(next_scaled, next_input, next_sums)[None]


def solution(mesh):
    in_specs = (
        P("section", "tp", None, None),
        P("section", "tp", None),
        P("section", "tp", None, None),
        P("section", "tp", None, None),
        P("section", None),
        P("section", None, "tp"),
        P("section", "tp"),
    )
    out_specs = P("section", None, "tp")
    return jax.shard_map(
        per_device, mesh=mesh, in_specs=in_specs, out_specs=out_specs, check_vma=False
    )
```

```python
import functools

import jax
import jax.numpy as jnp
from jax import lax
from jax.experimental import pallas as pl
from jax.experimental.pallas import tpu as pltpu
from jax.sharding import PartitionSpec as P

D = 12288
LANES = 128
PIECES = (0, 3, 5, 7, 8)
EXTRA = 16
HIDES = pl.CostEstimate(flops=1 << 35, bytes_accessed=1 << 25, transcendentals=0)


def passed_along(block, axis, distance):
    devices = range(lax.axis_size(axis))
    route = [((i - distance) % len(devices), i) for i in devices]
    return lax.ppermute(block, axis, route)


def swapped(block, axis, mask):
    return lax.ppermute(block, axis, [(i ^ mask, i) for i in range(lax.axis_size(axis))])


def in_vmem(array):
    return pltpu.with_memory_space_constraint(array, pltpu.VMEM)


def in_hbm(array):
    return pltpu.with_memory_space_constraint(array, pltpu.HBM)


def vmem_specs(count):
    return [pl.BlockSpec(memory_space=pltpu.VMEM)] * count


def as_row(column):
    return jnp.broadcast_to(column, (column.shape[0], column.shape[0])).T[:1]


def standing(rows):
    tokens = rows.shape[1]
    return jnp.concatenate([rows, jnp.zeros((tokens - rows.shape[0], tokens), rows.dtype)]).T


def split(values):
    parts = []
    for _ in range(3):
        parts.append(values.astype(jnp.bfloat16).astype(jnp.float32))
        values = values - parts[-1]
    return parts


def own_ratio(squares, inner):
    return inner / jnp.maximum(squares, 1e-30)


def as_parts(row):
    rest = jnp.zeros((EXTRA - 3, row.shape[1]), jnp.float32)
    return jnp.concatenate(split(row) + [rest]).astype(jnp.bfloat16)


def pack_kernel(own_ref, grad_ref, spare_ref, evicted_ref, *refs):
    out_ref, spare_out, taken_ref, flags, sems = refs
    copies = [
        pltpu.make_async_copy(evicted_ref, flags, sems.at[0]),
        pltpu.make_async_copy(own_ref, out_ref.at[0], sems.at[1]),
        pltpu.make_async_copy(grad_ref, out_ref.at[1], sems.at[2]),
        pltpu.make_async_copy(spare_ref, spare_out, sems.at[3]),
    ]
    for copy in copies:
        copy.start()
    copies[0].wait()
    tiles = evicted_ref.shape[1]
    rows = taken_ref.shape[0] // tiles
    for tile in range(tiles):
        part = pl.ds(tile * rows, rows)
        taken = jnp.full((rows, taken_ref.shape[1]), flags[0, tile], jnp.int32)
        taken_ref[part, :] = taken.astype(jnp.float32).astype(taken_ref.dtype)
    for copy in copies[1:]:
        copy.wait()


def pack(own, grad, spare, evicted):
    return pl.pallas_call(
        pack_kernel,
        out_shape=(
            pltpu.VMEM((2, *own.shape), own.dtype),
            pltpu.VMEM(spare.shape, spare.dtype),
            pltpu.VMEM(own.shape, own.dtype),
        ),
        in_specs=[pl.BlockSpec(memory_space=pltpu.HBM)] * 4,
        out_specs=tuple(vmem_specs(3)),
        scratch_shapes=[
            pltpu.SMEM(evicted.shape, evicted.dtype),
            pltpu.SemaphoreType.DMA((4,)),
        ],
        cost_estimate=HIDES,
        compiler_params=pltpu.CompilerParams(vmem_limit_bytes=4 << 20),
    )(*map(in_hbm, (own, grad, spare, evicted)))


def reach_kernel(weight_ref, input_ref, gain_ref, first_ref, reach_ref, own_ref):
    del first_ref
    tokens, features = input_ref.shape
    values = input_ref[...].astype(jnp.float32)
    reach_ref[tokens:, :] = jnp.zeros_like(reach_ref[tokens:, :])
    squares = as_row(jnp.sum(values * values, axis=1, keepdims=True))
    reach_ref[tokens:, :tokens] = as_parts(squares)
    gained = (values * gain_ref[...]).astype(jnp.bfloat16)
    reach = jnp.dot(gained, weight_ref[...], preferred_element_type=jnp.float32)
    reach_ref[:tokens, :] = reach.astype(reach_ref.dtype)
    own_ref[:tokens, :] = reach
    own_ref[tokens:, :] = reach_ref[tokens:, :].astype(own_ref.dtype)


def reach_of(weights, inputs, gain, first):
    return pl.pallas_call(
        reach_kernel,
        out_shape=tuple(
            pltpu.VMEM((inputs.shape[0] + EXTRA, weights.shape[1]), dtype)
            for dtype in (jnp.bfloat16, jnp.float32)
        ),
        in_specs=vmem_specs(4),
        out_specs=tuple(vmem_specs(2)),
        cost_estimate=HIDES,
        compiler_params=pltpu.CompilerParams(vmem_limit_bytes=8 << 20),
    )(*map(in_vmem, (weights, inputs, gain, first)))


def mix_kernel(taken_ref, *refs):
    out_ref = refs[-1]
    taken = taken_ref[...]
    for j in range(out_ref.shape[0]):
        packed_ref, spare_ref = refs[len(refs) - 2 - j], refs[j]
        out_ref[j] = lax.dot_general(
            packed_ref[0] * (1 - taken) + spare_ref[...] * taken,
            packed_ref[1],
            (((0,), (0,)), ((), ())),
            preferred_element_type=jnp.float32,
        ).astype(out_ref.dtype)


def value_gradients(taken, heads):
    return pl.pallas_call(
        mix_kernel,
        out_shape=pltpu.VMEM((len(heads), *heads[0][1].shape), jnp.bfloat16),
        in_specs=vmem_specs(1 + 2 * len(heads)),
        out_specs=pl.BlockSpec(memory_space=pltpu.VMEM),
        cost_estimate=HIDES,
        compiler_params=pltpu.CompilerParams(vmem_limit_bytes=4 << 20),
    )(*map(in_vmem, (taken, *[spare for _, spare in heads], *[packed for packed, _ in heads[::-1]])))


def column_tile(features):
    return 256 if features % 256 == 0 else features


def fill(flat, blocks, head_of, first):
    groups = []
    for ref in blocks:
        count = ref.shape[0]
        for j in range(count):
            start = pl.multiple_of(head_of(first + j) * LANES, LANES)
            flat[:, pl.ds(start, LANES)] = ref[j]
        width = count * LANES
        groups.append((pl.multiple_of(head_of(first) // count * width, width), width))
        first += count
    return groups


def times_weights(flat, groups, weight_ref, part):
    products = [
        lax.dot_general(
            flat[:, pl.ds(start, width)],
            weight_ref[part, pl.ds(start, width)],
            (((1,), (1,)), ((), ())),
            preferred_element_type=jnp.float32,
        )
        for start, width in groups
    ]
    return sum(products[1:], products[0])


def early_kernel(head_of, *refs):
    *blocks, weight_ref, out_ref, flat = refs
    groups = fill(flat, blocks, head_of, 0)
    features = weight_ref.shape[0]
    tile = column_tile(features)
    for start in range(0, features, tile):
        part = pl.ds(start, tile)
        out_ref[:, part] = times_weights(flat, groups, weight_ref, part)


def project_early(head_of, blocks, weights):
    tokens = blocks[0].shape[1]
    return pl.pallas_call(
        functools.partial(early_kernel, head_of),
        out_shape=pltpu.VMEM((tokens, weights.shape[0]), jnp.float32),
        in_specs=vmem_specs(len(blocks) + 1),
        out_specs=pl.BlockSpec(memory_space=pltpu.VMEM),
        scratch_shapes=[pltpu.VMEM((tokens, weights.shape[1]), jnp.bfloat16)],
        cost_estimate=pl.CostEstimate(flops=1 << 16, bytes_accessed=1 << 12, transcendentals=0),
        compiler_params=pltpu.CompilerParams(vmem_limit_bytes=16 << 20),
    )(*map(in_vmem, (*blocks, weights)))


def inner_part(head_of, blocks, first, reach_ref):
    total = None
    for ref in blocks:
        for j in range(ref.shape[0]):
            start = pl.multiple_of(head_of(first) * LANES, LANES)
            part = ref[j].astype(jnp.float32) * reach_ref[:, pl.ds(start, LANES)]
            total = part if total is None else total + part
            first += 1
    return total


def join_kernel(head_of, sizes, *refs):
    blocks, reach_refs = refs[: sizes[0]], refs[sizes[0] : sizes[0] + sizes[1]]
    reach_ref, folded_ref, squares_ref = refs[sizes[0] + sizes[1] :]
    tokens = reach_ref.shape[0]
    reach_ref[...] = sum(ref[:tokens, :].astype(jnp.float32) for ref in reach_refs)
    squares = sum(ref[tokens:, :tokens].astype(jnp.float32) for ref in reach_refs)
    squares_ref[...] = jnp.sum(squares, axis=0, keepdims=True)
    if blocks:
        folded_ref[...] = inner_part(head_of, blocks, 0, reach_ref)
    else:
        folded_ref[...] = jnp.zeros_like(folded_ref)


def join(head_of, blocks, reaches):
    tokens, columns = reaches[0].shape[0] - EXTRA, reaches[0].shape[1]
    operands = (*blocks, *reaches)
    return pl.pallas_call(
        functools.partial(join_kernel, head_of, (len(blocks), len(reaches))),
        out_shape=(
            pltpu.VMEM((tokens, columns), jnp.float32),
            pltpu.VMEM((tokens, LANES), jnp.float32),
            pltpu.VMEM((1, tokens), jnp.float32),
        ),
        in_specs=vmem_specs(len(operands)),
        out_specs=tuple(vmem_specs(3)),
        cost_estimate=pl.CostEstimate(flops=1 << 16, bytes_accessed=1 << 12, transcendentals=0),
        compiler_params=pltpu.CompilerParams(vmem_limit_bytes=8 << 20),
    )(*map(in_vmem, operands))


def project_kernel(head_of, first, count, *refs):
    blocks, rest = refs[:count], refs[count:]
    reach_ref, folded_ref, squares_ref, weight_ref, input_ref, gain_ref, *rest = rest
    *early_refs, scaled_ref, sums_ref, flat = rest
    tokens, features = input_ref.shape
    groups = fill(flat, blocks, head_of, first)
    squares = squares_ref[...]
    folded = folded_ref[...] + inner_part(head_of, blocks, first, reach_ref)
    inner = as_row(jnp.sum(folded, axis=1, keepdims=True))
    sums_ref[:1, :] = squares
    sums_ref[1:, :] = inner
    rho = own_ratio(squares, inner)
    rows = [*split(squares), *split(inner), rho, jnp.zeros((1, tokens), jnp.float32)]
    columns = standing(jnp.concatenate(rows))
    scaled_ref[:, features:] = columns.astype(scaled_ref.dtype)
    rho = columns[:, 6:7]
    tile = column_tile(features)
    for start in range(0, features, tile):
        part = pl.ds(start, tile)
        grad_normed = times_weights(flat, groups, weight_ref, part)
        for ref in early_refs:
            grad_normed = grad_normed + ref[:, part]
        values = input_ref[:, part].astype(jnp.float32)
        scaled_ref[:, part] = (grad_normed * gain_ref[:, part] - values * rho).astype(
            scaled_ref.dtype
        )


def project(head_of, first, blocks, joined, weights, inputs, gain, early):
    tokens, features = inputs.shape
    operands = (*blocks, *joined, weights, inputs, gain, *early)
    return pl.pallas_call(
        functools.partial(project_kernel, head_of, first, len(blocks)),
        out_shape=(
            pltpu.VMEM((tokens, features + LANES), jnp.bfloat16),
            pltpu.VMEM((2, tokens), jnp.float32),
        ),
        in_specs=vmem_specs(len(operands)),
        out_specs=tuple(vmem_specs(2)),
        scratch_shapes=[pltpu.VMEM((tokens, weights.shape[1]), jnp.bfloat16)],
        cost_estimate=HIDES,
        compiler_params=pltpu.CompilerParams(vmem_limit_bytes=16 << 20),
    )(*map(in_vmem, operands))


def finish_kernel(scaled_ref, input_ref, *refs):
    *sums_refs, out_ref, held, sems = refs
    tokens, features = input_ref.shape
    extra = scaled_ref[:, features:].astype(jnp.float32).T
    squares = extra[0:1] + extra[1:2] + extra[2:3]
    inner = extra[3:4] + extra[4:5] + extra[5:6]
    rho = own_ratio(squares, inner)
    for ref in sums_refs:
        squares = squares + ref[:1, :]
        inner = inner + ref[1:, :]
    inv = 1.0 / jnp.sqrt(squares / D + 1e-05)
    factor = inner * (inv * inv * inv) / D - inv * rho
    rows = jnp.concatenate([inv, factor, jnp.zeros((6, tokens), jnp.float32)])
    columns = standing(rows)
    inv, factor = columns[:, 0:1], columns[:, 1:2]
    copies = []
    for j in range(len(PIECES) - 1):
        part = slice(PIECES[j] * tokens // 8, PIECES[j + 1] * tokens // 8)
        scaled = scaled_ref[part, :features].astype(jnp.float32)
        values = input_ref[part, :].astype(jnp.float32)
        held[part, :] = (scaled * inv[part] - values * factor[part]).astype(held.dtype)
        copies.append(pltpu.make_async_copy(held.at[part], out_ref.at[part], sems.at[j]))
        copies[-1].start()
    for copy in copies:
        copy.wait()


def finish(scaled, inputs, sums):
    return pl.pallas_call(
        finish_kernel,
        out_shape=pltpu.HBM(inputs.shape, jnp.bfloat16),
        in_specs=vmem_specs(2 + len(sums)),
        out_specs=pl.BlockSpec(memory_space=pltpu.HBM),
        scratch_shapes=[
            pltpu.VMEM(inputs.shape, jnp.bfloat16),
            pltpu.SemaphoreType.DMA((len(PIECES) - 1,)),
        ],
        compiler_params=pltpu.CompilerParams(vmem_limit_bytes=8 << 20),
    )(*map(in_vmem, (scaled, inputs, *sums)))


FAR, NEAR, SIDE = 4, 2, 1
LINE = (FAR | NEAR, FAR, NEAR)
EARLY = 2


def handed_over(block, sections, count, distance, mask):
    route = [
        ((s - distance) % sections * count + (i ^ mask), s * count + i)
        for s in range(sections)
        for i in range(count)
    ]
    return lax.ppermute(block, ("section", "tp"), route)


def gathered(pair, axis):
    if lax.axis_size(axis) != 8:
        return [lax.all_gather(pair[0], axis)], lambda place: place
    blocks = [pair] + [swapped(pair, axis, mask) for mask in LINE]
    masks = [far | side for far in (0, *LINE) for side in (0, SIDE)]

    def head_of(place):
        return lax.axis_index(axis) ^ masks[place]

    return blocks, head_of


def per_device(grad_attn, w_value, probs_own, probs_spare, evicted, layer_input, gain):
    sections, count = lax.axis_size("section"), lax.axis_size("tp")
    packed, spares, taken = pack(probs_own[0, 0], grad_attn[0, 0], probs_spare[0, 0], evicted)
    heads = []
    for mask in (0, SIDE) if count == 8 else (0,):
        spare = handed_over(spares, sections, count, sections // 2, mask)
        heads.append((swapped(packed, "tp", mask) if mask else packed, spare))
    weights, inputs = w_value[0], layer_input[0]
    next_input = passed_along(inputs, "section", -1)
    reach, own_reach = reach_of(weights, inputs, gain, heads[-1][0])
    if count == 8:
        reaches = [own_reach, swapped(reach, "tp", SIDE)]
        reaches[1], next_input = lax.optimization_barrier((reaches[1], next_input))
    else:
        reaches = [lax.psum(own_reach, "tp")]
    pair = value_gradients(taken, heads)
    blocks, head_of = gathered(pair, "tp")
    soon, late = (blocks[:EARLY], blocks[EARLY:]) if count == 8 else ([], blocks)
    early = [project_early(head_of, soon, weights)] if soon else []
    joined = join(head_of, soon, reaches)
    first = sum(block.shape[0] for block in soon)
    scaled, sums = project(head_of, first, late, joined, weights, inputs, gain, early)
    next_scaled = passed_along(scaled, "section", -1)
    next_sums = []
    for mask in (NEAR, FAR | NEAR, FAR) if count == 8 else ():
        next_sums.append(handed_over(sums, sections, count, -1, mask))
    return finish(next_scaled, next_input, next_sums)[None]


def solution(mesh):
    in_specs = (
        P("section", "tp", None, None),
        P("section", "tp", None),
        P("section", "tp", None, None),
        P("section", "tp", None, None),
        P("section", None),
        P("section", None, "tp"),
        P("section", "tp"),
    )
    out_specs = P("section", None, "tp")
    return jax.shard_map(
        per_device, mesh=mesh, in_specs=in_specs, out_specs=out_specs, check_vma=False
    )
```

```python
import functools

import jax
import jax.numpy as jnp
from jax import lax
from jax.experimental import pallas as pl
from jax.experimental.pallas import tpu as pltpu
from jax.sharding import PartitionSpec as P

D = 12288
LANES = 128
PIECES = (0, 3, 5, 7, 8)
EXTRA = 16
HIDES = pl.CostEstimate(flops=1 << 35, bytes_accessed=1 << 25, transcendentals=0)


def passed_along(block, axis, distance):
    devices = range(lax.axis_size(axis))
    route = [((i - distance) % len(devices), i) for i in devices]
    return lax.ppermute(block, axis, route)


def swapped(block, axis, mask):
    return lax.ppermute(block, axis, [(i ^ mask, i) for i in range(lax.axis_size(axis))])


def in_vmem(array):
    return pltpu.with_memory_space_constraint(array, pltpu.VMEM)


def in_hbm(array):
    return pltpu.with_memory_space_constraint(array, pltpu.HBM)


def vmem_specs(count):
    return [pl.BlockSpec(memory_space=pltpu.VMEM)] * count


def as_row(column):
    return jnp.broadcast_to(column, (column.shape[0], column.shape[0])).T[:1]


def standing(rows):
    tokens = rows.shape[1]
    return jnp.concatenate([rows, jnp.zeros((tokens - rows.shape[0], tokens), rows.dtype)]).T


def split(values):
    parts = []
    for _ in range(3):
        parts.append(values.astype(jnp.bfloat16).astype(jnp.float32))
        values = values - parts[-1]
    return parts


def own_ratio(squares, inner):
    return inner / jnp.maximum(squares, 1e-30)


def as_parts(row):
    rest = jnp.zeros((EXTRA - 3, row.shape[1]), jnp.float32)
    return jnp.concatenate(split(row) + [rest]).astype(jnp.bfloat16)


def pack_kernel(own_ref, grad_ref, spare_ref, evicted_ref, *refs):
    out_ref, spare_out, taken_ref, flags, sems = refs
    copies = [
        pltpu.make_async_copy(evicted_ref, flags, sems.at[0]),
        pltpu.make_async_copy(own_ref, out_ref.at[0], sems.at[1]),
        pltpu.make_async_copy(grad_ref, out_ref.at[1], sems.at[2]),
        pltpu.make_async_copy(spare_ref, spare_out, sems.at[3]),
    ]
    for copy in copies:
        copy.start()
    copies[0].wait()
    tiles = evicted_ref.shape[1]
    rows = taken_ref.shape[0] // tiles
    for tile in range(tiles):
        part = pl.ds(tile * rows, rows)
        taken = jnp.full((rows, taken_ref.shape[1]), flags[0, tile], jnp.int32)
        taken_ref[part, :] = taken.astype(jnp.float32).astype(taken_ref.dtype)
    for copy in copies[1:]:
        copy.wait()


def pack(own, grad, spare, evicted):
    return pl.pallas_call(
        pack_kernel,
        out_shape=(
            pltpu.VMEM((2, *own.shape), own.dtype),
            pltpu.VMEM(spare.shape, spare.dtype),
            pltpu.VMEM(own.shape, own.dtype),
        ),
        in_specs=[pl.BlockSpec(memory_space=pltpu.HBM)] * 4,
        out_specs=tuple(vmem_specs(3)),
        scratch_shapes=[
            pltpu.SMEM(evicted.shape, evicted.dtype),
            pltpu.SemaphoreType.DMA((4,)),
        ],
        cost_estimate=HIDES,
        compiler_params=pltpu.CompilerParams(vmem_limit_bytes=4 << 20),
    )(*map(in_hbm, (own, grad, spare, evicted)))


def reach_kernel(weight_ref, input_ref, gain_ref, first_ref, reach_ref, own_ref):
    del first_ref
    tokens, features = input_ref.shape
    values = input_ref[...].astype(jnp.float32)
    reach_ref[tokens:, :] = jnp.zeros_like(reach_ref[tokens:, :])
    squares = as_row(jnp.sum(values * values, axis=1, keepdims=True))
    reach_ref[tokens:, :tokens] = as_parts(squares)
    gained = (values * gain_ref[...]).astype(jnp.bfloat16)
    reach = jnp.dot(gained, weight_ref[...], preferred_element_type=jnp.float32)
    reach_ref[:tokens, :] = reach.astype(reach_ref.dtype)
    own_ref[:tokens, :] = reach
    own_ref[tokens:, :] = reach_ref[tokens:, :].astype(own_ref.dtype)


def reach_of(weights, inputs, gain, first):
    return pl.pallas_call(
        reach_kernel,
        out_shape=tuple(
            pltpu.VMEM((inputs.shape[0] + EXTRA, weights.shape[1]), dtype)
            for dtype in (jnp.bfloat16, jnp.float32)
        ),
        in_specs=vmem_specs(4),
        out_specs=tuple(vmem_specs(2)),
        cost_estimate=HIDES,
        compiler_params=pltpu.CompilerParams(vmem_limit_bytes=8 << 20),
    )(*map(in_vmem, (weights, inputs, gain, first)))


def mix_kernel(taken_ref, *refs):
    out_ref = refs[-1]
    taken = taken_ref[...]
    for j in range(out_ref.shape[0]):
        packed_ref, spare_ref = refs[len(refs) - 2 - j], refs[out_ref.shape[0] - 1 - j]
        out_ref[j] = lax.dot_general(
            packed_ref[0] * (1 - taken) + spare_ref[...] * taken,
            packed_ref[1],
            (((0,), (0,)), ((), ())),
            preferred_element_type=jnp.float32,
        ).astype(out_ref.dtype)


def value_gradients(taken, heads):
    return pl.pallas_call(
        mix_kernel,
        out_shape=pltpu.VMEM((len(heads), *heads[0][1].shape), jnp.bfloat16),
        in_specs=vmem_specs(1 + 2 * len(heads)),
        out_specs=pl.BlockSpec(memory_space=pltpu.VMEM),
        cost_estimate=HIDES,
        compiler_params=pltpu.CompilerParams(vmem_limit_bytes=4 << 20),
    )(*map(in_vmem, (taken, *[spare for _, spare in heads[::-1]], *[packed for packed, _ in heads[::-1]])))


def column_tile(features):
    return 256 if features % 256 == 0 else features


def fill(flat, blocks, head_of, first):
    groups = []
    for ref in blocks:
        count = ref.shape[0]
        for j in range(count):
            start = pl.multiple_of(head_of(first + j) * LANES, LANES)
            flat[:, pl.ds(start, LANES)] = ref[j]
        width = count * LANES
        groups.append((pl.multiple_of(head_of(first) // count * width, width), width))
        first += count
    return groups


def times_weights(flat, groups, weight_ref, part):
    products = [
        lax.dot_general(
            flat[:, pl.ds(start, width)],
            weight_ref[part, pl.ds(start, width)],
            (((1,), (1,)), ((), ())),
            preferred_element_type=jnp.float32,
        )
        for start, width in groups
    ]
    return sum(products[1:], products[0])


def early_kernel(head_of, *refs):
    *blocks, weight_ref, out_ref, flat = refs
    groups = fill(flat, blocks, head_of, 0)
    features = weight_ref.shape[0]
    tile = column_tile(features)
    for start in range(0, features, tile):
        part = pl.ds(start, tile)
        out_ref[:, part] = times_weights(flat, groups, weight_ref, part)


def project_early(head_of, blocks, weights):
    tokens = blocks[0].shape[1]
    return pl.pallas_call(
        functools.partial(early_kernel, head_of),
        out_shape=pltpu.VMEM((tokens, weights.shape[0]), jnp.float32),
        in_specs=vmem_specs(len(blocks) + 1),
        out_specs=pl.BlockSpec(memory_space=pltpu.VMEM),
        scratch_shapes=[pltpu.VMEM((tokens, weights.shape[1]), jnp.bfloat16)],
        cost_estimate=pl.CostEstimate(flops=1 << 16, bytes_accessed=1 << 12, transcendentals=0),
        compiler_params=pltpu.CompilerParams(vmem_limit_bytes=16 << 20),
    )(*map(in_vmem, (*blocks, weights)))


def inner_part(head_of, blocks, first, reach_ref):
    total = None
    for ref in blocks:
        for j in range(ref.shape[0]):
            start = pl.multiple_of(head_of(first) * LANES, LANES)
            part = ref[j].astype(jnp.float32) * reach_ref[:, pl.ds(start, LANES)]
            total = part if total is None else total + part
            first += 1
    return total


def join_kernel(head_of, sizes, *refs):
    blocks, reach_refs = refs[: sizes[0]], refs[sizes[0] : sizes[0] + sizes[1]]
    reach_ref, folded_ref, squares_ref = refs[sizes[0] + sizes[1] :]
    tokens = reach_ref.shape[0]
    reach_ref[...] = sum(ref[:tokens, :].astype(jnp.float32) for ref in reach_refs)
    squares = sum(ref[tokens:, :tokens].astype(jnp.float32) for ref in reach_refs)
    squares_ref[...] = jnp.sum(squares, axis=0, keepdims=True)
    if blocks:
        folded_ref[...] = inner_part(head_of, blocks, 0, reach_ref)
    else:
        folded_ref[...] = jnp.zeros_like(folded_ref)


def join(head_of, blocks, reaches):
    tokens, columns = reaches[0].shape[0] - EXTRA, reaches[0].shape[1]
    operands = (*blocks, *reaches)
    return pl.pallas_call(
        functools.partial(join_kernel, head_of, (len(blocks), len(reaches))),
        out_shape=(
            pltpu.VMEM((tokens, columns), jnp.float32),
            pltpu.VMEM((tokens, LANES), jnp.float32),
            pltpu.VMEM((1, tokens), jnp.float32),
        ),
        in_specs=vmem_specs(len(operands)),
        out_specs=tuple(vmem_specs(3)),
        cost_estimate=pl.CostEstimate(flops=1 << 16, bytes_accessed=1 << 12, transcendentals=0),
        compiler_params=pltpu.CompilerParams(vmem_limit_bytes=8 << 20),
    )(*map(in_vmem, operands))


def project_kernel(head_of, first, count, *refs):
    blocks, rest = refs[:count], refs[count:]
    reach_ref, folded_ref, squares_ref, weight_ref, input_ref, gain_ref, *rest = rest
    *early_refs, scaled_ref, sums_ref, flat = rest
    tokens, features = input_ref.shape
    groups = fill(flat, blocks, head_of, first)
    squares = squares_ref[...]
    folded = folded_ref[...] + inner_part(head_of, blocks, first, reach_ref)
    inner = as_row(jnp.sum(folded, axis=1, keepdims=True))
    sums_ref[:1, :] = squares
    sums_ref[1:, :] = inner
    rho = own_ratio(squares, inner)
    rows = [*split(squares), *split(inner), rho, jnp.zeros((1, tokens), jnp.float32)]
    columns = standing(jnp.concatenate(rows))
    scaled_ref[:, features:] = columns.astype(scaled_ref.dtype)
    rho = columns[:, 6:7]
    tile = column_tile(features)
    for start in range(0, features, tile):
        part = pl.ds(start, tile)
        grad_normed = times_weights(flat, groups, weight_ref, part)
        for ref in early_refs:
            grad_normed = grad_normed + ref[:, part]
        values = input_ref[:, part].astype(jnp.float32)
        scaled_ref[:, part] = (grad_normed * gain_ref[:, part] - values * rho).astype(
            scaled_ref.dtype
        )


def project(head_of, first, blocks, joined, weights, inputs, gain, early):
    tokens, features = inputs.shape
    operands = (*blocks, *joined, weights, inputs, gain, *early)
    return pl.pallas_call(
        functools.partial(project_kernel, head_of, first, len(blocks)),
        out_shape=(
            pltpu.VMEM((tokens, features + LANES), jnp.bfloat16),
            pltpu.VMEM((2, tokens), jnp.float32),
        ),
        in_specs=vmem_specs(len(operands)),
        out_specs=tuple(vmem_specs(2)),
        scratch_shapes=[pltpu.VMEM((tokens, weights.shape[1]), jnp.bfloat16)],
        cost_estimate=HIDES,
        compiler_params=pltpu.CompilerParams(vmem_limit_bytes=16 << 20),
    )(*map(in_vmem, operands))


def finish_kernel(scaled_ref, input_ref, *refs):
    *sums_refs, out_ref, held, sems = refs
    tokens, features = input_ref.shape
    extra = scaled_ref[:, features:].astype(jnp.float32).T
    squares = extra[0:1] + extra[1:2] + extra[2:3]
    inner = extra[3:4] + extra[4:5] + extra[5:6]
    rho = own_ratio(squares, inner)
    for ref in sums_refs:
        squares = squares + ref[:1, :]
        inner = inner + ref[1:, :]
    inv = 1.0 / jnp.sqrt(squares / D + 1e-05)
    factor = inner * (inv * inv * inv) / D - inv * rho
    rows = jnp.concatenate([inv, factor, jnp.zeros((6, tokens), jnp.float32)])
    columns = standing(rows)
    inv, factor = columns[:, 0:1], columns[:, 1:2]
    copies = []
    for j in range(len(PIECES) - 1):
        part = slice(PIECES[j] * tokens // 8, PIECES[j + 1] * tokens // 8)
        scaled = scaled_ref[part, :features].astype(jnp.float32)
        values = input_ref[part, :].astype(jnp.float32)
        held[part, :] = (scaled * inv[part] - values * factor[part]).astype(held.dtype)
        copies.append(pltpu.make_async_copy(held.at[part], out_ref.at[part], sems.at[j]))
        copies[-1].start()
    for copy in copies:
        copy.wait()


def finish(scaled, inputs, sums):
    return pl.pallas_call(
        finish_kernel,
        out_shape=pltpu.HBM(inputs.shape, jnp.bfloat16),
        in_specs=vmem_specs(2 + len(sums)),
        out_specs=pl.BlockSpec(memory_space=pltpu.HBM),
        scratch_shapes=[
            pltpu.VMEM(inputs.shape, jnp.bfloat16),
            pltpu.SemaphoreType.DMA((len(PIECES) - 1,)),
        ],
        compiler_params=pltpu.CompilerParams(vmem_limit_bytes=8 << 20),
    )(*map(in_vmem, (scaled, inputs, *sums)))


FAR, NEAR, SIDE = 4, 2, 1
LINE = (FAR | NEAR, FAR, NEAR)
EARLY = 2


def handed_over(block, sections, count, distance, mask):
    route = [
        ((s - distance) % sections * count + (i ^ mask), s * count + i)
        for s in range(sections)
        for i in range(count)
    ]
    return lax.ppermute(block, ("section", "tp"), route)


def gathered(pair, axis):
    if lax.axis_size(axis) != 8:
        return [lax.all_gather(pair[0], axis)], lambda place: place
    blocks = [pair] + [swapped(pair, axis, mask) for mask in LINE]
    masks = [far | side for far in (0, *LINE) for side in (0, SIDE)]

    def head_of(place):
        return lax.axis_index(axis) ^ masks[place]

    return blocks, head_of


def per_device(grad_attn, w_value, probs_own, probs_spare, evicted, layer_input, gain):
    sections, count = lax.axis_size("section"), lax.axis_size("tp")
    packed, spares, taken = pack(probs_own[0, 0], grad_attn[0, 0], probs_spare[0, 0], evicted)
    heads = []
    for mask in (0, SIDE) if count == 8 else (0,):
        spare = handed_over(spares, sections, count, sections // 2, mask)
        heads.append((swapped(packed, "tp", mask) if mask else packed, spare))
    weights, inputs = w_value[0], layer_input[0]
    next_input = passed_along(inputs, "section", -1)
    reach, own_reach = reach_of(weights, inputs, gain, heads[-1][0])
    if count == 8:
        reaches = [own_reach, swapped(reach, "tp", SIDE)]
        reaches[1], next_input = lax.optimization_barrier((reaches[1], next_input))
    else:
        reaches = [lax.psum(own_reach, "tp")]
    pair = value_gradients(taken, heads)
    blocks, head_of = gathered(pair, "tp")
    soon, late = (blocks[:EARLY], blocks[EARLY:]) if count == 8 else ([], blocks)
    early = [project_early(head_of, soon, weights)] if soon else []
    joined = join(head_of, soon, reaches)
    first = sum(block.shape[0] for block in soon)
    scaled, sums = project(head_of, first, late, joined, weights, inputs, gain, early)
    next_scaled = passed_along(scaled, "section", -1)
    next_sums = []
    for mask in (NEAR, FAR | NEAR, FAR) if count == 8 else ():
        next_sums.append(handed_over(sums, sections, count, -1, mask))
    return finish(next_scaled, next_input, next_sums)[None]


def solution(mesh):
    in_specs = (
        P("section", "tp", None, None),
        P("section", "tp", None),
        P("section", "tp", None, None),
        P("section", "tp", None, None),
        P("section", None),
        P("section", None, "tp"),
        P("section", "tp"),
    )
    out_specs = P("section", None, "tp")
    return jax.shard_map(
        per_device, mesh=mesh, in_specs=in_specs, out_specs=out_specs, check_vma=False
    )
```

```python
import functools

import jax
import jax.numpy as jnp
from jax import lax
from jax.experimental import pallas as pl
from jax.experimental.pallas import tpu as pltpu
from jax.sharding import PartitionSpec as P

D = 12288
LANES = 128
PIECES = (0, 3, 5, 7, 8)
EXTRA = 16
HIDES = pl.CostEstimate(flops=1 << 35, bytes_accessed=1 << 25, transcendentals=0)


def passed_along(block, axis, distance):
    devices = range(lax.axis_size(axis))
    route = [((i - distance) % len(devices), i) for i in devices]
    return lax.ppermute(block, axis, route)


def swapped(block, axis, mask):
    return lax.ppermute(block, axis, [(i ^ mask, i) for i in range(lax.axis_size(axis))])


def in_vmem(array):
    return pltpu.with_memory_space_constraint(array, pltpu.VMEM)


def in_hbm(array):
    return pltpu.with_memory_space_constraint(array, pltpu.HBM)


def vmem_specs(count):
    return [pl.BlockSpec(memory_space=pltpu.VMEM)] * count


def as_row(column):
    return jnp.broadcast_to(column, (column.shape[0], column.shape[0])).T[:1]


def standing(rows):
    tokens = rows.shape[1]
    return jnp.concatenate([rows, jnp.zeros((tokens - rows.shape[0], tokens), rows.dtype)]).T


def split(values):
    parts = []
    for _ in range(3):
        parts.append(values.astype(jnp.bfloat16).astype(jnp.float32))
        values = values - parts[-1]
    return parts


def own_ratio(squares, inner):
    return inner / jnp.maximum(squares, 1e-30)


def as_parts(row):
    rest = jnp.zeros((EXTRA - 3, row.shape[1]), jnp.float32)
    return jnp.concatenate(split(row) + [rest]).astype(jnp.bfloat16)


def pack_kernel(own_ref, grad_ref, spare_ref, evicted_ref, *refs):
    out_ref, spare_out, taken_ref, flags, sems = refs
    copies = [
        pltpu.make_async_copy(evicted_ref, flags, sems.at[0]),
        pltpu.make_async_copy(own_ref, out_ref.at[0], sems.at[1]),
        pltpu.make_async_copy(grad_ref, out_ref.at[1], sems.at[2]),
        pltpu.make_async_copy(spare_ref, spare_out, sems.at[3]),
    ]
    for copy in copies:
        copy.start()
    copies[0].wait()
    tiles = evicted_ref.shape[1]
    rows = taken_ref.shape[0] // tiles
    for tile in range(tiles):
        part = pl.ds(tile * rows, rows)
        taken = jnp.full((rows, taken_ref.shape[1]), flags[0, tile], jnp.int32)
        taken_ref[part, :] = taken.astype(jnp.float32).astype(taken_ref.dtype)
    for copy in copies[1:]:
        copy.wait()


def pack(own, grad, spare, evicted):
    return pl.pallas_call(
        pack_kernel,
        out_shape=(
            pltpu.VMEM((2, *own.shape), own.dtype),
            pltpu.VMEM(spare.shape, spare.dtype),
            pltpu.VMEM(own.shape, own.dtype),
        ),
        in_specs=[pl.BlockSpec(memory_space=pltpu.HBM)] * 4,
        out_specs=tuple(vmem_specs(3)),
        scratch_shapes=[
            pltpu.SMEM(evicted.shape, evicted.dtype),
            pltpu.SemaphoreType.DMA((4,)),
        ],
        cost_estimate=HIDES,
        compiler_params=pltpu.CompilerParams(vmem_limit_bytes=4 << 20),
    )(*map(in_hbm, (own, grad, spare, evicted)))


def reach_kernel(weight_ref, input_ref, gain_ref, first_ref, reach_ref, own_ref):
    del first_ref
    tokens, features = input_ref.shape
    values = input_ref[...].astype(jnp.float32)
    reach_ref[tokens:, :] = jnp.zeros_like(reach_ref[tokens:, :])
    squares = as_row(jnp.sum(values * values, axis=1, keepdims=True))
    reach_ref[tokens:, :tokens] = as_parts(squares)
    gained = (values * gain_ref[...]).astype(jnp.bfloat16)
    reach = jnp.dot(gained, weight_ref[...], preferred_element_type=jnp.float32)
    reach_ref[:tokens, :] = reach.astype(reach_ref.dtype)
    own_ref[:tokens, :] = reach
    own_ref[tokens:, :] = reach_ref[tokens:, :].astype(own_ref.dtype)


def reach_of(weights, inputs, gain, first):
    return pl.pallas_call(
        reach_kernel,
        out_shape=tuple(
            pltpu.VMEM((inputs.shape[0] + EXTRA, weights.shape[1]), dtype)
            for dtype in (jnp.bfloat16, jnp.float32)
        ),
        in_specs=vmem_specs(4),
        out_specs=tuple(vmem_specs(2)),
        cost_estimate=HIDES,
        compiler_params=pltpu.CompilerParams(vmem_limit_bytes=8 << 20),
    )(*map(in_vmem, (weights, inputs, gain, first)))


def mix_kernel(upper, taken_ref, *refs):
    out_ref = refs[-1]
    taken = taken_ref[...]
    count = out_ref.shape[0]
    spares = [refs[count - 1 - j][...] for j in range(count)]
    if count == 2:
        swap = upper()
        spares = [jnp.where(swap, spares[1], spares[0]), jnp.where(swap, spares[0], spares[1])]
    for j in range(count):
        packed_ref = refs[len(refs) - 2 - j]
        out_ref[j] = lax.dot_general(
            packed_ref[0] * (1 - taken) + spares[j] * taken,
            packed_ref[1],
            (((0,), (0,)), ((), ())),
            preferred_element_type=jnp.float32,
        ).astype(out_ref.dtype)


def value_gradients(taken, spares, packs, upper):
    return pl.pallas_call(
        functools.partial(mix_kernel, upper),
        out_shape=pltpu.VMEM((len(packs), *spares[0].shape), jnp.bfloat16),
        in_specs=vmem_specs(1 + 2 * len(packs)),
        out_specs=pl.BlockSpec(memory_space=pltpu.VMEM),
        cost_estimate=HIDES,
        compiler_params=pltpu.CompilerParams(vmem_limit_bytes=4 << 20),
    )(*map(in_vmem, (taken, *spares[::-1], *packs[::-1])))


def column_tile(features):
    return 256 if features % 256 == 0 else features


def fill(flat, blocks, head_of, first):
    groups = []
    for ref in blocks:
        count = ref.shape[0]
        for j in range(count):
            start = pl.multiple_of(head_of(first + j) * LANES, LANES)
            flat[:, pl.ds(start, LANES)] = ref[j]
        width = count * LANES
        groups.append((pl.multiple_of(head_of(first) // count * width, width), width))
        first += count
    return groups


def times_weights(flat, groups, weight_ref, part):
    products = [
        lax.dot_general(
            flat[:, pl.ds(start, width)],
            weight_ref[part, pl.ds(start, width)],
            (((1,), (1,)), ((), ())),
            preferred_element_type=jnp.float32,
        )
        for start, width in groups
    ]
    return sum(products[1:], products[0])


def early_kernel(head_of, *refs):
    *blocks, weight_ref, out_ref, flat = refs
    groups = fill(flat, blocks, head_of, 0)
    features = weight_ref.shape[0]
    tile = column_tile(features)
    for start in range(0, features, tile):
        part = pl.ds(start, tile)
        out_ref[:, part] = times_weights(flat, groups, weight_ref, part)


def project_early(head_of, blocks, weights):
    tokens = blocks[0].shape[1]
    return pl.pallas_call(
        functools.partial(early_kernel, head_of),
        out_shape=pltpu.VMEM((tokens, weights.shape[0]), jnp.float32),
        in_specs=vmem_specs(len(blocks) + 1),
        out_specs=pl.BlockSpec(memory_space=pltpu.VMEM),
        scratch_shapes=[pltpu.VMEM((tokens, weights.shape[1]), jnp.bfloat16)],
        cost_estimate=pl.CostEstimate(flops=1 << 16, bytes_accessed=1 << 12, transcendentals=0),
        compiler_params=pltpu.CompilerParams(vmem_limit_bytes=16 << 20),
    )(*map(in_vmem, (*blocks, weights)))


def inner_part(head_of, blocks, first, reach_ref):
    total = None
    for ref in blocks:
        for j in range(ref.shape[0]):
            start = pl.multiple_of(head_of(first) * LANES, LANES)
            part = ref[j].astype(jnp.float32) * reach_ref[:, pl.ds(start, LANES)]
            total = part if total is None else total + part
            first += 1
    return total


def join_kernel(head_of, sizes, *refs):
    blocks, reach_refs = refs[: sizes[0]], refs[sizes[0] : sizes[0] + sizes[1]]
    reach_ref, folded_ref, squares_ref = refs[sizes[0] + sizes[1] :]
    tokens = reach_ref.shape[0]
    reach_ref[...] = sum(ref[:tokens, :].astype(jnp.float32) for ref in reach_refs)
    squares = sum(ref[tokens:, :tokens].astype(jnp.float32) for ref in reach_refs)
    squares_ref[...] = jnp.sum(squares, axis=0, keepdims=True)
    if blocks:
        folded_ref[...] = inner_part(head_of, blocks, 0, reach_ref)
    else:
        folded_ref[...] = jnp.zeros_like(folded_ref)


def join(head_of, blocks, reaches):
    tokens, columns = reaches[0].shape[0] - EXTRA, reaches[0].shape[1]
    operands = (*blocks, *reaches)
    return pl.pallas_call(
        functools.partial(join_kernel, head_of, (len(blocks), len(reaches))),
        out_shape=(
            pltpu.VMEM((tokens, columns), jnp.float32),
            pltpu.VMEM((tokens, LANES), jnp.float32),
            pltpu.VMEM((1, tokens), jnp.float32),
        ),
        in_specs=vmem_specs(len(operands)),
        out_specs=tuple(vmem_specs(3)),
        cost_estimate=pl.CostEstimate(flops=1 << 16, bytes_accessed=1 << 12, transcendentals=0),
        compiler_params=pltpu.CompilerParams(vmem_limit_bytes=8 << 20),
    )(*map(in_vmem, operands))


def project_kernel(head_of, first, count, *refs):
    blocks, rest = refs[:count], refs[count:]
    reach_ref, folded_ref, squares_ref, weight_ref, input_ref, gain_ref, *rest = rest
    *early_refs, scaled_ref, sums_ref, flat = rest
    tokens, features = input_ref.shape
    groups = fill(flat, blocks, head_of, first)
    squares = squares_ref[...]
    folded = folded_ref[...] + inner_part(head_of, blocks, first, reach_ref)
    inner = as_row(jnp.sum(folded, axis=1, keepdims=True))
    sums_ref[:1, :] = squares
    sums_ref[1:, :] = inner
    rho = own_ratio(squares, inner)
    rows = [*split(squares), *split(inner), rho, jnp.zeros((1, tokens), jnp.float32)]
    columns = standing(jnp.concatenate(rows))
    scaled_ref[:, features:] = columns.astype(scaled_ref.dtype)
    rho = columns[:, 6:7]
    tile = column_tile(features)
    for start in range(0, features, tile):
        part = pl.ds(start, tile)
        grad_normed = times_weights(flat, groups, weight_ref, part)
        for ref in early_refs:
            grad_normed = grad_normed + ref[:, part]
        values = input_ref[:, part].astype(jnp.float32)
        scaled_ref[:, part] = (grad_normed * gain_ref[:, part] - values * rho).astype(
            scaled_ref.dtype
        )


def project(head_of, first, blocks, joined, weights, inputs, gain, early):
    tokens, features = inputs.shape
    operands = (*blocks, *joined, weights, inputs, gain, *early)
    return pl.pallas_call(
        functools.partial(project_kernel, head_of, first, len(blocks)),
        out_shape=(
            pltpu.VMEM((tokens, features + LANES), jnp.bfloat16),
            pltpu.VMEM((2, tokens), jnp.float32),
        ),
        in_specs=vmem_specs(len(operands)),
        out_specs=tuple(vmem_specs(2)),
        scratch_shapes=[pltpu.VMEM((tokens, weights.shape[1]), jnp.bfloat16)],
        cost_estimate=HIDES,
        compiler_params=pltpu.CompilerParams(vmem_limit_bytes=16 << 20),
    )(*map(in_vmem, operands))


def finish_kernel(scaled_ref, input_ref, *refs):
    *sums_refs, out_ref, held, sems = refs
    tokens, features = input_ref.shape
    extra = scaled_ref[:, features:].astype(jnp.float32).T
    squares = extra[0:1] + extra[1:2] + extra[2:3]
    inner = extra[3:4] + extra[4:5] + extra[5:6]
    rho = own_ratio(squares, inner)
    for ref in sums_refs:
        squares = squares + ref[:1, :]
        inner = inner + ref[1:, :]
    inv = 1.0 / jnp.sqrt(squares / D + 1e-05)
    factor = inner * (inv * inv * inv) / D - inv * rho
    rows = jnp.concatenate([inv, factor, jnp.zeros((6, tokens), jnp.float32)])
    columns = standing(rows)
    inv, factor = columns[:, 0:1], columns[:, 1:2]
    copies = []
    for j in range(len(PIECES) - 1):
        part = slice(PIECES[j] * tokens // 8, PIECES[j + 1] * tokens // 8)
        scaled = scaled_ref[part, :features].astype(jnp.float32)
        values = input_ref[part, :].astype(jnp.float32)
        held[part, :] = (scaled * inv[part] - values * factor[part]).astype(held.dtype)
        copies.append(pltpu.make_async_copy(held.at[part], out_ref.at[part], sems.at[j]))
        copies[-1].start()
    for copy in copies:
        copy.wait()


def finish(scaled, inputs, sums):
    return pl.pallas_call(
        finish_kernel,
        out_shape=pltpu.HBM(inputs.shape, jnp.bfloat16),
        in_specs=vmem_specs(2 + len(sums)),
        out_specs=pl.BlockSpec(memory_space=pltpu.HBM),
        scratch_shapes=[
            pltpu.VMEM(inputs.shape, jnp.bfloat16),
            pltpu.SemaphoreType.DMA((len(PIECES) - 1,)),
        ],
        compiler_params=pltpu.CompilerParams(vmem_limit_bytes=8 << 20),
    )(*map(in_vmem, (scaled, inputs, *sums)))


FAR, NEAR, SIDE = 4, 2, 1
ORDER = ((0, SIDE), (SIDE, 0))
LINE = (FAR | NEAR, FAR, NEAR)
EARLY = 2


def handed_over(block, sections, count, distance, mask):
    route = [
        ((s - distance) % sections * count + (i ^ mask), s * count + i)
        for s in range(sections)
        for i in range(count)
    ]
    return lax.ppermute(block, ("section", "tp"), route)


def fetched(block, sections, count, masks):
    half = sections // 2
    route = []
    for s in range(sections):
        mask = masks[s // half] if count == 8 else 0
        for i in range(count):
            route.append(((s + half) % sections * count + (i ^ mask), s * count + i))
    return lax.ppermute(block, ("section", "tp"), route)


def gathered(pair, axis):
    if lax.axis_size(axis) != 8:
        return [lax.all_gather(pair[0], axis)], lambda place: place
    blocks = [pair] + [swapped(pair, axis, mask) for mask in LINE]
    masks = [far | side for far in (0, *LINE) for side in (0, SIDE)]

    def head_of(place):
        return lax.axis_index(axis) ^ masks[place]

    return blocks, head_of


def per_device(grad_attn, w_value, probs_own, probs_spare, evicted, layer_input, gain):
    sections, count = lax.axis_size("section"), lax.axis_size("tp")
    packed, spares, taken = pack(probs_own[0, 0], grad_attn[0, 0], probs_spare[0, 0], evicted)
    half = sections // 2
    packs = [packed, swapped(packed, "tp", SIDE)] if count == 8 else [packed]
    spares = [fetched(spares, sections, count, masks) for masks in ORDER[: len(packs)]]
    weights, inputs = w_value[0], layer_input[0]
    next_input = passed_along(inputs, "section", -1)
    reach, own_reach = reach_of(weights, inputs, gain, packs[-1])
    if count == 8:
        reaches = [own_reach, swapped(reach, "tp", SIDE)]
        reaches[1], next_input = lax.optimization_barrier((reaches[1], next_input))
    else:
        reaches = [lax.psum(own_reach, "tp")]
    pair = value_gradients(taken, spares, packs, lambda: lax.axis_index("section") >= half)
    blocks, head_of = gathered(pair, "tp")
    soon, late = (blocks[:EARLY], blocks[EARLY:]) if count == 8 else ([], blocks)
    early = [project_early(head_of, soon, weights)] if soon else []
    joined = join(head_of, soon, reaches)
    first = sum(block.shape[0] for block in soon)
    scaled, sums = project(head_of, first, late, joined, weights, inputs, gain, early)
    next_scaled = passed_along(scaled, "section", -1)
    next_sums = []
    for mask in (NEAR, FAR | NEAR, FAR) if count == 8 else ():
        next_sums.append(handed_over(sums, sections, count, -1, mask))
    return finish(next_scaled, next_input, next_sums)[None]


def solution(mesh):
    in_specs = (
        P("section", "tp", None, None),
        P("section", "tp", None),
        P("section", "tp", None, None),
        P("section", "tp", None, None),
        P("section", None),
        P("section", None, "tp"),
        P("section", "tp"),
    )
    out_specs = P("section", None, "tp")
    return jax.shard_map(
        per_device, mesh=mesh, in_specs=in_specs, out_specs=out_specs, check_vma=False
    )
```

```python
import functools

import jax
import jax.numpy as jnp
from jax import lax
from jax.experimental import pallas as pl
from jax.experimental.pallas import tpu as pltpu
from jax.sharding import PartitionSpec as P

D = 12288
LANES = 128
PIECES = (0, 3, 5, 7, 8)
EXTRA = 16
SHORT = pl.CostEstimate(flops=1 << 16, bytes_accessed=1 << 12, transcendentals=0)
HIDES = pl.CostEstimate(flops=1 << 35, bytes_accessed=1 << 25, transcendentals=0)


def passed_along(block, axis, distance):
    devices = range(lax.axis_size(axis))
    route = [((i - distance) % len(devices), i) for i in devices]
    return lax.ppermute(block, axis, route)


def swapped(block, axis, mask):
    return lax.ppermute(block, axis, [(i ^ mask, i) for i in range(lax.axis_size(axis))])


def in_vmem(array):
    return pltpu.with_memory_space_constraint(array, pltpu.VMEM)


def in_hbm(array):
    return pltpu.with_memory_space_constraint(array, pltpu.HBM)


def vmem_specs(count):
    return [pl.BlockSpec(memory_space=pltpu.VMEM)] * count


def as_row(column):
    return jnp.broadcast_to(column, (column.shape[0], column.shape[0])).T[:1]


def standing(rows):
    tokens = rows.shape[1]
    return jnp.concatenate([rows, jnp.zeros((tokens - rows.shape[0], tokens), rows.dtype)]).T


def split(values):
    parts = []
    for _ in range(3):
        parts.append(values.astype(jnp.bfloat16).astype(jnp.float32))
        values = values - parts[-1]
    return parts


def own_ratio(squares, inner):
    return inner / jnp.maximum(squares, 1e-30)


def as_parts(row):
    rest = jnp.zeros((EXTRA - 3, row.shape[1]), jnp.float32)
    return jnp.concatenate(split(row) + [rest]).astype(jnp.bfloat16)


def pack_kernel(own_ref, grad_ref, spare_ref, evicted_ref, *refs):
    out_ref, spare_out, taken_ref, flags, sems = refs
    copies = [
        pltpu.make_async_copy(evicted_ref, flags, sems.at[0]),
        pltpu.make_async_copy(own_ref, out_ref.at[0], sems.at[1]),
        pltpu.make_async_copy(grad_ref, out_ref.at[1], sems.at[2]),
        pltpu.make_async_copy(spare_ref, spare_out, sems.at[3]),
    ]
    for copy in copies:
        copy.start()
    copies[0].wait()
    tiles = evicted_ref.shape[1]
    rows = taken_ref.shape[0] // tiles
    for tile in range(tiles):
        part = pl.ds(tile * rows, rows)
        taken = jnp.full((rows, taken_ref.shape[1]), flags[0, tile], jnp.int32)
        taken_ref[part, :] = taken.astype(jnp.float32).astype(taken_ref.dtype)
    for copy in copies[1:]:
        copy.wait()


def pack(own, grad, spare, evicted):
    return pl.pallas_call(
        pack_kernel,
        out_shape=(
            pltpu.VMEM((2, *own.shape), own.dtype),
            pltpu.VMEM(spare.shape, spare.dtype),
            pltpu.VMEM(own.shape, own.dtype),
        ),
        in_specs=[pl.BlockSpec(memory_space=pltpu.HBM)] * 4,
        out_specs=tuple(vmem_specs(3)),
        scratch_shapes=[
            pltpu.SMEM(evicted.shape, evicted.dtype),
            pltpu.SemaphoreType.DMA((4,)),
        ],
        cost_estimate=HIDES,
        compiler_params=pltpu.CompilerParams(vmem_limit_bytes=4 << 20),
    )(*map(in_hbm, (own, grad, spare, evicted)))


def reach_kernel(weight_ref, input_ref, gain_ref, reach_ref, own_ref):
    tokens, features = input_ref.shape
    values = input_ref[...].astype(jnp.float32)
    reach_ref[tokens:, :] = jnp.zeros_like(reach_ref[tokens:, :])
    squares = as_row(jnp.sum(values * values, axis=1, keepdims=True))
    reach_ref[tokens:, :tokens] = as_parts(squares)
    gained = (values * gain_ref[...]).astype(jnp.bfloat16)
    reach = jnp.dot(gained, weight_ref[...], preferred_element_type=jnp.float32)
    reach_ref[:tokens, :] = reach.astype(reach_ref.dtype)
    own_ref[:tokens, :] = reach
    own_ref[tokens:, :] = reach_ref[tokens:, :].astype(own_ref.dtype)


def reach_of(weights, inputs, gain):
    return pl.pallas_call(
        reach_kernel,
        out_shape=tuple(
            pltpu.VMEM((inputs.shape[0] + EXTRA, weights.shape[1]), dtype)
            for dtype in (jnp.bfloat16, jnp.float32)
        ),
        in_specs=vmem_specs(3),
        out_specs=tuple(vmem_specs(2)),
        cost_estimate=SHORT,
        compiler_params=pltpu.CompilerParams(vmem_limit_bytes=8 << 20),
    )(*map(in_vmem, (weights, inputs, gain)))


def mix_kernel(upper, taken_ref, *refs):
    out_ref = refs[-1]
    taken = taken_ref[...]
    count = out_ref.shape[0]
    spares = [refs[j][...] for j in range(count)]
    if count == 2:
        swap = upper()
        spares = [jnp.where(swap, spares[1], spares[0]), jnp.where(swap, spares[0], spares[1])]
    for j in range(count):
        packed_ref = refs[len(refs) - 2 - j]
        out_ref[j] = lax.dot_general(
            packed_ref[0] * (1 - taken) + spares[j] * taken,
            packed_ref[1],
            (((0,), (0,)), ((), ())),
            preferred_element_type=jnp.float32,
        ).astype(out_ref.dtype)


def value_gradients(taken, spares, packs, upper):
    return pl.pallas_call(
        functools.partial(mix_kernel, upper),
        out_shape=pltpu.VMEM((len(packs), *spares[0].shape), jnp.bfloat16),
        in_specs=vmem_specs(1 + 2 * len(packs)),
        out_specs=pl.BlockSpec(memory_space=pltpu.VMEM),
        cost_estimate=HIDES,
        compiler_params=pltpu.CompilerParams(vmem_limit_bytes=4 << 20),
    )(*map(in_vmem, (taken, *spares, *packs[::-1])))


def column_tile(features):
    return 256 if features % 256 == 0 else features


def fill(flat, blocks, head_of, first):
    groups = []
    for ref in blocks:
        count = ref.shape[0]
        for j in range(count):
            start = pl.multiple_of(head_of(first + j) * LANES, LANES)
            flat[:, pl.ds(start, LANES)] = ref[j]
        width = count * LANES
        groups.append((pl.multiple_of(head_of(first) // count * width, width), width))
        first += count
    return groups


def times_weights(flat, groups, weight_ref, part):
    products = [
        lax.dot_general(
            flat[:, pl.ds(start, width)],
            weight_ref[part, pl.ds(start, width)],
            (((1,), (1,)), ((), ())),
            preferred_element_type=jnp.float32,
        )
        for start, width in groups
    ]
    return sum(products[1:], products[0])


def early_kernel(head_of, *refs):
    *blocks, weight_ref, out_ref, flat = refs
    groups = fill(flat, blocks, head_of, 0)
    features = weight_ref.shape[0]
    tile = column_tile(features)
    for start in range(0, features, tile):
        part = pl.ds(start, tile)
        out_ref[:, part] = times_weights(flat, groups, weight_ref, part)


def project_early(head_of, blocks, weights):
    tokens = blocks[0].shape[1]
    return pl.pallas_call(
        functools.partial(early_kernel, head_of),
        out_shape=pltpu.VMEM((tokens, weights.shape[0]), jnp.float32),
        in_specs=vmem_specs(len(blocks) + 1),
        out_specs=pl.BlockSpec(memory_space=pltpu.VMEM),
        scratch_shapes=[pltpu.VMEM((tokens, weights.shape[1]), jnp.bfloat16)],
        cost_estimate=SHORT,
        compiler_params=pltpu.CompilerParams(vmem_limit_bytes=16 << 20),
    )(*map(in_vmem, (*blocks, weights)))


def inner_part(head_of, blocks, first, reach_ref):
    total = None
    for ref in blocks:
        for j in range(ref.shape[0]):
            start = pl.multiple_of(head_of(first) * LANES, LANES)
            part = ref[j].astype(jnp.float32) * reach_ref[:, pl.ds(start, LANES)]
            total = part if total is None else total + part
            first += 1
    return total


def join_kernel(head_of, sizes, *refs):
    blocks, reach_refs = refs[: sizes[0]], refs[sizes[0] : sizes[0] + sizes[1]]
    reach_ref, folded_ref, squares_ref = refs[sizes[0] + sizes[1] :]
    tokens = reach_ref.shape[0]
    reach_ref[...] = sum(ref[:tokens, :].astype(jnp.float32) for ref in reach_refs)
    squares = sum(ref[tokens:, :tokens].astype(jnp.float32) for ref in reach_refs)
    squares_ref[...] = jnp.sum(squares, axis=0, keepdims=True)
    if blocks:
        folded_ref[...] = inner_part(head_of, blocks, 0, reach_ref)
    else:
        folded_ref[...] = jnp.zeros_like(folded_ref)


def join(head_of, blocks, reaches):
    tokens, columns = reaches[0].shape[0] - EXTRA, reaches[0].shape[1]
    operands = (*blocks, *reaches)
    return pl.pallas_call(
        functools.partial(join_kernel, head_of, (len(blocks), len(reaches))),
        out_shape=(
            pltpu.VMEM((tokens, columns), jnp.float32),
            pltpu.VMEM((tokens, LANES), jnp.float32),
            pltpu.VMEM((1, tokens), jnp.float32),
        ),
        in_specs=vmem_specs(len(operands)),
        out_specs=tuple(vmem_specs(3)),
        cost_estimate=SHORT,
        compiler_params=pltpu.CompilerParams(vmem_limit_bytes=8 << 20),
    )(*map(in_vmem, operands))


def project_kernel(head_of, first, count, *refs):
    blocks, rest = refs[:count], refs[count:]
    reach_ref, folded_ref, squares_ref, weight_ref, input_ref, gain_ref, *rest = rest
    *early_refs, scaled_ref, sums_ref, flat = rest
    tokens, features = input_ref.shape
    groups = fill(flat, blocks, head_of, first)
    squares = squares_ref[...]
    folded = folded_ref[...] + inner_part(head_of, blocks, first, reach_ref)
    inner = as_row(jnp.sum(folded, axis=1, keepdims=True))
    sums_ref[:1, :] = squares
    sums_ref[1:, :] = inner
    rho = own_ratio(squares, inner)
    rows = [*split(squares), *split(inner), rho, jnp.zeros((1, tokens), jnp.float32)]
    columns = standing(jnp.concatenate(rows))
    scaled_ref[:, features:] = columns.astype(scaled_ref.dtype)
    rho = columns[:, 6:7]
    tile = column_tile(features)
    for start in range(0, features, tile):
        part = pl.ds(start, tile)
        grad_normed = times_weights(flat, groups, weight_ref, part)
        for ref in early_refs:
            grad_normed = grad_normed + ref[:, part]
        values = input_ref[:, part].astype(jnp.float32)
        scaled_ref[:, part] = (grad_normed * gain_ref[:, part] - values * rho).astype(
            scaled_ref.dtype
        )


def project(head_of, first, blocks, joined, weights, inputs, gain, early):
    tokens, features = inputs.shape
    operands = (*blocks, *joined, weights, inputs, gain, *early)
    return pl.pallas_call(
        functools.partial(project_kernel, head_of, first, len(blocks)),
        out_shape=(
            pltpu.VMEM((tokens, features + LANES), jnp.bfloat16),
            pltpu.VMEM((2, tokens), jnp.float32),
        ),
        in_specs=vmem_specs(len(operands)),
        out_specs=tuple(vmem_specs(2)),
        scratch_shapes=[pltpu.VMEM((tokens, weights.shape[1]), jnp.bfloat16)],
        cost_estimate=HIDES,
        compiler_params=pltpu.CompilerParams(vmem_limit_bytes=16 << 20),
    )(*map(in_vmem, operands))


def finish_kernel(scaled_ref, input_ref, *refs):
    *sums_refs, out_ref, held, sems = refs
    tokens, features = input_ref.shape
    extra = scaled_ref[:, features:].astype(jnp.float32).T
    squares = extra[0:1] + extra[1:2] + extra[2:3]
    inner = extra[3:4] + extra[4:5] + extra[5:6]
    rho = own_ratio(squares, inner)
    for ref in sums_refs:
        squares = squares + ref[:1, :]
        inner = inner + ref[1:, :]
    inv = 1.0 / jnp.sqrt(squares / D + 1e-05)
    factor = inner * (inv * inv * inv) / D - inv * rho
    rows = jnp.concatenate([inv, factor, jnp.zeros((6, tokens), jnp.float32)])
    columns = standing(rows)
    inv, factor = columns[:, 0:1], columns[:, 1:2]
    copies = []
    for j in range(len(PIECES) - 1):
        part = slice(PIECES[j] * tokens // 8, PIECES[j + 1] * tokens // 8)
        scaled = scaled_ref[part, :features].astype(jnp.float32)
        values = input_ref[part, :].astype(jnp.float32)
        held[part, :] = (scaled * inv[part] - values * factor[part]).astype(held.dtype)
        copies.append(pltpu.make_async_copy(held.at[part], out_ref.at[part], sems.at[j]))
        copies[-1].start()
    for copy in copies:
        copy.wait()


def finish(scaled, inputs, sums):
    return pl.pallas_call(
        finish_kernel,
        out_shape=pltpu.HBM(inputs.shape, jnp.bfloat16),
        in_specs=vmem_specs(2 + len(sums)),
        out_specs=pl.BlockSpec(memory_space=pltpu.HBM),
        scratch_shapes=[
            pltpu.VMEM(inputs.shape, jnp.bfloat16),
            pltpu.SemaphoreType.DMA((len(PIECES) - 1,)),
        ],
        compiler_params=pltpu.CompilerParams(vmem_limit_bytes=8 << 20),
    )(*map(in_vmem, (scaled, inputs, *sums)))


FAR, NEAR, SIDE = 4, 2, 1
ORDER = ((0, SIDE), (SIDE, 0))
LINE = (FAR | NEAR, NEAR, FAR)
EARLY = 2


def handed_over(block, sections, count, distance, mask):
    route = [
        ((s - distance) % sections * count + (i ^ mask), s * count + i)
        for s in range(sections)
        for i in range(count)
    ]
    return lax.ppermute(block, ("section", "tp"), route)


def fetched(block, sections, count, masks):
    half = sections // 2
    route = []
    for s in range(sections):
        mask = masks[s // half] if count == 8 else 0
        for i in range(count):
            route.append(((s + half) % sections * count + (i ^ mask), s * count + i))
    return lax.ppermute(block, ("section", "tp"), route)


def gathered(pair, axis):
    if lax.axis_size(axis) != 8:
        return [lax.all_gather(pair[0], axis)], lambda place: place
    blocks = [pair] + [swapped(pair, axis, mask) for mask in LINE]
    masks = [far | side for far in (0, *LINE) for side in (0, SIDE)]

    def head_of(place):
        return lax.axis_index(axis) ^ masks[place]

    return blocks, head_of


def per_device(grad_attn, w_value, probs_own, probs_spare, evicted, layer_input, gain):
    sections, count = lax.axis_size("section"), lax.axis_size("tp")
    packed, spares, taken = pack(probs_own[0, 0], grad_attn[0, 0], probs_spare[0, 0], evicted)
    half = sections // 2
    packs = [packed, swapped(packed, "tp", SIDE)] if count == 8 else [packed]
    spares = [fetched(spares, sections, count, masks) for masks in ORDER[: len(packs)]]
    weights, inputs = w_value[0], layer_input[0]
    next_input = passed_along(inputs, "section", -1)
    reach, own_reach = reach_of(weights, inputs, gain)
    if count == 8:
        reach, packs[1] = lax.optimization_barrier((reach, packs[1]))
        reaches = [own_reach, swapped(reach, "tp", SIDE)]
        reaches[1], next_input = lax.optimization_barrier((reaches[1], next_input))
    else:
        reaches = [lax.psum(own_reach, "tp")]
    pair = value_gradients(taken, spares, packs, lambda: lax.axis_index("section") >= half)
    blocks, head_of = gathered(pair, "tp")
    soon, late = (blocks[:EARLY], blocks[EARLY:]) if count == 8 else ([], blocks)
    early = [project_early(head_of, soon, weights)] if soon else []
    joined = join(head_of, soon, reaches)
    first = sum(block.shape[0] for block in soon)
    scaled, sums = project(head_of, first, late, joined, weights, inputs, gain, early)
    next_scaled = passed_along(scaled, "section", -1)
    next_sums = []
    for mask in (NEAR, FAR, FAR | NEAR) if count == 8 else ():
        next_sums.append(handed_over(sums, sections, count, -1, mask))
    return finish(next_scaled, next_input, next_sums)[None]


def solution(mesh):
    in_specs = (
        P("section", "tp", None, None),
        P("section", "tp", None),
        P("section", "tp", None, None),
        P("section", "tp", None, None),
        P("section", None),
        P("section", None, "tp"),
        P("section", "tp"),
    )
    out_specs = P("section", None, "tp")
    return jax.shard_map(
        per_device, mesh=mesh, in_specs=in_specs, out_specs=out_specs, check_vma=False
    )
```

```python
import functools

import jax
import jax.numpy as jnp
from jax import lax
from jax.experimental import pallas as pl
from jax.experimental.pallas import tpu as pltpu
from jax.sharding import PartitionSpec as P

D = 12288
LANES = 128
PIECES = (0, 3, 5, 7, 8)
EXTRA = 16
HIDES = pl.CostEstimate(flops=1 << 35, bytes_accessed=1 << 25, transcendentals=0)


def passed_along(block, axis, distance):
    devices = range(lax.axis_size(axis))
    route = [((i - distance) % len(devices), i) for i in devices]
    return lax.ppermute(block, axis, route)


def swapped(block, axis, mask):
    return lax.ppermute(block, axis, [(i ^ mask, i) for i in range(lax.axis_size(axis))])


def in_vmem(array):
    return pltpu.with_memory_space_constraint(array, pltpu.VMEM)


def in_hbm(array):
    return pltpu.with_memory_space_constraint(array, pltpu.HBM)


def vmem_specs(count):
    return [pl.BlockSpec(memory_space=pltpu.VMEM)] * count


def as_row(column):
    return jnp.broadcast_to(column, (column.shape[0], column.shape[0])).T[:1]


def standing(rows):
    tokens = rows.shape[1]
    return jnp.concatenate([rows, jnp.zeros((tokens - rows.shape[0], tokens), rows.dtype)]).T


def split(values):
    parts = []
    for _ in range(3):
        parts.append(values.astype(jnp.bfloat16).astype(jnp.float32))
        values = values - parts[-1]
    return parts


def own_ratio(squares, inner):
    return inner / jnp.maximum(squares, 1e-30)


def as_parts(row):
    rest = jnp.zeros((EXTRA - 3, row.shape[1]), jnp.float32)
    return jnp.concatenate(split(row) + [rest]).astype(jnp.bfloat16)


def pack_kernel(own_ref, grad_ref, spare_ref, evicted_ref, *refs):
    out_ref, spare_out, taken_ref, flags, sems = refs
    copies = [
        pltpu.make_async_copy(evicted_ref, flags, sems.at[0]),
        pltpu.make_async_copy(own_ref, out_ref.at[0], sems.at[1]),
        pltpu.make_async_copy(grad_ref, out_ref.at[1], sems.at[2]),
        pltpu.make_async_copy(spare_ref, spare_out, sems.at[3]),
    ]
    for copy in copies:
        copy.start()
    copies[0].wait()
    tiles = evicted_ref.shape[1]
    rows = taken_ref.shape[0] // tiles
    for tile in range(tiles):
        part = pl.ds(tile * rows, rows)
        taken = jnp.full((rows, taken_ref.shape[1]), flags[0, tile], jnp.int32)
        taken_ref[part, :] = taken.astype(jnp.float32).astype(taken_ref.dtype)
    for copy in copies[1:]:
        copy.wait()


def pack(own, grad, spare, evicted):
    return pl.pallas_call(
        pack_kernel,
        out_shape=(
            pltpu.VMEM((2, *own.shape), own.dtype),
            pltpu.VMEM(spare.shape, spare.dtype),
            pltpu.VMEM(own.shape, own.dtype),
        ),
        in_specs=[pl.BlockSpec(memory_space=pltpu.HBM)] * 4,
        out_specs=tuple(vmem_specs(3)),
        scratch_shapes=[
            pltpu.SMEM(evicted.shape, evicted.dtype),
            pltpu.SemaphoreType.DMA((4,)),
        ],
        cost_estimate=HIDES,
        compiler_params=pltpu.CompilerParams(vmem_limit_bytes=4 << 20),
    )(*map(in_hbm, (own, grad, spare, evicted)))


def reach_kernel(weight_ref, input_ref, gain_ref, first_ref, reach_ref, own_ref):
    del first_ref
    tokens, features = input_ref.shape
    values = input_ref[...].astype(jnp.float32)
    reach_ref[tokens:, :] = jnp.zeros_like(reach_ref[tokens:, :])
    squares = as_row(jnp.sum(values * values, axis=1, keepdims=True))
    reach_ref[tokens:, :tokens] = as_parts(squares)
    gained = (values * gain_ref[...]).astype(jnp.bfloat16)
    reach = jnp.dot(gained, weight_ref[...], preferred_element_type=jnp.float32)
    reach_ref[:tokens, :] = reach.astype(reach_ref.dtype)
    own_ref[:tokens, :] = reach
    own_ref[tokens:, :] = reach_ref[tokens:, :].astype(own_ref.dtype)


def reach_of(weights, inputs, gain, first):
    return pl.pallas_call(
        reach_kernel,
        out_shape=tuple(
            pltpu.VMEM((inputs.shape[0] + EXTRA, weights.shape[1]), dtype)
            for dtype in (jnp.bfloat16, jnp.float32)
        ),
        in_specs=vmem_specs(4),
        out_specs=tuple(vmem_specs(2)),
        cost_estimate=HIDES,
        compiler_params=pltpu.CompilerParams(vmem_limit_bytes=8 << 20),
    )(*map(in_vmem, (weights, inputs, gain, first)))


def mix_kernel(upper, taken_ref, *refs):
    out_ref = refs[-1]
    taken = taken_ref[...]
    count = out_ref.shape[0]
    spares = [refs[count - 1 - j][...] for j in range(count)]
    if count == 2:
        swap = upper()
        spares = [jnp.where(swap, spares[1], spares[0]), jnp.where(swap, spares[0], spares[1])]
    for j in range(count):
        packed_ref = refs[len(refs) - 2 - j]
        out_ref[j] = lax.dot_general(
            packed_ref[0] * (1 - taken) + spares[j] * taken,
            packed_ref[1],
            (((0,), (0,)), ((), ())),
            preferred_element_type=jnp.float32,
        ).astype(out_ref.dtype)


def value_gradients(taken, spares, packs, upper):
    return pl.pallas_call(
        functools.partial(mix_kernel, upper),
        out_shape=pltpu.VMEM((len(packs), *spares[0].shape), jnp.bfloat16),
        in_specs=vmem_specs(1 + 2 * len(packs)),
        out_specs=pl.BlockSpec(memory_space=pltpu.VMEM),
        cost_estimate=HIDES,
        compiler_params=pltpu.CompilerParams(vmem_limit_bytes=4 << 20),
    )(*map(in_vmem, (taken, *spares[::-1], *packs[::-1])))


def column_tile(features):
    return 256 if features % 256 == 0 else features


def fill(flat, blocks, head_of, first):
    groups = []
    for ref in blocks:
        count = ref.shape[0]
        for j in range(count):
            start = pl.multiple_of(head_of(first + j) * LANES, LANES)
            flat[:, pl.ds(start, LANES)] = ref[j]
        width = count * LANES
        groups.append((pl.multiple_of(head_of(first) // count * width, width), width))
        first += count
    return groups


def times_weights(flat, groups, weight_ref, part):
    products = [
        lax.dot_general(
            flat[:, pl.ds(start, width)],
            weight_ref[part, pl.ds(start, width)],
            (((1,), (1,)), ((), ())),
            preferred_element_type=jnp.float32,
        )
        for start, width in groups
    ]
    return sum(products[1:], products[0])


def early_kernel(head_of, *refs):
    *blocks, weight_ref, out_ref, flat = refs
    groups = fill(flat, blocks, head_of, 0)
    features = weight_ref.shape[0]
    tile = column_tile(features)
    for start in range(0, features, tile):
        part = pl.ds(start, tile)
        out_ref[:, part] = times_weights(flat, groups, weight_ref, part)


def project_early(head_of, blocks, weights):
    tokens = blocks[0].shape[1]
    return pl.pallas_call(
        functools.partial(early_kernel, head_of),
        out_shape=pltpu.VMEM((tokens, weights.shape[0]), jnp.float32),
        in_specs=vmem_specs(len(blocks) + 1),
        out_specs=pl.BlockSpec(memory_space=pltpu.VMEM),
        scratch_shapes=[pltpu.VMEM((tokens, weights.shape[1]), jnp.bfloat16)],
        cost_estimate=pl.CostEstimate(flops=1 << 16, bytes_accessed=1 << 12, transcendentals=0),
        compiler_params=pltpu.CompilerParams(vmem_limit_bytes=16 << 20),
    )(*map(in_vmem, (*blocks, weights)))


def inner_part(head_of, blocks, first, reach_ref):
    total = None
    for ref in blocks:
        for j in range(ref.shape[0]):
            start = pl.multiple_of(head_of(first) * LANES, LANES)
            part = ref[j].astype(jnp.float32) * reach_ref[:, pl.ds(start, LANES)]
            total = part if total is None else total + part
            first += 1
    return total


def join_kernel(head_of, sizes, *refs):
    blocks, reach_refs = refs[: sizes[0]], refs[sizes[0] : sizes[0] + sizes[1]]
    reach_ref, folded_ref, squares_ref = refs[sizes[0] + sizes[1] :]
    tokens = reach_ref.shape[0]
    reach_ref[...] = sum(ref[:tokens, :].astype(jnp.float32) for ref in reach_refs)
    squares = sum(ref[tokens:, :tokens].astype(jnp.float32) for ref in reach_refs)
    squares_ref[...] = jnp.sum(squares, axis=0, keepdims=True)
    if blocks:
        folded_ref[...] = inner_part(head_of, blocks, 0, reach_ref)
    else:
        folded_ref[...] = jnp.zeros_like(folded_ref)


def join(head_of, blocks, reaches):
    tokens, columns = reaches[0].shape[0] - EXTRA, reaches[0].shape[1]
    operands = (*blocks, *reaches)
    return pl.pallas_call(
        functools.partial(join_kernel, head_of, (len(blocks), len(reaches))),
        out_shape=(
            pltpu.VMEM((tokens, columns), jnp.float32),
            pltpu.VMEM((tokens, LANES), jnp.float32),
            pltpu.VMEM((1, tokens), jnp.float32),
        ),
        in_specs=vmem_specs(len(operands)),
        out_specs=tuple(vmem_specs(3)),
        cost_estimate=pl.CostEstimate(flops=1 << 16, bytes_accessed=1 << 12, transcendentals=0),
        compiler_params=pltpu.CompilerParams(vmem_limit_bytes=8 << 20),
    )(*map(in_vmem, operands))


def project_kernel(head_of, first, count, *refs):
    blocks, rest = refs[:count], refs[count:]
    reach_ref, folded_ref, squares_ref, weight_ref, input_ref, gain_ref, *rest = rest
    *early_refs, scaled_ref, sums_ref, flat = rest
    tokens, features = input_ref.shape
    groups = fill(flat, blocks, head_of, first)
    squares = squares_ref[...]
    folded = folded_ref[...] + inner_part(head_of, blocks, first, reach_ref)
    inner = as_row(jnp.sum(folded, axis=1, keepdims=True))
    sums_ref[:1, :] = squares
    sums_ref[1:, :] = inner
    rho = own_ratio(squares, inner)
    rows = [*split(squares), *split(inner), rho, jnp.zeros((1, tokens), jnp.float32)]
    columns = standing(jnp.concatenate(rows))
    scaled_ref[:, features:] = columns.astype(scaled_ref.dtype)
    rho = columns[:, 6:7]
    tile = column_tile(features)
    for start in range(0, features, tile):
        part = pl.ds(start, tile)
        grad_normed = times_weights(flat, groups, weight_ref, part)
        for ref in early_refs:
            grad_normed = grad_normed + ref[:, part]
        values = input_ref[:, part].astype(jnp.float32)
        scaled_ref[:, part] = (grad_normed * gain_ref[:, part] - values * rho).astype(
            scaled_ref.dtype
        )


def project(head_of, first, blocks, joined, weights, inputs, gain, early):
    tokens, features = inputs.shape
    operands = (*blocks, *joined, weights, inputs, gain, *early)
    return pl.pallas_call(
        functools.partial(project_kernel, head_of, first, len(blocks)),
        out_shape=(
            pltpu.VMEM((tokens, features + LANES), jnp.bfloat16),
            pltpu.VMEM((2, tokens), jnp.float32),
        ),
        in_specs=vmem_specs(len(operands)),
        out_specs=tuple(vmem_specs(2)),
        scratch_shapes=[pltpu.VMEM((tokens, weights.shape[1]), jnp.bfloat16)],
        cost_estimate=HIDES,
        compiler_params=pltpu.CompilerParams(vmem_limit_bytes=16 << 20),
    )(*map(in_vmem, operands))


def finish_kernel(scaled_ref, input_ref, *refs):
    *sums_refs, out_ref, held, sems = refs
    tokens, features = input_ref.shape
    extra = scaled_ref[:, features:].astype(jnp.float32).T
    squares = extra[0:1] + extra[1:2] + extra[2:3]
    inner = extra[3:4] + extra[4:5] + extra[5:6]
    rho = own_ratio(squares, inner)
    for ref in sums_refs:
        squares = squares + ref[:1, :]
        inner = inner + ref[1:, :]
    inv = 1.0 / jnp.sqrt(squares / D + 1e-05)
    factor = inner * (inv * inv * inv) / D - inv * rho
    rows = jnp.concatenate([inv, factor, jnp.zeros((6, tokens), jnp.float32)])
    columns = standing(rows)
    inv, factor = columns[:, 0:1], columns[:, 1:2]
    copies = []
    for j in range(len(PIECES) - 1):
        part = slice(PIECES[j] * tokens // 8, PIECES[j + 1] * tokens // 8)
        scaled = scaled_ref[part, :features].astype(jnp.float32)
        values = input_ref[part, :].astype(jnp.float32)
        held[part, :] = (scaled * inv[part] - values * factor[part]).astype(held.dtype)
        copies.append(pltpu.make_async_copy(held.at[part], out_ref.at[part], sems.at[j]))
        copies[-1].start()
    for copy in copies:
        copy.wait()


def finish(scaled, inputs, sums):
    return pl.pallas_call(
        finish_kernel,
        out_shape=pltpu.HBM(inputs.shape, jnp.bfloat16),
        in_specs=vmem_specs(2 + len(sums)),
        out_specs=pl.BlockSpec(memory_space=pltpu.HBM),
        scratch_shapes=[
            pltpu.VMEM(inputs.shape, jnp.bfloat16),
            pltpu.SemaphoreType.DMA((len(PIECES) - 1,)),
        ],
        compiler_params=pltpu.CompilerParams(vmem_limit_bytes=8 << 20),
    )(*map(in_vmem, (scaled, inputs, *sums)))


FAR, NEAR, SIDE = 4, 2, 1
ORDER = ((0, SIDE), (SIDE, 0))
LINE = ((FAR | NEAR, FAR), (FAR, FAR | NEAR), (NEAR, NEAR))
EARLY = 2


def handed_over(block, sections, count, distance, mask):
    route = [
        ((s - distance) % sections * count + (i ^ mask), s * count + i)
        for s in range(sections)
        for i in range(count)
    ]
    return lax.ppermute(block, ("section", "tp"), route)


def fetched(block, sections, count, masks):
    half = sections // 2
    route = []
    for s in range(sections):
        mask = masks[s // half] if count == 8 else 0
        for i in range(count):
            route.append(((s + half) % sections * count + (i ^ mask), s * count + i))
    return lax.ppermute(block, ("section", "tp"), route)


def gathered(pair, axis, sections, count):
    if count != 8:
        return [lax.all_gather(pair[0], axis)], lambda place: place
    half = sections // 2
    blocks = [pair]
    for masks in LINE:
        route = [
            (s * count + (i ^ masks[s // half]), s * count + i)
            for s in range(sections)
            for i in range(count)
        ]
        blocks.append(lax.ppermute(pair, ("section", axis), route))

    def head_of(place):
        lower, upper = ((0, 0), *LINE)[place // 2]
        mask = lower + (lax.axis_index("section") // half) * (upper - lower)
        return lax.axis_index(axis) ^ mask ^ (place % 2 * SIDE)

    return blocks, head_of


def per_device(grad_attn, w_value, probs_own, probs_spare, evicted, layer_input, gain):
    sections, count = lax.axis_size("section"), lax.axis_size("tp")
    packed, spares, taken = pack(probs_own[0, 0], grad_attn[0, 0], probs_spare[0, 0], evicted)
    half = sections // 2
    packs = [packed, swapped(packed, "tp", SIDE)] if count == 8 else [packed]
    spares = [fetched(spares, sections, count, masks) for masks in ORDER[: len(packs)]]
    weights, inputs = w_value[0], layer_input[0]
    next_input = passed_along(inputs, "section", -1)
    reach, own_reach = reach_of(weights, inputs, gain, packs[-1])
    if count == 8:
        reaches = [own_reach, swapped(reach, "tp", SIDE)]
        reaches[1], next_input = lax.optimization_barrier((reaches[1], next_input))
    else:
        reaches = [lax.psum(own_reach, "tp")]
    pair = value_gradients(taken, spares, packs, lambda: lax.axis_index("section") >= half)
    blocks, head_of = gathered(pair, "tp", sections, count)
    soon, late = (blocks[:EARLY], blocks[EARLY:]) if count == 8 else ([], blocks)
    early = [project_early(head_of, soon, weights)] if soon else []
    joined = join(head_of, soon, reaches)
    first = sum(block.shape[0] for block in soon)
    scaled, sums = project(head_of, first, late, joined, weights, inputs, gain, early)
    next_scaled = passed_along(scaled, "section", -1)
    next_sums = []
    for mask in (NEAR, FAR | NEAR, FAR) if count == 8 else ():
        next_sums.append(handed_over(sums, sections, count, -1, mask))
    return finish(next_scaled, next_input, next_sums)[None]


def solution(mesh):
    in_specs = (
        P("section", "tp", None, None),
        P("section", "tp", None),
        P("section", "tp", None, None),
        P("section", "tp", None, None),
        P("section", None),
        P("section", None, "tp"),
        P("section", "tp"),
    )
    out_specs = P("section", None, "tp")
    return jax.shard_map(
        per_device, mesh=mesh, in_specs=in_specs, out_specs=out_specs, check_vma=False
    )
```

```python
import functools

import jax
import jax.numpy as jnp
from jax import lax
from jax.experimental import pallas as pl
from jax.experimental.pallas import tpu as pltpu
from jax.sharding import PartitionSpec as P

D = 12288
LANES = 128
PIECES = (0, 3, 5, 7, 8)
EXTRA = 16
HIDES = pl.CostEstimate(flops=1 << 35, bytes_accessed=1 << 25, transcendentals=0)


def passed_along(block, axis, distance):
    devices = range(lax.axis_size(axis))
    route = [((i - distance) % len(devices), i) for i in devices]
    return lax.ppermute(block, axis, route)


def swapped(block, axis, mask):
    return lax.ppermute(block, axis, [(i ^ mask, i) for i in range(lax.axis_size(axis))])


def in_vmem(array):
    return pltpu.with_memory_space_constraint(array, pltpu.VMEM)


def in_hbm(array):
    return pltpu.with_memory_space_constraint(array, pltpu.HBM)


def vmem_specs(count):
    return [pl.BlockSpec(memory_space=pltpu.VMEM)] * count


def as_row(column):
    return jnp.broadcast_to(column, (column.shape[0], column.shape[0])).T[:1]


def standing(rows):
    tokens = rows.shape[1]
    return jnp.concatenate([rows, jnp.zeros((tokens - rows.shape[0], tokens), rows.dtype)]).T


def split(values):
    parts = []
    for _ in range(3):
        parts.append(values.astype(jnp.bfloat16).astype(jnp.float32))
        values = values - parts[-1]
    return parts


def own_ratio(squares, inner):
    return inner / jnp.maximum(squares, 1e-30)


def as_parts(row):
    rest = jnp.zeros((EXTRA - 3, row.shape[1]), jnp.float32)
    return jnp.concatenate(split(row) + [rest]).astype(jnp.bfloat16)


def pack_kernel(own_ref, grad_ref, spare_ref, evicted_ref, *refs):
    out_ref, spare_out, taken_ref, flags, sems = refs
    copies = [
        pltpu.make_async_copy(evicted_ref, flags, sems.at[0]),
        pltpu.make_async_copy(own_ref, out_ref.at[0], sems.at[1]),
        pltpu.make_async_copy(grad_ref, out_ref.at[1], sems.at[2]),
        pltpu.make_async_copy(spare_ref, spare_out, sems.at[3]),
    ]
    for copy in copies:
        copy.start()
    copies[0].wait()
    tiles = evicted_ref.shape[1]
    rows = taken_ref.shape[0] // tiles
    for tile in range(tiles):
        part = pl.ds(tile * rows, rows)
        taken = jnp.full((rows, taken_ref.shape[1]), flags[0, tile], jnp.int32)
        taken_ref[part, :] = taken.astype(jnp.float32).astype(taken_ref.dtype)
    for copy in copies[1:]:
        copy.wait()


def pack(own, grad, spare, evicted):
    return pl.pallas_call(
        pack_kernel,
        out_shape=(
            pltpu.VMEM((2, *own.shape), own.dtype),
            pltpu.VMEM(spare.shape, spare.dtype),
            pltpu.VMEM(own.shape, own.dtype),
        ),
        in_specs=[pl.BlockSpec(memory_space=pltpu.HBM)] * 4,
        out_specs=tuple(vmem_specs(3)),
        scratch_shapes=[
            pltpu.SMEM(evicted.shape, evicted.dtype),
            pltpu.SemaphoreType.DMA((4,)),
        ],
        cost_estimate=HIDES,
        compiler_params=pltpu.CompilerParams(vmem_limit_bytes=4 << 20),
    )(*map(in_hbm, (own, grad, spare, evicted)))


def reach_kernel(weight_ref, input_ref, gain_ref, first_ref, reach_ref, own_ref):
    del first_ref
    tokens, features = input_ref.shape
    values = input_ref[...].astype(jnp.float32)
    reach_ref[tokens:, :] = jnp.zeros_like(reach_ref[tokens:, :])
    squares = as_row(jnp.sum(values * values, axis=1, keepdims=True))
    reach_ref[tokens:, :tokens] = as_parts(squares)
    gained = (values * gain_ref[...]).astype(jnp.bfloat16)
    reach = jnp.dot(gained, weight_ref[...], preferred_element_type=jnp.float32)
    reach_ref[:tokens, :] = reach.astype(reach_ref.dtype)
    own_ref[:tokens, :] = reach
    own_ref[tokens:, :] = reach_ref[tokens:, :].astype(own_ref.dtype)


def reach_of(weights, inputs, gain, first):
    return pl.pallas_call(
        reach_kernel,
        out_shape=tuple(
            pltpu.VMEM((inputs.shape[0] + EXTRA, weights.shape[1]), dtype)
            for dtype in (jnp.bfloat16, jnp.float32)
        ),
        in_specs=vmem_specs(4),
        out_specs=tuple(vmem_specs(2)),
        cost_estimate=HIDES,
        compiler_params=pltpu.CompilerParams(vmem_limit_bytes=8 << 20),
    )(*map(in_vmem, (weights, inputs, gain, first)))


def mix_kernel(upper, taken_ref, *refs):
    out_ref = refs[-1]
    taken = taken_ref[...]
    count = out_ref.shape[0]
    spares = [refs[count - 1 - j][...] for j in range(count)]
    if count == 2:
        swap = upper()
        spares = [jnp.where(swap, spares[1], spares[0]), jnp.where(swap, spares[0], spares[1])]
    for j in range(count):
        packed_ref = refs[len(refs) - 2 - j]
        out_ref[j] = lax.dot_general(
            packed_ref[0] * (1 - taken) + spares[j] * taken,
            packed_ref[1],
            (((0,), (0,)), ((), ())),
            preferred_element_type=jnp.float32,
        ).astype(out_ref.dtype)


def value_gradients(taken, spares, packs, upper):
    return pl.pallas_call(
        functools.partial(mix_kernel, upper),
        out_shape=pltpu.VMEM((len(packs), *spares[0].shape), jnp.bfloat16),
        in_specs=vmem_specs(1 + 2 * len(packs)),
        out_specs=pl.BlockSpec(memory_space=pltpu.VMEM),
        cost_estimate=HIDES,
        compiler_params=pltpu.CompilerParams(vmem_limit_bytes=4 << 20),
    )(*map(in_vmem, (taken, *spares[::-1], *packs[::-1])))


def column_tile(features):
    return 256 if features % 256 == 0 else features


def fill(flat, blocks, head_of, first):
    groups = []
    for ref in blocks:
        count = ref.shape[0]
        for j in range(count):
            start = pl.multiple_of(head_of(first + j) * LANES, LANES)
            flat[:, pl.ds(start, LANES)] = ref[j]
        width = count * LANES
        groups.append((pl.multiple_of(head_of(first) // count * width, width), width))
        first += count
    return groups


def times_weights(flat, groups, weight_ref, part):
    products = [
        lax.dot_general(
            flat[:, pl.ds(start, width)],
            weight_ref[part, pl.ds(start, width)],
            (((1,), (1,)), ((), ())),
            preferred_element_type=jnp.float32,
        )
        for start, width in groups
    ]
    return sum(products[1:], products[0])


def early_kernel(head_of, *refs):
    *blocks, weight_ref, out_ref, flat = refs
    groups = fill(flat, blocks, head_of, 0)
    features = weight_ref.shape[0]
    tile = column_tile(features)
    for start in range(0, features, tile):
        part = pl.ds(start, tile)
        out_ref[:, part] = times_weights(flat, groups, weight_ref, part)


def project_early(head_of, blocks, weights):
    tokens = blocks[0].shape[1]
    return pl.pallas_call(
        functools.partial(early_kernel, head_of),
        out_shape=pltpu.VMEM((tokens, weights.shape[0]), jnp.float32),
        in_specs=vmem_specs(len(blocks) + 1),
        out_specs=pl.BlockSpec(memory_space=pltpu.VMEM),
        scratch_shapes=[pltpu.VMEM((tokens, weights.shape[1]), jnp.bfloat16)],
        cost_estimate=pl.CostEstimate(flops=1 << 16, bytes_accessed=1 << 12, transcendentals=0),
        compiler_params=pltpu.CompilerParams(vmem_limit_bytes=16 << 20),
    )(*map(in_vmem, (*blocks, weights)))


def inner_part(head_of, blocks, first, reach_ref):
    total = None
    for ref in blocks:
        for j in range(ref.shape[0]):
            start = pl.multiple_of(head_of(first) * LANES, LANES)
            part = ref[j].astype(jnp.float32) * reach_ref[:, pl.ds(start, LANES)]
            total = part if total is None else total + part
            first += 1
    return total


def join_kernel(head_of, sizes, *refs):
    blocks, reach_refs = refs[: sizes[0]], refs[sizes[0] : sizes[0] + sizes[1]]
    reach_ref, folded_ref, squares_ref = refs[sizes[0] + sizes[1] :]
    tokens = reach_ref.shape[0]
    reach_ref[...] = sum(ref[:tokens, :].astype(jnp.float32) for ref in reach_refs)
    squares = sum(ref[tokens:, :tokens].astype(jnp.float32) for ref in reach_refs)
    squares_ref[...] = jnp.sum(squares, axis=0, keepdims=True)
    if blocks:
        folded_ref[...] = inner_part(head_of, blocks, 0, reach_ref)
    else:
        folded_ref[...] = jnp.zeros_like(folded_ref)


def join(head_of, blocks, reaches):
    tokens, columns = reaches[0].shape[0] - EXTRA, reaches[0].shape[1]
    operands = (*blocks, *reaches)
    return pl.pallas_call(
        functools.partial(join_kernel, head_of, (len(blocks), len(reaches))),
        out_shape=(
            pltpu.VMEM((tokens, columns), jnp.float32),
            pltpu.VMEM((tokens, LANES), jnp.float32),
            pltpu.VMEM((1, tokens), jnp.float32),
        ),
        in_specs=vmem_specs(len(operands)),
        out_specs=tuple(vmem_specs(3)),
        cost_estimate=pl.CostEstimate(flops=1 << 16, bytes_accessed=1 << 12, transcendentals=0),
        compiler_params=pltpu.CompilerParams(vmem_limit_bytes=8 << 20),
    )(*map(in_vmem, operands))


def project_kernel(head_of, first, count, *refs):
    blocks, rest = refs[:count], refs[count:]
    reach_ref, folded_ref, squares_ref, weight_ref, input_ref, gain_ref, *rest = rest
    *early_refs, scaled_ref, sums_ref, flat = rest
    tokens, features = input_ref.shape
    groups = fill(flat, blocks, head_of, first)
    squares = squares_ref[...]
    folded = folded_ref[...] + inner_part(head_of, blocks, first, reach_ref)
    inner = as_row(jnp.sum(folded, axis=1, keepdims=True))
    sums_ref[:1, :] = squares
    sums_ref[1:, :] = inner
    rho = own_ratio(squares, inner)
    rows = [*split(squares), *split(inner), rho, jnp.zeros((1, tokens), jnp.float32)]
    columns = standing(jnp.concatenate(rows))
    scaled_ref[:, features:] = columns.astype(scaled_ref.dtype)
    rho = columns[:, 6:7]
    tile = column_tile(features)
    for start in range(0, features, tile):
        part = pl.ds(start, tile)
        grad_normed = times_weights(flat, groups, weight_ref, part)
        for ref in early_refs:
            grad_normed = grad_normed + ref[:, part]
        values = input_ref[:, part].astype(jnp.float32)
        scaled_ref[:, part] = (grad_normed * gain_ref[:, part] - values * rho).astype(
            scaled_ref.dtype
        )


def project(head_of, first, blocks, joined, weights, inputs, gain, early):
    tokens, features = inputs.shape
    operands = (*blocks, *joined, weights, inputs, gain, *early)
    return pl.pallas_call(
        functools.partial(project_kernel, head_of, first, len(blocks)),
        out_shape=(
            pltpu.VMEM((tokens, features + LANES), jnp.bfloat16),
            pltpu.VMEM((2, tokens), jnp.float32),
        ),
        in_specs=vmem_specs(len(operands)),
        out_specs=tuple(vmem_specs(2)),
        scratch_shapes=[pltpu.VMEM((tokens, weights.shape[1]), jnp.bfloat16)],
        cost_estimate=HIDES,
        compiler_params=pltpu.CompilerParams(vmem_limit_bytes=16 << 20),
    )(*map(in_vmem, operands))


def finish_kernel(scaled_ref, input_ref, *refs):
    *sums_refs, out_ref, held, sems = refs
    tokens, features = input_ref.shape
    extra = scaled_ref[:, features:].astype(jnp.float32).T
    squares = extra[0:1] + extra[1:2] + extra[2:3]
    inner = extra[3:4] + extra[4:5] + extra[5:6]
    rho = own_ratio(squares, inner)
    for ref in sums_refs:
        squares = squares + ref[:1, :]
        inner = inner + ref[1:, :]
    inv = 1.0 / jnp.sqrt(squares / D + 1e-05)
    factor = inner * (inv * inv * inv) / D - inv * rho
    rows = jnp.concatenate([inv, factor, jnp.zeros((6, tokens), jnp.float32)])
    columns = standing(rows)
    inv, factor = columns[:, 0:1], columns[:, 1:2]
    copies = []
    for j in range(len(PIECES) - 1):
        part = slice(PIECES[j] * tokens // 8, PIECES[j + 1] * tokens // 8)
        scaled = scaled_ref[part, :features].astype(jnp.float32)
        values = input_ref[part, :].astype(jnp.float32)
        held[part, :] = (scaled * inv[part] - values * factor[part]).astype(held.dtype)
        copies.append(pltpu.make_async_copy(held.at[part], out_ref.at[part], sems.at[j]))
        copies[-1].start()
    for copy in copies:
        copy.wait()


def finish(scaled, inputs, sums):
    return pl.pallas_call(
        finish_kernel,
        out_shape=pltpu.HBM(inputs.shape, jnp.bfloat16),
        in_specs=vmem_specs(2 + len(sums)),
        out_specs=pl.BlockSpec(memory_space=pltpu.HBM),
        scratch_shapes=[
            pltpu.VMEM(inputs.shape, jnp.bfloat16),
            pltpu.SemaphoreType.DMA((len(PIECES) - 1,)),
        ],
        compiler_params=pltpu.CompilerParams(vmem_limit_bytes=8 << 20),
    )(*map(in_vmem, (scaled, inputs, *sums)))


FAR, NEAR, SIDE = 4, 2, 1
ORDER = ((0, SIDE), (SIDE, 0))
LINE = ((FAR, FAR | NEAR), (FAR | NEAR, FAR), (NEAR, NEAR))
EARLY = 2


def handed_over(block, sections, count, distance, mask):
    route = [
        ((s - distance) % sections * count + (i ^ mask), s * count + i)
        for s in range(sections)
        for i in range(count)
    ]
    return lax.ppermute(block, ("section", "tp"), route)


def fetched(block, sections, count, masks):
    half = sections // 2
    route = []
    for s in range(sections):
        mask = masks[s // half] if count == 8 else 0
        for i in range(count):
            route.append(((s + half) % sections * count + (i ^ mask), s * count + i))
    return lax.ppermute(block, ("section", "tp"), route)


def gathered(pair, axis, sections, count):
    if count != 8:
        return [lax.all_gather(pair[0], axis)], lambda place: place
    half = sections // 2
    blocks = [pair]
    for masks in LINE:
        route = [
            (s * count + (i ^ masks[s // half]), s * count + i)
            for s in range(sections)
            for i in range(count)
        ]
        blocks.append(lax.ppermute(pair, ("section", axis), route))

    def head_of(place):
        lower, upper = ((0, 0), *LINE)[place // 2]
        mask = lower + (lax.axis_index("section") // half) * (upper - lower)
        return lax.axis_index(axis) ^ mask ^ (place % 2 * SIDE)

    return blocks, head_of


def per_device(grad_attn, w_value, probs_own, probs_spare, evicted, layer_input, gain):
    sections, count = lax.axis_size("section"), lax.axis_size("tp")
    packed, spares, taken = pack(probs_own[0, 0], grad_attn[0, 0], probs_spare[0, 0], evicted)
    half = sections // 2
    packs = [packed, swapped(packed, "tp", SIDE)] if count == 8 else [packed]
    spares = [fetched(spares, sections, count, masks) for masks in ORDER[: len(packs)]]
    weights, inputs = w_value[0], layer_input[0]
    next_input = passed_along(inputs, "section", -1)
    reach, own_reach = reach_of(weights, inputs, gain, packs[-1])
    if count == 8:
        reaches = [own_reach, swapped(reach, "tp", SIDE)]
        reaches[1], next_input = lax.optimization_barrier((reaches[1], next_input))
    else:
        reaches = [lax.psum(own_reach, "tp")]
    pair = value_gradients(taken, spares, packs, lambda: lax.axis_index("section") >= half)
    blocks, head_of = gathered(pair, "tp", sections, count)
    soon, late = (blocks[:EARLY], blocks[EARLY:]) if count == 8 else ([], blocks)
    early = [project_early(head_of, soon, weights)] if soon else []
    joined = join(head_of, soon, reaches)
    first = sum(block.shape[0] for block in soon)
    scaled, sums = project(head_of, first, late, joined, weights, inputs, gain, early)
    next_scaled = passed_along(scaled, "section", -1)
    next_sums = []
    for mask in (NEAR, FAR | NEAR, FAR) if count == 8 else ():
        next_sums.append(handed_over(sums, sections, count, -1, mask))
    return finish(next_scaled, next_input, next_sums)[None]


def solution(mesh):
    in_specs = (
        P("section", "tp", None, None),
        P("section", "tp", None),
        P("section", "tp", None, None),
        P("section", "tp", None, None),
        P("section", None),
        P("section", None, "tp"),
        P("section", "tp"),
    )
    out_specs = P("section", None, "tp")
    return jax.shard_map(
        per_device, mesh=mesh, in_specs=in_specs, out_specs=out_specs, check_vma=False
    )
```

```python
import functools

import jax
import jax.numpy as jnp
from jax import lax
from jax.experimental import pallas as pl
from jax.experimental.pallas import tpu as pltpu
from jax.sharding import PartitionSpec as P

D = 12288
LANES = 128
PIECES = (0, 1, 2, 3, 4, 5, 6, 7, 8)
EXTRA = 16
HIDES = pl.CostEstimate(flops=1 << 35, bytes_accessed=1 << 25, transcendentals=0)


def passed_along(block, axis, distance):
    devices = range(lax.axis_size(axis))
    route = [((i - distance) % len(devices), i) for i in devices]
    return lax.ppermute(block, axis, route)


def swapped(block, axis, mask):
    return lax.ppermute(block, axis, [(i ^ mask, i) for i in range(lax.axis_size(axis))])


def in_vmem(array):
    return pltpu.with_memory_space_constraint(array, pltpu.VMEM)


def in_hbm(array):
    return pltpu.with_memory_space_constraint(array, pltpu.HBM)


def vmem_specs(count):
    return [pl.BlockSpec(memory_space=pltpu.VMEM)] * count


def as_row(column):
    return jnp.broadcast_to(column, (column.shape[0], column.shape[0])).T[:1]


def standing(rows):
    tokens = rows.shape[1]
    return jnp.concatenate([rows, jnp.zeros((tokens - rows.shape[0], tokens), rows.dtype)]).T


def split(values):
    parts = []
    for _ in range(3):
        parts.append(values.astype(jnp.bfloat16).astype(jnp.float32))
        values = values - parts[-1]
    return parts


def own_ratio(squares, inner):
    return inner / jnp.maximum(squares, 1e-30)


def as_parts(row):
    rest = jnp.zeros((EXTRA - 3, row.shape[1]), jnp.float32)
    return jnp.concatenate(split(row) + [rest]).astype(jnp.bfloat16)


def pack_kernel(own_ref, grad_ref, spare_ref, evicted_ref, *refs):
    out_ref, spare_out, taken_ref, flags, sems = refs
    copies = [
        pltpu.make_async_copy(evicted_ref, flags, sems.at[0]),
        pltpu.make_async_copy(own_ref, out_ref.at[0], sems.at[1]),
        pltpu.make_async_copy(grad_ref, out_ref.at[1], sems.at[2]),
        pltpu.make_async_copy(spare_ref, spare_out, sems.at[3]),
    ]
    for copy in copies:
        copy.start()
    copies[0].wait()
    tiles = evicted_ref.shape[1]
    rows = taken_ref.shape[0] // tiles
    for tile in range(tiles):
        part = pl.ds(tile * rows, rows)
        taken = jnp.full((rows, taken_ref.shape[1]), flags[0, tile], jnp.int32)
        taken_ref[part, :] = taken.astype(jnp.float32).astype(taken_ref.dtype)
    for copy in copies[1:]:
        copy.wait()


def pack(own, grad, spare, evicted):
    return pl.pallas_call(
        pack_kernel,
        out_shape=(
            pltpu.VMEM((2, *own.shape), own.dtype),
            pltpu.VMEM(spare.shape, spare.dtype),
            pltpu.VMEM(own.shape, own.dtype),
        ),
        in_specs=[pl.BlockSpec(memory_space=pltpu.HBM)] * 4,
        out_specs=tuple(vmem_specs(3)),
        scratch_shapes=[
            pltpu.SMEM(evicted.shape, evicted.dtype),
            pltpu.SemaphoreType.DMA((4,)),
        ],
        cost_estimate=HIDES,
        compiler_params=pltpu.CompilerParams(vmem_limit_bytes=4 << 20),
    )(*map(in_hbm, (own, grad, spare, evicted)))


def reach_kernel(weight_ref, input_ref, gain_ref, first_ref, reach_ref, own_ref):
    del first_ref
    tokens, features = input_ref.shape
    values = input_ref[...].astype(jnp.float32)
    reach_ref[tokens:, :] = jnp.zeros_like(reach_ref[tokens:, :])
    squares = as_row(jnp.sum(values * values, axis=1, keepdims=True))
    reach_ref[tokens:, :tokens] = as_parts(squares)
    gained = (values * gain_ref[...]).astype(jnp.bfloat16)
    reach = jnp.dot(gained, weight_ref[...], preferred_element_type=jnp.float32)
    reach_ref[:tokens, :] = reach.astype(reach_ref.dtype)
    own_ref[:tokens, :] = reach
    own_ref[tokens:, :] = reach_ref[tokens:, :].astype(own_ref.dtype)


def reach_of(weights, inputs, gain, first):
    return pl.pallas_call(
        reach_kernel,
        out_shape=tuple(
            pltpu.VMEM((inputs.shape[0] + EXTRA, weights.shape[1]), dtype)
            for dtype in (jnp.bfloat16, jnp.float32)
        ),
        in_specs=vmem_specs(4),
        out_specs=tuple(vmem_specs(2)),
        cost_estimate=HIDES,
        compiler_params=pltpu.CompilerParams(vmem_limit_bytes=8 << 20),
    )(*map(in_vmem, (weights, inputs, gain, first)))


def mix_kernel(upper, taken_ref, *refs):
    out_ref = refs[-1]
    taken = taken_ref[...]
    count = out_ref.shape[0]
    spares = [refs[count - 1 - j][...] for j in range(count)]
    if count == 2:
        swap = upper()
        spares = [jnp.where(swap, spares[1], spares[0]), jnp.where(swap, spares[0], spares[1])]
    for j in range(count):
        packed_ref = refs[len(refs) - 2 - j]
        out_ref[j] = lax.dot_general(
            packed_ref[0] * (1 - taken) + spares[j] * taken,
            packed_ref[1],
            (((0,), (0,)), ((), ())),
            preferred_element_type=jnp.float32,
        ).astype(out_ref.dtype)


def value_gradients(taken, spares, packs, upper):
    return pl.pallas_call(
        functools.partial(mix_kernel, upper),
        out_shape=pltpu.VMEM((len(packs), *spares[0].shape), jnp.bfloat16),
        in_specs=vmem_specs(1 + 2 * len(packs)),
        out_specs=pl.BlockSpec(memory_space=pltpu.VMEM),
        cost_estimate=HIDES,
        compiler_params=pltpu.CompilerParams(vmem_limit_bytes=4 << 20),
    )(*map(in_vmem, (taken, *spares[::-1], *packs[::-1])))


def column_tile(features):
    return 256 if features % 256 == 0 else features


def fill(flat, blocks, head_of, first):
    groups = []
    for ref in blocks:
        count = ref.shape[0]
        for j in range(count):
            start = pl.multiple_of(head_of(first + j) * LANES, LANES)
            flat[:, pl.ds(start, LANES)] = ref[j]
        width = count * LANES
        groups.append((pl.multiple_of(head_of(first) // count * width, width), width))
        first += count
    return groups


def times_weights(flat, groups, weight_ref, part):
    products = [
        lax.dot_general(
            flat[:, pl.ds(start, width)],
            weight_ref[part, pl.ds(start, width)],
            (((1,), (1,)), ((), ())),
            preferred_element_type=jnp.float32,
        )
        for start, width in groups
    ]
    return sum(products[1:], products[0])


def early_kernel(head_of, *refs):
    *blocks, weight_ref, out_ref, flat = refs
    groups = fill(flat, blocks, head_of, 0)
    features = weight_ref.shape[0]
    tile = column_tile(features)
    for start in range(0, features, tile):
        part = pl.ds(start, tile)
        out_ref[:, part] = times_weights(flat, groups, weight_ref, part)


def project_early(head_of, blocks, weights):
    tokens = blocks[0].shape[1]
    return pl.pallas_call(
        functools.partial(early_kernel, head_of),
        out_shape=pltpu.VMEM((tokens, weights.shape[0]), jnp.float32),
        in_specs=vmem_specs(len(blocks) + 1),
        out_specs=pl.BlockSpec(memory_space=pltpu.VMEM),
        scratch_shapes=[pltpu.VMEM((tokens, weights.shape[1]), jnp.bfloat16)],
        cost_estimate=pl.CostEstimate(flops=1 << 16, bytes_accessed=1 << 12, transcendentals=0),
        compiler_params=pltpu.CompilerParams(vmem_limit_bytes=16 << 20),
    )(*map(in_vmem, (*blocks, weights)))


def inner_part(head_of, blocks, first, reach_ref):
    total = None
    for ref in blocks:
        for j in range(ref.shape[0]):
            start = pl.multiple_of(head_of(first) * LANES, LANES)
            part = ref[j].astype(jnp.float32) * reach_ref[:, pl.ds(start, LANES)]
            total = part if total is None else total + part
            first += 1
    return total


def join_kernel(head_of, sizes, *refs):
    blocks, reach_refs = refs[: sizes[0]], refs[sizes[0] : sizes[0] + sizes[1]]
    reach_ref, folded_ref, squares_ref = refs[sizes[0] + sizes[1] :]
    tokens = reach_ref.shape[0]
    reach_ref[...] = sum(ref[:tokens, :].astype(jnp.float32) for ref in reach_refs)
    squares = sum(ref[tokens:, :tokens].astype(jnp.float32) for ref in reach_refs)
    squares_ref[...] = jnp.sum(squares, axis=0, keepdims=True)
    if blocks:
        folded_ref[...] = inner_part(head_of, blocks, 0, reach_ref)
    else:
        folded_ref[...] = jnp.zeros_like(folded_ref)


def join(head_of, blocks, reaches):
    tokens, columns = reaches[0].shape[0] - EXTRA, reaches[0].shape[1]
    operands = (*blocks, *reaches)
    return pl.pallas_call(
        functools.partial(join_kernel, head_of, (len(blocks), len(reaches))),
        out_shape=(
            pltpu.VMEM((tokens, columns), jnp.float32),
            pltpu.VMEM((tokens, LANES), jnp.float32),
            pltpu.VMEM((1, tokens), jnp.float32),
        ),
        in_specs=vmem_specs(len(operands)),
        out_specs=tuple(vmem_specs(3)),
        cost_estimate=pl.CostEstimate(flops=1 << 16, bytes_accessed=1 << 12, transcendentals=0),
        compiler_params=pltpu.CompilerParams(vmem_limit_bytes=8 << 20),
    )(*map(in_vmem, operands))


def project_kernel(head_of, first, count, *refs):
    blocks, rest = refs[:count], refs[count:]
    reach_ref, folded_ref, squares_ref, weight_ref, input_ref, gain_ref, *rest = rest
    *early_refs, scaled_ref, sums_ref, flat = rest
    tokens, features = input_ref.shape
    groups = fill(flat, blocks, head_of, first)
    squares = squares_ref[...]
    folded = folded_ref[...] + inner_part(head_of, blocks, first, reach_ref)
    inner = as_row(jnp.sum(folded, axis=1, keepdims=True))
    sums_ref[:1, :] = squares
    sums_ref[1:, :] = inner
    rho = own_ratio(squares, inner)
    rows = [*split(squares), *split(inner), rho, jnp.zeros((1, tokens), jnp.float32)]
    columns = standing(jnp.concatenate(rows))
    scaled_ref[:, features:] = columns.astype(scaled_ref.dtype)
    rho = columns[:, 6:7]
    tile = column_tile(features)
    for start in range(0, features, tile):
        part = pl.ds(start, tile)
        grad_normed = times_weights(flat, groups, weight_ref, part)
        for ref in early_refs:
            grad_normed = grad_normed + ref[:, part]
        values = input_ref[:, part].astype(jnp.float32)
        scaled_ref[:, part] = (grad_normed * gain_ref[:, part] - values * rho).astype(
            scaled_ref.dtype
        )


def project(head_of, first, blocks, joined, weights, inputs, gain, early):
    tokens, features = inputs.shape
    operands = (*blocks, *joined, weights, inputs, gain, *early)
    return pl.pallas_call(
        functools.partial(project_kernel, head_of, first, len(blocks)),
        out_shape=(
            pltpu.VMEM((tokens, features + LANES), jnp.bfloat16),
            pltpu.VMEM((2, tokens), jnp.float32),
        ),
        in_specs=vmem_specs(len(operands)),
        out_specs=tuple(vmem_specs(2)),
        scratch_shapes=[pltpu.VMEM((tokens, weights.shape[1]), jnp.bfloat16)],
        cost_estimate=HIDES,
        compiler_params=pltpu.CompilerParams(vmem_limit_bytes=16 << 20),
    )(*map(in_vmem, operands))


def finish_kernel(scaled_ref, input_ref, *refs):
    *sums_refs, out_ref, held, sems = refs
    tokens, features = input_ref.shape
    extra = scaled_ref[:, features:].astype(jnp.float32).T
    squares = extra[0:1] + extra[1:2] + extra[2:3]
    inner = extra[3:4] + extra[4:5] + extra[5:6]
    rho = own_ratio(squares, inner)
    for ref in sums_refs:
        squares = squares + ref[:1, :]
        inner = inner + ref[1:, :]
    inv = 1.0 / jnp.sqrt(squares / D + 1e-05)
    factor = inner * (inv * inv * inv) / D - inv * rho
    rows = jnp.concatenate([inv, factor, jnp.zeros((6, tokens), jnp.float32)])
    columns = standing(rows)
    inv, factor = columns[:, 0:1], columns[:, 1:2]
    copies = []
    for j in range(len(PIECES) - 1):
        part = slice(PIECES[j] * tokens // 8, PIECES[j + 1] * tokens // 8)
        scaled = scaled_ref[part, :features].astype(jnp.float32)
        values = input_ref[part, :].astype(jnp.float32)
        held[part, :] = (scaled * inv[part] - values * factor[part]).astype(held.dtype)
        copies.append(pltpu.make_async_copy(held.at[part], out_ref.at[part], sems.at[j]))
        copies[-1].start()
    for copy in copies:
        copy.wait()


def finish(scaled, inputs, sums):
    return pl.pallas_call(
        finish_kernel,
        out_shape=pltpu.HBM(inputs.shape, jnp.bfloat16),
        in_specs=vmem_specs(2 + len(sums)),
        out_specs=pl.BlockSpec(memory_space=pltpu.HBM),
        scratch_shapes=[
            pltpu.VMEM(inputs.shape, jnp.bfloat16),
            pltpu.SemaphoreType.DMA((len(PIECES) - 1,)),
        ],
        compiler_params=pltpu.CompilerParams(vmem_limit_bytes=8 << 20),
    )(*map(in_vmem, (scaled, inputs, *sums)))


FAR, NEAR, SIDE = 4, 2, 1
ORDER = ((0, SIDE), (SIDE, 0))
LINE = (FAR | NEAR, FAR, NEAR)
EARLY = 2


def handed_over(block, sections, count, distance, mask):
    route = [
        ((s - distance) % sections * count + (i ^ mask), s * count + i)
        for s in range(sections)
        for i in range(count)
    ]
    return lax.ppermute(block, ("section", "tp"), route)


def fetched(block, sections, count, masks):
    half = sections // 2
    route = []
    for s in range(sections):
        mask = masks[s // half] if count == 8 else 0
        for i in range(count):
            route.append(((s + half) % sections * count + (i ^ mask), s * count + i))
    return lax.ppermute(block, ("section", "tp"), route)


def gathered(pair, axis):
    if lax.axis_size(axis) != 8:
        return [lax.all_gather(pair[0], axis)], lambda place: place
    blocks = [pair] + [swapped(pair, axis, mask) for mask in LINE]
    masks = [far | side for far in (0, *LINE) for side in (0, SIDE)]

    def head_of(place):
        return lax.axis_index(axis) ^ masks[place]

    return blocks, head_of


def per_device(grad_attn, w_value, probs_own, probs_spare, evicted, layer_input, gain):
    sections, count = lax.axis_size("section"), lax.axis_size("tp")
    packed, spares, taken = pack(probs_own[0, 0], grad_attn[0, 0], probs_spare[0, 0], evicted)
    half = sections // 2
    packs = [packed, swapped(packed, "tp", SIDE)] if count == 8 else [packed]
    spares = [fetched(spares, sections, count, masks) for masks in ORDER[: len(packs)]]
    weights, inputs = w_value[0], layer_input[0]
    next_input = passed_along(inputs, "section", -1)
    reach, own_reach = reach_of(weights, inputs, gain, packs[-1])
    if count == 8:
        reaches = [own_reach, swapped(reach, "tp", SIDE)]
        reaches[1], next_input = lax.optimization_barrier((reaches[1], next_input))
    else:
        reaches = [lax.psum(own_reach, "tp")]
    pair = value_gradients(taken, spares, packs, lambda: lax.axis_index("section") >= half)
    blocks, head_of = gathered(pair, "tp")
    soon, late = (blocks[:EARLY], blocks[EARLY:]) if count == 8 else ([], blocks)
    early = [project_early(head_of, soon, weights)] if soon else []
    joined = join(head_of, soon, reaches)
    first = sum(block.shape[0] for block in soon)
    scaled, sums = project(head_of, first, late, joined, weights, inputs, gain, early)
    next_scaled = passed_along(scaled, "section", -1)
    next_sums = []
    for mask in (NEAR, FAR | NEAR, FAR) if count == 8 else ():
        next_sums.append(handed_over(sums, sections, count, -1, mask))
    return finish(next_scaled, next_input, next_sums)[None]


def solution(mesh):
    in_specs = (
        P("section", "tp", None, None),
        P("section", "tp", None),
        P("section", "tp", None, None),
        P("section", "tp", None, None),
        P("section", None),
        P("section", None, "tp"),
        P("section", "tp"),
    )
    out_specs = P("section", None, "tp")
    return jax.shard_map(
        per_device, mesh=mesh, in_specs=in_specs, out_specs=out_specs, check_vma=False
    )
```

```python
import functools

import jax
import jax.numpy as jnp
from jax import lax
from jax.experimental import pallas as pl
from jax.experimental.pallas import tpu as pltpu
from jax.sharding import PartitionSpec as P

D = 12288
LANES = 128
PIECES = (0, 1, 2, 3, 4, 5, 6, 7, 8)
EXTRA = 16
SHORT = pl.CostEstimate(flops=1 << 16, bytes_accessed=1 << 12, transcendentals=0)
HIDES = pl.CostEstimate(flops=1 << 35, bytes_accessed=1 << 25, transcendentals=0)


def passed_along(block, axis, distance):
    devices = range(lax.axis_size(axis))
    route = [((i - distance) % len(devices), i) for i in devices]
    return lax.ppermute(block, axis, route)


def swapped(block, axis, mask):
    return lax.ppermute(block, axis, [(i ^ mask, i) for i in range(lax.axis_size(axis))])


def in_vmem(array):
    return pltpu.with_memory_space_constraint(array, pltpu.VMEM)


def in_hbm(array):
    return pltpu.with_memory_space_constraint(array, pltpu.HBM)


def vmem_specs(count):
    return [pl.BlockSpec(memory_space=pltpu.VMEM)] * count


def as_row(column):
    return jnp.broadcast_to(column, (column.shape[0], column.shape[0])).T[:1]


def standing(rows):
    tokens = rows.shape[1]
    return jnp.concatenate([rows, jnp.zeros((tokens - rows.shape[0], tokens), rows.dtype)]).T


def split(values):
    parts = []
    for _ in range(3):
        parts.append(values.astype(jnp.bfloat16).astype(jnp.float32))
        values = values - parts[-1]
    return parts


def own_ratio(squares, inner):
    return inner / jnp.maximum(squares, 1e-30)


def as_parts(row):
    rest = jnp.zeros((EXTRA - 3, row.shape[1]), jnp.float32)
    return jnp.concatenate(split(row) + [rest]).astype(jnp.bfloat16)


def pack_kernel(own_ref, grad_ref, spare_ref, evicted_ref, *refs):
    out_ref, spare_out, taken_ref, flags, sems = refs
    copies = [
        pltpu.make_async_copy(evicted_ref, flags, sems.at[0]),
        pltpu.make_async_copy(own_ref, out_ref.at[0], sems.at[1]),
        pltpu.make_async_copy(grad_ref, out_ref.at[1], sems.at[2]),
        pltpu.make_async_copy(spare_ref, spare_out, sems.at[3]),
    ]
    for copy in copies:
        copy.start()
    copies[0].wait()
    tiles = evicted_ref.shape[1]
    rows = taken_ref.shape[0] // tiles
    for tile in range(tiles):
        part = pl.ds(tile * rows, rows)
        taken = jnp.full((rows, taken_ref.shape[1]), flags[0, tile], jnp.int32)
        taken_ref[part, :] = taken.astype(jnp.float32).astype(taken_ref.dtype)
    for copy in copies[1:]:
        copy.wait()


def pack(own, grad, spare, evicted):
    return pl.pallas_call(
        pack_kernel,
        out_shape=(
            pltpu.VMEM((2, *own.shape), own.dtype),
            pltpu.VMEM(spare.shape, spare.dtype),
            pltpu.VMEM(own.shape, own.dtype),
        ),
        in_specs=[pl.BlockSpec(memory_space=pltpu.HBM)] * 4,
        out_specs=tuple(vmem_specs(3)),
        scratch_shapes=[
            pltpu.SMEM(evicted.shape, evicted.dtype),
            pltpu.SemaphoreType.DMA((4,)),
        ],
        cost_estimate=HIDES,
        compiler_params=pltpu.CompilerParams(vmem_limit_bytes=4 << 20),
    )(*map(in_hbm, (own, grad, spare, evicted)))


def reach_kernel(weight_ref, input_ref, gain_ref, reach_ref, own_ref):
    tokens, features = input_ref.shape
    values = input_ref[...].astype(jnp.float32)
    reach_ref[tokens:, :] = jnp.zeros_like(reach_ref[tokens:, :])
    squares = as_row(jnp.sum(values * values, axis=1, keepdims=True))
    reach_ref[tokens:, :tokens] = as_parts(squares)
    gained = (values * gain_ref[...]).astype(jnp.bfloat16)
    reach = jnp.dot(gained, weight_ref[...], preferred_element_type=jnp.float32)
    reach_ref[:tokens, :] = reach.astype(reach_ref.dtype)
    own_ref[:tokens, :] = reach
    own_ref[tokens:, :] = reach_ref[tokens:, :].astype(own_ref.dtype)


def reach_of(weights, inputs, gain):
    return pl.pallas_call(
        reach_kernel,
        out_shape=tuple(
            pltpu.VMEM((inputs.shape[0] + EXTRA, weights.shape[1]), dtype)
            for dtype in (jnp.bfloat16, jnp.float32)
        ),
        in_specs=vmem_specs(3),
        out_specs=tuple(vmem_specs(2)),
        cost_estimate=SHORT,
        compiler_params=pltpu.CompilerParams(vmem_limit_bytes=8 << 20),
    )(*map(in_vmem, (weights, inputs, gain)))


def mix_kernel(upper, taken_ref, *refs):
    out_ref = refs[-1]
    taken = taken_ref[...]
    count = out_ref.shape[0]
    spares = [refs[j][...] for j in range(count)]
    if count == 2:
        swap = upper()
        spares = [jnp.where(swap, spares[1], spares[0]), jnp.where(swap, spares[0], spares[1])]
    for j in range(count):
        packed_ref = refs[len(refs) - 2 - j]
        out_ref[j] = lax.dot_general(
            packed_ref[0] * (1 - taken) + spares[j] * taken,
            packed_ref[1],
            (((0,), (0,)), ((), ())),
            preferred_element_type=jnp.float32,
        ).astype(out_ref.dtype)


def value_gradients(taken, spares, packs, upper):
    return pl.pallas_call(
        functools.partial(mix_kernel, upper),
        out_shape=pltpu.VMEM((len(packs), *spares[0].shape), jnp.bfloat16),
        in_specs=vmem_specs(1 + 2 * len(packs)),
        out_specs=pl.BlockSpec(memory_space=pltpu.VMEM),
        cost_estimate=HIDES,
        compiler_params=pltpu.CompilerParams(vmem_limit_bytes=4 << 20),
    )(*map(in_vmem, (taken, *spares, *packs[::-1])))


def column_tile(features):
    return 256 if features % 256 == 0 else features


def fill(flat, blocks, head_of, first):
    groups = []
    for ref in blocks:
        count = ref.shape[0]
        for j in range(count):
            start = pl.multiple_of(head_of(first + j) * LANES, LANES)
            flat[:, pl.ds(start, LANES)] = ref[j]
        width = count * LANES
        groups.append((pl.multiple_of(head_of(first) // count * width, width), width))
        first += count
    return groups


def times_weights(flat, groups, weight_ref, part):
    products = [
        lax.dot_general(
            flat[:, pl.ds(start, width)],
            weight_ref[part, pl.ds(start, width)],
            (((1,), (1,)), ((), ())),
            preferred_element_type=jnp.float32,
        )
        for start, width in groups
    ]
    return sum(products[1:], products[0])


def early_kernel(head_of, *refs):
    *blocks, weight_ref, out_ref, flat = refs
    groups = fill(flat, blocks, head_of, 0)
    features = weight_ref.shape[0]
    tile = column_tile(features)
    for start in range(0, features, tile):
        part = pl.ds(start, tile)
        out_ref[:, part] = times_weights(flat, groups, weight_ref, part)


def project_early(head_of, blocks, weights):
    tokens = blocks[0].shape[1]
    return pl.pallas_call(
        functools.partial(early_kernel, head_of),
        out_shape=pltpu.VMEM((tokens, weights.shape[0]), jnp.float32),
        in_specs=vmem_specs(len(blocks) + 1),
        out_specs=pl.BlockSpec(memory_space=pltpu.VMEM),
        scratch_shapes=[pltpu.VMEM((tokens, weights.shape[1]), jnp.bfloat16)],
        cost_estimate=SHORT,
        compiler_params=pltpu.CompilerParams(vmem_limit_bytes=16 << 20),
    )(*map(in_vmem, (*blocks, weights)))


def inner_part(head_of, blocks, first, reach_ref):
    total = None
    for ref in blocks:
        for j in range(ref.shape[0]):
            start = pl.multiple_of(head_of(first) * LANES, LANES)
            part = ref[j].astype(jnp.float32) * reach_ref[:, pl.ds(start, LANES)]
            total = part if total is None else total + part
            first += 1
    return total


def join_kernel(head_of, sizes, *refs):
    blocks, reach_refs = refs[: sizes[0]], refs[sizes[0] : sizes[0] + sizes[1]]
    reach_ref, folded_ref, squares_ref = refs[sizes[0] + sizes[1] :]
    tokens = reach_ref.shape[0]
    reach_ref[...] = sum(ref[:tokens, :].astype(jnp.float32) for ref in reach_refs)
    squares = sum(ref[tokens:, :tokens].astype(jnp.float32) for ref in reach_refs)
    squares_ref[...] = jnp.sum(squares, axis=0, keepdims=True)
    if blocks:
        folded_ref[...] = inner_part(head_of, blocks, 0, reach_ref)
    else:
        folded_ref[...] = jnp.zeros_like(folded_ref)


def join(head_of, blocks, reaches):
    tokens, columns = reaches[0].shape[0] - EXTRA, reaches[0].shape[1]
    operands = (*blocks, *reaches)
    return pl.pallas_call(
        functools.partial(join_kernel, head_of, (len(blocks), len(reaches))),
        out_shape=(
            pltpu.VMEM((tokens, columns), jnp.float32),
            pltpu.VMEM((tokens, LANES), jnp.float32),
            pltpu.VMEM((1, tokens), jnp.float32),
        ),
        in_specs=vmem_specs(len(operands)),
        out_specs=tuple(vmem_specs(3)),
        cost_estimate=SHORT,
        compiler_params=pltpu.CompilerParams(vmem_limit_bytes=8 << 20),
    )(*map(in_vmem, operands))


def project_kernel(head_of, first, count, *refs):
    blocks, rest = refs[:count], refs[count:]
    reach_ref, folded_ref, squares_ref, weight_ref, input_ref, gain_ref, *rest = rest
    *early_refs, scaled_ref, sums_ref, flat = rest
    tokens, features = input_ref.shape
    groups = fill(flat, blocks, head_of, first)
    squares = squares_ref[...]
    folded = folded_ref[...] + inner_part(head_of, blocks, first, reach_ref)
    inner = as_row(jnp.sum(folded, axis=1, keepdims=True))
    sums_ref[:1, :] = squares
    sums_ref[1:, :] = inner
    rho = own_ratio(squares, inner)
    rows = [*split(squares), *split(inner), rho, jnp.zeros((1, tokens), jnp.float32)]
    columns = standing(jnp.concatenate(rows))
    scaled_ref[:, features:] = columns.astype(scaled_ref.dtype)
    rho = columns[:, 6:7]
    tile = column_tile(features)
    for start in range(0, features, tile):
        part = pl.ds(start, tile)
        grad_normed = times_weights(flat, groups, weight_ref, part)
        for ref in early_refs:
            grad_normed = grad_normed + ref[:, part]
        values = input_ref[:, part].astype(jnp.float32)
        scaled_ref[:, part] = (grad_normed * gain_ref[:, part] - values * rho).astype(
            scaled_ref.dtype
        )


def project(head_of, first, blocks, joined, weights, inputs, gain, early):
    tokens, features = inputs.shape
    operands = (*blocks, *joined, weights, inputs, gain, *early)
    return pl.pallas_call(
        functools.partial(project_kernel, head_of, first, len(blocks)),
        out_shape=(
            pltpu.VMEM((tokens, features + LANES), jnp.bfloat16),
            pltpu.VMEM((2, tokens), jnp.float32),
        ),
        in_specs=vmem_specs(len(operands)),
        out_specs=tuple(vmem_specs(2)),
        scratch_shapes=[pltpu.VMEM((tokens, weights.shape[1]), jnp.bfloat16)],
        cost_estimate=HIDES,
        compiler_params=pltpu.CompilerParams(vmem_limit_bytes=16 << 20),
    )(*map(in_vmem, operands))


def finish_kernel(scaled_ref, input_ref, *refs):
    *sums_refs, out_ref, held, sems = refs
    tokens, features = input_ref.shape
    extra = scaled_ref[:, features:].astype(jnp.float32).T
    squares = extra[0:1] + extra[1:2] + extra[2:3]
    inner = extra[3:4] + extra[4:5] + extra[5:6]
    rho = own_ratio(squares, inner)
    for ref in sums_refs:
        squares = squares + ref[:1, :]
        inner = inner + ref[1:, :]
    inv = 1.0 / jnp.sqrt(squares / D + 1e-05)
    factor = inner * (inv * inv * inv) / D - inv * rho
    rows = jnp.concatenate([inv, factor, jnp.zeros((6, tokens), jnp.float32)])
    columns = standing(rows)
    inv, factor = columns[:, 0:1], columns[:, 1:2]
    copies = []
    for j in range(len(PIECES) - 1):
        part = slice(PIECES[j] * tokens // 8, PIECES[j + 1] * tokens // 8)
        scaled = scaled_ref[part, :features].astype(jnp.float32)
        values = input_ref[part, :].astype(jnp.float32)
        held[part, :] = (scaled * inv[part] - values * factor[part]).astype(held.dtype)
        copies.append(pltpu.make_async_copy(held.at[part], out_ref.at[part], sems.at[j]))
        copies[-1].start()
    for copy in copies:
        copy.wait()


def finish(scaled, inputs, sums):
    return pl.pallas_call(
        finish_kernel,
        out_shape=pltpu.HBM(inputs.shape, jnp.bfloat16),
        in_specs=vmem_specs(2 + len(sums)),
        out_specs=pl.BlockSpec(memory_space=pltpu.HBM),
        scratch_shapes=[
            pltpu.VMEM(inputs.shape, jnp.bfloat16),
            pltpu.SemaphoreType.DMA((len(PIECES) - 1,)),
        ],
        compiler_params=pltpu.CompilerParams(vmem_limit_bytes=8 << 20),
    )(*map(in_vmem, (scaled, inputs, *sums)))


FAR, NEAR, SIDE = 4, 2, 1
ORDER = ((0, SIDE), (SIDE, 0))
LINE = (FAR | NEAR, NEAR, FAR)
EARLY = 2


def handed_over(block, sections, count, distance, mask):
    route = [
        ((s - distance) % sections * count + (i ^ mask), s * count + i)
        for s in range(sections)
        for i in range(count)
    ]
    return lax.ppermute(block, ("section", "tp"), route)


def fetched(block, sections, count, masks):
    half = sections // 2
    route = []
    for s in range(sections):
        mask = masks[s // half] if count == 8 else 0
        for i in range(count):
            route.append(((s + half) % sections * count + (i ^ mask), s * count + i))
    return lax.ppermute(block, ("section", "tp"), route)


def gathered(pair, axis):
    if lax.axis_size(axis) != 8:
        return [lax.all_gather(pair[0], axis)], lambda place: place
    blocks = [pair] + [swapped(pair, axis, mask) for mask in LINE]
    masks = [far | side for far in (0, *LINE) for side in (0, SIDE)]

    def head_of(place):
        return lax.axis_index(axis) ^ masks[place]

    return blocks, head_of


def per_device(grad_attn, w_value, probs_own, probs_spare, evicted, layer_input, gain):
    sections, count = lax.axis_size("section"), lax.axis_size("tp")
    packed, spares, taken = pack(probs_own[0, 0], grad_attn[0, 0], probs_spare[0, 0], evicted)
    half = sections // 2
    packs = [packed, swapped(packed, "tp", SIDE)] if count == 8 else [packed]
    spares = [fetched(spares, sections, count, masks) for masks in ORDER[: len(packs)]]
    weights, inputs = w_value[0], layer_input[0]
    next_input = passed_along(inputs, "section", -1)
    reach, own_reach = reach_of(weights, inputs, gain)
    if count == 8:
        reach, packs[1] = lax.optimization_barrier((reach, packs[1]))
        reaches = [own_reach, swapped(reach, "tp", SIDE)]
        reaches[1], next_input = lax.optimization_barrier((reaches[1], next_input))
    else:
        reaches = [lax.psum(own_reach, "tp")]
    pair = value_gradients(taken, spares, packs, lambda: lax.axis_index("section") >= half)
    blocks, head_of = gathered(pair, "tp")
    soon, late = (blocks[:EARLY], blocks[EARLY:]) if count == 8 else ([], blocks)
    early = [project_early(head_of, soon, weights)] if soon else []
    joined = join(head_of, soon, reaches)
    first = sum(block.shape[0] for block in soon)
    scaled, sums = project(head_of, first, late, joined, weights, inputs, gain, early)
    next_scaled = passed_along(scaled, "section", -1)
    next_sums = []
    for mask in (NEAR, FAR, FAR | NEAR) if count == 8 else ():
        next_sums.append(handed_over(sums, sections, count, -1, mask))
    return finish(next_scaled, next_input, next_sums)[None]


def solution(mesh):
    in_specs = (
        P("section", "tp", None, None),
        P("section", "tp", None),
        P("section", "tp", None, None),
        P("section", "tp", None, None),
        P("section", None),
        P("section", None, "tp"),
        P("section", "tp"),
    )
    out_specs = P("section", None, "tp")
    return jax.shard_map(
        per_device, mesh=mesh, in_specs=in_specs, out_specs=out_specs, check_vma=False
    )
```
